32 devices in a mesh: dp: 8 (over z, y), rows: 4 (over x, core).
Axes of the slice: x: 2, y: 2, z: 4, core: 2. Of those that a mesh axis runs over, the one named last changes fastest.
Arguments:
- latents: float32 [16, 32, 32, 3], P('dp', 'rows'), may hold values from -6 to 6
- target_noise: float32 [16, 32, 32, 3], P('dp', 'rows'), may hold values from -6 to 6
- labels: int32 [16], P('dp'), may hold values from 0 to 999
- timesteps: int32 [16], P('dp'), may hold values from 0 to 999
- orient: int32 [16], P('dp'), may hold values from 0 to 1, as said below
- extent: int32 [16], P('dp'), may hold values from 8 to 32, as said below
- mat_params: float32 [12860416], P(('dp', 'rows'))
- mat_first: float32 [12860416], P(('dp', 'rows'))
- mat_second: float32 [12860416], P(('dp', 'rows')), as said below
- mat_ema: float32 [12860416], P(('dp', 'rows'))
- vec_params: float32 [16928], P(('dp', 'rows'))
- vec_first: float32 [16928], P(('dp', 'rows'))
- vec_second: float32 [16928], P(('dp', 'rows')), as said below
- vec_ema: float32 [16928], P(('dp', 'rows'))
Outputs:
- new_mat_params: float32 [12860416], P(('dp', 'rows'))
- new_mat_first: float32 [12860416], P(('dp', 'rows'))
- new_mat_second: float32 [12860416], P(('dp', 'rows'))
- new_mat_ema: float32 [12860416], P(('dp', 'rows'))
- new_vec_params: float32 [16928], P(('dp', 'rows'))
- new_vec_first: float32 [16928], P(('dp', 'rows'))
- new_vec_second: float32 [16928], P(('dp', 'rows'))
- new_vec_ema: float32 [16928], P(('dp', 'rows'))
- grad_norm: float32 [], replicated
- loss_sum: float32 [], replicated
- pixel_count: float32 [], replicated
The draws below stay inside these ranges and needn't reach their ends.
Inputs may be any that keep to these rules, and one draw needn't show every extreme that they name: `orient`: 1 where the image's bucket is portrait (long side along the rows), 0 for landscape; in each aligned group of 2 images one is portrait with extent 32. `extent`: valid length along the bucket's orientation (rows for portrait, columns for landscape); the other side is 16. `mat_second`: positive. `vec_second`: positive.
All inputs are finite; a program needn't handle non-finite values.
Results may differ from the reference program's by a relative error of at most 0.0006.
The reference program's roundings to bfloat16 on the way count: a program that leaves them out, or rounds other values in their place, can miss the bound.
Values may be sent and summed in bfloat16 or wider, within the bound.
No kernel may reach another device: no remote copies, remote signals or barrier semaphores. Data moves between devices by JAX's collectives and lax.ppermute only.
A program may use at most 320 MiB of HBM per device.

```python
import math
import jax
import jax.numpy as jnp
from jax import lax

C = 512
HEADS = 8
DHEAD = 64
FFI = 2048
TE = 256
TD = 1024
NCLS = 1000
LC = 3
GROUPS = 32
SIDE = 32
NT = 1000
STEP = 10
IMG_DEV = 2
IMAGES = 16
PM = 12860416
PV = 16899
MATS = 12860416
VECS = 16928


def mat_layout_drawn():
    return [('w_in', 9 * LC, C), ('w_t1', TE, TD), ('w_t2', TD, TD), ('w_tp', TD, C), ('table', NCLS, C), ('w_c1', 9 * C, C), ('w_c2', 9 * C, C), ('w_pin', C, C), ('w_qkv', C, 3 * C), ('w_o', C, C), ('w_cq', C, C), ('w_ckv', C, 2 * C), ('w_co', C, C), ('w_ff1', C, 2 * FFI), ('w_ff2', FFI, C), ('w_pout', C, C), ('w_out', 9 * C, LC)]


def vec_layout_drawn():
    names = ['b_tp', 'b_in', 'g1', 'bb1', 'b_c1', 'g2', 'bb2', 'b_c2', 'g3', 'bb3', 'b_pin', 'n1g', 'n1b', 'b_o', 'n2g', 'n2b', 'b_co', 'n3g', 'n3b']
    return [('b_t1', TD), ('b_t2', TD)] + [(name_one, C) for name_one in names] + [('b_ff1', 2 * FFI), ('b_ff2', C), ('b_pout', C), ('b_out', LC)]


def image_layout(key):
    group_total = IMAGES // IMG_DEV
    image_index = jnp.arange(IMAGES)
    group_of = image_index // IMG_DEV
    orient = jax.random.randint(jax.random.fold_in(key, 11), (IMAGES,), 0, 2)
    base_len = SIDE // 4 + SIDE * 9 // 16 * group_of // max(group_total - 1, 1)
    extent = jnp.minimum(base_len + jax.random.randint(jax.random.fold_in(key, 12), (IMAGES,), 0, SIDE // 5 + 1), SIDE)
    chosen_slot = jax.random.randint(jax.random.fold_in(key, 13), (group_total,), 0, IMG_DEV)
    chosen = image_index % IMG_DEV == chosen_slot[group_of]
    return (jnp.where(chosen, 1, orient).astype(jnp.int32), jnp.where(chosen, SIDE, extent).astype(jnp.int32))


def draw_orient(key, part):
    return image_layout(key)[0]


def draw_extent(key, part):
    return image_layout(key)[1]


def unit_draw(key, length):
    return jax.random.normal(key, (length,), jnp.float32)


def mat_scales():
    pieces = []
    for record in mat_layout_drawn():
        factor = record[1] ** (-0.5)
        if record[0] == 'table':
            factor = 1.0
        if record[0] == 'w_o':
            factor = 4.0 * record[1] ** (-0.5)
        pieces.append(jnp.full((record[1] * record[2],), factor, jnp.float32))
    pieces.append(jnp.full((MATS - PM,), C ** (-0.5), jnp.float32))
    return jnp.concatenate(pieces)


def vec_shape():
    centers = []
    spreads = []
    for record in vec_layout_drawn():
        is_gain = record[0] in ('g1', 'g2', 'g3', 'n1g', 'n2g', 'n3g')
        center = 1.0 if is_gain else 0.0
        if record[0] == 'b_out':
            center = 1.0
        centers.append(jnp.full((record[1],), center, jnp.float32))
        spreads.append(jnp.full((record[1],), 0.1 if is_gain else 0.2, jnp.float32))
    centers.append(jnp.zeros((VECS - PV,), jnp.float32))
    spreads.append(jnp.full((VECS - PV,), 0.2, jnp.float32))
    return (jnp.concatenate(centers), jnp.concatenate(spreads))


def moment_first(key, length, grad_size):
    magnitude = jnp.exp(jax.random.uniform(jax.random.fold_in(key, 21), (length,), jnp.float32, math.log(0.5), math.log(2.0)))
    sign_vec = jnp.where(jax.random.bernoulli(jax.random.fold_in(key, 22), 0.5, (length,)), 1.0, -1.0)
    return sign_vec * magnitude * (0.1 / 0.9) * grad_size


def moment_second(key, length, grad_size):
    magnitude = jnp.exp(jax.random.uniform(jax.random.fold_in(key, 23), (length,), jnp.float32, math.log(0.5), math.log(8.0)))
    return magnitude * (0.001 / 0.999) * grad_size * grad_size


def draw_mat_params(key, part):
    return unit_draw(jax.random.fold_in(key, 1), MATS) * mat_scales()


def draw_mat_ema(key, part):
    return unit_draw(jax.random.fold_in(key, 2), MATS) * mat_scales()


def draw_mat_first(key, part):
    return moment_first(jax.random.fold_in(key, 3), MATS, 0.1 / math.sqrt(PM + PV))


def draw_mat_second(key, part):
    return moment_second(jax.random.fold_in(key, 4), MATS, 0.1 / math.sqrt(PM + PV))


def draw_vec_params(key, part):
    centers, spreads = vec_shape()
    return centers + spreads * unit_draw(jax.random.fold_in(key, 5), VECS)


def draw_vec_ema(key, part):
    centers, spreads = vec_shape()
    return centers + spreads * unit_draw(jax.random.fold_in(key, 6), VECS)


def draw_vec_first(key, part):
    return moment_first(jax.random.fold_in(key, 7), VECS, 0.4 / math.sqrt(PM + PV))


def draw_vec_second(key, part):
    return moment_second(jax.random.fold_in(key, 8), VECS, 0.4 / math.sqrt(PM + PV))


def place_ends(drawn, own_key, smallest, top_value):
    shape = drawn.shape
    index_at = [jax.random.randint(jax.random.fold_in(own_key, axis), (), 0, shape[axis]) for axis in range(len(shape))]
    drawn = drawn.at[tuple(index_at)].set(smallest)
    longest = shape.index(max(shape))
    index_at[longest] = (index_at[longest] + 1) % shape[longest]
    return drawn.at[tuple(index_at)].set(top_value)


def shard_levels(rng, shape, split, smallest, high):
    factor_of, own = 1.0, jax.random.fold_in(rng, 6)
    for dim, parts in split:
        heights = jnp.exp(jax.random.uniform(jax.random.fold_in(own, dim), (parts,), jnp.float32, smallest / len(split), high / len(split)))
        factor_of = factor_of * jnp.repeat(heights, shape[dim] // parts).reshape([-1 if axis == dim else 1 for axis in range(len(shape))])
    return factor_of


def noise(stream_key, shape, width, bound, shards=(), kind=jnp.bfloat16):
    array = jax.random.normal(stream_key, shape, jnp.float32) * width
    if len(shards) > 0:
        array = shard_levels(stream_key, shape, shards, -0.22, 0.18) * array
    return jnp.clip(array, min=-bound, max=bound).astype(kind)


def setup_inputs(seed: int = 0) -> dict:
    arg_keys = jax.random.split(jax.random.key(seed), 15)
    return {
        "latents": noise(arg_keys[0], (IMAGES, SIDE, SIDE, LC), 1.0, 6.0, ((0, 8), (1, 4)), jnp.float32),
        "target_noise": noise(arg_keys[1], (IMAGES, SIDE, SIDE, LC), 1.0, 6.0, ((0, 8), (1, 4)), jnp.float32),
        "labels": place_ends(jax.random.randint(arg_keys[2], (IMAGES,), 0, NCLS), jax.random.fold_in(arg_keys[2], 1), 0, NCLS - 1).astype(jnp.int32),
        "timesteps": place_ends(jax.random.randint(arg_keys[3], (IMAGES,), 0, NT), jax.random.fold_in(arg_keys[3], 1), 0, NT - 1).astype(jnp.int32),
        "orient": draw_orient(jax.random.fold_in(arg_keys[14], 71), 0),
        "extent": draw_extent(jax.random.fold_in(arg_keys[14], 71), 0),
        "mat_params": draw_mat_params(jax.random.fold_in(arg_keys[14], 71), 0),
        "mat_first": draw_mat_first(jax.random.fold_in(arg_keys[14], 71), 0),
        "mat_second": draw_mat_second(jax.random.fold_in(arg_keys[14], 71), 0),
        "mat_ema": draw_mat_ema(jax.random.fold_in(arg_keys[14], 71), 0),
        "vec_params": draw_vec_params(jax.random.fold_in(arg_keys[14], 71), 0),
        "vec_first": draw_vec_first(jax.random.fold_in(arg_keys[14], 71), 0),
        "vec_second": draw_vec_second(jax.random.fold_in(arg_keys[14], 71), 0),
        "vec_ema": draw_vec_ema(jax.random.fold_in(arg_keys[14], 71), 0),
    }


@jax.custom_vjp
def low(v):
    return lax.optimization_barrier(v.astype(jnp.bfloat16)).astype(jnp.float32)

@jax.custom_vjp
def low_back(v):
    return v

def low_keep(v):
    return (low(v), None)

def low_pass(kept, grad):
    return (grad,)

def back_keep(v):
    return (v, None)

def back_low(kept, grad):
    return (low(grad),)
low.defvjp(low_keep, low_pass)
low_back.defvjp(back_keep, back_low)
tap_offsets = [(-1, -1), (-1, 0), (-1, 1), (0, -1), (0, 0), (0, 1), (1, -1), (1, 0), (1, 1)]
eps_group = 1e-06
eps_layer = 1e-05
beta_first = 0.00085
beta_last = 0.012
adam_one = 0.9
adam_two = 0.999
adam_eps = 1e-08
learn_rate = 0.05
weight_decay = 0.01
ema_ceiling = 0.9999
clip_norm = 0.1
highest = lax.Precision.HIGHEST

def mat_layout():
    return [('w_in', 9 * LC, C), ('w_t1', TE, TD), ('w_t2', TD, TD), ('w_tp', TD, C), ('table', NCLS, C), ('w_c1', 9 * C, C), ('w_c2', 9 * C, C), ('w_pin', C, C), ('w_qkv', C, 3 * C), ('w_o', C, C), ('w_cq', C, C), ('w_ckv', C, 2 * C), ('w_co', C, C), ('w_ff1', C, 2 * FFI), ('w_ff2', FFI, C), ('w_pout', C, C), ('w_out', 9 * C, LC)]

def vec_layout():
    names = ['b_tp', 'b_in', 'g1', 'bb1', 'b_c1', 'g2', 'bb2', 'b_c2', 'g3', 'bb3', 'b_pin', 'n1g', 'n1b', 'b_o', 'n2g', 'n2b', 'b_co', 'n3g', 'n3b']
    return [('b_t1', TD), ('b_t2', TD)] + [(name_one, C) for name_one in names] + [('b_ff1', 2 * FFI), ('b_ff2', C), ('b_pout', C), ('b_out', LC)]

def unpack(joined, layout):
    pieces = {}
    start_at = 0
    for record in layout:
        length = 1
        for extent_one in record[1:]:
            length = length * extent_one
        pieces[record[0]] = joined[start_at:start_at + length].reshape(record[1:])
        start_at = start_at + length
    return pieces

def matmul(left, right):
    return jnp.dot(left, right, precision=highest, preferred_element_type=jnp.float32)

def conv_full(values, weight):
    inner_dim = values.shape[-1]
    padded = jnp.pad(values, ((1, 1), (1, 1), (0, 0)))
    result = jnp.zeros((SIDE, SIDE, weight.shape[1]), jnp.float32)
    for tap_index, (row_off, col_off) in enumerate(tap_offsets):
        window = padded[1 + row_off:1 + row_off + SIDE, 1 + col_off:1 + col_off + SIDE, :]
        result = result + jnp.einsum('rwc,co->rwo', window, weight[tap_index * inner_dim:(tap_index + 1) * inner_dim], precision=highest)
    return result

def group_norm(values, valid_map, gain_vec, bias_vec):
    grouped = values.reshape(SIDE, SIDE, GROUPS, C // GROUPS)
    spread = valid_map[:, :, None, None]
    denominator = jnp.sum(valid_map) * (C // GROUPS)
    mean_val = lax.optimization_barrier(jnp.sum(grouped * spread, axis=(0, 1, 3))) / denominator
    centered = grouped - mean_val[None, None, :, None]
    var_val = lax.optimization_barrier(jnp.sum(centered * centered * spread, axis=(0, 1, 3))) / denominator
    normed = (centered * lax.rsqrt(var_val + eps_group)[None, None, :, None]).reshape(SIDE, SIDE, C)
    return normed * gain_vec + bias_vec

def layer_norm(values, gain_vec, bias_vec):
    mean_val = lax.optimization_barrier(jnp.mean(values, axis=-1, keepdims=True))
    centered = values - mean_val
    var_val = lax.optimization_barrier(jnp.mean(centered * centered, axis=-1, keepdims=True))
    return centered * lax.rsqrt(var_val + eps_layer) * gain_vec + bias_vec

def image_mask(orient_one, extent_one):
    row_idx = jnp.arange(SIDE)[:, None]
    col_idx = jnp.arange(SIDE)[None, :]
    short_side = SIDE // 2
    portrait = (row_idx < extent_one) & (col_idx < short_side)
    landscape = (row_idx < short_side) & (col_idx < extent_one)
    return jnp.where(orient_one == 1, portrait, landscape).astype(jnp.float32)

def noise_level(step_value):
    steps_idx = jnp.arange(NT).astype(jnp.float32)
    root_beta = math.sqrt(beta_first) + (math.sqrt(beta_last) - math.sqrt(beta_first)) * steps_idx / (NT - 1)
    log_keep = jnp.log1p(-root_beta * root_beta)
    return jnp.exp(jnp.sum(jnp.where(jnp.arange(NT) <= step_value, log_keep, 0.0)))

def time_embed(step_value):
    frequency = jnp.exp(-math.log(10000.0) * jnp.arange(TE // 2).astype(jnp.float32) / (TE // 2))
    angles = step_value.astype(jnp.float32) * frequency
    return jnp.concatenate([jnp.cos(angles), jnp.sin(angles)])

def image_loss(params, latent, noise_img, label, step_value, orient_one, extent_one):
    valid_map = image_mask(orient_one, extent_one)
    valid_cube = valid_map[:, :, None]
    noise_share = noise_level(step_value)
    noisy_input = valid_cube * (jnp.sqrt(noise_share) * latent + jnp.sqrt(1.0 - noise_share) * noise_img)
    embed_in = low(time_embed(step_value))[None, :]
    hidden_one = low(jax.nn.silu(low_back(matmul(embed_in, params['w_t1'])) + params['b_t1']))
    hidden_two = low(jax.nn.silu(low_back(matmul(hidden_one, params['w_t2'])) + params['b_t2']))
    time_vec = low_back(matmul(hidden_two, params['w_tp']))[0] + params['b_tp']
    class_vec = matmul(jax.nn.one_hot(label, NCLS, dtype=jnp.float32)[None, :], params['table'])[0]
    state_zero = valid_cube * (low_back(conv_full(low(noisy_input), params['w_in'])) + params['b_in'])
    act_one = low(valid_cube * jax.nn.silu(group_norm(state_zero, valid_map, params['g1'], params['bb1'])))
    conv_one = valid_cube * (low_back(conv_full(act_one, params['w_c1'])) + params['b_c1'] + time_vec)
    act_two = low(valid_cube * jax.nn.silu(group_norm(conv_one, valid_map, params['g2'], params['bb2'])))
    state_one = state_zero + valid_cube * (low_back(conv_full(act_two, params['w_c2'])) + params['b_c2'])
    token_in = low(group_norm(state_one, valid_map, params['g3'], params['bb3'])).reshape(SIDE * SIDE, C)
    resid_zero = low_back(matmul(token_in, params['w_pin'])) + params['b_pin']
    packed = low(low_back(matmul(low(layer_norm(resid_zero, params['n1g'], params['n1b'])), params['w_qkv'])))
    packed = packed.reshape(SIDE * SIDE, 3, HEADS, DHEAD)
    raw_scores = low_back(jnp.einsum('qhd,khd->hqk', packed[:, 0], packed[:, 1], precision=highest)) * 0.125
    key_valid = valid_map.reshape(-1)
    scores = jnp.where(key_valid[None, None, :] > 0, raw_scores, -1e+30)
    attn_prob = jax.nn.softmax(scores, axis=-1)
    attended = low(low_back(jnp.einsum('hqk,khd->qhd', low(attn_prob), packed[:, 2], precision=highest)))
    resid_one = resid_zero + low_back(matmul(attended.reshape(SIDE * SIDE, C), params['w_o'])) + params['b_o']
    cross_query = low(low_back(matmul(low(layer_norm(resid_one, params['n2g'], params['n2b'])), params['w_cq'])))
    cross_query = cross_query.reshape(SIDE * SIDE, HEADS, DHEAD)
    context = low(jnp.stack([class_vec, time_vec]))
    context_kv = low(low_back(matmul(context, params['w_ckv'])))
    context_key = context_kv[:, :C].reshape(2, HEADS, DHEAD)
    context_value = context_kv[:, C:].reshape(2, HEADS, DHEAD)
    cross_prob = jax.nn.softmax(jnp.einsum('thd,jhd->thj', cross_query, context_key, precision=highest) * 0.125, axis=-1)
    cross_out = low(low_back(jnp.einsum('thj,jhd->thd', cross_prob, context_value, precision=highest))).reshape(SIDE * SIDE, C)
    resid_two = resid_one + low_back(matmul(cross_out, params['w_co'])) + params['b_co']
    projected = low_back(matmul(low(layer_norm(resid_two, params['n3g'], params['n3b'])), params['w_ff1'])) + params['b_ff1']
    gated = low(projected[:, :FFI] * jax.nn.gelu(projected[:, FFI:], approximate=False))
    resid_three = resid_two + low_back(matmul(gated, params['w_ff2'])) + params['b_ff2']
    branch = low_back(matmul(low(resid_three), params['w_pout'])) + params['b_pout']
    state_two = state_one + valid_cube * branch.reshape(SIDE, SIDE, C)
    predicted = low_back(conv_full(low(state_two), params['w_out'])) + params['b_out']
    residual_err = predicted - noise_img
    return jnp.sum(valid_cube * residual_err * residual_err)

def adam_update(params, first_mom, second, gradient, decay_rate):
    first_new = adam_one * first_mom + (1.0 - adam_one) * gradient
    second_new = adam_two * second + (1.0 - adam_two) * gradient * gradient
    step_size = first_new / (1.0 - adam_one ** STEP) / (jnp.sqrt(second_new / (1.0 - adam_two ** STEP)) + adam_eps)
    return (params - learn_rate * (step_size + decay_rate * params), first_new, second_new)

def reference(latents, target_noise, labels, timesteps, orient, extent, mat_params, mat_first, mat_second, mat_ema, vec_params, vec_first, vec_second, vec_ema):

    def loss_total(mat_flat, vec_flat):
        params = unpack(low(mat_flat), mat_layout())
        params.update(unpack(low(vec_flat), vec_layout()))
        per_image = lax.map(jax.checkpoint(lambda record: image_loss(params, *record)), (latents, target_noise, labels, timesteps, orient, extent))
        return jnp.sum(per_image)
    loss_sum, back_fn = jax.vjp(loss_total, mat_params, vec_params)
    grad_mat, grad_vec = back_fn(jnp.ones((), jnp.float32))
    pixel_count = jnp.sum(jax.vmap(image_mask)(orient, extent))
    grad_mat = grad_mat / pixel_count
    grad_vec = grad_vec / pixel_count
    grad_norm = jnp.sqrt(jnp.sum(grad_mat * grad_mat) + jnp.sum(grad_vec * grad_vec))
    factor = clip_norm / jnp.maximum(grad_norm, clip_norm)
    new_mat, mat_first_new, mat_second_new = adam_update(mat_params, mat_first, mat_second, grad_mat * factor, weight_decay)
    new_vec, vec_first_new, vec_second_new = adam_update(vec_params, vec_first, vec_second, grad_vec * factor, 0.0)
    ema_rate = min(ema_ceiling, (1.0 + STEP) / (10.0 + STEP))
    mat_ema_new = ema_rate * mat_ema + (1.0 - ema_rate) * new_mat
    vec_ema_new = ema_rate * vec_ema + (1.0 - ema_rate) * new_vec
    return (new_mat, mat_first_new, mat_second_new, mat_ema_new, new_vec, vec_first_new, vec_second_new, vec_ema_new, grad_norm, loss_sum, pixel_count)
```

```python
import math

import jax
import jax.numpy as jnp
from jax import lax
from jax.sharding import PartitionSpec as P

C = 512
HEADS = 8
DHEAD = 64
FFI = 2048
TE = 256
TD = 1024
NCLS = 1000
LC = 3
GROUPS = 32
SIDE = 32
NT = 1000
STEP = 10


tap_offsets = [(-1, -1), (-1, 0), (-1, 1), (0, -1), (0, 0), (0, 1), (1, -1), (1, 0), (1, 1)]
eps_group = 1e-06
eps_layer = 1e-05
beta_first = 0.00085
beta_last = 0.012
adam_one = 0.9
adam_two = 0.999
adam_eps = 1e-08
learn_rate = 0.05
weight_decay = 0.01
ema_ceiling = 0.9999
clip_norm = 0.1


def mat_layout():
    return [
        ("w_in", 9 * LC, C),
        ("w_t1", TE, TD),
        ("w_t2", TD, TD),
        ("w_tp", TD, C),
        ("table", NCLS, C),
        ("w_c1", 9 * C, C),
        ("w_c2", 9 * C, C),
        ("w_pin", C, C),
        ("w_qkv", C, 3 * C),
        ("w_o", C, C),
        ("w_cq", C, C),
        ("w_ckv", C, 2 * C),
        ("w_co", C, C),
        ("w_ff1", C, 2 * FFI),
        ("w_ff2", FFI, C),
        ("w_pout", C, C),
        ("w_out", 9 * C, LC),
    ]


def vec_layout():
    names = [
        "b_tp",
        "b_in",
        "g1",
        "bb1",
        "b_c1",
        "g2",
        "bb2",
        "b_c2",
        "g3",
        "bb3",
        "b_pin",
        "n1g",
        "n1b",
        "b_o",
        "n2g",
        "n2b",
        "b_co",
        "n3g",
        "n3b",
    ]
    return (
        [("b_t1", TD), ("b_t2", TD)]
        + [(name_one, C) for name_one in names]
        + [("b_ff1", 2 * FFI), ("b_ff2", C), ("b_pout", C), ("b_out", LC)]
    )


def unpack(joined, layout):
    pieces = {}
    start_at = 0
    for record in layout:
        length = 1
        for extent_one in record[1:]:
            length = length * extent_one
        pieces[record[0]] = joined[start_at : start_at + length].reshape(record[1:])
        start_at = start_at + length
    return pieces


def noise_level(step_value):
    steps_idx = jnp.arange(NT).astype(jnp.float32)
    root_beta = math.sqrt(beta_first) + (
        math.sqrt(beta_last) - math.sqrt(beta_first)
    ) * steps_idx / (NT - 1)
    log_keep = jnp.log1p(-root_beta * root_beta)
    return jnp.exp(jnp.sum(jnp.where(jnp.arange(NT) <= step_value, log_keep, 0.0)))


def time_embed(step_value):
    frequency = jnp.exp(-math.log(10000.0) * jnp.arange(TE // 2).astype(jnp.float32) / (TE // 2))
    angles = step_value.astype(jnp.float32) * frequency
    return jnp.concatenate([jnp.cos(angles), jnp.sin(angles)])


WIDE = 512
HALF = 256
LEAD = 5
FRAME = 16
TOKENS = SIDE * FRAME
LOCAL_HEADS = HEADS // 2
WIRE_TOP = 16384.0


def silu_slope(values):
    logistic = jax.nn.sigmoid(values)
    return logistic * (1.0 + values * (1.0 - logistic))


def dot(left, right):
    return jnp.dot(left, right, preferred_element_type=jnp.float32)


def dot_t(left, right):
    return lax.dot_general(
        left, right, (((1,), (1,)), ((), ())), preferred_element_type=jnp.float32
    )


def t_dot(left, right):
    return lax.dot_general(
        left, right, (((0,), (0,)), ((), ())), preferred_element_type=jnp.float32
    )


def low(values):
    return values.astype(jnp.bfloat16)


class Place:
    def __init__(self):
        self.dp, self.rows = (lax.axis_size("dp"), lax.axis_size("rows"))
        self.count = self.dp * self.rows
        self.index = lax.axis_index("dp") * self.rows + lax.axis_index("rows")
        self.side = self.index % 2
        self.slot = (self.index // 2) % 2
        digits, left = ([], self.dp)
        while left > 4:
            digits.append(4)
            left //= 4
        digits.append(left)
        self.digits = digits + [2]
        strides, step = ([], 2)
        for size in reversed(self.digits):
            strides.insert(0, step)
            step *= size
        self.strides = strides
        self.coords = [(self.index // s) % n for s, n in zip(strides, self.digits)]

    def move(self, value, pairs):
        return lax.ppermute(value, ("dp", "rows"), pairs)

    def swap(self, value, stride=1):
        return self.move(value, [(k, k ^ stride) for k in range(self.count)])

    def shift(self, value, by):
        return self.move(
            value, [(k, k + by) for k in range(self.count) if 0 <= k + by < self.count]
        )

    def step(self, value, axis, direction, hops):
        stride, size = (self.strides[axis], self.digits[axis])
        pairs = []
        for k in range(self.count):
            at = (k // stride) % size
            rank = at if direction > 0 else size - 1 - at
            if rank <= hops and rank < size - 1:
                pairs.append((k, k + direction * stride))
        return self.move(value, pairs)

    def half(self, value, axis=-1):
        axis = axis % value.ndim
        return lax.dynamic_slice_in_dim(value, self.side * HALF, HALF, axis)

    def join(self, mine, other):
        first = jnp.where(self.side == 0, mine, other)
        second = jnp.where(self.side == 0, other, mine)
        return jnp.concatenate([first, second], axis=-1)

    def full(self, mine):
        return self.join(mine, self.swap(mine))

    def chip_sum(self, value):
        stride = 2
        while stride < self.count:
            value = value + self.swap(value, stride)
            stride *= 2
        return value


def shard_rows(flat_len, count):
    length = flat_len // count
    rows = -(-(LEAD * WIDE + flat_len) // (WIDE * count))
    rows = -(-rows // 8) * 8
    while rows * WIDE - length < LEAD * WIDE:
        rows += 8
    return rows


def to_blocks(place, shard, rows):
    length, block = (shard.shape[0], rows * WIDE)
    drift = block - length
    reach = drift * (place.count - 1) - LEAD * WIDE + block
    parts, hop = ([jnp.zeros((LEAD * WIDE,), shard.dtype), shard], 1)
    while hop * length < reach:
        take = min(length, reach - hop * length)
        take = min(length, -(-take // 1024) * 1024)
        parts.append(place.shift(shard[:take], -hop))
        hop += 1
    joined = jnp.concatenate(parts)
    lack = drift * (place.count - 1) + block - joined.shape[0]
    if lack > 0:
        joined = jnp.pad(joined, (0, lack))
    return lax.dynamic_slice(joined, (drift * place.index,), (block,)).reshape(rows, WIDE)


def from_blocks(place, block, length):
    flat = block.reshape(-1)
    drift = flat.shape[0] - length
    reach = drift * (place.count - 1) - LEAD * WIDE
    parts, hop, lead = ([flat], 1, 0)
    while lead < reach:
        take = min(flat.shape[0], -(-(reach - lead) // 1024) * 1024)
        parts.insert(0, place.shift(flat[flat.shape[0] - take :], hop))
        lead += take
        hop += 1
    joined = jnp.concatenate(parts)
    start = lead + LEAD * WIDE - drift * place.index
    return lax.dynamic_slice(joined, (start,), (length,))


def wire_out(values, bound):
    return (values * (WIRE_TOP / bound)).astype(jnp.float16)


def wire_in(values, bound):
    return values.astype(jnp.float32) * (bound * (1.0 / WIRE_TOP))


def pick(values, index, axis):
    return lax.dynamic_index_in_dim(values, index, axis, keepdims=False)


def scatter_pair(place, held, bound, axis, dim):
    me, stride = (place.coords[axis], place.strides[axis])
    got = place.swap(wire_out(pick(held, 1 - me, dim), bound), stride)
    other = place.swap(bound, stride)
    return (pick(held, me, dim) + wire_in(got, other), bound + other)


def scatter_line(place, held, bound, axis, dim):
    me, size = (place.coords[axis], place.digits[axis])
    total, limit = (pick(held, me, dim), bound)
    for direction in (1, -1):
        rank = me if direction > 0 else size - 1 - me
        got, other = (None, None)
        for hops in range(size - 1):
            aim = jnp.minimum(size - 1 - hops + rank, size - 1)
            aim = aim if direction > 0 else size - 1 - aim
            value, top = (pick(held, aim, dim), bound)
            if got is not None:
                value, top = (value + wire_in(got, other), top + other)
            got = place.step(wire_out(value, top), axis, direction, hops)
            other = place.step(top, axis, direction, hops)
        total, limit = (total + wire_in(got, other), limit + other)
    return (total, limit)


def scatter_part(place, held, bound, order):
    left = list(range(len(place.digits)))
    for axis in order:
        dim = left.index(axis)
        if place.digits[axis] == 2:
            held, bound = scatter_pair(place, held, bound, axis, dim)
        else:
            held, bound = scatter_line(place, held, bound, axis, dim)
        left.remove(axis)
    return held


def scatter_sum(place, grads, rows):
    bound = jnp.maximum(jnp.max(jnp.abs(grads)), 1e-30).reshape(1, 1)
    bound = jnp.broadcast_to(bound, (8, 128))[:1, :1]
    held = grads.reshape(*place.digits, 2 * rows, HALF)
    axes = list(range(len(place.digits)))[::-1]
    shares = [0.45, 0.45, 0.1]
    total = 2 * rows
    cuts = [0] + [int(total * sum(shares[: i + 1]) / 8 + 0.5) * 8 for i in range(2)] + [total]
    parts = []
    for i in range(3):
        order = axes[i:] + axes[:i]
        piece = held[..., cuts[i] : cuts[i + 1], :]
        parts.append(scatter_part(place, piece, bound, order))
    chip = jnp.concatenate(parts, axis=0).reshape(2, rows, HALF)
    mine = pick(chip, place.side, 0)
    other = place.swap(pick(chip, 1 - place.side, 0))
    return place.join(mine, other)


def gather_small(place, value):
    stride, joined = (1, value[None])
    while stride < place.count:
        other = place.swap(joined, stride)
        upper = (place.index // stride) % 2 == 1
        joined = jnp.where(
            upper,
            jnp.concatenate([other, joined], axis=0),
            jnp.concatenate([joined, other], axis=0),
        )
        stride *= 2
    return joined


def windows(values, turned, sign):
    width = values.shape[1]
    col = (lax.iota(jnp.int32, TOKENS) % FRAME)[:, None]
    zero_one = jnp.zeros((1, width), values.dtype)
    zero_row = jnp.zeros((FRAME, width), values.dtype)
    none = jnp.zeros((), values.dtype)
    across = {
        -1: jnp.where(col > 0, jnp.concatenate([zero_one, values[:-1]], axis=0), none),
        0: values,
        1: jnp.where(col < FRAME - 1, jnp.concatenate([values[1:], zero_one], axis=0), none),
    }
    moved = {}
    for col_off, value in across.items():
        moved[-1, col_off] = jnp.concatenate([zero_row, value[:-FRAME]], axis=0)
        moved[0, col_off] = value
        moved[1, col_off] = jnp.concatenate([value[FRAME:], zero_row], axis=0)
    out = []
    for row_off, col_off in tap_offsets:
        plain = moved[sign * row_off, sign * col_off]
        other = moved[sign * col_off, sign * row_off]
        out.append(plain if row_off == col_off else jnp.where(turned, other, plain))
    return jnp.concatenate(out, axis=1)


def group_spread(channel_sums):
    at = lax.iota(jnp.int32, HALF) // (C // GROUPS)
    same = (at[:, None] == at[None, :]).astype(jnp.float32)
    return jnp.dot(channel_sums, same, precision=lax.Precision.HIGHEST)


def group_forward(values, mask, denominator, gain_vec, bias_vec):
    mean_val = group_spread(jnp.sum(values * mask, axis=0)[None]) / denominator
    centered = values - mean_val
    var_val = group_spread(jnp.sum(centered * centered * mask, axis=0)[None]) / denominator
    inv_std = lax.rsqrt(var_val + eps_group)
    normed = centered * inv_std
    return (normed * gain_vec + bias_vec, normed, inv_std)


def group_backward(gradient, normed, inv_std, mask, denominator, gain_vec):
    scaled = gradient * gain_vec
    sums = group_spread(
        jnp.stack([jnp.sum(scaled * mask, axis=0), jnp.sum(scaled * normed * mask, axis=0)])
    )
    input_grad = mask * inv_std * (
        scaled - sums[0:1] / denominator - normed * (sums[1:2] / denominator)
    )
    return (input_grad, jnp.sum(gradient * normed, axis=0), jnp.sum(gradient, axis=0))


def layer_forward(values, gain_vec, bias_vec):
    mean_val = jnp.mean(values, axis=-1, keepdims=True)
    centered = values - mean_val
    var_val = jnp.mean(centered * centered, axis=-1, keepdims=True)
    inv_std = lax.rsqrt(var_val + eps_layer)
    normed = centered * inv_std
    return (low(normed * gain_vec + bias_vec), normed, inv_std)


def layer_backward(gradient, normed, inv_std, gain_vec):
    scaled = gradient * gain_vec
    first = jnp.mean(scaled, axis=-1, keepdims=True)
    second = jnp.mean(scaled * normed, axis=-1, keepdims=True)
    input_grad = inv_std * (scaled - first - normed * second)
    return (input_grad, jnp.sum(gradient * normed, axis=0), jnp.sum(gradient, axis=0))


def heads_of(value):
    return value.reshape(value.shape[0], LOCAL_HEADS, DHEAD)


def head_scores(query, key, key_mask):
    scores = jnp.einsum("qhd,khd->hqk", query, key, preferred_element_type=jnp.float32) * 0.125
    return jnp.where(key_mask, scores, -1e30)


def attend(query, key, value, key_mask):
    scores = head_scores(query, key, key_mask)
    row_max = jnp.max(scores, axis=-1, keepdims=True)
    exponent = jnp.exp(scores - row_max)
    totals = jnp.sum(exponent, axis=-1, keepdims=True)
    out = jnp.einsum(
        "hqk,khd->qhd", low(exponent / totals), value, preferred_element_type=jnp.float32
    )
    return (low(out).reshape(TOKENS, HALF), row_max + jnp.log(totals))


def attend_back(query, key, value, key_mask, log_total, out_grad):
    probs = jnp.exp(head_scores(query, key, key_mask) - log_total)
    prob_grad = jnp.einsum("qhd,khd->hqk", out_grad, value, preferred_element_type=jnp.float32)
    inner = jnp.sum(probs * prob_grad, axis=-1, keepdims=True)
    score_grad = low(probs * (prob_grad - inner) * 0.125)
    query_grad = jnp.einsum("hqk,khd->qhd", score_grad, key, preferred_element_type=jnp.float32)
    key_grad = jnp.einsum("hqk,qhd->khd", score_grad, query, preferred_element_type=jnp.float32)
    value_grad = jnp.einsum(
        "hqk,qhd->khd", low(probs), out_grad, preferred_element_type=jnp.float32
    )
    return low(
        jnp.concatenate(
            [part.reshape(TOKENS, HALF) for part in (query_grad, key_grad, value_grad)], axis=1
        )
    )


def cross_split(context_kv):
    return (
        context_kv[:, :HALF].reshape(2, LOCAL_HEADS, DHEAD),
        context_kv[:, HALF:].reshape(2, LOCAL_HEADS, DHEAD),
    )


def cross_attend(query, context_kv):
    key, value = cross_split(context_kv)
    scores = jnp.einsum("thd,jhd->thj", query, key, preferred_element_type=jnp.float32) * 0.125
    probs = jax.nn.softmax(scores, axis=-1)
    out = jnp.einsum("thj,jhd->thd", probs, value.astype(jnp.float32))
    return (probs, low(out).reshape(TOKENS, HALF))


def cross_back(query, context_kv, probs, out_grad):
    key, value = cross_split(context_kv)
    prob_grad = jnp.einsum("thd,jhd->thj", out_grad, value, preferred_element_type=jnp.float32)
    score_grad = probs * (prob_grad - jnp.sum(probs * prob_grad, axis=-1, keepdims=True)) * 0.125
    query_grad = jnp.einsum("thj,jhd->thd", score_grad, key.astype(jnp.float32))
    key_grad = jnp.einsum("thj,thd->jhd", score_grad, query.astype(jnp.float32))
    value_grad = jnp.einsum("thj,thd->jhd", probs, out_grad.astype(jnp.float32))
    return (
        query_grad.reshape(TOKENS, HALF),
        jnp.concatenate([key_grad.reshape(2, HALF), value_grad.reshape(2, HALF)], axis=1),
    )


def own_columns(place, weight):
    split = weight.reshape(weight.shape[0], -1, 2, HALF)
    return pick(split, place.side, 2).reshape(weight.shape[0], -1)


def frame_of(place, latents, target_noise, turned):
    both = jnp.concatenate([latents, target_noise], axis=-1)
    stride, joined = (1, both[None])
    while stride < place.rows:
        other = place.swap(joined, stride)
        upper = (place.index // stride) % 2 == 1
        joined = jnp.where(
            upper,
            jnp.concatenate([other, joined], axis=0),
            jnp.concatenate([joined, other], axis=0),
        )
        stride *= 2
    image = pick(joined, place.slot, 1).reshape(SIDE, SIDE, 2 * LC)
    portrait = image[:, :FRAME]
    landscape = jnp.transpose(image[:FRAME], (1, 0, 2))
    return jnp.where(turned, landscape, portrait).reshape(TOKENS, 2 * LC)


def train_step(place, mats, vecs, latents, target_noise, label, step_value, orient, extent):
    grads, bias_grads = ({}, {})
    half, full = (place.half, place.full)
    turned = orient != 1
    seen = lax.iota(jnp.int32, TOKENS) < extent * FRAME
    mask = seen.astype(jnp.float32)[:, None]
    denominator = (extent * FRAME * (C // GROUPS)).astype(jnp.float32)
    frame = frame_of(place, latents, target_noise, turned)
    noise_img = frame[:, LC:]
    share = noise_level(step_value)
    noisy = mask * (jnp.sqrt(share) * frame[:, :LC] + jnp.sqrt(1.0 - share) * noise_img)

    embed_in = low(time_embed(step_value))[None]
    pre_one = dot(embed_in, mats["w_t1"]) + vecs["b_t1"]
    hidden_one = low(jax.nn.silu(pre_one))
    pre_two = dot(hidden_one, mats["w_t2"]) + vecs["b_t2"]
    hidden_two = low(jax.nn.silu(pre_two))
    time_vec = dot(hidden_two, mats["w_tp"]) + vecs["b_tp"]
    class_vec = lax.dynamic_slice(mats["table"], (label, 0), (1, C)).astype(jnp.float32)

    pad_in = windows(low(noisy), turned, 1)
    state_zero = mask * (dot(pad_in, half(mats["w_in"])) + half(vecs["b_in"]))
    norm_one, normed_one, inv_one = group_forward(
        state_zero, mask, denominator, half(vecs["g1"]), half(vecs["bb1"])
    )
    pad_one = windows(full(low(mask * jax.nn.silu(norm_one))), turned, 1)
    conv_one = mask * (
        dot(pad_one, half(mats["w_c1"])) + half(vecs["b_c1"]) + half(time_vec)
    )
    norm_two, normed_two, inv_two = group_forward(
        conv_one, mask, denominator, half(vecs["g2"]), half(vecs["bb2"])
    )
    pad_two = windows(full(low(mask * jax.nn.silu(norm_two))), turned, 1)
    state_one = state_zero + mask * (dot(pad_two, half(mats["w_c2"])) + half(vecs["b_c2"]))
    norm_three, normed_three, inv_three = group_forward(
        state_one, mask, denominator, half(vecs["g3"]), half(vecs["bb3"])
    )
    token_in = full(low(norm_three))
    resid_zero = dot(token_in, mats["w_pin"]) + vecs["b_pin"]
    ln_one, normed_ln1, inv_ln1 = layer_forward(resid_zero, vecs["n1g"], vecs["n1b"])
    qkv_own = own_columns(place, mats["w_qkv"])
    packed = low(dot(ln_one, qkv_own))
    query, key, value = [heads_of(packed[:, i * HALF : (i + 1) * HALF]) for i in range(3)]
    attended_own, log_total = attend(query, key, value, seen)
    attended = full(attended_own)
    resid_one = resid_zero + dot(attended, mats["w_o"]) + vecs["b_o"]
    ln_two, normed_ln2, inv_ln2 = layer_forward(resid_one, vecs["n2g"], vecs["n2b"])
    cq_own = half(mats["w_cq"])
    cross_query = heads_of(low(dot(ln_two, cq_own)))
    context = low(jnp.concatenate([class_vec, time_vec], axis=0))
    ckv_own = own_columns(place, mats["w_ckv"])
    context_kv = low(dot(context, ckv_own))
    cross_prob, cross_own = cross_attend(cross_query, context_kv)
    cross_out = full(cross_own)
    resid_two = resid_one + dot(cross_out, mats["w_co"]) + vecs["b_co"]
    ln_three, normed_ln3, inv_ln3 = layer_forward(resid_two, vecs["n3g"], vecs["n3b"])
    ff1_own = own_columns(place, mats["w_ff1"])
    projected = dot(ln_three, ff1_own) + own_columns(place, vecs["b_ff1"][None])
    wide = FFI // 2
    lift, gate = (projected[:, :wide], projected[:, wide:])
    cdf = 0.5 * (1.0 + lax.erf(gate * math.sqrt(0.5)))
    gated_own = low(lift * gate * cdf)
    gated_peer = place.swap(gated_own)
    gated = jnp.concatenate(
        [
            place.join(gated_own[:, i * HALF : (i + 1) * HALF], gated_peer[:, i * HALF : (i + 1) * HALF])
            for i in range(FFI // WIDE)
        ],
        axis=1,
    )
    resid_three = resid_two + dot(gated, mats["w_ff2"]) + vecs["b_ff2"]
    out_in = low(resid_three)
    branch = dot(out_in, half(mats["w_pout"])) + half(vecs["b_pout"])
    state_two = state_one + mask * branch
    pad_out = windows(full(low(state_two)), turned, 1)
    predicted = dot(pad_out, mats["w_out"]) + vecs["b_out"]
    residual_err = predicted - noise_img
    loss = jnp.sum(mask * residual_err * residual_err)

    out_grad = 2.0 * mask * residual_err
    bias_grads["b_out"] = jnp.sum(out_grad, axis=0)
    out_low = low(out_grad)
    grads["w_out"] = half(t_dot(pad_out, out_low).reshape(9 * LC, C))
    w_out_back = jnp.transpose(mats["w_out"].reshape(9, C, LC), (0, 2, 1)).reshape(9 * LC, C)
    state_grad = dot(windows(out_low, turned, -1), w_out_back)
    branch_grad = mask * state_grad
    state_grad = half(state_grad)
    bias_grads["b_pout"] = half(jnp.sum(branch_grad, axis=0))
    grad_low = low(branch_grad)
    grads["w_pout"] = t_dot(out_in, half(grad_low))
    resid_grad = dot_t(grad_low, mats["w_pout"])
    bias_grads["b_ff2"] = half(jnp.sum(resid_grad, axis=0))
    grad_low = low(resid_grad)
    grads["w_ff2"] = t_dot(gated, half(grad_low))
    ff2_own = pick(mats["w_ff2"].reshape(-1, 2, HALF, C), place.side, 1).reshape(wide, C)
    gated_grad = dot_t(grad_low, ff2_own)
    density = jnp.exp(-0.5 * gate * gate) * (1.0 / math.sqrt(2.0 * math.pi))
    proj_grad = jnp.concatenate(
        [gated_grad * gate * cdf, gated_grad * lift * (cdf + gate * density)], axis=1
    )
    bias_grads["b_ff1"] = jnp.sum(proj_grad, axis=0)
    grad_low = low(proj_grad)
    grads["w_ff1"] = t_dot(ln_three, grad_low)
    ln_grad = dot_t(grad_low, ff1_own)
    ln_grad = ln_grad + place.swap(ln_grad)
    ln_grad, gain, bias = layer_backward(ln_grad, normed_ln3, inv_ln3, vecs["n3g"])
    bias_grads["n3g"], bias_grads["n3b"] = (half(gain), half(bias))
    resid_grad = resid_grad + ln_grad
    bias_grads["b_co"] = half(jnp.sum(resid_grad, axis=0))
    grad_low = low(resid_grad)
    grads["w_co"] = t_dot(cross_out, half(grad_low))
    cross_grad = heads_of(low(dot_t(grad_low, half(mats["w_co"], 0))))
    query_grad, kv_grad = cross_back(cross_query, context_kv, cross_prob, cross_grad)
    query_low, kv_low = (low(query_grad), low(kv_grad))
    grads["w_cq"] = t_dot(ln_two, query_low)
    grads["w_ckv"] = t_dot(context, kv_low)
    context_grad = dot_t(kv_low, ckv_own)
    context_grad = context_grad + place.swap(context_grad)
    ln_grad = dot_t(full(query_low), mats["w_cq"])
    ln_grad, gain, bias = layer_backward(ln_grad, normed_ln2, inv_ln2, vecs["n2g"])
    bias_grads["n2g"], bias_grads["n2b"] = (half(gain), half(bias))
    resid_grad = resid_grad + ln_grad
    bias_grads["b_o"] = half(jnp.sum(resid_grad, axis=0))
    grad_low = low(resid_grad)
    grads["w_o"] = t_dot(attended, half(grad_low))
    attended_grad = heads_of(low(dot_t(grad_low, half(mats["w_o"], 0))))
    packed_grad = attend_back(query, key, value, seen, log_total, attended_grad)
    grads["w_qkv"] = t_dot(ln_one, packed_grad)
    ln_grad = dot_t(packed_grad, qkv_own)
    ln_grad = ln_grad + place.swap(ln_grad)
    ln_grad, gain, bias = layer_backward(ln_grad, normed_ln1, inv_ln1, vecs["n1g"])
    bias_grads["n1g"], bias_grads["n1b"] = (half(gain), half(bias))
    resid_grad = resid_grad + ln_grad
    bias_grads["b_pin"] = half(jnp.sum(resid_grad, axis=0))
    grad_low = low(resid_grad)
    grads["w_pin"] = t_dot(token_in, half(grad_low))
    token_grad = dot_t(grad_low, half(mats["w_pin"], 0))
    norm_grad, bias_grads["g3"], bias_grads["bb3"] = group_backward(
        token_grad, normed_three, inv_three, mask, denominator, half(vecs["g3"])
    )
    state_grad = state_grad + norm_grad

    conv_grad = mask * state_grad
    bias_grads["b_c2"] = jnp.sum(conv_grad, axis=0)
    conv_low = low(conv_grad)
    grads["w_c2"] = t_dot(pad_two, conv_low)
    act_grad = conv_input_grad(place, full(conv_low), mats["w_c2"], turned)
    conv_grad, bias_grads["g2"], bias_grads["bb2"] = group_backward(
        mask * act_grad * silu_slope(norm_two),
        normed_two,
        inv_two,
        mask,
        denominator,
        half(vecs["g2"]),
    )
    conv_sum = jnp.sum(conv_grad, axis=0)
    bias_grads["b_c1"] = conv_sum
    conv_low = low(conv_grad)
    grads["w_c1"] = t_dot(pad_one, conv_low)
    act_grad = conv_input_grad(place, full(conv_low), mats["w_c1"], turned)
    norm_grad, bias_grads["g1"], bias_grads["bb1"] = group_backward(
        mask * act_grad * silu_slope(norm_one),
        normed_one,
        inv_one,
        mask,
        denominator,
        half(vecs["g1"]),
    )
    in_grad = mask * (state_grad + norm_grad)
    bias_grads["b_in"] = jnp.sum(in_grad, axis=0)
    grads["w_in"] = t_dot(pad_in, low(in_grad))

    time_grad = full(conv_sum[None]) + context_grad[1:2]
    bias_grads["b_tp"] = half(time_grad[0])
    time_low = low(time_grad)
    grads["w_tp"] = outer(hidden_two, half(time_low))
    pre_grad = dot_t(time_low, mats["w_tp"]) * silu_slope(pre_two)
    bias_grads["b_t2"] = own_columns(place, pre_grad)[0]
    pre_low = low(pre_grad)
    grads["w_t2"] = outer(hidden_one, own_columns(place, pre_low))
    pre_grad = dot_t(pre_low, mats["w_t2"]) * silu_slope(pre_one)
    bias_grads["b_t1"] = own_columns(place, pre_grad)[0]
    grads["w_t1"] = outer(embed_in, own_columns(place, low(pre_grad)))
    rows = lax.iota(jnp.int32, NCLS)[:, None] == label
    grads["table"] = jnp.where(rows, half(context_grad[0:1]), 0.0)
    return (grads, bias_grads, loss)


def outer(inputs, gradient):
    return inputs.astype(jnp.float32).reshape(-1, 1) * gradient.astype(jnp.float32)


def conv_input_grad(place, gradient, weight, turned):
    moved = windows(gradient, turned, -1).reshape(TOKENS, 9, C)
    own = place.half(weight.reshape(9, C, C), 1)
    return lax.dot_general(
        moved, own, (((1, 2), (0, 2)), ((), ())), preferred_element_type=jnp.float32
    )


def adam_update(params, first_mom, second, gradient, decay_rate):
    first_new = adam_one * first_mom + (1.0 - adam_one) * gradient
    second_new = adam_two * second + (1.0 - adam_two) * gradient * gradient
    step_size = (
        first_new
        / (1.0 - adam_one**STEP)
        / (jnp.sqrt(second_new / (1.0 - adam_two**STEP)) + adam_eps)
    )
    return (params - learn_rate * (step_size + decay_rate * params), first_new, second_new)


def local(
    latents,
    target_noise,
    labels,
    timesteps,
    orient,
    extent,
    mat_params,
    mat_first,
    mat_second,
    mat_ema,
    vec_params,
    vec_first,
    vec_second,
    vec_ema,
):
    place = Place()
    length = mat_params.shape[0]
    rows = shard_rows(length * place.count, place.count)
    block = to_blocks(place, mat_params.astype(jnp.bfloat16), rows)
    table = lax.all_gather(block, ("dp", "rows"), axis=0, tiled=True)
    mats, at = ({}, LEAD)
    for name, depth, width in mat_layout():
        count = depth * width // WIDE
        mats[name] = table[at : at + count].reshape(depth, width)
        if name == "w_in":
            mats[name] = table[at : at + count]
        at += count
    vec_len = vec_params.shape[0]
    vec_wide = -(-vec_len // 128) * 128
    padded = jnp.pad(vec_params, (0, vec_wide - vec_len)).reshape(-1, 128)
    vec_all = gather_small(place, padded).reshape(place.count, vec_wide)[:, :vec_len]
    vec_all = vec_all.reshape(-1).astype(jnp.bfloat16).astype(jnp.float32)
    vecs = unpack(vec_all, vec_layout())
    own = lambda values: pick(values, place.slot, 0)
    grads, bias_grads, loss = train_step(
        place,
        mats,
        vecs,
        latents,
        target_noise,
        own(labels),
        own(timesteps),
        own(orient),
        own(extent),
    )
    pieces = [jnp.zeros((LEAD, HALF), jnp.float32)]
    pieces += [grads[record[0]].reshape(-1, HALF) for record in mat_layout()]
    used = sum(piece.shape[0] for piece in pieces)
    pieces.append(jnp.zeros((place.count * rows - used, HALF), jnp.float32))
    grad_rows = jnp.concatenate(pieces, axis=0)

    small = [bias_grads[record[0]].reshape(-1, HALF) for record in vec_layout()[:-1]]
    count_local = (own(extent) * FRAME).astype(jnp.float32)
    extra = jnp.concatenate([bias_grads["b_out"], jnp.stack([loss, count_local])])
    extra = jnp.pad(extra, (0, HALF - LC - 2))[None]
    small = jnp.concatenate(small + [extra], axis=0)
    small = jnp.pad(small, ((0, -small.shape[0] % 8), (0, 0)))
    small = place.full(place.chip_sum(small))
    body = sum(record[1] for record in vec_layout()[:-1]) // WIDE
    loss_sum, pixel_count = (small[body, LC], small[body, LC + 1])
    vec_flat = jnp.concatenate([small[:body].reshape(-1), small[body, :LC]])
    vec_flat = jnp.pad(vec_flat, (0, vec_len * place.count - vec_flat.shape[0]))
    shard_vec = lax.dynamic_slice(vec_flat, (vec_len * place.index,), (vec_len,))

    block_grad = scatter_sum(place, grad_rows, rows)
    shard_mat = from_blocks(place, block_grad, length)
    square = jnp.sum(block_grad * block_grad).reshape(1, 1)
    square = place.chip_sum(square + place.swap(square))[0, 0]
    square = square + jnp.sum(vec_flat * vec_flat)
    inverse = 1.0 / pixel_count
    grad_norm = jnp.sqrt(square) * inverse
    factor = clip_norm / jnp.maximum(grad_norm, clip_norm) * inverse
    new_mat, mat_first_new, mat_second_new = adam_update(
        mat_params, mat_first, mat_second, shard_mat * factor, weight_decay
    )
    new_vec, vec_first_new, vec_second_new = adam_update(
        vec_params, vec_first, vec_second, shard_vec * factor, 0.0
    )
    ema_rate = min(ema_ceiling, (1.0 + STEP) / (10.0 + STEP))
    mat_ema_new = ema_rate * mat_ema + (1.0 - ema_rate) * new_mat
    vec_ema_new = ema_rate * vec_ema + (1.0 - ema_rate) * new_vec
    return (
        new_mat,
        mat_first_new,
        mat_second_new,
        mat_ema_new,
        new_vec,
        vec_first_new,
        vec_second_new,
        vec_ema_new,
        grad_norm,
        loss_sum,
        pixel_count,
    )


def solution(mesh):
    return jax.shard_map(
        local,
        mesh=mesh,
        in_specs=(
            P("dp", "rows", None, None),
            P("dp", "rows", None, None),
            P("dp"),
            P("dp"),
            P("dp"),
            P("dp"),
            P(("dp", "rows")),
            P(("dp", "rows")),
            P(("dp", "rows")),
            P(("dp", "rows")),
            P(("dp", "rows")),
            P(("dp", "rows")),
            P(("dp", "rows")),
            P(("dp", "rows")),
        ),
        out_specs=(
            P(("dp", "rows")),
            P(("dp", "rows")),
            P(("dp", "rows")),
            P(("dp", "rows")),
            P(("dp", "rows")),
            P(("dp", "rows")),
            P(("dp", "rows")),
            P(("dp", "rows")),
            P(),
            P(),
            P(),
        ),
        check_vma=False,
    )
```

```python
import math

import jax
import jax.numpy as jnp
from jax import lax
from jax.experimental import pallas as pl
from jax.experimental.pallas import tpu as pltpu
from jax.sharding import PartitionSpec as P

C = 512
HEADS = 8
DHEAD = 64
FFI = 2048
TE = 256
TD = 1024
NCLS = 1000
LC = 3
GROUPS = 32
SIDE = 32
NT = 1000
STEP = 10


tap_offsets = [(-1, -1), (-1, 0), (-1, 1), (0, -1), (0, 0), (0, 1), (1, -1), (1, 0), (1, 1)]
eps_group = 1e-06
eps_layer = 1e-05
beta_first = 0.00085
beta_last = 0.012
adam_one = 0.9
adam_two = 0.999
adam_eps = 1e-08
learn_rate = 0.05
weight_decay = 0.01
ema_ceiling = 0.9999
clip_norm = 0.1


def mat_layout():
    return [
        ("w_in", 9 * LC, C),
        ("w_t1", TE, TD),
        ("w_t2", TD, TD),
        ("w_tp", TD, C),
        ("table", NCLS, C),
        ("w_c1", 9 * C, C),
        ("w_c2", 9 * C, C),
        ("w_pin", C, C),
        ("w_qkv", C, 3 * C),
        ("w_o", C, C),
        ("w_cq", C, C),
        ("w_ckv", C, 2 * C),
        ("w_co", C, C),
        ("w_ff1", C, 2 * FFI),
        ("w_ff2", FFI, C),
        ("w_pout", C, C),
        ("w_out", 9 * C, LC),
    ]


def vec_layout():
    names = [
        "b_tp",
        "b_in",
        "g1",
        "bb1",
        "b_c1",
        "g2",
        "bb2",
        "b_c2",
        "g3",
        "bb3",
        "b_pin",
        "n1g",
        "n1b",
        "b_o",
        "n2g",
        "n2b",
        "b_co",
        "n3g",
        "n3b",
    ]
    return (
        [("b_t1", TD), ("b_t2", TD)]
        + [(name_one, C) for name_one in names]
        + [("b_ff1", 2 * FFI), ("b_ff2", C), ("b_pout", C), ("b_out", LC)]
    )


def unpack(joined, layout):
    pieces = {}
    start_at = 0
    for record in layout:
        length = 1
        for extent_one in record[1:]:
            length = length * extent_one
        pieces[record[0]] = joined[start_at : start_at + length].reshape(record[1:])
        start_at = start_at + length
    return pieces


def noise_level(step_value):
    steps_idx = jnp.arange(NT).astype(jnp.float32)
    root_beta = math.sqrt(beta_first) + (
        math.sqrt(beta_last) - math.sqrt(beta_first)
    ) * steps_idx / (NT - 1)
    log_keep = jnp.log1p(-root_beta * root_beta)
    return jnp.exp(jnp.sum(jnp.where(jnp.arange(NT) <= step_value, log_keep, 0.0)))


def time_embed(step_value):
    frequency = jnp.exp(-math.log(10000.0) * jnp.arange(TE // 2).astype(jnp.float32) / (TE // 2))
    angles = step_value.astype(jnp.float32) * frequency
    return jnp.concatenate([jnp.cos(angles), jnp.sin(angles)])


WIDE = 512
HALF = 256
LEAD = 5
FRAME = 16
TOKENS = SIDE * FRAME
LOCAL_HEADS = HEADS // 2
WIRE_TOP = 32768.0


def silu_slope(values):
    logistic = jax.nn.sigmoid(values)
    return logistic * (1.0 + values * (1.0 - logistic))


def dot(left, right):
    return jnp.dot(left, right, preferred_element_type=jnp.float32)


def dot_t(left, right):
    return lax.dot_general(
        left, right, (((1,), (1,)), ((), ())), preferred_element_type=jnp.float32
    )


def t_dot(left, right):
    return lax.dot_general(
        left, right, (((0,), (0,)), ((), ())), preferred_element_type=jnp.float32
    )


def low(values):
    return values.astype(jnp.bfloat16)


class Place:
    def __init__(self):
        self.dp, self.rows = (lax.axis_size("dp"), lax.axis_size("rows"))
        self.count = self.dp * self.rows
        self.index = lax.axis_index("dp") * self.rows + lax.axis_index("rows")
        self.side = self.index % 2
        self.slot = (self.index // 2) % 2
        digits, left = ([], self.dp)
        while left > 4:
            digits.append(4)
            left //= 4
        digits.append(left)
        self.digits = digits + [2]
        strides, step = ([], 2)
        for size in reversed(self.digits):
            strides.insert(0, step)
            step *= size
        self.strides = strides
        self.coords = [(self.index // s) % n for s, n in zip(strides, self.digits)]

    def move(self, value, pairs):
        return lax.ppermute(value, ("dp", "rows"), pairs)

    def swap(self, value, stride=1):
        return self.move(value, [(k, k ^ stride) for k in range(self.count)])

    def shift(self, value, by):
        return self.move(
            value, [(k, k + by) for k in range(self.count) if 0 <= k + by < self.count]
        )

    def rotate(self, value, axis, by):
        stride, size = (self.strides[axis], self.digits[axis])
        pairs = []
        for k in range(self.count):
            at = (k // stride) % size
            pairs.append((k, k + ((at + by) % size - at) * stride))
        return self.move(value, pairs)

    def step(self, value, axis, direction, hops):
        stride, size = (self.strides[axis], self.digits[axis])
        pairs = []
        for k in range(self.count):
            at = (k // stride) % size
            rank = at if direction > 0 else size - 1 - at
            if rank <= hops and rank < size - 1:
                pairs.append((k, k + direction * stride))
        return self.move(value, pairs)

    def half(self, value, axis=-1):
        axis = axis % value.ndim
        return lax.dynamic_slice_in_dim(value, self.side * HALF, HALF, axis)

    def join(self, mine, other):
        first = jnp.where(self.side == 0, mine, other)
        second = jnp.where(self.side == 0, other, mine)
        return jnp.concatenate([first, second], axis=-1)

    def full(self, mine):
        return self.join(mine, self.swap(mine))

    def chip_sum(self, value):
        stride = 2
        while stride < self.count:
            value = value + self.swap(value, stride)
            stride *= 2
        return value


def shard_rows(flat_len, count):
    length = flat_len // count
    rows = -(-(LEAD * WIDE + flat_len) // (WIDE * count))
    rows = -(-rows // 8) * 8
    while rows * WIDE - length < LEAD * WIDE:
        rows += 8
    return rows


def to_blocks(place, shard, rows):
    length, block = (shard.shape[0], rows * WIDE)
    drift = block - length
    reach = drift * (place.count - 1) - LEAD * WIDE + block
    parts, hop = ([jnp.zeros((LEAD * WIDE,), shard.dtype), shard], 1)
    while hop * length < reach:
        take = min(length, reach - hop * length)
        take = min(length, -(-take // 1024) * 1024)
        parts.append(place.shift(shard[:take], -hop))
        hop += 1
    joined = jnp.concatenate(parts)
    lack = drift * (place.count - 1) + block - joined.shape[0]
    if lack > 0:
        joined = jnp.pad(joined, (0, lack))
    return lax.dynamic_slice(joined, (drift * place.index,), (block,)).reshape(rows, WIDE)


def from_blocks(place, block, length):
    flat = block.reshape(-1)
    drift = flat.shape[0] - length
    reach = drift * (place.count - 1) - LEAD * WIDE
    parts, hop, lead = ([flat], 1, 0)
    while lead < reach:
        take = min(flat.shape[0], -(-(reach - lead) // 1024) * 1024)
        parts.insert(0, place.shift(flat[flat.shape[0] - take :], hop))
        lead += take
        hop += 1
    joined = jnp.concatenate(parts)
    start = lead + LEAD * WIDE - drift * place.index
    return lax.dynamic_slice(joined, (start,), (length,))


def pick(values, index, axis):
    return lax.dynamic_index_in_dim(values, index, axis, keepdims=False)


def wire(values):
    return values.astype(jnp.float16)


def plain(values):
    return values.astype(jnp.float32)


def largest_of_all(place, top):
    stride = 1
    while stride < place.count:
        top = jnp.maximum(top, place.swap(top, stride))
        stride *= 2
    return top


def scatter_part(place, grads, low_row, rows, order, scale):
    held, left, first, factor = (grads, list(range(len(place.digits))), low_row, scale)

    def part_of(dim, index):
        starts, sizes, shape = ([], [], [])
        for at, axis in enumerate(left):
            starts.append(index if at == dim else 0)
            sizes.append(1 if at == dim else place.digits[axis])
            if at != dim:
                shape.append(place.digits[axis])
        out = lax.dynamic_slice(held, starts + [first, 0], sizes + [rows, HALF])
        return out.reshape(shape + [rows, HALF]) * factor

    for axis in order:
        dim = left.index(axis)
        me, size = (place.coords[axis], place.digits[axis])
        total = part_of(dim, me)
        if size == 2 or axis == order[-1]:
            for away in range(1, size):
                sent = wire(part_of(dim, (me + away) % size))
                total = total + plain(place.rotate(sent, axis, away))
        else:
            flows = {1: None, -1: None}
            for hops in range(size - 1):
                for direction in (1, -1):
                    rank = me if direction > 0 else size - 1 - me
                    aim = jnp.minimum(size - 1 - hops + rank, size - 1)
                    aim = aim if direction > 0 else size - 1 - aim
                    value = part_of(dim, aim)
                    if flows[direction] is not None:
                        value = value + plain(flows[direction])
                    flows[direction] = place.step(wire(value), axis, direction, hops)
            total = total + plain(flows[1]) + plain(flows[-1])
        held, first, factor = (total, 0, 1.0)
        left.remove(axis)
    return held


SHARES = (0.39, 0.39)


def scatter_sum(place, grads, scale, rows):
    held = grads.reshape(*place.digits, 2 * rows, HALF)
    axes = list(range(len(place.digits)))[::-1]
    total = 2 * rows
    cuts = [0] + [int(total * sum(SHARES[: i + 1]) / 8 + 0.5) * 8 for i in range(2)] + [total]
    parts = []
    for i in range(3):
        order = axes[i:] + axes[:i]
        parts.append(scatter_part(place, held, cuts[i], cuts[i + 1] - cuts[i], order, scale))
    chip = jnp.concatenate(parts, axis=0).reshape(2, rows, HALF) * (1.0 / scale)
    mine = pick(chip, place.side, 0)
    other = place.swap(pick(chip, 1 - place.side, 0))
    return place.join(mine, other)


class Store:
    def __init__(self, place, rows):
        self.total = place.count * rows
        self.buffer = None
        self.top = jnp.zeros((1, 1), jnp.float32)
        self.places, at = ({}, LEAD)
        for name, depth, width in mat_layout():
            self.places[name] = at
            at += depth * width // WIDE

    def write(self, out, top):
        self.buffer = out
        if top is not None:
            self.top = jnp.maximum(self.top, top)

    def add(self, name, inputs, gradient):
        if inputs.shape[0] < 16:
            spare = ((0, 16 - inputs.shape[0]), (0, 0))
            inputs, gradient = (jnp.pad(inputs, spare), jnp.pad(gradient, spare))
        grad_into(self, inputs, gradient, self.places[name])

    def put(self, at, values):
        self.top = jnp.maximum(self.top, jnp.max(jnp.abs(values)).reshape(1, 1))
        self.buffer = lax.dynamic_update_slice(self.buffer, values, (at, 0))


def store_specs(store, at, tile):
    old = [] if store.buffer is None else [store.buffer]
    out = pl.BlockSpec(
        (pl.Element(tile), pl.Element(HALF)), lambda i, *_: (pl.multiple_of(at + tile * i, 8), 0)
    )
    shape = jax.ShapeDtypeStruct((store.total, HALF), jnp.float32)
    return (old, [pl.BlockSpec(memory_space=pl.ANY) for _ in old], out, shape)


def grad_into(store, inputs, gradient, at):
    tokens, depth = inputs.shape
    pieces = gradient.shape[1] // HALF
    tile = min(depth, 512 if pieces == 1 else 256 if pieces < 8 else 128)
    rows, tiles = (tile * pieces, depth // tile)
    old, old_specs, out_spec, out_shape = store_specs(store, at, rows)

    def body(*refs):
        refs = refs[len(old) :]
        input_ref, gradient_ref, out_ref, top_out = refs[:4]
        step = pl.program_id(0)
        part = t_dot(input_ref[...], gradient_ref[...])
        if pieces == 1:
            out_ref[...] = part
        else:
            mixed = refs[-1]
            for side in range(HALF // 128):
                for j in range(pieces):
                    column = j * HALF + side * 128
                    mixed[pl.ds(j, tile, stride=pieces), :] = part[:, column : column + 128]
                out_ref[:, side * 128 : (side + 1) * 128] = mixed[...]
        largest = jnp.max(jnp.abs(part))

        @pl.when(step == 0)
        def _():
            top_out[0, 0] = largest

        @pl.when(step > 0)
        def _():
            top_out[0, 0] = jnp.maximum(top_out[0, 0], largest)

    out, top = pl.pallas_call(
        body,
        grid=(tiles,),
        in_specs=old_specs
        + [
            pl.BlockSpec((tokens, tile), lambda i: (0, i)),
            pl.BlockSpec(gradient.shape, lambda i: (0, 0)),
        ],
        out_specs=[out_spec, pl.BlockSpec(memory_space=pltpu.SMEM)],
        out_shape=[out_shape, jax.ShapeDtypeStruct((1, 1), jnp.float32)],
        scratch_shapes=[] if pieces == 1 else [pltpu.VMEM((rows, 128), jnp.float32)],
        input_output_aliases={k: k for k in range(len(old))},
        compiler_params=params(),
        cost_estimate=cost(
            2 * tokens * depth * gradient.shape[1],
            depth * gradient.shape[1] * 4 + tokens * depth * 2,
        ),
    )(*old, inputs, gradient)
    store.write(out, top)


VMEM_LIMIT = 50 * 1024 * 1024
PADDED = TOKENS + 2 * FRAME


def params():
    return pltpu.CompilerParams(vmem_limit_bytes=VMEM_LIMIT)


def whole(shape):
    return pl.BlockSpec(shape, lambda *_: (0,) * len(shape))


def cost(flops, nbytes):
    return pl.CostEstimate(flops=flops, bytes_accessed=nbytes, transcendentals=0)


def token_mask(limit):
    return (lax.broadcasted_iota(jnp.int32, (TOKENS, 1), 0) < limit).astype(jnp.float32)


def columns_moved(values, col_off):
    if col_off == 0:
        return values
    col = lax.broadcasted_iota(jnp.int32, (TOKENS, 1), 0) % FRAME
    keep = col > 0 if col_off < 0 else col < FRAME - 1
    return jnp.where(keep, pltpu.roll(values, (-col_off) % TOKENS, 0), 0.0)


def two_sides(side, mine, other):
    first = jnp.where(side == 0, mine, other)
    second = jnp.where(side == 0, other, mine)
    return jnp.concatenate([first, second], axis=1)


def fill_moved(moved, values):
    width = moved.shape[2]
    empty = jnp.zeros((FRAME, width), moved.dtype)
    for slab in range(3):
        moved[slab, 0:FRAME, :] = empty
        moved[slab, FRAME : FRAME + TOKENS, :] = columns_moved(values, slab - 1).astype(moved.dtype)
        moved[slab, FRAME + TOKENS : PADDED, :] = empty


def tap_of(step, turned):
    row_off, col_off = (step // 3 - 1, step % 3 - 1)
    return (
        jnp.where(turned == 1, col_off, row_off),
        jnp.where(turned == 1, row_off, col_off),
    )


def rows_from(row_off):
    return pl.ds(pl.multiple_of(FRAME * (1 + row_off), FRAME), TOKENS)


def group_same():
    left = lax.broadcasted_iota(jnp.int32, (HALF, HALF), 0) // (C // GROUPS)
    right = lax.broadcasted_iota(jnp.int32, (HALF, HALF), 1) // (C // GROUPS)
    return (left == right).astype(jnp.float32)


def spread_in(sums, same):
    wide = jnp.broadcast_to(sums, (8, HALF))
    return jnp.dot(
        wide, same, precision=lax.Precision.HIGHEST, preferred_element_type=jnp.float32
    )[0:1]


def norm_in(value, mask, limit, gain, bias):
    same = group_same()
    share = 1.0 / (limit.astype(jnp.float32) * (C // GROUPS))
    mean_val = spread_in(jnp.sum(value * mask, axis=0, keepdims=True), same) * share
    centered = value - mean_val
    var_val = spread_in(jnp.sum(centered * centered * mask, axis=0, keepdims=True), same) * share
    inv_std = lax.rsqrt(var_val + eps_group)
    normed = centered * inv_std
    return (normed * gain + bias, normed, inv_std)


def silu_in(values):
    return values / (1.0 + jnp.exp(-values))


def finish_forward(total, limit, base, rows, act, act_out, normed_out, inv_out, value_out):
    mask = token_mask(limit)
    value = mask * (total + rows[0:1])
    if base is not None:
        value = value + base
    norm, normed, inv_std = norm_in(value, mask, limit, rows[1:2], rows[2:3])
    result = mask * silu_in(norm) if act else norm
    low_result = result.astype(jnp.bfloat16)
    act_out[...] = low_result
    normed_out[...] = normed
    inv_out[0:1] = inv_std
    inv_out[1:2] = column_squares(low_result)
    if value_out is not None:
        value_out[...] = value


def forward_outs(with_value):
    shapes = [
        jax.ShapeDtypeStruct((TOKENS, HALF), jnp.bfloat16),
        jax.ShapeDtypeStruct((TOKENS, HALF), jnp.float32),
        jax.ShapeDtypeStruct((8, HALF), jnp.float32),
    ]
    if with_value:
        shapes.append(jax.ShapeDtypeStruct((TOKENS, HALF), jnp.float32))
    return shapes


def first_forward(info, inputs, weight, rows):
    def body(info_ref, input_ref, weight_ref, rows_ref, *outs):
        total = dot(input_ref[...], weight_ref[...])
        finish_forward(total, info_ref[2], None, rows_ref[...], True, *outs)

    outs = forward_outs(True)
    return pl.pallas_call(
        body,
        grid_spec=pltpu.PrefetchScalarGridSpec(
            num_scalar_prefetch=1,
            grid=(1,),
            in_specs=[whole(inputs.shape), whole(weight.shape), whole(rows.shape)],
            out_specs=[whole(one.shape) for one in outs],
        ),
        out_shape=outs,
        compiler_params=params(),
        cost_estimate=cost(2 * TOKENS * 27 * HALF, 3 * TOKENS * HALF * 4),
    )(info, inputs, weight, rows)


def conv_forward(info, mine, other, table, at, base, rows, act):
    with_base = base is not None

    def body(info_ref, mine_ref, other_ref, weight_ref, rows_ref, *rest):
        base_ref = rest[0] if with_base else None
        outs, (moved, total) = (rest[int(with_base) : -2], rest[-2:])
        step = pl.program_id(0)

        @pl.when(step == 0)
        def _():
            both = two_sides(info_ref[0], mine_ref[...], other_ref[...])
            fill_moved(moved, both.astype(jnp.float32))
            total[...] = jnp.zeros_like(total)

        row_off, col_off = tap_of(step, info_ref[1])
        total[...] += dot(moved[col_off + 1, rows_from(row_off), :], weight_ref[...])

        @pl.when(step == 8)
        def _():
            value_out = outs[3] if with_base else None
            held = base_ref[...] if with_base else None
            finish_forward(
                total[...], info_ref[2], held, rows_ref[...], act, *outs[:3], value_out
            )

    outs = forward_outs(with_base)
    extra = [base] if with_base else []
    return pl.pallas_call(
        body,
        grid_spec=pltpu.PrefetchScalarGridSpec(
            num_scalar_prefetch=1,
            grid=(9,),
            in_specs=[
                whole(mine.shape),
                whole(other.shape),
                pl.BlockSpec(
                    (pl.Element(C), pl.Element(HALF)),
                    lambda i, info_ref: (
                        pl.multiple_of(at + C * i, 8),
                        pl.multiple_of(HALF * info_ref[0], HALF),
                    ),
                ),
                whole(rows.shape),
            ]
            + [whole(one.shape) for one in extra],
            out_specs=[whole(one.shape) for one in outs],
            scratch_shapes=[
                pltpu.VMEM((3, PADDED, C), jnp.bfloat16),
                pltpu.VMEM((TOKENS, HALF), jnp.float32),
            ],
        ),
        out_shape=outs,
        compiler_params=params(),
        cost_estimate=cost(18 * TOKENS * C * HALF, 9 * C * HALF * 2 + 6 * TOKENS * HALF * 4),
    )(info, mine, other, table, rows, *extra)


def conv_backward(info, grad_mine, grad_other, act_mine, act_other, table, store, at, saved, rows, base):
    with_base = base is not None
    old, old_specs, out_spec, out_shape = store_specs(store, at, C)

    def body(info_ref, *refs):
        refs = refs[len(old) :]
        gm_ref, go_ref, am_ref, ao_ref, weight_ref, normed_ref, inv_ref, rows_ref = refs[:8]
        base_ref = refs[8] if with_base else None
        refs = refs[8 + int(with_base) :]
        out_ref, low_out, sums_out = refs[:3]
        moved, turned_act, shifted, total = refs[-4:]
        step = pl.program_id(0)

        @pl.when(step == 0)
        def _():
            both = two_sides(info_ref[0], gm_ref[...], go_ref[...])
            fill_moved(moved, both.astype(jnp.float32))
            act = two_sides(info_ref[0], am_ref[...], ao_ref[...]).astype(jnp.float32)
            for slab in range(3):
                turned_act[slab] = columns_moved(act, slab - 1).T.astype(jnp.bfloat16)
            empty = jnp.zeros((FRAME, HALF), jnp.bfloat16)
            shifted[0:FRAME, :] = empty
            shifted[FRAME : FRAME + TOKENS, :] = gm_ref[...]
            shifted[FRAME + TOKENS : PADDED, :] = empty
            total[...] = jnp.zeros_like(total)

        row_off, col_off = tap_of(step, info_ref[1])
        out_ref[...] = dot(turned_act[col_off + 1], shifted[rows_from(-row_off), :])
        total[...] += dot_t(moved[1 - col_off, rows_from(-row_off), :], weight_ref[...])

        @pl.when(step == 8)
        def _():
            mask = token_mask(info_ref[2])
            gain, normed, inv_std = (rows_ref[0:1], normed_ref[...], inv_ref[0:1])
            norm = normed * gain + rows_ref[1:2]
            logistic = 1.0 / (1.0 + jnp.exp(-norm))
            gradient = mask * total[...] * (logistic * (1.0 + norm * (1.0 - logistic)))
            result, gain_grad, bias_grad = norm_back(
                gradient, normed, inv_std, mask, info_ref[2], gain
            )
            if with_base:
                result = mask * (result + base_ref[...])
            low_result = result.astype(jnp.bfloat16)
            low_out[...] = low_result
            sums_out[3:4] = column_squares(low_result)
            sums_out[0:1] = jnp.sum(result, axis=0, keepdims=True)
            sums_out[1:2] = gain_grad
            sums_out[2:3] = bias_grad

    extra = [base] if with_base else []
    operands = [grad_mine, grad_other, act_mine, act_other]
    result = pl.pallas_call(
        body,
        grid_spec=pltpu.PrefetchScalarGridSpec(
            num_scalar_prefetch=1,
            grid=(9,),
            in_specs=old_specs
            + [whole(one.shape) for one in operands]
            + [
                pl.BlockSpec(
                    (pl.Element(HALF), pl.Element(C)),
                    lambda i, info_ref: (
                        pl.multiple_of(at + C * i + HALF * info_ref[0], 8),
                        0,
                    ),
                ),
                whole((TOKENS, HALF)),
                whole((8, HALF)),
                whole(rows.shape),
            ]
            + [whole(one.shape) for one in extra],
            out_specs=[
                out_spec,
                whole((TOKENS, HALF)),
                whole((8, HALF)),
            ],
            scratch_shapes=[
                pltpu.VMEM((3, PADDED, C), jnp.bfloat16),
                pltpu.VMEM((3, C, TOKENS), jnp.bfloat16),
                pltpu.VMEM((PADDED, HALF), jnp.bfloat16),
                pltpu.VMEM((TOKENS, HALF), jnp.float32),
            ],
        ),
        out_shape=[
            out_shape,
            jax.ShapeDtypeStruct((TOKENS, HALF), jnp.bfloat16),
            jax.ShapeDtypeStruct((8, HALF), jnp.float32),
        ],
        input_output_aliases={1 + k: k for k in range(len(old))},
        compiler_params=params(),
        cost_estimate=cost(36 * TOKENS * C * HALF, 9 * C * HALF * 6 + 6 * TOKENS * HALF * 4),
    )(info, *old, *operands, table, *saved, rows, *extra)
    store.write(result[0], None)
    return (result[1], result[2])


def column_squares(values):
    wide = values.astype(jnp.float32)
    return jnp.sum(wide * wide, axis=0, keepdims=True)


def norm_back(gradient, normed, inv_std, mask, limit, gain):
    same = group_same()
    share = 1.0 / (limit.astype(jnp.float32) * (C // GROUPS))
    scaled = gradient * gain
    first = spread_in(jnp.sum(scaled * mask, axis=0, keepdims=True), same) * share
    second = spread_in(jnp.sum(scaled * normed * mask, axis=0, keepdims=True), same) * share
    result = mask * inv_std * (scaled - first - normed * second)
    return (
        result,
        jnp.sum(gradient * normed, axis=0, keepdims=True),
        jnp.sum(gradient, axis=0, keepdims=True),
    )


def gather_small(place, value):
    stride, joined = (1, value[None])
    while stride < place.count:
        other = place.swap(joined, stride)
        upper = (place.index // stride) % 2 == 1
        joined = jnp.where(
            upper,
            jnp.concatenate([other, joined], axis=0),
            jnp.concatenate([joined, other], axis=0),
        )
        stride *= 2
    return joined


def windows(values, turned, sign):
    width = values.shape[1]
    col = (lax.iota(jnp.int32, TOKENS) % FRAME)[:, None]
    zero_one = jnp.zeros((1, width), values.dtype)
    zero_row = jnp.zeros((FRAME, width), values.dtype)
    none = jnp.zeros((), values.dtype)
    across = {
        -1: jnp.where(col > 0, jnp.concatenate([zero_one, values[:-1]], axis=0), none),
        0: values,
        1: jnp.where(col < FRAME - 1, jnp.concatenate([values[1:], zero_one], axis=0), none),
    }
    moved = {}
    for col_off, value in across.items():
        moved[-1, col_off] = jnp.concatenate([zero_row, value[:-FRAME]], axis=0)
        moved[0, col_off] = value
        moved[1, col_off] = jnp.concatenate([value[FRAME:], zero_row], axis=0)
    out = []
    for row_off, col_off in tap_offsets:
        plain = moved[sign * row_off, sign * col_off]
        other = moved[sign * col_off, sign * row_off]
        out.append(plain if row_off == col_off else jnp.where(turned, other, plain))
    return jnp.concatenate(out, axis=1)


def group_spread(channel_sums):
    at = lax.iota(jnp.int32, HALF) // (C // GROUPS)
    same = (at[:, None] == at[None, :]).astype(jnp.float32)
    return jnp.dot(channel_sums, same, precision=lax.Precision.HIGHEST)


def group_backward(gradient, normed, inv_std, mask, denominator, gain_vec):
    scaled = gradient * gain_vec
    sums = group_spread(
        jnp.stack([jnp.sum(scaled * mask, axis=0), jnp.sum(scaled * normed * mask, axis=0)])
    )
    input_grad = mask * inv_std * (
        scaled - sums[0:1] / denominator - normed * (sums[1:2] / denominator)
    )
    return (input_grad, jnp.sum(gradient * normed, axis=0), jnp.sum(gradient, axis=0))


def layer_forward(values, gain_vec, bias_vec):
    mean_val = jnp.mean(values, axis=-1, keepdims=True)
    centered = values - mean_val
    var_val = jnp.mean(centered * centered, axis=-1, keepdims=True)
    inv_std = lax.rsqrt(var_val + eps_layer)
    normed = centered * inv_std
    return (low(normed * gain_vec + bias_vec), normed, inv_std)


def layer_backward(gradient, normed, inv_std, gain_vec):
    scaled = gradient * gain_vec
    first = jnp.mean(scaled, axis=-1, keepdims=True)
    second = jnp.mean(scaled * normed, axis=-1, keepdims=True)
    input_grad = inv_std * (scaled - first - normed * second)
    return (input_grad, jnp.sum(gradient * normed, axis=0), jnp.sum(gradient, axis=0))


def heads_of(value):
    return value.reshape(value.shape[0], LOCAL_HEADS, DHEAD)


def head_scores(query, key, key_mask):
    scores = jnp.einsum("qhd,khd->hqk", query, key, preferred_element_type=jnp.float32) * 0.125
    return jnp.where(key_mask, scores, -1e30)


def attend(query, key, value, key_mask):
    scores = head_scores(query, key, key_mask)
    row_max = jnp.max(scores, axis=-1, keepdims=True)
    exponent = jnp.exp(scores - row_max)
    totals = jnp.sum(exponent, axis=-1, keepdims=True)
    out = jnp.einsum(
        "hqk,khd->qhd", low(exponent / totals), value, preferred_element_type=jnp.float32
    )
    return (low(out).reshape(TOKENS, HALF), row_max + jnp.log(totals))


def attend_back(query, key, value, key_mask, log_total, out_grad):
    probs = jnp.exp(head_scores(query, key, key_mask) - log_total)
    prob_grad = jnp.einsum("qhd,khd->hqk", out_grad, value, preferred_element_type=jnp.float32)
    inner = jnp.sum(probs * prob_grad, axis=-1, keepdims=True)
    score_grad = low(probs * (prob_grad - inner) * 0.125)
    query_grad = jnp.einsum("hqk,khd->qhd", score_grad, key, preferred_element_type=jnp.float32)
    key_grad = jnp.einsum("hqk,qhd->khd", score_grad, query, preferred_element_type=jnp.float32)
    value_grad = jnp.einsum(
        "hqk,qhd->khd", low(probs), out_grad, preferred_element_type=jnp.float32
    )
    return low(
        jnp.concatenate(
            [part.reshape(TOKENS, HALF) for part in (query_grad, key_grad, value_grad)], axis=1
        )
    )


def cross_split(context_kv):
    return (
        context_kv[:, :HALF].reshape(2, LOCAL_HEADS, DHEAD),
        context_kv[:, HALF:].reshape(2, LOCAL_HEADS, DHEAD),
    )


def cross_attend(query, context_kv):
    key, value = cross_split(context_kv)
    scores = jnp.einsum("thd,jhd->thj", query, key, preferred_element_type=jnp.float32) * 0.125
    probs = jax.nn.softmax(scores, axis=-1)
    out = jnp.einsum("thj,jhd->thd", probs, value.astype(jnp.float32))
    return (probs, low(out).reshape(TOKENS, HALF))


def cross_back(query, context_kv, probs, out_grad):
    key, value = cross_split(context_kv)
    prob_grad = jnp.einsum("thd,jhd->thj", out_grad, value, preferred_element_type=jnp.float32)
    score_grad = probs * (prob_grad - jnp.sum(probs * prob_grad, axis=-1, keepdims=True)) * 0.125
    query_grad = jnp.einsum("thj,jhd->thd", score_grad, key.astype(jnp.float32))
    key_grad = jnp.einsum("thj,thd->jhd", score_grad, query.astype(jnp.float32))
    value_grad = jnp.einsum("thj,thd->jhd", probs, out_grad.astype(jnp.float32))
    return (
        query_grad.reshape(TOKENS, HALF),
        jnp.concatenate([key_grad.reshape(2, HALF), value_grad.reshape(2, HALF)], axis=1),
    )


def own_columns(place, weight):
    split = weight.reshape(weight.shape[0], -1, 2, HALF)
    return pick(split, place.side, 2).reshape(weight.shape[0], -1)


def frame_of(place, latents, target_noise, turned):
    both = jnp.concatenate([latents, target_noise], axis=-1)
    stride, joined = (1, both[None])
    while stride < place.rows:
        other = place.swap(joined, stride)
        upper = (place.index // stride) % 2 == 1
        joined = jnp.where(
            upper,
            jnp.concatenate([other, joined], axis=0),
            jnp.concatenate([joined, other], axis=0),
        )
        stride *= 2
    image = pick(joined, place.slot, 1).reshape(SIDE, SIDE, 2 * LC)
    portrait = image[:, :FRAME]
    landscape = jnp.transpose(image[:FRAME], (1, 0, 2))
    return jnp.where(turned, landscape, portrait).reshape(TOKENS, 2 * LC)


def train_step(place, store, table, mats, vecs, latents, target_noise, label, step_value, orient, extent):
    bias_grads = {}
    half, full = (place.half, place.full)
    turned = orient != 1
    seen = lax.iota(jnp.int32, TOKENS) < extent * FRAME
    mask = seen.astype(jnp.float32)[:, None]
    denominator = (extent * FRAME * (C // GROUPS)).astype(jnp.float32)
    frame = frame_of(place, latents, target_noise, turned)
    noise_img = frame[:, LC:]
    share = noise_level(step_value)
    noisy = mask * (jnp.sqrt(share) * frame[:, :LC] + jnp.sqrt(1.0 - share) * noise_img)

    embed_in = low(time_embed(step_value))[None]
    pre_one = dot(embed_in, mats["w_t1"]) + vecs["b_t1"]
    hidden_one = low(jax.nn.silu(pre_one))
    pre_two = dot(hidden_one, mats["w_t2"]) + vecs["b_t2"]
    hidden_two = low(jax.nn.silu(pre_two))
    time_vec = dot(hidden_two, mats["w_tp"]) + vecs["b_tp"]
    class_vec = lax.dynamic_slice(mats["table"], (label, 0), (1, C)).astype(jnp.float32)

    info = jnp.stack([place.side, turned.astype(jnp.int32), extent * FRAME]).astype(jnp.int32)
    side_row = lambda name: half(vecs[name])[None]
    stack = lambda *rows: jnp.concatenate(rows, axis=0)
    at = store.places
    pad_in = windows(low(noisy), turned, 1)
    act_one, normed_one, inv_one, state_zero = first_forward(
        info,
        pad_in,
        half(mats["w_in"]),
        stack(side_row("b_in"), side_row("g1"), side_row("bb1")),
    )
    act_one_peer = place.swap(act_one)
    act_two, normed_two, inv_two = conv_forward(
        info,
        act_one,
        act_one_peer,
        table,
        at["w_c1"],
        None,
        stack(side_row("b_c1") + half(time_vec), side_row("g2"), side_row("bb2")),
        True,
    )
    act_two_peer = place.swap(act_two)
    token_own, normed_three, inv_three, state_one = conv_forward(
        info,
        act_two,
        act_two_peer,
        table,
        at["w_c2"],
        state_zero,
        stack(side_row("b_c2"), side_row("g3"), side_row("bb3")),
        False,
    )
    token_in = full(token_own)
    resid_zero = dot(token_in, mats["w_pin"]) + vecs["b_pin"]
    ln_one, normed_ln1, inv_ln1 = layer_forward(resid_zero, vecs["n1g"], vecs["n1b"])
    qkv_own = own_columns(place, mats["w_qkv"])
    packed = low(dot(ln_one, qkv_own))
    query, key, value = [heads_of(packed[:, i * HALF : (i + 1) * HALF]) for i in range(3)]
    attended_own, log_total = attend(query, key, value, seen)
    attended = full(attended_own)
    resid_one = resid_zero + dot(attended, mats["w_o"]) + vecs["b_o"]
    ln_two, normed_ln2, inv_ln2 = layer_forward(resid_one, vecs["n2g"], vecs["n2b"])
    cq_own = half(mats["w_cq"])
    cross_query = heads_of(low(dot(ln_two, cq_own)))
    context = low(jnp.concatenate([class_vec, time_vec], axis=0))
    ckv_own = own_columns(place, mats["w_ckv"])
    context_kv = low(dot(context, ckv_own))
    cross_prob, cross_own = cross_attend(cross_query, context_kv)
    cross_out = full(cross_own)
    resid_two = resid_one + dot(cross_out, mats["w_co"]) + vecs["b_co"]
    ln_three, normed_ln3, inv_ln3 = layer_forward(resid_two, vecs["n3g"], vecs["n3b"])
    ff1_own = own_columns(place, mats["w_ff1"])
    projected = dot(ln_three, ff1_own) + own_columns(place, vecs["b_ff1"][None])
    wide = FFI // 2
    lift, gate = (projected[:, :wide], projected[:, wide:])
    cdf = 0.5 * (1.0 + lax.erf(gate * math.sqrt(0.5)))
    gated_own = low(lift * gate * cdf)
    gated_peer = place.swap(gated_own)
    gated = jnp.concatenate(
        [
            place.join(gated_own[:, i * HALF : (i + 1) * HALF], gated_peer[:, i * HALF : (i + 1) * HALF])
            for i in range(FFI // WIDE)
        ],
        axis=1,
    )
    resid_three = resid_two + dot(gated, mats["w_ff2"]) + vecs["b_ff2"]
    out_in = low(resid_three)
    branch = dot(out_in, half(mats["w_pout"])) + half(vecs["b_pout"])
    state_two = state_one + mask * branch
    pad_out = windows(full(low(state_two)), turned, 1)
    predicted = dot(pad_out, mats["w_out"]) + vecs["b_out"]
    residual_err = predicted - noise_img
    loss = jnp.sum(mask * residual_err * residual_err)

    out_grad = 2.0 * mask * residual_err
    bias_grads["b_out"] = jnp.sum(out_grad, axis=0)
    out_low = low(out_grad)
    w_out_back = jnp.transpose(mats["w_out"].reshape(9, C, LC), (0, 2, 1)).reshape(9 * LC, C)
    state_grad = dot(windows(out_low, turned, -1), w_out_back)
    branch_grad = mask * state_grad
    state_grad = half(state_grad)
    bias_grads["b_pout"] = half(jnp.sum(branch_grad, axis=0))
    grad_low = low(branch_grad)
    store.add("w_pout", out_in, half(grad_low))
    w_out_grad = half(t_dot(pad_out, out_low).reshape(9 * LC, C))
    last = store.total - store.places["w_out"] - 9 * LC
    store.put(store.places["w_out"], jnp.pad(w_out_grad, ((0, last), (0, 0))))
    resid_grad = dot_t(grad_low, mats["w_pout"])
    bias_grads["b_ff2"] = half(jnp.sum(resid_grad, axis=0))
    grad_low = low(resid_grad)
    store.add("w_ff2", gated, half(grad_low))
    ff2_own = pick(mats["w_ff2"].reshape(-1, 2, HALF, C), place.side, 1).reshape(wide, C)
    gated_grad = dot_t(grad_low, ff2_own)
    density = jnp.exp(-0.5 * gate * gate) * (1.0 / math.sqrt(2.0 * math.pi))
    proj_grad = jnp.concatenate(
        [gated_grad * gate * cdf, gated_grad * lift * (cdf + gate * density)], axis=1
    )
    bias_grads["b_ff1"] = jnp.sum(proj_grad, axis=0)
    grad_low = low(proj_grad)
    store.add("w_ff1", ln_three, grad_low)
    ln_grad = dot_t(grad_low, ff1_own)
    ln_grad = ln_grad + place.swap(ln_grad)
    ln_grad, gain, bias = layer_backward(ln_grad, normed_ln3, inv_ln3, vecs["n3g"])
    bias_grads["n3g"], bias_grads["n3b"] = (half(gain), half(bias))
    resid_grad = resid_grad + ln_grad
    bias_grads["b_co"] = half(jnp.sum(resid_grad, axis=0))
    grad_low = low(resid_grad)
    store.add("w_co", cross_out, half(grad_low))
    cross_grad = heads_of(low(dot_t(grad_low, half(mats["w_co"], 0))))
    query_grad, kv_grad = cross_back(cross_query, context_kv, cross_prob, cross_grad)
    query_low, kv_low = (low(query_grad), low(kv_grad))
    store.add("w_cq", ln_two, query_low)
    store.add("w_ckv", context, kv_low)
    context_grad = dot_t(kv_low, ckv_own)
    context_grad = context_grad + place.swap(context_grad)
    ln_grad = dot_t(full(query_low), mats["w_cq"])
    ln_grad, gain, bias = layer_backward(ln_grad, normed_ln2, inv_ln2, vecs["n2g"])
    bias_grads["n2g"], bias_grads["n2b"] = (half(gain), half(bias))
    resid_grad = resid_grad + ln_grad
    bias_grads["b_o"] = half(jnp.sum(resid_grad, axis=0))
    grad_low = low(resid_grad)
    store.add("w_o", attended, half(grad_low))
    attended_grad = heads_of(low(dot_t(grad_low, half(mats["w_o"], 0))))
    packed_grad = attend_back(query, key, value, seen, log_total, attended_grad)
    store.add("w_qkv", ln_one, packed_grad)
    ln_grad = dot_t(packed_grad, qkv_own)
    ln_grad = ln_grad + place.swap(ln_grad)
    ln_grad, gain, bias = layer_backward(ln_grad, normed_ln1, inv_ln1, vecs["n1g"])
    bias_grads["n1g"], bias_grads["n1b"] = (half(gain), half(bias))
    resid_grad = resid_grad + ln_grad
    bias_grads["b_pin"] = half(jnp.sum(resid_grad, axis=0))
    grad_low = low(resid_grad)
    store.add("w_pin", token_in, half(grad_low))
    token_grad = dot_t(grad_low, half(mats["w_pin"], 0))
    norm_grad, bias_grads["g3"], bias_grads["bb3"] = group_backward(
        token_grad, normed_three, inv_three[0:1], mask, denominator, half(vecs["g3"])
    )
    state_grad = state_grad + norm_grad

    conv_grad = mask * state_grad
    bias_grads["b_c2"] = jnp.sum(conv_grad, axis=0)
    conv_low = low(conv_grad)
    c2_squares = column_squares(conv_low)
    conv_low, sums = conv_backward(
        info,
        conv_low,
        place.swap(conv_low),
        act_two,
        act_two_peer,
        table,
        store,
        at["w_c2"],
        (normed_two, inv_two),
        stack(side_row("g2"), side_row("bb2")),
        None,
    )
    conv_sum, bias_grads["g2"], bias_grads["bb2"] = (sums[0], sums[1], sums[2])
    bias_grads["b_c1"] = conv_sum
    time_grad = full(conv_sum[None]) + context_grad[1:2]
    bias_grads["b_tp"] = half(time_grad[0])
    time_low = low(time_grad)
    store.add("w_tp", hidden_two, half(time_low))
    pre_grad = dot_t(time_low, mats["w_tp"]) * silu_slope(pre_two)
    bias_grads["b_t2"] = own_columns(place, pre_grad)[0]
    pre_low = low(pre_grad)
    store.add("w_t2", hidden_one, own_columns(place, pre_low))
    pre_grad = dot_t(pre_low, mats["w_t2"]) * silu_slope(pre_one)
    bias_grads["b_t1"] = own_columns(place, pre_grad)[0]
    store.add("w_t1", embed_in, own_columns(place, low(pre_grad)))
    rows = lax.iota(jnp.int32, NCLS)[:, None] == label
    store.put(store.places["table"], jnp.where(rows, half(context_grad[0:1]), 0.0))
    store.put(0, jnp.zeros((store.places["w_t1"], HALF), jnp.float32))

    squares = [jnp.max(rows_of).reshape(1, 1) for rows_of in (inv_one[1], inv_two[1], c2_squares, sums[3])]
    tops = largest_of_all(place, jnp.concatenate([store.top] + squares, axis=1))[0]
    bound = jnp.maximum(tops[0], 1.01 * jnp.sqrt(tops[1] * tops[4]))
    bound = jnp.maximum(bound, 1.01 * jnp.sqrt(tops[2] * tops[3]))
    scale = (WIRE_TOP / (place.count // 2)) / jnp.maximum(bound, 1e-30)
    in_low, sums = conv_backward(
        info,
        conv_low,
        place.swap(conv_low),
        act_one,
        act_one_peer,
        table,
        store,
        at["w_c1"],
        (normed_one, inv_one),
        stack(side_row("g1"), side_row("bb1")),
        state_grad,
    )
    bias_grads["b_in"], bias_grads["g1"], bias_grads["bb1"] = (sums[0], sums[1], sums[2])
    w_in_grad = t_dot(pad_in, in_low)
    return (bias_grads, w_in_grad, scale, loss)


def adam_update(params, first_mom, second, gradient, decay_rate):
    first_new = adam_one * first_mom + (1.0 - adam_one) * gradient
    second_new = adam_two * second + (1.0 - adam_two) * gradient * gradient
    step_size = (
        first_new
        / (1.0 - adam_one**STEP)
        / (jnp.sqrt(second_new / (1.0 - adam_two**STEP)) + adam_eps)
    )
    return (params - learn_rate * (step_size + decay_rate * params), first_new, second_new)


def local(
    latents,
    target_noise,
    labels,
    timesteps,
    orient,
    extent,
    mat_params,
    mat_first,
    mat_second,
    mat_ema,
    vec_params,
    vec_first,
    vec_second,
    vec_ema,
):
    place = Place()
    length = mat_params.shape[0]
    rows = shard_rows(length * place.count, place.count)
    block = to_blocks(place, mat_params.astype(jnp.bfloat16), rows)
    table = lax.all_gather(block, ("dp", "rows"), axis=0, tiled=True)
    mats, at = ({}, LEAD)
    for name, depth, width in mat_layout():
        count = depth * width // WIDE
        mats[name] = table[at : at + count].reshape(depth, width)
        if name == "w_in":
            mats[name] = table[at : at + count]
        at += count
    vec_len = vec_params.shape[0]
    vec_wide = -(-vec_len // 128) * 128
    padded = jnp.pad(vec_params, (0, vec_wide - vec_len)).reshape(-1, 128)
    vec_all = gather_small(place, padded).reshape(place.count, vec_wide)[:, :vec_len]
    vec_all = vec_all.reshape(-1).astype(jnp.bfloat16).astype(jnp.float32)
    vecs = unpack(vec_all, vec_layout())
    own = lambda values: pick(values, place.slot, 0)
    store = Store(place, rows)
    bias_grads, w_in_grad, scale, loss = train_step(
        place,
        store,
        table,
        mats,
        vecs,
        latents,
        target_noise,
        own(labels),
        own(timesteps),
        own(orient),
        own(extent),
    )
    small = [bias_grads[record[0]].reshape(-1, HALF) for record in vec_layout()[:-1]]
    count_local = (own(extent) * FRAME).astype(jnp.float32)
    extra = jnp.concatenate([bias_grads["b_out"], jnp.stack([loss, count_local])])
    extra = jnp.pad(extra, (0, HALF - LC - 2))[None]
    small = jnp.concatenate(small + [extra, w_in_grad], axis=0)
    small = jnp.pad(small, ((0, -small.shape[0] % 8), (0, 0)))
    small = place.full(place.chip_sum(small))
    body = sum(record[1] for record in vec_layout()[:-1]) // WIDE
    loss_sum, pixel_count = (small[body, LC], small[body, LC + 1])
    w_in_sum = small[body + 1 : body + 1 + 9 * LC]
    vec_flat = jnp.concatenate([small[:body].reshape(-1), small[body, :LC]])
    vec_flat = jnp.pad(vec_flat, (0, vec_len * place.count - vec_flat.shape[0]))
    shard_vec = lax.dynamic_slice(vec_flat, (vec_len * place.index,), (vec_len,))

    block_grad = scatter_sum(place, store.buffer, scale, rows)
    held = jnp.where(place.index == 0, w_in_sum, block_grad[LEAD : LEAD + 9 * LC])
    block_grad = lax.dynamic_update_slice(block_grad, held, (LEAD, 0))
    shard_mat = from_blocks(place, block_grad, length)
    square = jnp.sum(block_grad * block_grad).reshape(1, 1)
    square = place.chip_sum(square + place.swap(square))[0, 0]
    square = square + jnp.sum(vec_flat * vec_flat)
    inverse = 1.0 / pixel_count
    grad_norm = jnp.sqrt(square) * inverse
    factor = clip_norm / jnp.maximum(grad_norm, clip_norm) * inverse
    new_mat, mat_first_new, mat_second_new = adam_update(
        mat_params, mat_first, mat_second, shard_mat * factor, weight_decay
    )
    new_vec, vec_first_new, vec_second_new = adam_update(
        vec_params, vec_first, vec_second, shard_vec * factor, 0.0
    )
    ema_rate = min(ema_ceiling, (1.0 + STEP) / (10.0 + STEP))
    mat_ema_new = ema_rate * mat_ema + (1.0 - ema_rate) * new_mat
    vec_ema_new = ema_rate * vec_ema + (1.0 - ema_rate) * new_vec
    return (
        new_mat,
        mat_first_new,
        mat_second_new,
        mat_ema_new,
        new_vec,
        vec_first_new,
        vec_second_new,
        vec_ema_new,
        grad_norm,
        loss_sum,
        pixel_count,
    )


def solution(mesh):
    return jax.shard_map(
        local,
        mesh=mesh,
        in_specs=(
            P("dp", "rows", None, None),
            P("dp", "rows", None, None),
            P("dp"),
            P("dp"),
            P("dp"),
            P("dp"),
            P(("dp", "rows")),
            P(("dp", "rows")),
            P(("dp", "rows")),
            P(("dp", "rows")),
            P(("dp", "rows")),
            P(("dp", "rows")),
            P(("dp", "rows")),
            P(("dp", "rows")),
        ),
        out_specs=(
            P(("dp", "rows")),
            P(("dp", "rows")),
            P(("dp", "rows")),
            P(("dp", "rows")),
            P(("dp", "rows")),
            P(("dp", "rows")),
            P(("dp", "rows")),
            P(("dp", "rows")),
            P(),
            P(),
            P(),
        ),
        check_vma=False,
    )
```

```python
import math

import jax
import jax.numpy as jnp
from jax import lax
from jax.experimental import pallas as pl
from jax.experimental.pallas import tpu as pltpu
from jax.sharding import PartitionSpec as P

C = 512
HEADS = 8
DHEAD = 64
FFI = 2048
TE = 256
TD = 1024
NCLS = 1000
LC = 3
GROUPS = 32
SIDE = 32
NT = 1000
STEP = 10


tap_offsets = [(-1, -1), (-1, 0), (-1, 1), (0, -1), (0, 0), (0, 1), (1, -1), (1, 0), (1, 1)]
eps_group = 1e-06
eps_layer = 1e-05
beta_first = 0.00085
beta_last = 0.012
adam_one = 0.9
adam_two = 0.999
adam_eps = 1e-08
learn_rate = 0.05
weight_decay = 0.01
ema_ceiling = 0.9999
clip_norm = 0.1


def mat_layout():
    return [
        ("w_in", 9 * LC, C),
        ("w_t1", TE, TD),
        ("w_t2", TD, TD),
        ("w_tp", TD, C),
        ("table", NCLS, C),
        ("w_c1", 9 * C, C),
        ("w_c2", 9 * C, C),
        ("w_pin", C, C),
        ("w_qkv", C, 3 * C),
        ("w_o", C, C),
        ("w_cq", C, C),
        ("w_ckv", C, 2 * C),
        ("w_co", C, C),
        ("w_ff1", C, 2 * FFI),
        ("w_ff2", FFI, C),
        ("w_pout", C, C),
        ("w_out", 9 * C, LC),
    ]


def vec_layout():
    names = [
        "b_tp",
        "b_in",
        "g1",
        "bb1",
        "b_c1",
        "g2",
        "bb2",
        "b_c2",
        "g3",
        "bb3",
        "b_pin",
        "n1g",
        "n1b",
        "b_o",
        "n2g",
        "n2b",
        "b_co",
        "n3g",
        "n3b",
    ]
    return (
        [("b_t1", TD), ("b_t2", TD)]
        + [(name_one, C) for name_one in names]
        + [("b_ff1", 2 * FFI), ("b_ff2", C), ("b_pout", C), ("b_out", LC)]
    )


def unpack(joined, layout):
    pieces = {}
    start_at = 0
    for record in layout:
        length = 1
        for extent_one in record[1:]:
            length = length * extent_one
        pieces[record[0]] = joined[start_at : start_at + length].reshape(record[1:])
        start_at = start_at + length
    return pieces


def noise_level(step_value):
    steps_idx = jnp.arange(NT).astype(jnp.float32)
    root_beta = math.sqrt(beta_first) + (
        math.sqrt(beta_last) - math.sqrt(beta_first)
    ) * steps_idx / (NT - 1)
    log_keep = jnp.log1p(-root_beta * root_beta)
    return jnp.exp(jnp.sum(jnp.where(jnp.arange(NT) <= step_value, log_keep, 0.0)))


def time_embed(step_value):
    frequency = jnp.exp(-math.log(10000.0) * jnp.arange(TE // 2).astype(jnp.float32) / (TE // 2))
    angles = step_value.astype(jnp.float32) * frequency
    return jnp.concatenate([jnp.cos(angles), jnp.sin(angles)])


WIDE = 512
HALF = 256
LEAD = 5
FRAME = 16
TOKENS = SIDE * FRAME
LOCAL_HEADS = HEADS // 2
WIRE_TOP = 32768.0


def silu_slope(values):
    logistic = jax.nn.sigmoid(values)
    return logistic * (1.0 + values * (1.0 - logistic))


def dot(left, right):
    return jnp.dot(left, right, preferred_element_type=jnp.float32)


def dot_t(left, right):
    return lax.dot_general(
        left, right, (((1,), (1,)), ((), ())), preferred_element_type=jnp.float32
    )


def t_dot(left, right):
    return lax.dot_general(
        left, right, (((0,), (0,)), ((), ())), preferred_element_type=jnp.float32
    )


def low(values):
    return values.astype(jnp.bfloat16)


class Place:
    def __init__(self):
        self.dp, self.rows = (lax.axis_size("dp"), lax.axis_size("rows"))
        self.count = self.dp * self.rows
        self.index = lax.axis_index("dp") * self.rows + lax.axis_index("rows")
        self.side = self.index % 2
        self.slot = (self.index // 2) % 2
        digits, left = ([], self.dp)
        while left > 4:
            digits.append(4)
            left //= 4
        digits.append(left)
        self.digits = digits + [2]
        strides, step = ([], 2)
        for size in reversed(self.digits):
            strides.insert(0, step)
            step *= size
        self.strides = strides
        self.coords = [(self.index // s) % n for s, n in zip(strides, self.digits)]

    def move(self, value, pairs):
        return lax.ppermute(value, ("dp", "rows"), pairs)

    def swap(self, value, stride=1):
        return self.move(value, [(k, k ^ stride) for k in range(self.count)])

    def shift(self, value, by):
        return self.move(
            value, [(k, k + by) for k in range(self.count) if 0 <= k + by < self.count]
        )

    def rotate(self, value, axis, by):
        stride, size = (self.strides[axis], self.digits[axis])
        pairs = []
        for k in range(self.count):
            at = (k // stride) % size
            pairs.append((k, k + ((at + by) % size - at) * stride))
        return self.move(value, pairs)

    def step(self, value, axis, direction, hops):
        stride, size = (self.strides[axis], self.digits[axis])
        pairs = []
        for k in range(self.count):
            at = (k // stride) % size
            rank = at if direction > 0 else size - 1 - at
            if rank <= hops and rank < size - 1:
                pairs.append((k, k + direction * stride))
        return self.move(value, pairs)

    def half(self, value, axis=-1):
        axis = axis % value.ndim
        return lax.dynamic_slice_in_dim(value, self.side * HALF, HALF, axis)

    def join(self, mine, other):
        first = jnp.where(self.side == 0, mine, other)
        second = jnp.where(self.side == 0, other, mine)
        return jnp.concatenate([first, second], axis=-1)

    def full(self, mine):
        return self.join(mine, self.swap(mine))

    def chip_sum(self, value):
        stride = 2
        while stride < self.count:
            value = value + self.swap(value, stride)
            stride *= 2
        return value


def shard_rows(flat_len, count):
    length = flat_len // count
    rows = -(-(LEAD * WIDE + flat_len) // (WIDE * count))
    rows = -(-rows // 8) * 8
    while rows * WIDE - length < LEAD * WIDE:
        rows += 8
    return rows


def to_blocks(place, shard, rows):
    length, block = (shard.shape[0], rows * WIDE)
    drift = block - length
    reach = drift * (place.count - 1) - LEAD * WIDE + block
    parts, hop = ([jnp.zeros((LEAD * WIDE,), shard.dtype), shard], 1)
    while hop * length < reach:
        take = min(length, reach - hop * length)
        take = min(length, -(-take // 1024) * 1024)
        parts.append(place.shift(shard[:take], -hop))
        hop += 1
    joined = jnp.concatenate(parts)
    lack = drift * (place.count - 1) + block - joined.shape[0]
    if lack > 0:
        joined = jnp.pad(joined, (0, lack))
    return lax.dynamic_slice(joined, (drift * place.index,), (block,)).reshape(rows, WIDE)


def from_blocks(place, block, length):
    flat = block.reshape(-1)
    drift = flat.shape[0] - length
    reach = drift * (place.count - 1) - LEAD * WIDE
    parts, hop, lead = ([flat], 1, 0)
    while lead < reach:
        take = min(flat.shape[0], -(-(reach - lead) // 1024) * 1024)
        parts.insert(0, place.shift(flat[flat.shape[0] - take :], hop))
        lead += take
        hop += 1
    joined = jnp.concatenate(parts)
    start = lead + LEAD * WIDE - drift * place.index
    return lax.dynamic_slice(joined, (start,), (length,))


def pick(values, index, axis):
    return lax.dynamic_index_in_dim(values, index, axis, keepdims=False)


def wire(values):
    return values.astype(jnp.float16)


def plain(values):
    return values.astype(jnp.float32)


def lane_row(values):
    lane = lax.broadcasted_iota(jnp.int32, (1, 128), 1)
    row = jnp.zeros((1, 128), jnp.float32)
    for i, value in enumerate(values):
        row = jnp.where(lane == i, value, row)
    return row


SQUARE_AT = 8


class Largest:
    def __init__(self, place, values):
        self.place, self.values, self.stride = (place, values, 1)

    def exchange(self, beside=None):
        if self.stride < self.place.count:
            got = self.place.swap(self.values, self.stride)
            if beside is not None:
                got, beside = lax.optimization_barrier((got, beside))
            self.values = jnp.maximum(self.values, got)
            self.stride *= 2
        return beside

    def finish(self):
        while self.stride < self.place.count:
            self.exchange()
        return self.values


def scatter_part(place, grads, low_row, rows, order, scale):
    held, left, first, factor = (grads, list(range(len(place.digits))), low_row, scale)

    def part_of(dim, index):
        starts, sizes, shape = ([], [], [])
        for at, axis in enumerate(left):
            starts.append(index if at == dim else 0)
            sizes.append(1 if at == dim else place.digits[axis])
            if at != dim:
                shape.append(place.digits[axis])
        out = lax.dynamic_slice(held, starts + [first, 0], sizes + [rows, HALF])
        return out.reshape(shape + [rows, HALF]) * factor

    for axis in order:
        dim = left.index(axis)
        me, size = (place.coords[axis], place.digits[axis])
        total = part_of(dim, me)
        if size == 2 or axis == order[-1]:
            for away in range(1, size):
                sent = wire(part_of(dim, (me + away) % size))
                total = total + plain(place.rotate(sent, axis, away))
        else:
            flows = {1: None, -1: None}
            for hops in range(size - 1):
                for direction in (1, -1):
                    rank = me if direction > 0 else size - 1 - me
                    aim = jnp.minimum(size - 1 - hops + rank, size - 1)
                    aim = aim if direction > 0 else size - 1 - aim
                    value = part_of(dim, aim)
                    if flows[direction] is not None:
                        value = value + plain(flows[direction])
                    flows[direction] = place.step(wire(value), axis, direction, hops)
            total = total + plain(flows[1]) + plain(flows[-1])
        held, first, factor = (total, 0, 1.0)
        left.remove(axis)
    return held


SHARES = (0.39, 0.39)


def scatter_sum(place, grads, scale, rows):
    held = grads.reshape(*place.digits, 2 * rows, HALF)
    axes = list(range(len(place.digits)))[::-1]
    total = 2 * rows
    cuts = [0] + [int(total * sum(SHARES[: i + 1]) / 8 + 0.5) * 8 for i in range(2)] + [total]
    parts = []
    for i in range(3):
        order = axes[i:] + axes[:i]
        parts.append(scatter_part(place, held, cuts[i], cuts[i + 1] - cuts[i], order, scale))
    unit = 1.0 / scale
    parts = [part * unit for part in parts]
    square = sum(jnp.sum(part * part) for part in parts).reshape(1, 1)
    chip = jnp.concatenate(parts, axis=0).reshape(2, rows, HALF)
    mine = pick(chip, place.side, 0)
    other = place.swap(pick(chip, 1 - place.side, 0))
    return (place.join(mine, other), square)


class Store:
    def __init__(self, place, rows):
        self.total = place.count * rows
        self.buffer = None
        self.top = jnp.zeros((1, 1), jnp.float32)
        self.places, at = ({}, LEAD)
        for name, depth, width in mat_layout():
            self.places[name] = at
            at += depth * width // WIDE

    def write(self, out, top):
        self.buffer = out
        if top is not None:
            self.top = jnp.maximum(self.top, top)

    def add(self, name, inputs, gradient):
        if inputs.shape[0] < 16:
            spare = ((0, 16 - inputs.shape[0]), (0, 0))
            inputs, gradient = (jnp.pad(inputs, spare), jnp.pad(gradient, spare))
        grad_into(self, inputs, gradient, self.places[name])

    def put(self, at, values):
        self.buffer = lax.dynamic_update_slice(self.buffer, values, (at, 0))


def store_specs(store, at, tile):
    old = [] if store.buffer is None else [store.buffer]
    out = pl.BlockSpec(
        (pl.Element(tile), pl.Element(HALF)), lambda i, *_: (pl.multiple_of(at + tile * i, 8), 0)
    )
    shape = jax.ShapeDtypeStruct((store.total, HALF), jnp.float32)
    return (old, [pl.BlockSpec(memory_space=pl.ANY) for _ in old], out, shape)


def grad_into(store, inputs, gradient, at):
    tokens, depth = inputs.shape
    pieces = gradient.shape[1] // HALF
    tile = min(depth, 512 if pieces == 1 else 256 if pieces < 8 else 128)
    rows, tiles = (tile * pieces, depth // tile)
    old, old_specs, out_spec, out_shape = store_specs(store, at, rows)

    def body(*refs):
        refs = refs[len(old) :]
        input_ref, gradient_ref, out_ref, top_out = refs[:4]
        step = pl.program_id(0)
        part = t_dot(input_ref[...], gradient_ref[...])
        if pieces == 1:
            out_ref[...] = part
        else:
            mixed = refs[-1]
            for side in range(HALF // 128):
                for j in range(pieces):
                    column = j * HALF + side * 128
                    mixed[pl.ds(j, tile, stride=pieces), :] = part[:, column : column + 128]
                out_ref[:, side * 128 : (side + 1) * 128] = mixed[...]
        largest = jnp.max(jnp.abs(part))

        @pl.when(step == 0)
        def _():
            top_out[0, 0] = largest

        @pl.when(step > 0)
        def _():
            top_out[0, 0] = jnp.maximum(top_out[0, 0], largest)

    out, top = pl.pallas_call(
        body,
        grid=(tiles,),
        in_specs=old_specs
        + [
            pl.BlockSpec((tokens, tile), lambda i: (0, i)),
            pl.BlockSpec(gradient.shape, lambda i: (0, 0)),
        ],
        out_specs=[out_spec, pl.BlockSpec(memory_space=pltpu.SMEM)],
        out_shape=[out_shape, jax.ShapeDtypeStruct((1, 1), jnp.float32)],
        scratch_shapes=[] if pieces == 1 else [pltpu.VMEM((rows, 128), jnp.float32)],
        input_output_aliases={k: k for k in range(len(old))},
        compiler_params=params(),
        cost_estimate=cost(
            2 * tokens * depth * gradient.shape[1],
            depth * gradient.shape[1] * 4 + tokens * depth * 2,
        ),
    )(*old, inputs, gradient)
    store.write(out, top)


VMEM_LIMIT = 50 * 1024 * 1024
PADDED = TOKENS + 2 * FRAME


def params():
    return pltpu.CompilerParams(vmem_limit_bytes=VMEM_LIMIT)


def whole(shape):
    return pl.BlockSpec(shape, lambda *_: (0,) * len(shape))


def cost(flops, nbytes):
    return pl.CostEstimate(flops=flops, bytes_accessed=nbytes, transcendentals=0)


def token_mask(limit):
    return (lax.broadcasted_iota(jnp.int32, (TOKENS, 1), 0) < limit).astype(jnp.float32)


def columns_moved(values, col_off):
    if col_off == 0:
        return values
    col = lax.broadcasted_iota(jnp.int32, (TOKENS, 1), 0) % FRAME
    keep = col > 0 if col_off < 0 else col < FRAME - 1
    return jnp.where(keep, pltpu.roll(values, (-col_off) % TOKENS, 0), 0.0)


def two_sides(side, mine, other):
    first = jnp.where(side == 0, mine, other)
    second = jnp.where(side == 0, other, mine)
    return jnp.concatenate([first, second], axis=1)


def fill_moved(moved, values):
    width = moved.shape[2]
    empty = jnp.zeros((FRAME, width), moved.dtype)
    for slab in range(3):
        moved[slab, 0:FRAME, :] = empty
        moved[slab, FRAME : FRAME + TOKENS, :] = columns_moved(values, slab - 1).astype(moved.dtype)
        moved[slab, FRAME + TOKENS : PADDED, :] = empty


def tap_of(step, turned):
    row_off, col_off = (step // 3 - 1, step % 3 - 1)
    return (
        jnp.where(turned == 1, col_off, row_off),
        jnp.where(turned == 1, row_off, col_off),
    )


def rows_from(row_off):
    return pl.ds(pl.multiple_of(FRAME * (1 + row_off), FRAME), TOKENS)


def group_same():
    left = lax.broadcasted_iota(jnp.int32, (HALF, HALF), 0) // (C // GROUPS)
    right = lax.broadcasted_iota(jnp.int32, (HALF, HALF), 1) // (C // GROUPS)
    return (left == right).astype(jnp.float32)


def spread_in(sums, same):
    wide = jnp.broadcast_to(sums, (8, HALF))
    return jnp.dot(
        wide, same, precision=lax.Precision.HIGHEST, preferred_element_type=jnp.float32
    )[0:1]


def norm_in(value, mask, limit, gain, bias):
    same = group_same()
    share = 1.0 / (limit.astype(jnp.float32) * (C // GROUPS))
    mean_val = spread_in(jnp.sum(value * mask, axis=0, keepdims=True), same) * share
    centered = value - mean_val
    var_val = spread_in(jnp.sum(centered * centered * mask, axis=0, keepdims=True), same) * share
    inv_std = lax.rsqrt(var_val + eps_group)
    normed = centered * inv_std
    return (normed * gain + bias, normed, inv_std)


def silu_in(values):
    return values / (1.0 + jnp.exp(-values))


def finish_forward(total, limit, base, rows, act, act_out, normed_out, inv_out, value_out):
    mask = token_mask(limit)
    value = mask * (total + rows[0:1])
    if base is not None:
        value = value + base
    norm, normed, inv_std = norm_in(value, mask, limit, rows[1:2], rows[2:3])
    result = mask * silu_in(norm) if act else norm
    low_result = result.astype(jnp.bfloat16)
    act_out[...] = low_result
    normed_out[...] = normed
    inv_out[0:1] = inv_std
    inv_out[1:2] = column_squares(low_result)
    if value_out is not None:
        value_out[...] = value


def forward_outs(with_value):
    shapes = [
        jax.ShapeDtypeStruct((TOKENS, HALF), jnp.bfloat16),
        jax.ShapeDtypeStruct((TOKENS, HALF), jnp.float32),
        jax.ShapeDtypeStruct((8, HALF), jnp.float32),
    ]
    if with_value:
        shapes.append(jax.ShapeDtypeStruct((TOKENS, HALF), jnp.float32))
    return shapes


def first_forward(info, inputs, weight, rows):
    def body(info_ref, input_ref, weight_ref, rows_ref, *outs):
        total = dot(input_ref[...], weight_ref[...])
        finish_forward(total, info_ref[2], None, rows_ref[...], True, *outs)

    outs = forward_outs(True)
    return pl.pallas_call(
        body,
        grid_spec=pltpu.PrefetchScalarGridSpec(
            num_scalar_prefetch=1,
            grid=(1,),
            in_specs=[whole(inputs.shape), whole(weight.shape), whole(rows.shape)],
            out_specs=[whole(one.shape) for one in outs],
        ),
        out_shape=outs,
        compiler_params=params(),
        cost_estimate=cost(2 * TOKENS * 27 * HALF, 3 * TOKENS * HALF * 4),
    )(info, inputs, weight, rows)


def conv_forward(info, mine, other, table, at, base, rows, act):
    with_base = base is not None

    def body(info_ref, mine_ref, other_ref, weight_ref, rows_ref, *rest):
        base_ref = rest[0] if with_base else None
        outs, (moved, total) = (rest[int(with_base) : -2], rest[-2:])
        step = pl.program_id(0)

        @pl.when(step == 0)
        def _():
            both = two_sides(info_ref[0], mine_ref[...], other_ref[...])
            fill_moved(moved, both.astype(jnp.float32))
            total[...] = jnp.zeros_like(total)

        part = None
        for j in range(3):
            row_off, col_off = tap_of(3 * step + j, info_ref[1])
            one = dot(moved[col_off + 1, rows_from(row_off), :], weight_ref[C * j : C * (j + 1), :])
            part = one if part is None else part + one
        total[...] += part

        @pl.when(step == 2)
        def _():
            value_out = outs[3] if with_base else None
            held = base_ref[...] if with_base else None
            finish_forward(
                total[...], info_ref[2], held, rows_ref[...], act, *outs[:3], value_out
            )

    outs = forward_outs(with_base)
    extra = [base] if with_base else []
    return pl.pallas_call(
        body,
        grid_spec=pltpu.PrefetchScalarGridSpec(
            num_scalar_prefetch=1,
            grid=(3,),
            in_specs=[
                whole(mine.shape),
                whole(other.shape),
                pl.BlockSpec(
                    (pl.Element(3 * C), pl.Element(HALF)),
                    lambda i, info_ref: (
                        pl.multiple_of(at + 3 * C * i, 8),
                        pl.multiple_of(HALF * info_ref[0], HALF),
                    ),
                ),
                whole(rows.shape),
            ]
            + [whole(one.shape) for one in extra],
            out_specs=[whole(one.shape) for one in outs],
            scratch_shapes=[
                pltpu.VMEM((3, PADDED, C), jnp.bfloat16),
                pltpu.VMEM((TOKENS, HALF), jnp.float32),
            ],
        ),
        out_shape=outs,
        compiler_params=params(),
        cost_estimate=cost(18 * TOKENS * C * HALF, 9 * C * HALF * 2 + 6 * TOKENS * HALF * 4),
    )(info, mine, other, table, rows, *extra)


def conv_backward(info, grad_mine, grad_other, act_mine, act_other, table, store, at, saved, rows, base):
    with_base = base is not None
    old, old_specs, out_spec, out_shape = store_specs(store, at, 3 * C)

    def body(info_ref, *refs):
        refs = refs[len(old) :]
        gm_ref, go_ref, am_ref, ao_ref = refs[:4]
        weight_refs, (normed_ref, inv_ref, rows_ref) = (refs[4:7], refs[7:10])
        base_ref = refs[10] if with_base else None
        refs = refs[10 + int(with_base) :]
        out_ref, low_out, sums_out = refs[:3]
        moved, turned_act, shifted, total = refs[-4:]
        step = pl.program_id(0)

        @pl.when(step == 0)
        def _():
            both = two_sides(info_ref[0], gm_ref[...], go_ref[...])
            fill_moved(moved, both.astype(jnp.float32))
            act = two_sides(info_ref[0], am_ref[...], ao_ref[...]).astype(jnp.float32)
            for slab in range(3):
                turned_act[slab] = columns_moved(act, slab - 1).T.astype(jnp.bfloat16)
            empty = jnp.zeros((FRAME, HALF), jnp.bfloat16)
            shifted[0:FRAME, :] = empty
            shifted[FRAME : FRAME + TOKENS, :] = gm_ref[...]
            shifted[FRAME + TOKENS : PADDED, :] = empty
            total[...] = jnp.zeros_like(total)

        part = None
        for j in range(3):
            row_off, col_off = tap_of(3 * step + j, info_ref[1])
            rows_at = rows_from(-row_off)
            out_ref[C * j : C * (j + 1), :] = dot(turned_act[col_off + 1], shifted[rows_at, :])
            one = dot_t(moved[1 - col_off, rows_at, :], weight_refs[j][...])
            part = one if part is None else part + one
        total[...] += part

        @pl.when(step == 2)
        def _():
            mask = token_mask(info_ref[2])
            gain, normed, inv_std = (rows_ref[0:1], normed_ref[...], inv_ref[0:1])
            norm = normed * gain + rows_ref[1:2]
            logistic = 1.0 / (1.0 + jnp.exp(-norm))
            gradient = mask * total[...] * (logistic * (1.0 + norm * (1.0 - logistic)))
            result, gain_grad, bias_grad = norm_back(
                gradient, normed, inv_std, mask, info_ref[2], gain
            )
            if with_base:
                result = mask * (result + base_ref[...])
            low_result = result.astype(jnp.bfloat16)
            low_out[...] = low_result
            sums_out[3:4] = column_squares(low_result)
            sums_out[0:1] = jnp.sum(result, axis=0, keepdims=True)
            sums_out[1:2] = gain_grad
            sums_out[2:3] = bias_grad

    def tap_rows(j):
        return pl.BlockSpec(
            (pl.Element(HALF), pl.Element(C)),
            lambda i, info_ref: (pl.multiple_of(at + C * (3 * i + j) + HALF * info_ref[0], 8), 0),
        )

    extra = [base] if with_base else []
    operands = [grad_mine, grad_other, act_mine, act_other]
    result = pl.pallas_call(
        body,
        grid_spec=pltpu.PrefetchScalarGridSpec(
            num_scalar_prefetch=1,
            grid=(3,),
            in_specs=old_specs
            + [whole(one.shape) for one in operands]
            + [
                tap_rows(j) for j in range(3)
            ]
            + [
                whole((TOKENS, HALF)),
                whole((8, HALF)),
                whole(rows.shape),
            ]
            + [whole(one.shape) for one in extra],
            out_specs=[
                out_spec,
                whole((TOKENS, HALF)),
                whole((8, HALF)),
            ],
            scratch_shapes=[
                pltpu.VMEM((3, PADDED, C), jnp.bfloat16),
                pltpu.VMEM((3, C, TOKENS), jnp.bfloat16),
                pltpu.VMEM((PADDED, HALF), jnp.bfloat16),
                pltpu.VMEM((TOKENS, HALF), jnp.float32),
            ],
        ),
        out_shape=[
            out_shape,
            jax.ShapeDtypeStruct((TOKENS, HALF), jnp.bfloat16),
            jax.ShapeDtypeStruct((8, HALF), jnp.float32),
        ],
        input_output_aliases={1 + k: k for k in range(len(old))},
        compiler_params=params(),
        cost_estimate=cost(36 * TOKENS * C * HALF, 9 * C * HALF * 6 + 6 * TOKENS * HALF * 4),
    )(info, *old, *operands, table, table, table, *saved, rows, *extra)
    store.write(result[0], None)
    return (result[1], result[2])


def column_squares(values):
    wide = values.astype(jnp.float32)
    return jnp.sum(wide * wide, axis=0, keepdims=True)


def norm_back(gradient, normed, inv_std, mask, limit, gain):
    same = group_same()
    share = 1.0 / (limit.astype(jnp.float32) * (C // GROUPS))
    scaled = gradient * gain
    first = spread_in(jnp.sum(scaled * mask, axis=0, keepdims=True), same) * share
    second = spread_in(jnp.sum(scaled * normed * mask, axis=0, keepdims=True), same) * share
    result = mask * inv_std * (scaled - first - normed * second)
    return (
        result,
        jnp.sum(gradient * normed, axis=0, keepdims=True),
        jnp.sum(gradient, axis=0, keepdims=True),
    )


def unmix(info, table, at, depth, pieces, columns):
    tile = min(depth, 128 if pieces > 4 else 256)

    def body(info_ref, rows_ref, out_ref, mixed):
        for side in range(columns // 128):
            mixed[...] = rows_ref[:, side * 128 : (side + 1) * 128].astype(jnp.float32)
            for j in range(pieces):
                column = j * columns + side * 128
                out_ref[:, column : column + 128] = low(mixed[pl.ds(j, tile, stride=pieces), :])

    return pl.pallas_call(
        body,
        grid_spec=pltpu.PrefetchScalarGridSpec(
            num_scalar_prefetch=1,
            grid=(depth // tile,),
            in_specs=[
                pl.BlockSpec(
                    (pl.Element(tile * pieces), pl.Element(columns)),
                    lambda i, info_ref: (
                        pl.multiple_of(at + tile * pieces * i, 8),
                        pl.multiple_of(HALF * info_ref[0] * int(columns == HALF), HALF),
                    ),
                )
            ],
            out_specs=pl.BlockSpec((tile, pieces * columns), lambda i, info_ref: (i, 0)),
            scratch_shapes=[pltpu.VMEM((tile * pieces, 128), jnp.float32)],
        ),
        out_shape=jax.ShapeDtypeStruct((depth, pieces * columns), jnp.bfloat16),
        compiler_params=params(),
        cost_estimate=cost(0, 4 * depth * pieces * columns),
    )(info, table)


class Rows:
    def __init__(self, at, count, side_columns=False, side_rows=False):
        self.at, self.count = (at, count)
        self.side_columns, self.side_rows = (side_columns, side_rows)

    def spec(self):
        at, columns, rows = (self.at, int(self.side_columns), int(self.side_rows))
        return pl.BlockSpec(
            (pl.Element(self.count), pl.Element(HALF if columns else WIDE)),
            lambda i, info_ref: (
                pl.multiple_of(at + HALF * info_ref[0] * rows, 8),
                pl.multiple_of(HALF * info_ref[0] * columns, HALF),
            ),
        )


def one_step(body, info, table, operands, outs, flops):
    arrays = [table if isinstance(one, Rows) else one for one in operands]
    specs = [one.spec() if isinstance(one, Rows) else whole(one.shape) for one in operands]
    shapes = [jax.ShapeDtypeStruct(shape, kind) for shape, kind in outs]
    nbytes = sum(math.prod(one.shape) * one.dtype.itemsize for one in shapes)
    return pl.pallas_call(
        body,
        grid_spec=pltpu.PrefetchScalarGridSpec(
            num_scalar_prefetch=1,
            grid=(1,),
            in_specs=specs,
            out_specs=[whole(one.shape) for one in shapes],
        ),
        out_shape=shapes,
        compiler_params=params(),
        cost_estimate=cost(flops, 2 * nbytes),
    )(info, *arrays)


f32, bf16 = (jnp.float32, jnp.bfloat16)


def side_of(side, values):
    return jnp.where(side == 0, values[:, :HALF], values[:, HALF:])


def layer_parts(values):
    centered = values - jnp.mean(values, axis=-1, keepdims=True)
    var_val = jnp.mean(centered * centered, axis=-1, keepdims=True)
    inv_std = lax.rsqrt(var_val + eps_layer)
    return (centered * inv_std, inv_std)


def layer_back(gradient, values, gain, base, side, sums_ref):
    normed, inv_std = layer_parts(values)
    scaled = gradient * gain
    first = jnp.mean(scaled, axis=-1, keepdims=True)
    second = jnp.mean(scaled * normed, axis=-1, keepdims=True)
    result = base + inv_std * (scaled - first - normed * second)
    sums_ref[0:1] = side_of(side, jnp.sum(result, axis=0, keepdims=True))
    sums_ref[1:2] = side_of(side, jnp.sum(gradient * normed, axis=0, keepdims=True))
    sums_ref[2:3] = side_of(side, jnp.sum(gradient, axis=0, keepdims=True))
    return result


def head_lanes(head):
    return lax.broadcasted_iota(jnp.int32, (1, HALF), 1) // DHEAD == head


def head_probs(query, key, head, limit):
    mine = jnp.where(head_lanes(head), query, jnp.zeros((), bf16))
    scores = dot_t(mine, key) * 0.125
    seen = lax.broadcasted_iota(jnp.int32, (1, TOKENS), 1) < limit
    scores = jnp.where(seen, scores, -1e30)
    exponent = jnp.exp(scores - jnp.max(scores, axis=-1, keepdims=True))
    return exponent / jnp.sum(exponent, axis=-1, keepdims=True)


def self_front(info, table, mine, other, weight, rows, qkv):
    def body(info_ref, mine_ref, other_ref, weight_ref, rows_ref, qkv_ref, *outs):
        token_ref, resid_ref, ln_ref, packed_ref, out_ref = outs
        token = two_sides(info_ref[0], mine_ref[...], other_ref[...])
        token_ref[...] = token
        resid = dot(token, weight_ref[...]) + rows_ref[0:1]
        resid_ref[...] = resid
        ln = low(layer_parts(resid)[0] * rows_ref[1:2] + rows_ref[2:3])
        ln_ref[...] = ln
        packed_ref[...] = low(dot(ln, qkv_ref[...]))
        query, key = (packed_ref[:, 0:HALF], packed_ref[:, HALF : 2 * HALF])
        value = packed_ref[:, 2 * HALF : 3 * HALF]
        total = jnp.zeros((TOKENS, HALF), f32)
        for head in range(LOCAL_HEADS):
            probs = head_probs(query, key, head, info_ref[2])
            total = jnp.where(head_lanes(head), dot(low(probs), value), total)
        out_ref[...] = low(total)

    outs = [
        ((TOKENS, C), bf16),
        ((TOKENS, C), f32),
        ((TOKENS, C), bf16),
        ((TOKENS, 3 * HALF), bf16),
        ((TOKENS, HALF), bf16),
    ]
    flops = 2 * TOKENS * C * (C + 3 * HALF) + 4 * LOCAL_HEADS * TOKENS * TOKENS * HALF
    return one_step(body, info, table, [mine, other, weight, rows, qkv], outs, flops)


def same_head():
    left = lax.broadcasted_iota(jnp.int32, (HALF, HALF), 0) // DHEAD
    right = lax.broadcasted_iota(jnp.int32, (HALF, HALF), 1) // DHEAD
    return (left == right).astype(f32)


def head_sums(values, same):
    return jnp.dot(values, same, precision=lax.Precision.HIGHEST, preferred_element_type=f32)


def cross_probs(query, context, same):
    first = head_sums(query * context[0:1, :HALF], same) * 0.125
    second = head_sums(query * context[1:2, :HALF], same) * 0.125
    top = jnp.maximum(first, second)
    first, second = (jnp.exp(first - top), jnp.exp(second - top))
    total = first + second
    return (first / total, second / total)


def cross_front(info, table, mine, other, weight, rows, resid, query_weight, context):
    def body(info_ref, mine_ref, other_ref, weight_ref, rows_ref, old_ref, qw_ref, kv_ref, *outs):
        full_ref, resid_ref, ln_ref, query_ref, out_ref = outs
        joined = two_sides(info_ref[0], mine_ref[...], other_ref[...])
        full_ref[...] = joined
        resid_now = old_ref[...] + dot(joined, weight_ref[...]) + rows_ref[0:1]
        resid_ref[...] = resid_now
        ln = low(layer_parts(resid_now)[0] * rows_ref[1:2] + rows_ref[2:3])
        ln_ref[...] = ln
        query = low(dot(ln, qw_ref[...]))
        query_ref[...] = query
        both = kv_ref[...].astype(f32)
        first, second = cross_probs(query.astype(f32), both, same_head())
        out_ref[...] = low(first * both[0:1, HALF:] + second * both[1:2, HALF:])

    outs = [
        ((TOKENS, C), bf16),
        ((TOKENS, C), f32),
        ((TOKENS, C), bf16),
        ((TOKENS, HALF), bf16),
        ((TOKENS, HALF), bf16),
    ]
    operands = [mine, other, weight, rows, resid, query_weight, context]
    return one_step(body, info, table, operands, outs, 2 * TOKENS * C * (C + 13 * HALF))


def gelu_parts(gate):
    return 0.5 * (1.0 + lax.erf(gate * math.sqrt(0.5)))


WIDE_FF = FFI // 2


def ff_front(info, table, mine, other, weight, rows, resid, ff_weight, ff_bias):
    def body(info_ref, mine_ref, other_ref, weight_ref, rows_ref, old_ref, fw_ref, fb_ref, *outs):
        full_ref, resid_ref, ln_ref, proj_ref, out_ref = outs
        joined = two_sides(info_ref[0], mine_ref[...], other_ref[...])
        full_ref[...] = joined
        resid_now = old_ref[...] + dot(joined, weight_ref[...]) + rows_ref[0:1]
        resid_ref[...] = resid_now
        ln = low(layer_parts(resid_now)[0] * rows_ref[1:2] + rows_ref[2:3])
        ln_ref[...] = ln
        for at in range(0, WIDE_FF, HALF):
            gate_at = WIDE_FF + at
            lift = dot(ln, fw_ref[:, at : at + HALF]) + fb_ref[:, at : at + HALF]
            gate = dot(ln, fw_ref[:, gate_at : gate_at + HALF]) + fb_ref[:, gate_at : gate_at + HALF]
            proj_ref[:, at : at + HALF] = lift
            proj_ref[:, gate_at : gate_at + HALF] = gate
            out_ref[:, at : at + HALF] = low(lift * gate * gelu_parts(gate))

    outs = [
        ((TOKENS, C), bf16),
        ((TOKENS, C), f32),
        ((TOKENS, C), bf16),
        ((TOKENS, FFI), f32),
        ((TOKENS, WIDE_FF), bf16),
    ]
    operands = [mine, other, weight, rows, resid, ff_weight, ff_bias]
    return one_step(body, info, table, operands, outs, 2 * TOKENS * C * (C + FFI))


def ff_finish(info, table, mine, other, weight, rows, resid, out_weight, out_bias, state):
    def body(info_ref, mine_ref, other_ref, weight_ref, rows_ref, old_ref, ow_ref, ob_ref, state_ref, *outs):
        full_ref, resid_ref, out_ref = outs
        side = info_ref[0]
        for at in range(0, WIDE_FF, HALF):
            own, peer = (mine_ref[:, at : at + HALF], other_ref[:, at : at + HALF])
            full_ref[:, 2 * at : 2 * at + WIDE] = two_sides(side, own, peer)
        resid_now = old_ref[...] + dot(full_ref[...], weight_ref[...]) + rows_ref[0:1]
        inner = low(resid_now)
        resid_ref[...] = inner
        branch = dot(inner, ow_ref[...]) + ob_ref[0:1]
        out_ref[...] = low(state_ref[...] + token_mask(info_ref[2]) * branch)

    outs = [((TOKENS, FFI), bf16), ((TOKENS, C), bf16), ((TOKENS, HALF), bf16)]
    operands = [mine, other, weight, rows, resid, out_weight, out_bias, state]
    return one_step(body, info, table, operands, outs, 2 * TOKENS * C * (FFI + HALF))


def lanes_moved(values, row_off, col_off):
    token = lax.broadcasted_iota(jnp.int32, (1, TOKENS), 1)
    row, col = (token // FRAME + row_off, token % FRAME + col_off)
    keep = (row >= 0) & (row < SIDE) & (col >= 0) & (col < FRAME)
    away = FRAME * row_off + col_off
    return jnp.where(keep, pltpu.roll(values, lax.rem(TOKENS - away, TOKENS), 1), 0.0)


OUT_ROWS = 8


def loss_back(info, table, mine, other, out_weight, noise, bias, pout, ff2, projected, ff1):
    def body(info_ref, *refs):
        mine_ref, other_ref, ow_ref, noise_ref, bias_ref, pout_ref, ff2_ref, proj_ref, ff1_ref = refs[:9]
        ow_grad, small_out, state_out, pout_low, ff2_low, resid_out, proj_low, ln_out, sums, ff_sums = refs[9:]
        side, turned, limit = (info_ref[0], info_ref[1], info_ref[2])
        state = two_sides(side, mine_ref[...], other_ref[...])
        raw = dot_t(ow_ref[...], state)
        predicted = bias_ref[:, 0:1]
        for tap in range(9):
            row_off, col_off = tap_of(tap, turned)
            part = raw[tap * OUT_ROWS : (tap + 1) * OUT_ROWS]
            predicted = predicted + lanes_moved(part, row_off, col_off)
        token = lax.broadcasted_iota(jnp.int32, (OUT_ROWS, TOKENS), 1)
        channel = lax.broadcasted_iota(jnp.int32, (OUT_ROWS, TOKENS), 0)
        error = jnp.where((token < limit) & (channel < LC), predicted - noise_ref[...], 0.0)
        loss = jnp.sum(jnp.sum(error * error, axis=1, keepdims=True), axis=0, keepdims=True)
        gradient = 2.0 * error
        small_out[:, 0:128] = jnp.broadcast_to(jnp.sum(gradient, axis=1, keepdims=True), (OUT_ROWS, 128))
        small_out[:, 128:256] = jnp.broadcast_to(loss, (OUT_ROWS, 128))
        gradient = low(gradient).astype(f32)
        moved = []
        for tap in range(9):
            row_off, col_off = tap_of(tap, turned)
            moved.append(lanes_moved(gradient, -row_off, -col_off))
        moved = low(jnp.concatenate(moved, axis=0))
        ow_grad[...] = dot(moved, state)
        state_grad = t_dot(moved, ow_ref[...])
        state_out[...] = side_of(side, state_grad)
        branch = token_mask(limit) * state_grad
        sums[1:2] = side_of(side, jnp.sum(branch, axis=0, keepdims=True))
        branch = low(branch)
        pout_low[...] = side_of(side, branch)
        resid_grad = dot_t(branch, pout_ref[...])
        resid_out[...] = resid_grad
        sums[0:1] = side_of(side, jnp.sum(resid_grad, axis=0, keepdims=True))
        resid_low = low(resid_grad)
        ff2_low[...] = side_of(side, resid_low)
        total = jnp.zeros((TOKENS, C), f32)
        for j in range(WIDE_FF // HALF):
            at, gate_at = (j * HALF, WIDE_FF + j * HALF)
            own = pl.ds(pl.multiple_of(WIDE * j + HALF * side, HALF), HALF)
            gated_grad = dot_t(resid_low, ff2_ref[own, :])
            lift, gate = (proj_ref[:, at : at + HALF], proj_ref[:, gate_at : gate_at + HALF])
            cdf = gelu_parts(gate)
            density = jnp.exp(-0.5 * gate * gate) * (1.0 / math.sqrt(2.0 * math.pi))
            lift_grad = gated_grad * gate * cdf
            gate_grad = gated_grad * lift * (cdf + gate * density)
            ff_sums[j : j + 1] = jnp.sum(lift_grad, axis=0, keepdims=True)
            ff_sums[4 + j : 5 + j] = jnp.sum(gate_grad, axis=0, keepdims=True)
            lift_grad, gate_grad = (low(lift_grad), low(gate_grad))
            proj_low[:, at : at + HALF] = lift_grad
            proj_low[:, gate_at : gate_at + HALF] = gate_grad
            total = total + dot_t(lift_grad, ff1_ref[:, at : at + HALF])
            total = total + dot_t(gate_grad, ff1_ref[:, gate_at : gate_at + HALF])
        ln_out[...] = total

    outs = [
        ((9 * OUT_ROWS, C), f32),
        ((OUT_ROWS, HALF), f32),
        ((TOKENS, HALF), f32),
        ((TOKENS, HALF), bf16),
        ((TOKENS, HALF), bf16),
        ((TOKENS, C), f32),
        ((TOKENS, FFI), bf16),
        ((TOKENS, C), f32),
        ((8, HALF), f32),
        ((8, HALF), f32),
    ]
    operands = [mine, other, out_weight, noise, bias, pout, ff2, projected, ff1]
    return one_step(body, info, table, operands, outs, 2 * TOKENS * C * (C + FFI + WIDE_FF))


def cross_back(info, table, mine, other, resid, gain, base, weight, query, context):
    def body(info_ref, mine_ref, other_ref, resid_ref, gain_ref, base_ref, weight_ref, query_ref, kv_ref, *outs):
        resid_out, co_low, query_low, kv_grad, sums = outs
        side = info_ref[0]
        result = layer_back(
            mine_ref[...] + other_ref[...], resid_ref[...], gain_ref[0:1], base_ref[...], side, sums
        )
        resid_out[...] = result
        result = low(result)
        co_low[...] = side_of(side, result)
        out_grad = low(dot_t(result, weight_ref[...])).astype(f32)
        same, both, query_now = (same_head(), kv_ref[...].astype(f32), query_ref[...].astype(f32))
        first, second = cross_probs(query_now, both, same)
        first_grad = head_sums(out_grad * both[0:1, HALF:], same)
        second_grad = head_sums(out_grad * both[1:2, HALF:], same)
        inner = first * first_grad + second * second_grad
        first_grad = first * (first_grad - inner) * 0.125
        second_grad = second * (second_grad - inner) * 0.125
        query_low[...] = low(first_grad * both[0:1, :HALF] + second_grad * both[1:2, :HALF])
        for row, (prob, score) in enumerate(((first, first_grad), (second, second_grad))):
            kv_grad[row : row + 1, :HALF] = jnp.sum(score * query_now, axis=0, keepdims=True)
            kv_grad[row : row + 1, HALF:] = jnp.sum(prob * out_grad, axis=0, keepdims=True)

    outs = [
        ((TOKENS, C), f32),
        ((TOKENS, HALF), bf16),
        ((TOKENS, HALF), bf16),
        ((8, WIDE), f32),
        ((8, HALF), f32),
    ]
    operands = [mine, other, resid, gain, base, weight, query, context]
    return one_step(body, info, table, operands, outs, 2 * TOKENS * C * 14 * HALF)


def self_back(info, table, mine, other, query_weight, resid, gain, base, weight, packed, qkv):
    def body(info_ref, mine_ref, other_ref, qw_ref, resid_ref, gain_ref, base_ref, weight_ref, packed_ref, qkv_ref, *outs):
        resid_out, o_low, packed_low, ln_out, sums = outs
        side, limit = (info_ref[0], info_ref[2])
        joined = two_sides(side, mine_ref[...], other_ref[...])
        result = layer_back(
            dot_t(joined, qw_ref[...]), resid_ref[...], gain_ref[0:1], base_ref[...], side, sums
        )
        resid_out[...] = result
        result = low(result)
        o_low[...] = side_of(side, result)
        out_grad = low(dot_t(result, weight_ref[...]))
        query, key = (packed_ref[:, 0:HALF], packed_ref[:, HALF : 2 * HALF])
        value = packed_ref[:, 2 * HALF : 3 * HALF]
        parts = [jnp.zeros((TOKENS, HALF), f32) for _ in range(3)]
        for head in range(LOCAL_HEADS):
            lanes = head_lanes(head)
            probs = head_probs(query, key, head, limit)
            mine_grad = jnp.where(lanes, out_grad, jnp.zeros((), bf16))
            prob_grad = dot_t(mine_grad, value)
            inner = jnp.sum(probs * prob_grad, axis=-1, keepdims=True)
            score_grad = low(probs * (prob_grad - inner) * 0.125)
            parts[0] = jnp.where(lanes, dot(score_grad, key), parts[0])
            parts[1] = jnp.where(lanes, t_dot(score_grad, query), parts[1])
            parts[2] = jnp.where(lanes, t_dot(low(probs), out_grad), parts[2])
        joined = low(jnp.concatenate(parts, axis=1))
        packed_low[...] = joined
        ln_out[...] = dot_t(joined, qkv_ref[...])

    outs = [
        ((TOKENS, C), f32),
        ((TOKENS, HALF), bf16),
        ((TOKENS, 3 * HALF), bf16),
        ((TOKENS, C), f32),
        ((8, HALF), f32),
    ]
    operands = [mine, other, query_weight, resid, gain, base, weight, packed, qkv]
    flops = 2 * TOKENS * C * 6 * HALF + 10 * LOCAL_HEADS * TOKENS * TOKENS * HALF
    return one_step(body, info, table, operands, outs, flops)


def token_back(info, table, mine, other, resid, gain, base, weight, normed, rows, gain_three, state):
    def body(info_ref, mine_ref, other_ref, resid_ref, gain_ref, base_ref, weight_ref, normed_ref, inv_ref, g3_ref, state_ref, *outs):
        pin_low, state_out, conv_low, sums, sums_three = outs
        side, limit = (info_ref[0], info_ref[2])
        result = layer_back(
            mine_ref[...] + other_ref[...], resid_ref[...], gain_ref[0:1], base_ref[...], side, sums
        )
        result = low(result)
        pin_low[...] = side_of(side, result)
        token_grad = dot_t(result, weight_ref[...])
        mask = token_mask(limit)
        norm_grad, gain_grad, bias_grad = norm_back(
            token_grad, normed_ref[...], inv_ref[0:1], mask, limit, g3_ref[0:1]
        )
        state_now = state_ref[...] + norm_grad
        state_out[...] = state_now
        conv_grad = mask * state_now
        low_grad = low(conv_grad)
        conv_low[...] = low_grad
        sums_three[0:1] = jnp.sum(conv_grad, axis=0, keepdims=True)
        sums_three[1:2] = gain_grad
        sums_three[2:3] = bias_grad
        sums_three[3:4] = column_squares(low_grad)

    outs = [
        ((TOKENS, HALF), bf16),
        ((TOKENS, HALF), f32),
        ((TOKENS, HALF), bf16),
        ((8, HALF), f32),
        ((8, HALF), f32),
    ]
    operands = [mine, other, resid, gain, base, weight, normed, rows, gain_three, state]
    return one_step(body, info, table, operands, outs, 2 * TOKENS * C * HALF)


def channel_mix():
    flat = lax.iota(jnp.int32, LC * C)[:, None]
    split = lax.iota(jnp.int32, LC * C)[None]
    return flat == LC * (split % C) + split // C


def gather_small(place, value):
    stride, joined = (1, value[None])
    while stride < place.count:
        other = place.swap(joined, stride)
        upper = (place.index // stride) % 2 == 1
        joined = jnp.where(
            upper,
            jnp.concatenate([other, joined], axis=0),
            jnp.concatenate([joined, other], axis=0),
        )
        stride *= 2
    return joined


def windows(values, turned, sign):
    width = values.shape[1]
    col = (lax.iota(jnp.int32, TOKENS) % FRAME)[:, None]
    zero_one = jnp.zeros((1, width), values.dtype)
    zero_row = jnp.zeros((FRAME, width), values.dtype)
    none = jnp.zeros((), values.dtype)
    across = {
        -1: jnp.where(col > 0, jnp.concatenate([zero_one, values[:-1]], axis=0), none),
        0: values,
        1: jnp.where(col < FRAME - 1, jnp.concatenate([values[1:], zero_one], axis=0), none),
    }
    moved = {}
    for col_off, value in across.items():
        moved[-1, col_off] = jnp.concatenate([zero_row, value[:-FRAME]], axis=0)
        moved[0, col_off] = value
        moved[1, col_off] = jnp.concatenate([value[FRAME:], zero_row], axis=0)
    out = []
    for row_off, col_off in tap_offsets:
        plain = moved[sign * row_off, sign * col_off]
        other = moved[sign * col_off, sign * row_off]
        out.append(plain if row_off == col_off else jnp.where(turned, other, plain))
    return jnp.concatenate(out, axis=1)


def frame_of(place, latents, target_noise, turned):
    both = jnp.concatenate([latents, target_noise], axis=-1)
    stride, joined = (1, both[None])
    while stride < place.rows:
        other = place.swap(joined, stride)
        upper = (place.index // stride) % 2 == 1
        joined = jnp.where(
            upper,
            jnp.concatenate([other, joined], axis=0),
            jnp.concatenate([joined, other], axis=0),
        )
        stride *= 2
    image = pick(joined, place.slot, 1).reshape(SIDE, SIDE, 2 * LC)
    portrait = image[:, :FRAME]
    landscape = jnp.transpose(image[:FRAME], (1, 0, 2))
    return jnp.where(turned, landscape, portrait).reshape(TOKENS, 2 * LC)


def train_step(place, store, table, vecs, latents, target_noise, label, step_value, orient, extent):
    half, at = (place.half, store.places)
    turned = orient != 1
    info = jnp.stack([place.side, turned.astype(jnp.int32), extent * FRAME]).astype(jnp.int32)
    mask = (lax.iota(jnp.int32, TOKENS) < extent * FRAME).astype(jnp.float32)[:, None]
    frame = frame_of(place, latents, target_noise, turned)
    share = noise_level(step_value)
    noisy = mask * (jnp.sqrt(share) * frame[:, :LC] + jnp.sqrt(1.0 - share) * frame[:, LC:])
    pad_in = windows(low(noisy), turned, 1)
    noise_rows = jnp.pad(frame[:, LC:].T, ((0, OUT_ROWS - LC), (0, 0)))
    embed_in = low(time_embed(step_value))[None]
    mix = channel_mix()
    row = lambda *names: jnp.stack([vecs[name] for name in names])
    side_rows = lambda *names: half(row(*names))

    def part(name, depth=C, **kind):
        return Rows(at[name], depth, **kind)

    def own_rows(name):
        return Rows(at[name], HALF, side_rows=True)

    w_t1 = unmix(info, table, at["w_t1"], TE, TD // WIDE, C)
    w_t2 = unmix(info, table, at["w_t2"], TD, TD // WIDE, C)
    qkv = unmix(info, table, at["w_qkv"], C, 3, HALF)
    ckv = unmix(info, table, at["w_ckv"], C, 2, HALF)
    ff1 = unmix(info, table, at["w_ff1"], C, 2 * FFI // WIDE, HALF)
    w_tp = table[at["w_tp"] : at["w_tp"] + TD]
    w_in = half(table[at["w_in"] : at["w_in"] + 9 * LC])
    w_out = dot(table[at["w_out"] : at["w_out"] + 9 * LC].reshape(9, LC * C), low(mix))
    w_out = low(jnp.pad(w_out.reshape(9, LC, C), ((0, 0), (0, OUT_ROWS - LC), (0, 0))))
    w_out = w_out.reshape(9 * OUT_ROWS, C)

    pre_one = dot(embed_in, w_t1) + vecs["b_t1"]
    hidden_one = low(jax.nn.silu(pre_one))
    pre_two = dot(hidden_one, w_t2) + vecs["b_t2"]
    hidden_two = low(jax.nn.silu(pre_two))
    time_vec = dot(hidden_two, w_tp) + vecs["b_tp"]
    class_vec = lax.dynamic_slice(table, (at["table"] + label, 0), (1, C)).astype(jnp.float32)
    context = low(jnp.concatenate([class_vec, time_vec], axis=0))
    context_kv = jnp.pad(low(dot(context, ckv)), ((0, 6), (0, 0)))

    act_one, normed_one, inv_one, state_zero = first_forward(
        info, pad_in, w_in, side_rows("b_in", "g1", "bb1")
    )
    act_one_peer = place.swap(act_one)
    rows_two = side_rows("b_c1", "g2", "bb2")
    rows_two = jnp.concatenate([rows_two[0:1] + half(time_vec), rows_two[1:]], axis=0)
    act_two, normed_two, inv_two = conv_forward(
        info, act_one, act_one_peer, table, at["w_c1"], None, rows_two, True
    )
    act_two_peer = place.swap(act_two)
    token_own, normed_three, inv_three, state_one = conv_forward(
        info, act_two, act_two_peer, table, at["w_c2"], state_zero, side_rows("b_c2", "g3", "bb3"), False
    )
    token_in, resid_zero, ln_one, packed, attended_own = self_front(
        info, table, token_own, place.swap(token_own), part("w_pin"), row("b_pin", "n1g", "n1b"), qkv
    )
    attended, resid_one, ln_two, cross_query, cross_own = cross_front(
        info,
        table,
        attended_own,
        place.swap(attended_own),
        part("w_o"),
        row("b_o", "n2g", "n2b"),
        resid_zero,
        part("w_cq", side_columns=True),
        context_kv,
    )
    b_ff1 = half(vecs["b_ff1"].reshape(-1, WIDE)).reshape(1, FFI)
    cross_out, resid_two, ln_three, projected, gated_own = ff_front(
        info,
        table,
        cross_own,
        place.swap(cross_own),
        part("w_co"),
        row("b_co", "n3g", "n3b"),
        resid_one,
        ff1,
        b_ff1,
    )
    gated, out_in, state_own = ff_finish(
        info,
        table,
        gated_own,
        place.swap(gated_own),
        part("w_ff2", FFI),
        row("b_ff2"),
        resid_two,
        part("w_pout", side_columns=True),
        side_rows("b_pout"),
        state_one,
    )
    b_out = jnp.broadcast_to(jnp.pad(vecs["b_out"], (0, OUT_ROWS - LC))[:, None], (OUT_ROWS, 128))
    (
        w_out_grad,
        small_out,
        state_grad,
        pout_low,
        ff2_low,
        resid_grad,
        proj_low,
        ln_part,
        sums_out,
        sums_ff,
    ) = loss_back(
        info,
        table,
        state_own,
        place.swap(state_own),
        w_out,
        noise_rows,
        b_out,
        part("w_pout"),
        part("w_ff2", FFI),
        projected,
        ff1,
    )
    ln_peer = place.swap(ln_part)
    store.add("w_pout", out_in, pout_low)
    store.add("w_ff2", gated, ff2_low)
    store.add("w_ff1", ln_three, proj_low)
    w_out_grad = w_out_grad.reshape(9, OUT_ROWS, C)[:, :LC].reshape(9, LC * C)
    w_out_grad = lax.dot_general(
        w_out_grad,
        mix.astype(jnp.float32),
        (((1,), (1,)), ((), ())),
        precision=lax.Precision.HIGHEST,
        preferred_element_type=jnp.float32,
    )
    w_out_grad = half(w_out_grad.reshape(9 * LC, C))
    store.put(at["w_out"], jnp.zeros((store.total - at["w_out"], HALF), jnp.float32))
    resid_grad, co_low, query_low, kv_grad, sums_co = cross_back(
        info,
        table,
        ln_part,
        ln_peer,
        resid_two,
        row("n3g"),
        resid_grad,
        own_rows("w_co"),
        cross_query,
        context_kv,
    )
    query_peer = place.swap(query_low)
    kv_low = low(kv_grad[:2])
    context_grad = dot_t(kv_low, ckv)
    context_grad = context_grad + place.swap(context_grad)
    store.add("w_co", cross_out, co_low)
    store.add("w_cq", ln_two, query_low)
    store.add("w_ckv", context, kv_low)
    resid_grad, o_low, packed_low, ln_part, sums_o = self_back(
        info,
        table,
        query_low,
        query_peer,
        part("w_cq"),
        resid_one,
        row("n2g"),
        resid_grad,
        own_rows("w_o"),
        packed,
        qkv,
    )
    ln_peer = place.swap(ln_part)
    store.add("w_o", attended, o_low)
    store.add("w_qkv", ln_one, packed_low)
    pin_low, state_grad, conv_low, sums_pin, sums_two = token_back(
        info,
        table,
        ln_part,
        ln_peer,
        resid_zero,
        row("n1g"),
        resid_grad,
        own_rows("w_pin"),
        normed_three,
        inv_three,
        side_rows("g3"),
        state_grad,
    )
    conv_peer = place.swap(conv_low)
    store.add("w_pin", token_in, pin_low)
    conv_low, sums_one = conv_backward(
        info,
        conv_low,
        conv_peer,
        act_two,
        act_two_peer,
        table,
        store,
        at["w_c2"],
        (normed_two, inv_two),
        side_rows("g2", "bb2"),
        None,
    )
    conv_peer = place.swap(conv_low)
    time_grad = place.full(sums_one[0:1]) + context_grad[1:2]
    b_tp = half(time_grad)
    time_low = low(time_grad)
    pre_grad = dot_t(time_low, w_tp) * silu_slope(pre_two)
    b_t2 = half(pre_grad.reshape(-1, WIDE))
    two_low = low(pre_grad)
    pre_grad = dot_t(two_low, w_t2) * silu_slope(pre_one)
    b_t1 = half(pre_grad.reshape(-1, WIDE))
    one_low = low(pre_grad)
    size = lambda one: jnp.max(jnp.abs(one.astype(jnp.float32)))
    local = jnp.maximum(store.top[0, 0], size(context_grad[0]))
    for left, right in ((hidden_two, time_low), (hidden_one, two_low), (embed_in, one_low)):
        local = jnp.maximum(local, 1.01 * size(left) * size(right))
    squares = [size(one) for one in (inv_one[1], inv_two[1], sums_two[3], sums_one[3])]
    largest = Largest(place, lane_row([local] + squares))
    store.add("w_tp", hidden_two, half(time_low))
    store.buffer = largest.exchange(store.buffer)
    store.add("w_t2", hidden_one, half(two_low.reshape(-1, WIDE)).reshape(1, -1))
    store.buffer = largest.exchange(store.buffer)
    store.add("w_t1", embed_in, half(one_low.reshape(-1, WIDE)).reshape(1, -1))
    chosen = lax.iota(jnp.int32, NCLS)[:, None] == label
    store.put(at["table"], jnp.where(chosen, half(context_grad[0:1]), 0.0))
    store.put(0, jnp.zeros((at["w_t1"], HALF), jnp.float32))
    store.buffer = largest.exchange(store.buffer)
    in_low, sums_in = conv_backward(
        info,
        conv_low,
        conv_peer,
        act_one,
        act_one_peer,
        table,
        store,
        at["w_c1"],
        (normed_one, inv_one),
        side_rows("g1", "bb1"),
        state_grad,
    )
    store.buffer = largest.exchange(store.buffer)
    tops = largest.finish()[0]
    bound = jnp.maximum(tops[0], 1.01 * jnp.sqrt(tops[1] * tops[4]))
    bound = jnp.maximum(bound, 1.01 * jnp.sqrt(tops[2] * tops[3]))
    scale = (WIRE_TOP / (place.count // 2)) / jnp.maximum(bound, 1e-30)
    w_in_grad = t_dot(pad_in, in_low)
    small = [b_t1, b_t2, b_tp, sums_in[:3], sums_one[:3], sums_two[:3], sums_pin[:3], sums_o[:3]]
    small += [sums_co[:3], sums_ff, sums_out[:2]]
    extra = [small_out[:LC, 0], small_out[0:1, 128], (extent * FRAME).astype(jnp.float32)[None]]
    extra = jnp.pad(jnp.concatenate(extra), (0, HALF - LC - 2))[None]
    return (jnp.concatenate(small + [extra, w_in_grad, w_out_grad], axis=0), scale)


def adam_update(params, first_mom, second, gradient, decay_rate):
    first_new = adam_one * first_mom + (1.0 - adam_one) * gradient
    second_new = adam_two * second + (1.0 - adam_two) * gradient * gradient
    step_size = (
        first_new
        / (1.0 - adam_one**STEP)
        / (jnp.sqrt(second_new / (1.0 - adam_two**STEP)) + adam_eps)
    )
    return (params - learn_rate * (step_size + decay_rate * params), first_new, second_new)


def local(
    latents,
    target_noise,
    labels,
    timesteps,
    orient,
    extent,
    mat_params,
    mat_first,
    mat_second,
    mat_ema,
    vec_params,
    vec_first,
    vec_second,
    vec_ema,
):
    place = Place()
    length = mat_params.shape[0]
    rows = shard_rows(length * place.count, place.count)
    block = to_blocks(place, mat_params.astype(jnp.bfloat16), rows)
    table = lax.all_gather(block, ("dp", "rows"), axis=0, tiled=True)
    vec_len = vec_params.shape[0]
    vec_wide = -(-vec_len // 128) * 128
    padded = jnp.pad(vec_params, (0, vec_wide - vec_len)).reshape(-1, 128)
    vec_all = gather_small(place, padded).reshape(place.count, vec_wide)[:, :vec_len]
    vec_all = vec_all.reshape(-1).astype(jnp.bfloat16).astype(jnp.float32)
    vecs = unpack(vec_all, vec_layout())
    own = lambda values: pick(values, place.slot, 0)
    store = Store(place, rows)
    small, scale = train_step(
        place,
        store,
        table,
        vecs,
        latents,
        target_noise,
        own(labels),
        own(timesteps),
        own(orient),
        own(extent),
    )
    block_grad, square = scatter_sum(place, store.buffer, scale, rows)
    small = jnp.pad(small, ((0, -small.shape[0] % 8), (0, 0)))
    body = sum(record[1] for record in vec_layout()[:-1]) // WIDE
    lane = lax.broadcasted_iota(jnp.int32, small.shape, 1)
    line = lax.broadcasted_iota(jnp.int32, small.shape, 0)
    small = jnp.where((lane == SQUARE_AT) & (line == body), square, small)
    small = place.full(place.chip_sum(small))
    loss_sum, pixel_count = (small[body, LC], small[body, LC + 1])
    vec_flat = jnp.concatenate([small[:body].reshape(-1), small[body, :LC]])
    vec_flat = jnp.pad(vec_flat, (0, vec_len * place.count - vec_flat.shape[0]))
    shard_vec = lax.dynamic_slice(vec_flat, (vec_len * place.index,), (vec_len,))
    square = small[body, SQUARE_AT] + small[body, HALF + SQUARE_AT] + jnp.sum(vec_flat * vec_flat)
    shard_mat = from_blocks(place, block_grad, length)
    for i, name in enumerate(("w_in", "w_out")):
        values = small[body + 1 + 9 * LC * i : body + 1 + 9 * LC * (i + 1)]
        square = square + jnp.sum(values * values)
        owner, offset = divmod((store.places[name] - LEAD) * WIDE, length)
        old = lax.dynamic_slice(shard_mat, (offset,), (9 * LC * C,))
        new = jnp.where(place.index == owner, values.reshape(-1), old)
        shard_mat = lax.dynamic_update_slice(shard_mat, new, (offset,))
    inverse = 1.0 / pixel_count
    grad_norm = jnp.sqrt(square) * inverse
    factor = clip_norm / jnp.maximum(grad_norm, clip_norm) * inverse
    new_mat, mat_first_new, mat_second_new = adam_update(
        mat_params, mat_first, mat_second, shard_mat * factor, weight_decay
    )
    new_vec, vec_first_new, vec_second_new = adam_update(
        vec_params, vec_first, vec_second, shard_vec * factor, 0.0
    )
    ema_rate = min(ema_ceiling, (1.0 + STEP) / (10.0 + STEP))
    mat_ema_new = ema_rate * mat_ema + (1.0 - ema_rate) * new_mat
    vec_ema_new = ema_rate * vec_ema + (1.0 - ema_rate) * new_vec
    return (
        new_mat,
        mat_first_new,
        mat_second_new,
        mat_ema_new,
        new_vec,
        vec_first_new,
        vec_second_new,
        vec_ema_new,
        grad_norm,
        loss_sum,
        pixel_count,
    )


def solution(mesh):
    return jax.shard_map(
        local,
        mesh=mesh,
        in_specs=(
            P("dp", "rows", None, None),
            P("dp", "rows", None, None),
            P("dp"),
            P("dp"),
            P("dp"),
            P("dp"),
            P(("dp", "rows")),
            P(("dp", "rows")),
            P(("dp", "rows")),
            P(("dp", "rows")),
            P(("dp", "rows")),
            P(("dp", "rows")),
            P(("dp", "rows")),
            P(("dp", "rows")),
        ),
        out_specs=(
            P(("dp", "rows")),
            P(("dp", "rows")),
            P(("dp", "rows")),
            P(("dp", "rows")),
            P(("dp", "rows")),
            P(("dp", "rows")),
            P(("dp", "rows")),
            P(("dp", "rows")),
            P(),
            P(),
            P(),
        ),
        check_vma=False,
    )
```

```python
import math

import jax
import jax.numpy as jnp
import ml_dtypes
import numpy as np
from jax import lax
from jax.experimental import pallas as pl
from jax.experimental.pallas import tpu as pltpu
from jax.sharding import PartitionSpec as P

C = 512
HEADS = 8
DHEAD = 64
FFI = 2048
TE = 256
TD = 1024
NCLS = 1000
LC = 3
GROUPS = 32
SIDE = 32
NT = 1000
STEP = 10


tap_offsets = [(-1, -1), (-1, 0), (-1, 1), (0, -1), (0, 0), (0, 1), (1, -1), (1, 0), (1, 1)]
eps_group = 1e-06
eps_layer = 1e-05
beta_first = 0.00085
beta_last = 0.012
adam_one = 0.9
adam_two = 0.999
adam_eps = 1e-08
learn_rate = 0.05
weight_decay = 0.01
ema_ceiling = 0.9999
clip_norm = 0.1


def mat_layout():
    return [
        ("w_in", 9 * LC, C),
        ("w_t1", TE, TD),
        ("w_t2", TD, TD),
        ("w_tp", TD, C),
        ("table", NCLS, C),
        ("w_c1", 9 * C, C),
        ("w_c2", 9 * C, C),
        ("w_pin", C, C),
        ("w_qkv", C, 3 * C),
        ("w_o", C, C),
        ("w_cq", C, C),
        ("w_ckv", C, 2 * C),
        ("w_co", C, C),
        ("w_ff1", C, 2 * FFI),
        ("w_ff2", FFI, C),
        ("w_pout", C, C),
        ("w_out", 9 * C, LC),
    ]


def vec_layout():
    names = [
        "b_tp",
        "b_in",
        "g1",
        "bb1",
        "b_c1",
        "g2",
        "bb2",
        "b_c2",
        "g3",
        "bb3",
        "b_pin",
        "n1g",
        "n1b",
        "b_o",
        "n2g",
        "n2b",
        "b_co",
        "n3g",
        "n3b",
    ]
    return (
        [("b_t1", TD), ("b_t2", TD)]
        + [(name_one, C) for name_one in names]
        + [("b_ff1", 2 * FFI), ("b_ff2", C), ("b_pout", C), ("b_out", LC)]
    )


def unpack(joined, layout):
    pieces = {}
    start_at = 0
    for record in layout:
        length = 1
        for extent_one in record[1:]:
            length = length * extent_one
        pieces[record[0]] = joined[start_at : start_at + length].reshape(record[1:])
        start_at = start_at + length
    return pieces


def noise_level(step_value):
    steps_idx = jnp.arange(NT).astype(jnp.float32)
    root_beta = math.sqrt(beta_first) + (
        math.sqrt(beta_last) - math.sqrt(beta_first)
    ) * steps_idx / (NT - 1)
    log_keep = jnp.log1p(-root_beta * root_beta)
    return jnp.exp(jnp.sum(jnp.where(jnp.arange(NT) <= step_value, log_keep, 0.0)))


def time_embed(step_value):
    frequency = jnp.exp(-math.log(10000.0) * jnp.arange(TE // 2).astype(jnp.float32) / (TE // 2))
    angles = step_value.astype(jnp.float32) * frequency
    return jnp.concatenate([jnp.cos(angles), jnp.sin(angles)])


WIDE = 512
HALF = 256
LEAD = 5
FRAME = 16
TOKENS = SIDE * FRAME
LOCAL_HEADS = HEADS // 2
WIRE_TOP = 32768.0


def silu_slope(values):
    logistic = jax.nn.sigmoid(values)
    return logistic * (1.0 + values * (1.0 - logistic))


def dot(left, right):
    return jnp.dot(left, right, preferred_element_type=jnp.float32)


def dot_t(left, right):
    return lax.dot_general(
        left, right, (((1,), (1,)), ((), ())), preferred_element_type=jnp.float32
    )


def t_dot(left, right):
    return lax.dot_general(
        left, right, (((0,), (0,)), ((), ())), preferred_element_type=jnp.float32
    )


def low(values):
    return values.astype(jnp.bfloat16)


class Place:
    def __init__(self):
        self.dp, self.rows = (lax.axis_size("dp"), lax.axis_size("rows"))
        self.count = self.dp * self.rows
        self.index = lax.axis_index("dp") * self.rows + lax.axis_index("rows")
        self.side = self.index % 2
        self.slot = (self.index // 2) % 2
        digits, left = ([], self.dp)
        while left > 4:
            digits.append(4)
            left //= 4
        digits.append(left)
        self.digits = digits + [2]
        strides, step = ([], 2)
        for size in reversed(self.digits):
            strides.insert(0, step)
            step *= size
        self.strides = strides
        self.coords = [(self.index // s) % n for s, n in zip(strides, self.digits)]

    def move(self, value, pairs):
        return lax.ppermute(value, ("dp", "rows"), pairs)

    def swap(self, value, stride=1):
        return self.move(value, [(k, k ^ stride) for k in range(self.count)])

    def shift(self, value, by):
        return self.move(
            value, [(k, k + by) for k in range(self.count) if 0 <= k + by < self.count]
        )

    def rotate(self, value, axis, by):
        stride, size = (self.strides[axis], self.digits[axis])
        pairs = []
        for k in range(self.count):
            at = (k // stride) % size
            pairs.append((k, k + ((at + by) % size - at) * stride))
        return self.move(value, pairs)

    def step(self, value, axis, direction, hops):
        stride, size = (self.strides[axis], self.digits[axis])
        pairs = []
        for k in range(self.count):
            at = (k // stride) % size
            rank = at if direction > 0 else size - 1 - at
            if rank <= hops and rank < size - 1:
                pairs.append((k, k + direction * stride))
        return self.move(value, pairs)

    def half(self, value, axis=-1):
        axis = axis % value.ndim
        return lax.dynamic_slice_in_dim(value, self.side * HALF, HALF, axis)

    def join(self, mine, other):
        first = jnp.where(self.side == 0, mine, other)
        second = jnp.where(self.side == 0, other, mine)
        return jnp.concatenate([first, second], axis=-1)

    def full(self, mine):
        return self.join(mine, self.swap(mine))

    def chip_sum(self, value):
        stride = 2
        while stride < self.count:
            value = value + self.swap(value, stride)
            stride *= 2
        return value


def shard_rows(flat_len, count):
    length = flat_len // count
    rows = -(-(LEAD * WIDE + flat_len) // (WIDE * count))
    rows = -(-rows // 8) * 8
    while rows * WIDE - length < LEAD * WIDE:
        rows += 8
    return rows


def to_blocks(place, shard, rows):
    length, block = (shard.shape[0], rows * WIDE)
    drift = block - length
    reach = drift * (place.count - 1) - LEAD * WIDE + block
    parts, hop = ([jnp.zeros((LEAD * WIDE,), shard.dtype), shard], 1)
    while hop * length < reach:
        take = min(length, reach - hop * length)
        take = min(length, -(-take // 1024) * 1024)
        parts.append(place.shift(shard[:take], -hop))
        hop += 1
    joined = jnp.concatenate(parts)
    lack = drift * (place.count - 1) + block - joined.shape[0]
    if lack > 0:
        joined = jnp.pad(joined, (0, lack))
    return lax.dynamic_slice(joined, (drift * place.index,), (block,)).reshape(rows, WIDE)


def from_blocks(place, block, length):
    flat = block.reshape(-1)
    drift = flat.shape[0] - length
    reach = drift * (place.count - 1) - LEAD * WIDE
    parts, hop, lead = ([flat], 1, 0)
    while lead < reach:
        take = min(flat.shape[0], -(-(reach - lead) // 1024) * 1024)
        parts.insert(0, place.shift(flat[flat.shape[0] - take :], hop))
        lead += take
        hop += 1
    joined = jnp.concatenate(parts)
    start = lead + LEAD * WIDE - drift * place.index
    return lax.dynamic_slice(joined, (start,), (length,))


def pick(values, index, axis):
    return lax.dynamic_index_in_dim(values, index, axis, keepdims=False)


def wire(values):
    return values.astype(jnp.float16)


def plain(values):
    return values.astype(jnp.float32)


SQUARE_AT = 8


class Largest:
    def __init__(self, place, values):
        self.place, self.values, self.stride = (place, values, 1)

    def exchange(self, beside=None):
        if self.stride < self.place.count:
            got = self.place.swap(self.values, self.stride)
            if beside is not None:
                got, beside = lax.optimization_barrier((got, beside))
            self.values = lax.optimization_barrier(jnp.maximum(self.values, got))
            self.stride *= 2
        return beside

    def finish(self):
        while self.stride < self.place.count:
            self.exchange()
        return self.values


def scatter_part(place, grads, low_row, rows, order, scale):
    held, left, first, factor = (grads, list(range(len(place.digits))), low_row, scale)

    def part_of(dim, index):
        starts, sizes, shape = ([], [], [])
        for at, axis in enumerate(left):
            starts.append(index if at == dim else 0)
            sizes.append(1 if at == dim else place.digits[axis])
            if at != dim:
                shape.append(place.digits[axis])
        out = lax.dynamic_slice(held, starts + [first, 0], sizes + [rows, HALF])
        return out.reshape(shape + [rows, HALF]) * factor

    for axis in order:
        dim = left.index(axis)
        me, size = (place.coords[axis], place.digits[axis])
        total = part_of(dim, me)
        if size == 2 or axis != order[0]:
            for away in range(1, size):
                sent = wire(part_of(dim, (me + away) % size))
                total = total + plain(place.rotate(sent, axis, away))
        else:
            flows = {1: None, -1: None}
            for hops in range(size - 1):
                for direction in (1, -1):
                    rank = me if direction > 0 else size - 1 - me
                    aim = jnp.minimum(size - 1 - hops + rank, size - 1)
                    aim = aim if direction > 0 else size - 1 - aim
                    value = part_of(dim, aim)
                    if flows[direction] is not None:
                        value = value + plain(flows[direction])
                    flows[direction] = place.step(wire(value), axis, direction, hops)
            total = total + plain(flows[1]) + plain(flows[-1])
        held, first, factor = (total, 0, 1.0)
        left.remove(axis)
    return held


SHARES = (0.42, 0.33)


def scatter_sum(place, grads, scale, rows):
    held = grads.reshape(*place.digits, 2 * rows, HALF)
    axes = list(range(len(place.digits)))[::-1]
    total = 2 * rows
    cuts = [0] + [int(total * sum(SHARES[: i + 1]) / 8 + 0.5) * 8 for i in range(2)] + [total]
    parts = []
    for i in range(3):
        order = axes[i:] + axes[:i]
        parts.append(scatter_part(place, held, cuts[i], cuts[i + 1] - cuts[i], order, scale))
    unit = 1.0 / scale
    parts = [part * unit for part in parts]
    square = sum(jnp.sum(part * part) for part in parts).reshape(1, 1)
    chip = jnp.concatenate(parts, axis=0).reshape(2, rows, HALF)
    mine = pick(chip, place.side, 0)
    other = place.swap(pick(chip, 1 - place.side, 0))
    return (place.join(mine, other), square)


class Store:
    def __init__(self, place, rows):
        self.total = place.count * rows
        self.buffer = None
        self.top = jnp.zeros((1, 1), jnp.float32)
        self.places, at = ({}, LEAD)
        for name, depth, width in mat_layout():
            self.places[name] = at
            at += depth * width // WIDE

    def write(self, out, top):
        self.buffer = out
        if top is not None:
            self.top = jnp.maximum(self.top, top)

    def add(self, name, inputs, gradient):
        if inputs.shape[0] < 16:
            spare = ((0, 16 - inputs.shape[0]), (0, 0))
            inputs, gradient = (jnp.pad(inputs, spare), jnp.pad(gradient, spare))
        grad_into(self, inputs, gradient, self.places[name])

    def put(self, at, values):
        self.buffer = lax.dynamic_update_slice(self.buffer, values, (at, 0))


def store_specs(store, at, tile):
    old = [] if store.buffer is None else [store.buffer]
    out = pl.BlockSpec(
        (pl.Element(tile), pl.Element(HALF)), lambda i, *_: (pl.multiple_of(at + tile * i, 8), 0)
    )
    shape = jax.ShapeDtypeStruct((store.total, HALF), jnp.float32)
    return (old, [pl.BlockSpec(memory_space=pl.ANY) for _ in old], out, shape)


def grad_into(store, inputs, gradient, at):
    tokens, depth = inputs.shape
    pieces = gradient.shape[1] // HALF
    tile = min(depth, 512 if pieces == 1 else 256 if pieces < 8 else 128)
    rows, tiles = (tile * pieces, depth // tile)
    old, old_specs, out_spec, out_shape = store_specs(store, at, rows)

    def body(*refs):
        refs = refs[len(old) :]
        input_ref, gradient_ref, out_ref, top_out = refs[:4]
        step = pl.program_id(0)
        part = t_dot(input_ref[...], gradient_ref[...])
        if pieces == 1:
            out_ref[...] = part
        else:
            mixed = refs[-1]
            for side in range(HALF // 128):
                for j in range(pieces):
                    column = j * HALF + side * 128
                    mixed[pl.ds(j, tile, stride=pieces), :] = part[:, column : column + 128]
                out_ref[:, side * 128 : (side + 1) * 128] = mixed[...]
        largest = jnp.max(jnp.abs(part))

        @pl.when(step == 0)
        def _():
            top_out[0, 0] = largest

        @pl.when(step > 0)
        def _():
            top_out[0, 0] = jnp.maximum(top_out[0, 0], largest)

    out, top = pl.pallas_call(
        body,
        grid=(tiles,),
        in_specs=old_specs
        + [
            pl.BlockSpec((tokens, tile), lambda i: (0, i)),
            pl.BlockSpec(gradient.shape, lambda i: (0, 0)),
        ],
        out_specs=[out_spec, pl.BlockSpec(memory_space=pltpu.SMEM)],
        out_shape=[out_shape, jax.ShapeDtypeStruct((1, 1), jnp.float32)],
        scratch_shapes=[] if pieces == 1 else [pltpu.VMEM((rows, 128), jnp.float32)],
        input_output_aliases={k: k for k in range(len(old))},
        compiler_params=params(),
        cost_estimate=cost(
            2 * tokens * depth * gradient.shape[1],
            depth * gradient.shape[1] * 4 + tokens * depth * 2,
        ),
    )(*old, inputs, gradient)
    store.write(out, top)


VMEM_LIMIT = 50 * 1024 * 1024
PADDED = TOKENS + 2 * FRAME


def params():
    return pltpu.CompilerParams(vmem_limit_bytes=VMEM_LIMIT)


def whole(shape):
    return pl.BlockSpec(shape, lambda *_: (0,) * len(shape))


def cost(flops, nbytes):
    return pl.CostEstimate(flops=flops, bytes_accessed=nbytes, transcendentals=0)


def token_mask(limit):
    return (lax.broadcasted_iota(jnp.int32, (TOKENS, 1), 0) < limit).astype(jnp.float32)


def columns_moved(values, col_off):
    if col_off == 0:
        return values
    col = lax.broadcasted_iota(jnp.int32, (TOKENS, 1), 0) % FRAME
    keep = col > 0 if col_off < 0 else col < FRAME - 1
    return jnp.where(keep, pltpu.roll(values, (-col_off) % TOKENS, 0), 0.0)


def two_sides(side, mine, other):
    first = jnp.where(side == 0, mine, other)
    second = jnp.where(side == 0, other, mine)
    return jnp.concatenate([first, second], axis=1)


def fill_moved(moved, values):
    width = moved.shape[2]
    empty = jnp.zeros((FRAME, width), moved.dtype)
    for slab in range(3):
        moved[slab, 0:FRAME, :] = empty
        moved[slab, FRAME : FRAME + TOKENS, :] = columns_moved(values, slab - 1).astype(moved.dtype)
        moved[slab, FRAME + TOKENS : PADDED, :] = empty


def tap_of(step, turned):
    row_off, col_off = (step // 3 - 1, step % 3 - 1)
    return (
        jnp.where(turned == 1, col_off, row_off),
        jnp.where(turned == 1, row_off, col_off),
    )


def rows_from(row_off):
    return pl.ds(pl.multiple_of(FRAME * (1 + row_off), FRAME), TOKENS)


def group_same():
    left = lax.broadcasted_iota(jnp.int32, (HALF, HALF), 0) // (C // GROUPS)
    right = lax.broadcasted_iota(jnp.int32, (HALF, HALF), 1) // (C // GROUPS)
    return (left == right).astype(jnp.float32)


def spread_in(sums, same):
    wide = jnp.broadcast_to(sums, (8, HALF))
    return jnp.dot(
        wide, same, precision=lax.Precision.HIGHEST, preferred_element_type=jnp.float32
    )[0:1]


def norm_in(value, mask, limit, gain, bias):
    same = group_same()
    share = 1.0 / (limit.astype(jnp.float32) * (C // GROUPS))
    mean_val = spread_in(jnp.sum(value * mask, axis=0, keepdims=True), same) * share
    centered = value - mean_val
    var_val = spread_in(jnp.sum(centered * centered * mask, axis=0, keepdims=True), same) * share
    inv_std = lax.rsqrt(var_val + eps_group)
    normed = centered * inv_std
    return (normed * gain + bias, normed, inv_std)


def silu_in(values):
    return values / (1.0 + jnp.exp(-values))


def finish_forward(total, limit, base, rows, act, act_out, normed_out, inv_out, value_out):
    mask = token_mask(limit)
    value = mask * (total + rows[0:1])
    if base is not None:
        value = value + base
    norm, normed, inv_std = norm_in(value, mask, limit, rows[1:2], rows[2:3])
    result = mask * silu_in(norm) if act else norm
    low_result = result.astype(jnp.bfloat16)
    act_out[...] = low_result
    normed_out[...] = normed
    inv_out[0:1] = inv_std
    inv_out[1:2] = column_squares(low_result)
    if value_out is not None:
        value_out[...] = value


def forward_outs(with_value):
    shapes = [
        jax.ShapeDtypeStruct((TOKENS, HALF), jnp.bfloat16),
        jax.ShapeDtypeStruct((TOKENS, HALF), jnp.float32),
        jax.ShapeDtypeStruct((8, HALF), jnp.float32),
    ]
    if with_value:
        shapes.append(jax.ShapeDtypeStruct((TOKENS, HALF), jnp.float32))
    return shapes


def first_forward(info, inputs, weight, rows):
    def body(info_ref, input_ref, weight_ref, rows_ref, *outs):
        total = dot(input_ref[...], weight_ref[...])
        finish_forward(total, info_ref[2], None, rows_ref[...], True, *outs)

    outs = forward_outs(True)
    return pl.pallas_call(
        body,
        grid_spec=pltpu.PrefetchScalarGridSpec(
            num_scalar_prefetch=1,
            grid=(1,),
            in_specs=[whole(inputs.shape), whole(weight.shape), whole(rows.shape)],
            out_specs=[whole(one.shape) for one in outs],
        ),
        out_shape=outs,
        compiler_params=params(),
        cost_estimate=cost(2 * TOKENS * 27 * HALF, 3 * TOKENS * HALF * 4),
    )(info, inputs, weight, rows)


def conv_forward(info, mine, other, table, at, base, rows, act):
    with_base = base is not None

    def body(info_ref, mine_ref, other_ref, weight_ref, rows_ref, *rest):
        base_ref = rest[0] if with_base else None
        outs, (moved, total) = (rest[int(with_base) : -2], rest[-2:])
        step = pl.program_id(0)

        @pl.when(step == 0)
        def _():
            both = two_sides(info_ref[0], mine_ref[...], other_ref[...])
            fill_moved(moved, both.astype(jnp.float32))
            total[...] = jnp.zeros_like(total)

        part = None
        for j in range(3):
            row_off, col_off = tap_of(3 * step + j, info_ref[1])
            one = dot(moved[col_off + 1, rows_from(row_off), :], weight_ref[C * j : C * (j + 1), :])
            part = one if part is None else part + one
        total[...] += part

        @pl.when(step == 2)
        def _():
            value_out = outs[3] if with_base else None
            held = base_ref[...] if with_base else None
            finish_forward(
                total[...], info_ref[2], held, rows_ref[...], act, *outs[:3], value_out
            )

    outs = forward_outs(with_base)
    extra = [base] if with_base else []
    return pl.pallas_call(
        body,
        grid_spec=pltpu.PrefetchScalarGridSpec(
            num_scalar_prefetch=1,
            grid=(3,),
            in_specs=[
                whole(mine.shape),
                whole(other.shape),
                pl.BlockSpec(
                    (pl.Element(3 * C), pl.Element(HALF)),
                    lambda i, info_ref: (
                        pl.multiple_of(at + 3 * C * i, 8),
                        pl.multiple_of(HALF * info_ref[0], HALF),
                    ),
                ),
                whole(rows.shape),
            ]
            + [whole(one.shape) for one in extra],
            out_specs=[whole(one.shape) for one in outs],
            scratch_shapes=[
                pltpu.VMEM((3, PADDED, C), jnp.bfloat16),
                pltpu.VMEM((TOKENS, HALF), jnp.float32),
            ],
        ),
        out_shape=outs,
        compiler_params=params(),
        cost_estimate=cost(18 * TOKENS * C * HALF, 9 * C * HALF * 2 + 6 * TOKENS * HALF * 4),
    )(info, mine, other, table, rows, *extra)


def conv_backward(info, grad_mine, grad_other, act_mine, act_other, table, store, at, saved, rows, base):
    with_base = base is not None
    old, old_specs, out_spec, out_shape = store_specs(store, at, 3 * C)

    def body(info_ref, *refs):
        refs = refs[len(old) :]
        gm_ref, go_ref, am_ref, ao_ref = refs[:4]
        weight_refs, (normed_ref, inv_ref, rows_ref) = (refs[4:7], refs[7:10])
        base_ref = refs[10] if with_base else None
        refs = refs[10 + int(with_base) :]
        out_ref, low_out, sums_out = refs[:3]
        moved, turned_act, shifted, total = refs[-4:]
        step = pl.program_id(0)

        @pl.when(step == 0)
        def _():
            both = two_sides(info_ref[0], gm_ref[...], go_ref[...])
            fill_moved(moved, both.astype(jnp.float32))
            act = two_sides(info_ref[0], am_ref[...], ao_ref[...]).astype(jnp.float32)
            for slab in range(3):
                turned_act[slab] = columns_moved(act, slab - 1).T.astype(jnp.bfloat16)
            empty = jnp.zeros((FRAME, HALF), jnp.bfloat16)
            shifted[0:FRAME, :] = empty
            shifted[FRAME : FRAME + TOKENS, :] = gm_ref[...]
            shifted[FRAME + TOKENS : PADDED, :] = empty
            total[...] = jnp.zeros_like(total)

        part = None
        for j in range(3):
            row_off, col_off = tap_of(3 * step + j, info_ref[1])
            rows_at = rows_from(-row_off)
            out_ref[C * j : C * (j + 1), :] = dot(turned_act[col_off + 1], shifted[rows_at, :])
            one = dot_t(moved[1 - col_off, rows_at, :], weight_refs[j][...])
            part = one if part is None else part + one
        total[...] += part

        @pl.when(step == 2)
        def _():
            mask = token_mask(info_ref[2])
            gain, normed, inv_std = (rows_ref[0:1], normed_ref[...], inv_ref[0:1])
            norm = normed * gain + rows_ref[1:2]
            logistic = 1.0 / (1.0 + jnp.exp(-norm))
            gradient = mask * total[...] * (logistic * (1.0 + norm * (1.0 - logistic)))
            result, gain_grad, bias_grad = norm_back(
                gradient, normed, inv_std, mask, info_ref[2], gain
            )
            if with_base:
                result = mask * (result + base_ref[...])
            low_result = result.astype(jnp.bfloat16)
            low_out[...] = low_result
            sums_out[3:4] = column_squares(low_result)
            sums_out[0:1] = jnp.sum(result, axis=0, keepdims=True)
            sums_out[1:2] = gain_grad
            sums_out[2:3] = bias_grad

    def tap_rows(j):
        return pl.BlockSpec(
            (pl.Element(HALF), pl.Element(C)),
            lambda i, info_ref: (pl.multiple_of(at + C * (3 * i + j) + HALF * info_ref[0], 8), 0),
        )

    extra = [base] if with_base else []
    operands = [grad_mine, grad_other, act_mine, act_other]
    result = pl.pallas_call(
        body,
        grid_spec=pltpu.PrefetchScalarGridSpec(
            num_scalar_prefetch=1,
            grid=(3,),
            in_specs=old_specs
            + [whole(one.shape) for one in operands]
            + [
                tap_rows(j) for j in range(3)
            ]
            + [
                whole((TOKENS, HALF)),
                whole((8, HALF)),
                whole(rows.shape),
            ]
            + [whole(one.shape) for one in extra],
            out_specs=[
                out_spec,
                whole((TOKENS, HALF)),
                whole((8, HALF)),
            ],
            scratch_shapes=[
                pltpu.VMEM((3, PADDED, C), jnp.bfloat16),
                pltpu.VMEM((3, C, TOKENS), jnp.bfloat16),
                pltpu.VMEM((PADDED, HALF), jnp.bfloat16),
                pltpu.VMEM((TOKENS, HALF), jnp.float32),
            ],
        ),
        out_shape=[
            out_shape,
            jax.ShapeDtypeStruct((TOKENS, HALF), jnp.bfloat16),
            jax.ShapeDtypeStruct((8, HALF), jnp.float32),
        ],
        input_output_aliases={1 + k: k for k in range(len(old))},
        compiler_params=params(),
        cost_estimate=cost(36 * TOKENS * C * HALF, 9 * C * HALF * 6 + 6 * TOKENS * HALF * 4),
    )(info, *old, *operands, table, table, table, *saved, rows, *extra)
    store.write(result[0], None)
    return (result[1], result[2])


def column_squares(values):
    wide = values.astype(jnp.float32)
    return jnp.sum(wide * wide, axis=0, keepdims=True)


def norm_back(gradient, normed, inv_std, mask, limit, gain):
    same = group_same()
    share = 1.0 / (limit.astype(jnp.float32) * (C // GROUPS))
    scaled = gradient * gain
    first = spread_in(jnp.sum(scaled * mask, axis=0, keepdims=True), same) * share
    second = spread_in(jnp.sum(scaled * normed * mask, axis=0, keepdims=True), same) * share
    result = mask * inv_std * (scaled - first - normed * second)
    return (
        result,
        jnp.sum(gradient * normed, axis=0, keepdims=True),
        jnp.sum(gradient, axis=0, keepdims=True),
    )


def unmix(info, table, at, depth, pieces, columns):
    tile = min(depth, 128 if pieces > 4 else 256)

    def body(info_ref, rows_ref, out_ref, mixed):
        for side in range(columns // 128):
            mixed[...] = rows_ref[:, side * 128 : (side + 1) * 128].astype(jnp.float32)
            for j in range(pieces):
                column = j * columns + side * 128
                out_ref[:, column : column + 128] = low(mixed[pl.ds(j, tile, stride=pieces), :])

    return pl.pallas_call(
        body,
        grid_spec=pltpu.PrefetchScalarGridSpec(
            num_scalar_prefetch=1,
            grid=(depth // tile,),
            in_specs=[
                pl.BlockSpec(
                    (pl.Element(tile * pieces), pl.Element(columns)),
                    lambda i, info_ref: (
                        pl.multiple_of(at + tile * pieces * i, 8),
                        pl.multiple_of(HALF * info_ref[0] * int(columns == HALF), HALF),
                    ),
                )
            ],
            out_specs=pl.BlockSpec((tile, pieces * columns), lambda i, info_ref: (i, 0)),
            scratch_shapes=[pltpu.VMEM((tile * pieces, 128), jnp.float32)],
        ),
        out_shape=jax.ShapeDtypeStruct((depth, pieces * columns), jnp.bfloat16),
        compiler_params=params(),
        cost_estimate=cost(0, 4 * depth * pieces * columns),
    )(info, table)


class Rows:
    def __init__(self, at, count, side_columns=False, side_rows=False):
        self.at, self.count = (at, count)
        self.side_columns, self.side_rows = (side_columns, side_rows)

    def spec(self):
        at, columns, rows = (self.at, int(self.side_columns), int(self.side_rows))
        return pl.BlockSpec(
            (pl.Element(self.count), pl.Element(HALF if columns else WIDE)),
            lambda i, info_ref: (
                pl.multiple_of(at + HALF * info_ref[0] * rows, 8),
                pl.multiple_of(HALF * info_ref[0] * columns, HALF),
            ),
        )


def one_step(body, info, table, operands, outs, flops):
    arrays = [table if isinstance(one, Rows) else one for one in operands]
    specs = [one.spec() if isinstance(one, Rows) else whole(one.shape) for one in operands]
    shapes = [jax.ShapeDtypeStruct(shape, kind) for shape, kind in outs]
    nbytes = sum(math.prod(one.shape) * one.dtype.itemsize for one in shapes)
    return pl.pallas_call(
        body,
        grid_spec=pltpu.PrefetchScalarGridSpec(
            num_scalar_prefetch=1,
            grid=(1,),
            in_specs=specs,
            out_specs=[whole(one.shape) for one in shapes],
        ),
        out_shape=shapes,
        compiler_params=params(),
        cost_estimate=cost(flops, 2 * nbytes),
    )(info, *arrays)


f32, bf16 = (jnp.float32, jnp.bfloat16)


def side_of(side, values):
    return jnp.where(side == 0, values[:, :HALF], values[:, HALF:])


def layer_parts(values):
    centered = values - jnp.mean(values, axis=-1, keepdims=True)
    var_val = jnp.mean(centered * centered, axis=-1, keepdims=True)
    inv_std = lax.rsqrt(var_val + eps_layer)
    return (centered * inv_std, inv_std)


def layer_back(gradient, values, gain, base, side, sums_ref):
    normed, inv_std = layer_parts(values)
    scaled = gradient * gain
    first = jnp.mean(scaled, axis=-1, keepdims=True)
    second = jnp.mean(scaled * normed, axis=-1, keepdims=True)
    result = base + inv_std * (scaled - first - normed * second)
    sums_ref[0:1] = side_of(side, jnp.sum(result, axis=0, keepdims=True))
    sums_ref[1:2] = side_of(side, jnp.sum(gradient * normed, axis=0, keepdims=True))
    sums_ref[2:3] = side_of(side, jnp.sum(gradient, axis=0, keepdims=True))
    return result


def head_lanes(head):
    return lax.broadcasted_iota(jnp.int32, (1, HALF), 1) // DHEAD == head


def head_probs(query, key, head, limit):
    mine = jnp.where(head_lanes(head), query, jnp.zeros((), bf16))
    scores = dot_t(mine, key) * 0.125
    seen = lax.broadcasted_iota(jnp.int32, (1, TOKENS), 1) < limit
    scores = jnp.where(seen, scores, -1e30)
    exponent = jnp.exp(scores - jnp.max(scores, axis=-1, keepdims=True))
    return exponent / jnp.sum(exponent, axis=-1, keepdims=True)


def self_front(info, table, mine, other, weight, rows, qkv):
    def body(info_ref, mine_ref, other_ref, weight_ref, rows_ref, qkv_ref, *outs):
        token_ref, resid_ref, ln_ref, packed_ref, out_ref = outs
        token = two_sides(info_ref[0], mine_ref[...], other_ref[...])
        token_ref[...] = token
        resid = dot(token, weight_ref[...]) + rows_ref[0:1]
        resid_ref[...] = resid
        ln = low(layer_parts(resid)[0] * rows_ref[1:2] + rows_ref[2:3])
        ln_ref[...] = ln
        packed_ref[...] = low(dot(ln, qkv_ref[...]))
        query, key = (packed_ref[:, 0:HALF], packed_ref[:, HALF : 2 * HALF])
        value = packed_ref[:, 2 * HALF : 3 * HALF]
        total = jnp.zeros((TOKENS, HALF), f32)
        for head in range(LOCAL_HEADS):
            probs = head_probs(query, key, head, info_ref[2])
            total = jnp.where(head_lanes(head), dot(low(probs), value), total)
        out_ref[...] = low(total)

    outs = [
        ((TOKENS, C), bf16),
        ((TOKENS, C), f32),
        ((TOKENS, C), bf16),
        ((TOKENS, 3 * HALF), bf16),
        ((TOKENS, HALF), bf16),
    ]
    flops = 2 * TOKENS * C * (C + 3 * HALF) + 4 * LOCAL_HEADS * TOKENS * TOKENS * HALF
    return one_step(body, info, table, [mine, other, weight, rows, qkv], outs, flops)


def same_head():
    left = lax.broadcasted_iota(jnp.int32, (HALF, HALF), 0) // DHEAD
    right = lax.broadcasted_iota(jnp.int32, (HALF, HALF), 1) // DHEAD
    return (left == right).astype(f32)


def head_sums(values, same):
    return jnp.dot(values, same, precision=lax.Precision.HIGHEST, preferred_element_type=f32)


def cross_probs(query, context, same):
    first = head_sums(query * context[0:1, :HALF], same) * 0.125
    second = head_sums(query * context[1:2, :HALF], same) * 0.125
    top = jnp.maximum(first, second)
    first, second = (jnp.exp(first - top), jnp.exp(second - top))
    total = first + second
    return (first / total, second / total)


def cross_front(info, table, mine, other, weight, rows, resid, query_weight, context):
    def body(info_ref, mine_ref, other_ref, weight_ref, rows_ref, old_ref, qw_ref, kv_ref, *outs):
        full_ref, resid_ref, ln_ref, query_ref, out_ref = outs
        joined = two_sides(info_ref[0], mine_ref[...], other_ref[...])
        full_ref[...] = joined
        resid_now = old_ref[...] + dot(joined, weight_ref[...]) + rows_ref[0:1]
        resid_ref[...] = resid_now
        ln = low(layer_parts(resid_now)[0] * rows_ref[1:2] + rows_ref[2:3])
        ln_ref[...] = ln
        query = low(dot(ln, qw_ref[...]))
        query_ref[...] = query
        both = kv_ref[...].astype(f32)
        first, second = cross_probs(query.astype(f32), both, same_head())
        out_ref[...] = low(first * both[0:1, HALF:] + second * both[1:2, HALF:])

    outs = [
        ((TOKENS, C), bf16),
        ((TOKENS, C), f32),
        ((TOKENS, C), bf16),
        ((TOKENS, HALF), bf16),
        ((TOKENS, HALF), bf16),
    ]
    operands = [mine, other, weight, rows, resid, query_weight, context]
    return one_step(body, info, table, operands, outs, 2 * TOKENS * C * (C + 13 * HALF))


def gelu_parts(gate):
    return 0.5 * (1.0 + lax.erf(gate * math.sqrt(0.5)))


WIDE_FF = FFI // 2


def ff_front(info, table, mine, other, weight, rows, resid, ff_weight, ff_bias):
    def body(info_ref, mine_ref, other_ref, weight_ref, rows_ref, old_ref, fw_ref, fb_ref, *outs):
        full_ref, resid_ref, ln_ref, proj_ref, out_ref = outs
        joined = two_sides(info_ref[0], mine_ref[...], other_ref[...])
        full_ref[...] = joined
        resid_now = old_ref[...] + dot(joined, weight_ref[...]) + rows_ref[0:1]
        resid_ref[...] = resid_now
        ln = low(layer_parts(resid_now)[0] * rows_ref[1:2] + rows_ref[2:3])
        ln_ref[...] = ln
        for at in range(0, WIDE_FF, HALF):
            gate_at = WIDE_FF + at
            lift = dot(ln, fw_ref[:, at : at + HALF]) + fb_ref[:, at : at + HALF]
            gate = dot(ln, fw_ref[:, gate_at : gate_at + HALF]) + fb_ref[:, gate_at : gate_at + HALF]
            proj_ref[:, at : at + HALF] = lift
            proj_ref[:, gate_at : gate_at + HALF] = gate
            out_ref[:, at : at + HALF] = low(lift * gate * gelu_parts(gate))

    outs = [
        ((TOKENS, C), bf16),
        ((TOKENS, C), f32),
        ((TOKENS, C), bf16),
        ((TOKENS, FFI), f32),
        ((TOKENS, WIDE_FF), bf16),
    ]
    operands = [mine, other, weight, rows, resid, ff_weight, ff_bias]
    return one_step(body, info, table, operands, outs, 2 * TOKENS * C * (C + FFI))


def ff_finish(info, table, mine, other, weight, rows, resid, out_weight, out_bias, state):
    def body(info_ref, mine_ref, other_ref, weight_ref, rows_ref, old_ref, ow_ref, ob_ref, state_ref, *outs):
        full_ref, resid_ref, out_ref = outs
        side = info_ref[0]
        for at in range(0, WIDE_FF, HALF):
            own, peer = (mine_ref[:, at : at + HALF], other_ref[:, at : at + HALF])
            full_ref[:, 2 * at : 2 * at + WIDE] = two_sides(side, own, peer)
        resid_now = old_ref[...] + dot(full_ref[...], weight_ref[...]) + rows_ref[0:1]
        inner = low(resid_now)
        resid_ref[...] = inner
        branch = dot(inner, ow_ref[...]) + ob_ref[0:1]
        out_ref[...] = low(state_ref[...] + token_mask(info_ref[2]) * branch)

    outs = [((TOKENS, FFI), bf16), ((TOKENS, C), bf16), ((TOKENS, HALF), bf16)]
    operands = [mine, other, weight, rows, resid, out_weight, out_bias, state]
    return one_step(body, info, table, operands, outs, 2 * TOKENS * C * (FFI + HALF))


def lanes_moved(values, row_off, col_off):
    token = lax.broadcasted_iota(jnp.int32, (1, TOKENS), 1)
    row, col = (token // FRAME + row_off, token % FRAME + col_off)
    keep = (row >= 0) & (row < SIDE) & (col >= 0) & (col < FRAME)
    away = FRAME * row_off + col_off
    return jnp.where(keep, pltpu.roll(values, lax.rem(TOKENS - away, TOKENS), 1), 0.0)


OUT_ROWS = 8


def loss_back(info, table, mine, other, out_weight, noise, bias, pout, ff2, projected, ff1):
    def body(info_ref, *refs):
        mine_ref, other_ref, ow_ref, noise_ref, bias_ref, pout_ref, ff2_ref, proj_ref, ff1_ref = refs[:9]
        ow_grad, small_out, state_out, pout_low, ff2_low, resid_out, proj_low, ln_out, sums, ff_sums = refs[9:]
        side, turned, limit = (info_ref[0], info_ref[1], info_ref[2])
        state = two_sides(side, mine_ref[...], other_ref[...])
        raw = dot_t(ow_ref[...], state)
        predicted = bias_ref[:, 0:1]
        for tap in range(9):
            row_off, col_off = tap_of(tap, turned)
            part = raw[tap * OUT_ROWS : (tap + 1) * OUT_ROWS]
            predicted = predicted + lanes_moved(part, row_off, col_off)
        token = lax.broadcasted_iota(jnp.int32, (OUT_ROWS, TOKENS), 1)
        channel = lax.broadcasted_iota(jnp.int32, (OUT_ROWS, TOKENS), 0)
        error = jnp.where((token < limit) & (channel < LC), predicted - noise_ref[...], 0.0)
        loss = jnp.sum(jnp.sum(error * error, axis=1, keepdims=True), axis=0, keepdims=True)
        gradient = 2.0 * error
        small_out[:, 0:128] = jnp.broadcast_to(jnp.sum(gradient, axis=1, keepdims=True), (OUT_ROWS, 128))
        small_out[:, 128:256] = jnp.broadcast_to(loss, (OUT_ROWS, 128))
        gradient = low(gradient).astype(f32)
        moved = []
        for tap in range(9):
            row_off, col_off = tap_of(tap, turned)
            moved.append(lanes_moved(gradient, -row_off, -col_off))
        moved = low(jnp.concatenate(moved, axis=0))
        ow_grad[...] = dot(moved, state)
        state_grad = t_dot(moved, ow_ref[...])
        state_out[...] = side_of(side, state_grad)
        branch = token_mask(limit) * state_grad
        sums[1:2] = side_of(side, jnp.sum(branch, axis=0, keepdims=True))
        branch = low(branch)
        pout_low[...] = side_of(side, branch)
        resid_grad = dot_t(branch, pout_ref[...])
        resid_out[...] = resid_grad
        sums[0:1] = side_of(side, jnp.sum(resid_grad, axis=0, keepdims=True))
        resid_low = low(resid_grad)
        ff2_low[...] = side_of(side, resid_low)
        total = jnp.zeros((TOKENS, C), f32)
        for j in range(WIDE_FF // HALF):
            at, gate_at = (j * HALF, WIDE_FF + j * HALF)
            own = pl.ds(pl.multiple_of(WIDE * j + HALF * side, HALF), HALF)
            gated_grad = dot_t(resid_low, ff2_ref[own, :])
            lift, gate = (proj_ref[:, at : at + HALF], proj_ref[:, gate_at : gate_at + HALF])
            cdf = gelu_parts(gate)
            density = jnp.exp(-0.5 * gate * gate) * (1.0 / math.sqrt(2.0 * math.pi))
            lift_grad = gated_grad * gate * cdf
            gate_grad = gated_grad * lift * (cdf + gate * density)
            ff_sums[j : j + 1] = jnp.sum(lift_grad, axis=0, keepdims=True)
            ff_sums[4 + j : 5 + j] = jnp.sum(gate_grad, axis=0, keepdims=True)
            lift_grad, gate_grad = (low(lift_grad), low(gate_grad))
            proj_low[:, at : at + HALF] = lift_grad
            proj_low[:, gate_at : gate_at + HALF] = gate_grad
            total = total + dot_t(lift_grad, ff1_ref[:, at : at + HALF])
            total = total + dot_t(gate_grad, ff1_ref[:, gate_at : gate_at + HALF])
        ln_out[...] = total

    outs = [
        ((9 * OUT_ROWS, C), f32),
        ((OUT_ROWS, HALF), f32),
        ((TOKENS, HALF), f32),
        ((TOKENS, HALF), bf16),
        ((TOKENS, HALF), bf16),
        ((TOKENS, C), f32),
        ((TOKENS, FFI), bf16),
        ((TOKENS, C), f32),
        ((8, HALF), f32),
        ((8, HALF), f32),
    ]
    operands = [mine, other, out_weight, noise, bias, pout, ff2, projected, ff1]
    return one_step(body, info, table, operands, outs, 2 * TOKENS * C * (C + FFI + WIDE_FF))


def cross_back(info, table, mine, other, resid, gain, base, weight, query, context, ckv):
    def body(info_ref, mine_ref, other_ref, resid_ref, gain_ref, base_ref, weight_ref, query_ref, kv_ref, ckv_ref, *outs):
        resid_out, co_low, query_low, kv_grad, sums, context_out = outs
        side = info_ref[0]
        result = layer_back(
            mine_ref[...] + other_ref[...], resid_ref[...], gain_ref[0:1], base_ref[...], side, sums
        )
        resid_out[...] = result
        result = low(result)
        co_low[...] = side_of(side, result)
        out_grad = low(dot_t(result, weight_ref[...])).astype(f32)
        same, both, query_now = (same_head(), kv_ref[...].astype(f32), query_ref[...].astype(f32))
        first, second = cross_probs(query_now, both, same)
        first_grad = head_sums(out_grad * both[0:1, HALF:], same)
        second_grad = head_sums(out_grad * both[1:2, HALF:], same)
        inner = first * first_grad + second * second_grad
        first_grad = first * (first_grad - inner) * 0.125
        second_grad = second * (second_grad - inner) * 0.125
        query_low[...] = low(first_grad * both[0:1, :HALF] + second_grad * both[1:2, :HALF])
        for row, (prob, score) in enumerate(((first, first_grad), (second, second_grad))):
            kv_grad[row : row + 1, :HALF] = jnp.sum(score * query_now, axis=0, keepdims=True)
            kv_grad[row : row + 1, HALF:] = jnp.sum(prob * out_grad, axis=0, keepdims=True)
        kv_grad[2:8, :] = jnp.zeros((6, WIDE), f32)
        halves = [low(kv_grad[:, HALF * j : HALF * (j + 1)]) for j in range(2)]
        context_out[...] = unstuffed([dot_t(one, ckv_ref[...]) for one in halves])

    outs = [
        ((TOKENS, C), f32),
        ((TOKENS, HALF), bf16),
        ((TOKENS, HALF), bf16),
        ((8, WIDE), f32),
        ((8, HALF), f32),
        ((8, WIDE), f32),
    ]
    operands = [mine, other, resid, gain, base, weight, query, context, ckv]
    return one_step(body, info, table, operands, outs, 2 * TOKENS * C * 14 * HALF)


def self_back(info, table, mine, other, query_weight, resid, gain, base, weight, packed, qkv):
    def body(info_ref, mine_ref, other_ref, qw_ref, resid_ref, gain_ref, base_ref, weight_ref, packed_ref, qkv_ref, *outs):
        resid_out, o_low, packed_low, ln_out, sums = outs
        side, limit = (info_ref[0], info_ref[2])
        joined = two_sides(side, mine_ref[...], other_ref[...])
        result = layer_back(
            dot_t(joined, qw_ref[...]), resid_ref[...], gain_ref[0:1], base_ref[...], side, sums
        )
        resid_out[...] = result
        result = low(result)
        o_low[...] = side_of(side, result)
        out_grad = low(dot_t(result, weight_ref[...]))
        query, key = (packed_ref[:, 0:HALF], packed_ref[:, HALF : 2 * HALF])
        value = packed_ref[:, 2 * HALF : 3 * HALF]
        parts = [jnp.zeros((TOKENS, HALF), f32) for _ in range(3)]
        for head in range(LOCAL_HEADS):
            lanes = head_lanes(head)
            probs = head_probs(query, key, head, limit)
            mine_grad = jnp.where(lanes, out_grad, jnp.zeros((), bf16))
            prob_grad = dot_t(mine_grad, value)
            inner = jnp.sum(probs * prob_grad, axis=-1, keepdims=True)
            score_grad = low(probs * (prob_grad - inner) * 0.125)
            parts[0] = jnp.where(lanes, dot(score_grad, key), parts[0])
            parts[1] = jnp.where(lanes, t_dot(score_grad, query), parts[1])
            parts[2] = jnp.where(lanes, t_dot(low(probs), out_grad), parts[2])
        joined = low(jnp.concatenate(parts, axis=1))
        packed_low[...] = joined
        ln_out[...] = dot_t(joined, qkv_ref[...])

    outs = [
        ((TOKENS, C), f32),
        ((TOKENS, HALF), bf16),
        ((TOKENS, 3 * HALF), bf16),
        ((TOKENS, C), f32),
        ((8, HALF), f32),
    ]
    operands = [mine, other, query_weight, resid, gain, base, weight, packed, qkv]
    flops = 2 * TOKENS * C * 6 * HALF + 10 * LOCAL_HEADS * TOKENS * TOKENS * HALF
    return one_step(body, info, table, operands, outs, flops)


def token_back(info, table, mine, other, resid, gain, base, weight, normed, rows, gain_three, state):
    def body(info_ref, mine_ref, other_ref, resid_ref, gain_ref, base_ref, weight_ref, normed_ref, inv_ref, g3_ref, state_ref, *outs):
        pin_low, state_out, conv_low, sums, sums_three = outs
        side, limit = (info_ref[0], info_ref[2])
        result = layer_back(
            mine_ref[...] + other_ref[...], resid_ref[...], gain_ref[0:1], base_ref[...], side, sums
        )
        result = low(result)
        pin_low[...] = side_of(side, result)
        token_grad = dot_t(result, weight_ref[...])
        mask = token_mask(limit)
        norm_grad, gain_grad, bias_grad = norm_back(
            token_grad, normed_ref[...], inv_ref[0:1], mask, limit, g3_ref[0:1]
        )
        state_now = state_ref[...] + norm_grad
        state_out[...] = state_now
        conv_grad = mask * state_now
        low_grad = low(conv_grad)
        conv_low[...] = low_grad
        sums_three[0:1] = jnp.sum(conv_grad, axis=0, keepdims=True)
        sums_three[1:2] = gain_grad
        sums_three[2:3] = bias_grad
        sums_three[3:4] = column_squares(low_grad)

    outs = [
        ((TOKENS, HALF), bf16),
        ((TOKENS, HALF), f32),
        ((TOKENS, HALF), bf16),
        ((8, HALF), f32),
        ((8, HALF), f32),
    ]
    operands = [mine, other, resid, gain, base, weight, normed, rows, gain_three, state]
    return one_step(body, info, table, operands, outs, 2 * TOKENS * C * HALF)


class LabelRows(Rows):
    def spec(self):
        at = self.at
        return pl.BlockSpec(
            (pl.Element(8), pl.Element(WIDE)),
            lambda i, info_ref: (pl.multiple_of(at + info_ref[3] // 8 * 8, 8), 0),
        )


def stuffing(parity, kind):
    row = lax.broadcasted_iota(jnp.int32, (WIDE, 2 * WIDE), 0)
    column = lax.broadcasted_iota(jnp.int32, (WIDE, 2 * WIDE), 1)
    return (column == 2 * row + parity).astype(f32).astype(kind)


def unstuffed(parts):
    total = None
    for parity, part in enumerate(parts):
        thirds, left = ([], part)
        for _ in range(3):
            thirds.append(low(left).astype(f32))
            left = left - thirds[-1]
        one = dot_t(low(jnp.concatenate(thirds, axis=0)), stuffing(parity, bf16))
        one = one[0:8] + one[8:16] + one[16:24]
        total = one if total is None else total + one
    return total


def first_row(values):
    row = lax.broadcasted_iota(jnp.int32, values.shape, 0)
    return jnp.where(row == 0, values, 0.0)


def time_front(info, table, at, embed, biases):
    def body(info_ref, embed_ref, bias_ref, one_ref, two_ref, out_ref, class_ref, kv_ref, *outs):
        inner, both, context_kv = outs
        spread = [stuffing(parity, bf16) for parity in range(2)]
        inner[...] = jnp.zeros_like(inner)
        hidden = []
        for j in range(2):
            pre = dot(low(embed_ref[8 * j : 8 * j + 8, :]), one_ref[...]) + bias_ref[j : j + 1]
            act = low(silu_in(pre))
            inner[0:1, WIDE * j : WIDE * (j + 1)] = pre[0:1]
            inner[2:3, WIDE * j : WIDE * (j + 1)] = act.astype(f32)[0:1]
            hidden.append(act)
        last = []
        for j in range(2):
            pre = bias_ref[2 + j : 3 + j]
            for p in range(2):
                wide = low(dot(hidden[p], spread[j]))
                pre = pre + dot(wide, two_ref[2 * WIDE * p : 2 * WIDE * (p + 1), :])
            act = low(silu_in(pre))
            inner[1:2, WIDE * j : WIDE * (j + 1)] = pre[0:1]
            inner[3:4, WIDE * j : WIDE * (j + 1)] = act.astype(f32)[0:1]
            last.append(act)
        time_vec = bias_ref[4:5]
        for p in range(2):
            time_vec = time_vec + dot(last[p], out_ref[WIDE * p : WIDE * (p + 1), :])
        row = lax.broadcasted_iota(jnp.int32, (8, WIDE), 0)
        rows = class_ref[...].astype(f32)
        class_vec = jnp.sum(jnp.where(row == lax.rem(info_ref[3], 8), rows, 0.0), axis=0, keepdims=True)
        context = jnp.where(row == 0, class_vec, jnp.where(row == 1, time_vec[0:1], 0.0))
        both[...] = context
        context = low(context)
        for j in range(2):
            wide = low(dot(context, spread[j]))
            context_kv[:, HALF * j : HALF * (j + 1)] = low(dot(wide, kv_ref[...]))

    operands = [
        embed,
        biases,
        Rows(at["w_t1"], 2 * TE),
        Rows(at["w_t2"], 2 * TD),
        Rows(at["w_tp"], TD),
        LabelRows(at["table"], 8),
        Rows(at["w_ckv"], 2 * C, side_columns=True),
    ]
    outs = [((8, 2 * WIDE), f32), ((8, WIDE), f32), ((8, WIDE), bf16)]
    return one_step(body, info, table, operands, outs, 2 * 8 * 4096 * WIDE)


def time_back(info, table, at, time_grad, inner, top, context_grad, squares):
    def body(info_ref, grad_ref, inner_ref, two_ref, out_ref, top_ref, context_ref, *rest):
        square_refs, (outs, bound_out) = (rest[:-2], rest[-2:])
        time_low = low(grad_ref[...])
        largest = lambda value: jnp.max(jnp.max(jnp.abs(value), axis=1, keepdims=True), axis=0, keepdims=True)

        def slope(values):
            logistic = 1.0 / (1.0 + jnp.exp(-values))
            return logistic * (1.0 + values * (1.0 - logistic))

        outs[...] = jnp.zeros_like(outs)
        two = []
        for p in range(2):
            cols = slice(WIDE * p, WIDE * (p + 1))
            grad = dot_t(time_low, out_ref[WIDE * p : WIDE * (p + 1), :])
            grad = first_row(grad * slope(inner_ref[1:2, cols]))
            outs[0:1, cols] = grad[0:1]
            two.append(low(grad))
        for p in range(2):
            cols = slice(WIDE * p, WIDE * (p + 1))
            rows = two_ref[2 * WIDE * p : 2 * WIDE * (p + 1), :]
            grad = unstuffed([dot_t(two[j], rows) for j in range(2)])
            outs[1:2, cols] = grad[0:1] * slope(inner_ref[0:1, cols])
        bound = largest(inner_ref[3:4, :]) * largest(time_low.astype(f32))
        bound = jnp.maximum(bound, largest(inner_ref[2:3, :]) * largest(outs[0:1, :]))
        bound = jnp.maximum(bound, largest(outs[1:2, :]))
        bound = jnp.maximum(1.02 * bound, largest(context_ref[0:1, :]))
        bound = jnp.maximum(bound, top_ref[...])
        lane = lax.broadcasted_iota(jnp.int32, (8, 128), 1)
        row = jnp.broadcast_to(bound, (8, 128))
        for i, (ref, (_, at_row)) in enumerate(zip(square_refs, squares)):
            row = jnp.where(lane == i + 1, largest(ref[at_row : at_row + 1, :]), row)
        bound_out[...] = row

    operands = [time_grad, inner, Rows(at["w_t2"], 2 * TD), Rows(at["w_tp"], TD), top, context_grad]
    operands += [one for one, _ in squares]
    outs = [((8, 2 * WIDE), f32), ((8, 128), f32)]
    return one_step(body, info, table, operands, outs, 2 * 8 * 3072 * WIDE)


def channel_mix():
    flat = np.arange(LC * C)[:, None]
    split = np.arange(LC * C)[None]
    return jnp.asarray((flat == LC * (split % C) + split // C).astype(ml_dtypes.bfloat16))


def gather_small(place, value):
    stride, joined = (1, value[None])
    while stride < place.count:
        other = place.swap(joined, stride)
        upper = (place.index // stride) % 2 == 1
        joined = jnp.where(
            upper,
            jnp.concatenate([other, joined], axis=0),
            jnp.concatenate([joined, other], axis=0),
        )
        stride *= 2
    return joined


def windows(values, turned, sign):
    width = values.shape[1]
    col = (lax.iota(jnp.int32, TOKENS) % FRAME)[:, None]
    zero_one = jnp.zeros((1, width), values.dtype)
    zero_row = jnp.zeros((FRAME, width), values.dtype)
    none = jnp.zeros((), values.dtype)
    across = {
        -1: jnp.where(col > 0, jnp.concatenate([zero_one, values[:-1]], axis=0), none),
        0: values,
        1: jnp.where(col < FRAME - 1, jnp.concatenate([values[1:], zero_one], axis=0), none),
    }
    moved = {}
    for col_off, value in across.items():
        moved[-1, col_off] = jnp.concatenate([zero_row, value[:-FRAME]], axis=0)
        moved[0, col_off] = value
        moved[1, col_off] = jnp.concatenate([value[FRAME:], zero_row], axis=0)
    out = []
    for row_off, col_off in tap_offsets:
        plain = moved[sign * row_off, sign * col_off]
        other = moved[sign * col_off, sign * row_off]
        out.append(plain if row_off == col_off else jnp.where(turned, other, plain))
    return jnp.concatenate(out, axis=1)


def frame_of(place, latents, target_noise, turned):
    both = jnp.concatenate([latents, target_noise], axis=-1)
    stride, joined = (1, both[None])
    while stride < place.rows:
        other = place.swap(joined, stride)
        upper = (place.index // stride) % 2 == 1
        joined = jnp.where(
            upper,
            jnp.concatenate([other, joined], axis=0),
            jnp.concatenate([joined, other], axis=0),
        )
        stride *= 2
    image = pick(joined, place.slot, 1).reshape(SIDE, SIDE, 2 * LC)
    portrait = image[:, :FRAME]
    landscape = jnp.transpose(image[:FRAME], (1, 0, 2))
    return jnp.where(turned, landscape, portrait).reshape(TOKENS, 2 * LC)


def train_step(place, store, table, vecs, latents, target_noise, label, step_value, orient, extent):
    half, at = (place.half, store.places)
    turned = orient != 1
    info = jnp.stack([place.side, turned.astype(jnp.int32), extent * FRAME, label]).astype(jnp.int32)
    mask = (lax.iota(jnp.int32, TOKENS) < extent * FRAME).astype(jnp.float32)[:, None]
    frame = frame_of(place, latents, target_noise, turned)
    share = noise_level(step_value)
    noisy = mask * (jnp.sqrt(share) * frame[:, :LC] + jnp.sqrt(1.0 - share) * frame[:, LC:])
    pad_in = windows(low(noisy), turned, 1)
    noise_rows = jnp.pad(frame[:, LC:].T, ((0, OUT_ROWS - LC), (0, 0)))
    embed_in = low(time_embed(step_value))[None]
    mix = channel_mix()
    row = lambda *names: jnp.stack([vecs[name] for name in names])
    side_rows = lambda *names: half(row(*names))

    def part(name, depth=C, **kind):
        return Rows(at[name], depth, **kind)

    def own_rows(name):
        return Rows(at[name], HALF, side_rows=True)

    qkv = unmix(info, table, at["w_qkv"], C, 3, HALF)
    ff1 = unmix(info, table, at["w_ff1"], C, 2 * FFI // WIDE, HALF)
    w_in = half(table[at["w_in"] : at["w_in"] + 9 * LC])
    w_out = dot(table[at["w_out"] : at["w_out"] + 9 * LC].reshape(9, LC * C), mix)
    w_out = low(jnp.pad(w_out.reshape(9, LC, C), ((0, 0), (0, OUT_ROWS - LC), (0, 0))))
    w_out = w_out.reshape(9 * OUT_ROWS, C)

    twice = jnp.repeat(embed_in.astype(jnp.float32), 2, axis=1)
    parity = lax.iota(jnp.int32, 2 * TE)[None] % 2
    stuffed = [jnp.pad(jnp.where(parity == j, twice, 0.0), ((0, 7), (0, 0))) for j in range(2)]
    biases = [vecs["b_t1"].reshape(2, WIDE), vecs["b_t2"].reshape(2, WIDE), vecs["b_tp"][None]]
    biases = jnp.pad(jnp.concatenate(biases, axis=0), ((0, 3), (0, 0)))
    inner, both, context_kv = time_front(info, table, at, jnp.concatenate(stuffed, axis=0), biases)
    context, time_vec = (low(both[:2]), both[1:2])
    hidden_one, hidden_two = (low(inner[2:3]), low(inner[3:4]))

    act_one, normed_one, inv_one, state_zero = first_forward(
        info, pad_in, w_in, side_rows("b_in", "g1", "bb1")
    )
    act_one_peer = place.swap(act_one)
    rows_two = side_rows("b_c1", "g2", "bb2")
    rows_two = jnp.concatenate([rows_two[0:1] + half(time_vec), rows_two[1:]], axis=0)
    act_two, normed_two, inv_two = conv_forward(
        info, act_one, act_one_peer, table, at["w_c1"], None, rows_two, True
    )
    act_two_peer = place.swap(act_two)
    token_own, normed_three, inv_three, state_one = conv_forward(
        info, act_two, act_two_peer, table, at["w_c2"], state_zero, side_rows("b_c2", "g3", "bb3"), False
    )
    token_in, resid_zero, ln_one, packed, attended_own = self_front(
        info, table, token_own, place.swap(token_own), part("w_pin"), row("b_pin", "n1g", "n1b"), qkv
    )
    attended, resid_one, ln_two, cross_query, cross_own = cross_front(
        info,
        table,
        attended_own,
        place.swap(attended_own),
        part("w_o"),
        row("b_o", "n2g", "n2b"),
        resid_zero,
        part("w_cq", side_columns=True),
        context_kv,
    )
    b_ff1 = half(vecs["b_ff1"].reshape(-1, WIDE)).reshape(1, FFI)
    cross_out, resid_two, ln_three, projected, gated_own = ff_front(
        info,
        table,
        cross_own,
        place.swap(cross_own),
        part("w_co"),
        row("b_co", "n3g", "n3b"),
        resid_one,
        ff1,
        b_ff1,
    )
    gated, out_in, state_own = ff_finish(
        info,
        table,
        gated_own,
        place.swap(gated_own),
        part("w_ff2", FFI),
        row("b_ff2"),
        resid_two,
        part("w_pout", side_columns=True),
        side_rows("b_pout"),
        state_one,
    )
    b_out = jnp.broadcast_to(jnp.pad(vecs["b_out"], (0, OUT_ROWS - LC))[:, None], (OUT_ROWS, 128))
    (
        w_out_grad,
        small_out,
        state_grad,
        pout_low,
        ff2_low,
        resid_grad,
        proj_low,
        ln_part,
        sums_out,
        sums_ff,
    ) = loss_back(
        info,
        table,
        state_own,
        place.swap(state_own),
        w_out,
        noise_rows,
        b_out,
        part("w_pout"),
        part("w_ff2", FFI),
        projected,
        ff1,
    )
    ln_peer = place.swap(ln_part)
    store.add("w_pout", out_in, pout_low)
    store.add("w_ff2", gated, ff2_low)
    store.add("w_ff1", ln_three, proj_low)
    w_out_grad = w_out_grad.reshape(9, OUT_ROWS, C)[:, :LC].reshape(9, LC * C)
    thirds, left = ([], w_out_grad)
    for _ in range(3):
        thirds.append(lax.reduce_precision(left, 8, 7))
        left = left - thirds[-1]
    thirds = dot_t(low(jnp.concatenate(thirds, axis=0)), mix)
    w_out_grad = thirds[:9] + thirds[9:18] + thirds[18:]
    w_out_grad = half(w_out_grad.reshape(9 * LC, C))
    store.put(at["w_out"], jnp.zeros((store.total - at["w_out"], HALF), jnp.float32))
    resid_grad, co_low, query_low, kv_grad, sums_co, context_grad = cross_back(
        info,
        table,
        ln_part,
        ln_peer,
        resid_two,
        row("n3g"),
        resid_grad,
        own_rows("w_co"),
        cross_query,
        context_kv,
        Rows(at["w_ckv"], 2 * C, side_columns=True),
    )
    query_peer = place.swap(query_low)
    kv_low = low(kv_grad[:2])
    context_grad = context_grad + place.swap(context_grad)
    store.add("w_co", cross_out, co_low)
    store.add("w_cq", ln_two, query_low)
    store.add("w_ckv", context, kv_low)
    resid_grad, o_low, packed_low, ln_part, sums_o = self_back(
        info,
        table,
        query_low,
        query_peer,
        part("w_cq"),
        resid_one,
        row("n2g"),
        resid_grad,
        own_rows("w_o"),
        packed,
        qkv,
    )
    ln_peer = place.swap(ln_part)
    store.add("w_o", attended, o_low)
    store.add("w_qkv", ln_one, packed_low)
    pin_low, state_grad, conv_low, sums_pin, sums_two = token_back(
        info,
        table,
        ln_part,
        ln_peer,
        resid_zero,
        row("n1g"),
        resid_grad,
        own_rows("w_pin"),
        normed_three,
        inv_three,
        side_rows("g3"),
        state_grad,
    )
    conv_peer = place.swap(conv_low)
    store.add("w_pin", token_in, pin_low)
    conv_low, sums_one = conv_backward(
        info,
        conv_low,
        conv_peer,
        act_two,
        act_two_peer,
        table,
        store,
        at["w_c2"],
        (normed_two, inv_two),
        side_rows("g2", "bb2"),
        None,
    )
    conv_peer = place.swap(conv_low)
    time_grad = place.full(sums_one[0:1]) + context_grad[1:2]
    b_tp = half(time_grad)
    time_low = low(time_grad)
    outer, bounds = time_back(
        info,
        table,
        at,
        jnp.pad(time_grad, ((0, 7), (0, 0))),
        inner,
        store.top,
        context_grad,
        ((inv_one, 1), (inv_two, 1), (sums_two, 3), (sums_one, 3)),
    )
    b_t2, b_t1 = (half(outer[0].reshape(-1, WIDE)), half(outer[1].reshape(-1, WIDE)))
    two_low, one_low = (low(b_t2), low(b_t1))
    largest = Largest(place, bounds)
    store.add("w_tp", hidden_two, half(time_low))
    store.buffer = largest.exchange(store.buffer)
    store.add("w_t2", hidden_one, two_low.reshape(1, -1))
    store.buffer = largest.exchange(store.buffer)
    store.add("w_t1", embed_in, one_low.reshape(1, -1))
    chosen = lax.iota(jnp.int32, NCLS)[:, None] == label
    store.put(at["table"], jnp.where(chosen, half(context_grad[0:1]), 0.0))
    store.put(0, jnp.zeros((at["w_t1"], HALF), jnp.float32))
    store.buffer = largest.exchange(store.buffer)
    in_low, sums_in = conv_backward(
        info,
        conv_low,
        conv_peer,
        act_one,
        act_one_peer,
        table,
        store,
        at["w_c1"],
        (normed_one, inv_one),
        side_rows("g1", "bb1"),
        state_grad,
    )
    store.buffer = largest.exchange(store.buffer)
    tops = largest.finish()[0]
    bound = jnp.maximum(tops[0], 1.01 * jnp.sqrt(tops[1] * tops[4]))
    bound = jnp.maximum(bound, 1.01 * jnp.sqrt(tops[2] * tops[3]))
    scale = (WIRE_TOP / (place.count // 2)) / jnp.maximum(bound, 1e-30)
    w_in_grad = t_dot(pad_in, in_low)
    small = [b_t1, b_t2, b_tp, sums_in[:3], sums_one[:3], sums_two[:3], sums_pin[:3], sums_o[:3]]
    small += [sums_co[:3], sums_ff, sums_out[:2]]
    extra = [small_out[:LC, 0], small_out[0:1, 128], (extent * FRAME).astype(jnp.float32)[None]]
    extra = jnp.pad(jnp.concatenate(extra), (0, HALF - LC - 2))[None]
    return (jnp.concatenate(small + [extra, w_in_grad, w_out_grad], axis=0), scale)


def adam_update(params, first_mom, second, gradient, decay_rate):
    first_new = adam_one * first_mom + (1.0 - adam_one) * gradient
    second_new = adam_two * second + (1.0 - adam_two) * gradient * gradient
    step_size = (
        first_new
        / (1.0 - adam_one**STEP)
        / (jnp.sqrt(second_new / (1.0 - adam_two**STEP)) + adam_eps)
    )
    return (params - learn_rate * (step_size + decay_rate * params), first_new, second_new)


def local(
    latents,
    target_noise,
    labels,
    timesteps,
    orient,
    extent,
    mat_params,
    mat_first,
    mat_second,
    mat_ema,
    vec_params,
    vec_first,
    vec_second,
    vec_ema,
):
    place = Place()
    length = mat_params.shape[0]
    rows = shard_rows(length * place.count, place.count)
    block = to_blocks(place, mat_params.astype(jnp.bfloat16), rows)
    table = lax.all_gather(block, ("dp", "rows"), axis=0, tiled=True)
    vec_len = vec_params.shape[0]
    vec_wide = -(-vec_len // 128) * 128
    padded = jnp.pad(vec_params, (0, vec_wide - vec_len)).reshape(-1, 128)
    vec_all = gather_small(place, padded).reshape(place.count, vec_wide)[:, :vec_len]
    vec_all = vec_all.reshape(-1).astype(jnp.bfloat16).astype(jnp.float32)
    vecs = unpack(vec_all, vec_layout())
    own = lambda values: pick(values, place.slot, 0)
    store = Store(place, rows)
    small, scale = train_step(
        place,
        store,
        table,
        vecs,
        latents,
        target_noise,
        own(labels),
        own(timesteps),
        own(orient),
        own(extent),
    )
    block_grad, square = scatter_sum(place, store.buffer, scale, rows)
    small = jnp.pad(small, ((0, -small.shape[0] % 8), (0, 0)))
    body = sum(record[1] for record in vec_layout()[:-1]) // WIDE
    lane = lax.broadcasted_iota(jnp.int32, small.shape, 1)
    line = lax.broadcasted_iota(jnp.int32, small.shape, 0)
    small = jnp.where((lane == SQUARE_AT) & (line == body), square, small)
    small = place.full(place.chip_sum(small))
    loss_sum, pixel_count = (small[body, LC], small[body, LC + 1])
    vec_flat = jnp.concatenate([small[:body].reshape(-1), small[body, :LC]])
    vec_flat = jnp.pad(vec_flat, (0, vec_len * place.count - vec_flat.shape[0]))
    shard_vec = lax.dynamic_slice(vec_flat, (vec_len * place.index,), (vec_len,))
    square = small[body, SQUARE_AT] + small[body, HALF + SQUARE_AT] + jnp.sum(vec_flat * vec_flat)
    shard_mat = from_blocks(place, block_grad, length)
    for i, name in enumerate(("w_in", "w_out")):
        values = small[body + 1 + 9 * LC * i : body + 1 + 9 * LC * (i + 1)]
        square = square + jnp.sum(values * values)
        owner, offset = divmod((store.places[name] - LEAD) * WIDE, length)
        old = lax.dynamic_slice(shard_mat, (offset,), (9 * LC * C,))
        new = jnp.where(place.index == owner, values.reshape(-1), old)
        shard_mat = lax.dynamic_update_slice(shard_mat, new, (offset,))
    inverse = 1.0 / pixel_count
    grad_norm = jnp.sqrt(square) * inverse
    factor = clip_norm / jnp.maximum(grad_norm, clip_norm) * inverse
    new_mat, mat_first_new, mat_second_new = adam_update(
        mat_params, mat_first, mat_second, shard_mat * factor, weight_decay
    )
    new_vec, vec_first_new, vec_second_new = adam_update(
        vec_params, vec_first, vec_second, shard_vec * factor, 0.0
    )
    ema_rate = min(ema_ceiling, (1.0 + STEP) / (10.0 + STEP))
    mat_ema_new = ema_rate * mat_ema + (1.0 - ema_rate) * new_mat
    vec_ema_new = ema_rate * vec_ema + (1.0 - ema_rate) * new_vec
    return (
        new_mat,
        mat_first_new,
        mat_second_new,
        mat_ema_new,
        new_vec,
        vec_first_new,
        vec_second_new,
        vec_ema_new,
        grad_norm,
        loss_sum,
        pixel_count,
    )


def solution(mesh):
    return jax.shard_map(
        local,
        mesh=mesh,
        in_specs=(
            P("dp", "rows", None, None),
            P("dp", "rows", None, None),
            P("dp"),
            P("dp"),
            P("dp"),
            P("dp"),
            P(("dp", "rows")),
            P(("dp", "rows")),
            P(("dp", "rows")),
            P(("dp", "rows")),
            P(("dp", "rows")),
            P(("dp", "rows")),
            P(("dp", "rows")),
            P(("dp", "rows")),
        ),
        out_specs=(
            P(("dp", "rows")),
            P(("dp", "rows")),
            P(("dp", "rows")),
            P(("dp", "rows")),
            P(("dp", "rows")),
            P(("dp", "rows")),
            P(("dp", "rows")),
            P(("dp", "rows")),
            P(),
            P(),
            P(),
        ),
        check_vma=False,
    )
```

```python
import math

import jax
import jax.numpy as jnp
import ml_dtypes
import numpy as np
from jax import lax
from jax.experimental import pallas as pl
from jax.experimental.pallas import tpu as pltpu
from jax.sharding import PartitionSpec as P

C = 512
HEADS = 8
DHEAD = 64
FFI = 2048
TE = 256
TD = 1024
NCLS = 1000
LC = 3
GROUPS = 32
SIDE = 32
NT = 1000
STEP = 10


tap_offsets = [(-1, -1), (-1, 0), (-1, 1), (0, -1), (0, 0), (0, 1), (1, -1), (1, 0), (1, 1)]
eps_group = 1e-06
eps_layer = 1e-05
beta_first = 0.00085
beta_last = 0.012
adam_one = 0.9
adam_two = 0.999
adam_eps = 1e-08
learn_rate = 0.05
weight_decay = 0.01
ema_ceiling = 0.9999
clip_norm = 0.1


def mat_layout():
    return [
        ("w_in", 9 * LC, C),
        ("w_t1", TE, TD),
        ("w_t2", TD, TD),
        ("w_tp", TD, C),
        ("table", NCLS, C),
        ("w_c1", 9 * C, C),
        ("w_c2", 9 * C, C),
        ("w_pin", C, C),
        ("w_qkv", C, 3 * C),
        ("w_o", C, C),
        ("w_cq", C, C),
        ("w_ckv", C, 2 * C),
        ("w_co", C, C),
        ("w_ff1", C, 2 * FFI),
        ("w_ff2", FFI, C),
        ("w_pout", C, C),
        ("w_out", 9 * C, LC),
    ]


def vec_layout():
    names = [
        "b_tp",
        "b_in",
        "g1",
        "bb1",
        "b_c1",
        "g2",
        "bb2",
        "b_c2",
        "g3",
        "bb3",
        "b_pin",
        "n1g",
        "n1b",
        "b_o",
        "n2g",
        "n2b",
        "b_co",
        "n3g",
        "n3b",
    ]
    return (
        [("b_t1", TD), ("b_t2", TD)]
        + [(name_one, C) for name_one in names]
        + [("b_ff1", 2 * FFI), ("b_ff2", C), ("b_pout", C), ("b_out", LC)]
    )


def unpack(joined, layout):
    pieces = {}
    start_at = 0
    for record in layout:
        length = 1
        for extent_one in record[1:]:
            length = length * extent_one
        pieces[record[0]] = joined[start_at : start_at + length].reshape(record[1:])
        start_at = start_at + length
    return pieces


def noise_level(step_value):
    steps_idx = jnp.arange(NT).astype(jnp.float32)
    root_beta = math.sqrt(beta_first) + (
        math.sqrt(beta_last) - math.sqrt(beta_first)
    ) * steps_idx / (NT - 1)
    log_keep = jnp.log1p(-root_beta * root_beta)
    return jnp.exp(jnp.sum(jnp.where(jnp.arange(NT) <= step_value, log_keep, 0.0)))


def time_embed(step_value):
    frequency = jnp.exp(-math.log(10000.0) * jnp.arange(TE // 2).astype(jnp.float32) / (TE // 2))
    angles = step_value.astype(jnp.float32) * frequency
    return jnp.concatenate([jnp.cos(angles), jnp.sin(angles)])


WIDE = 512
HALF = 256
LEAD = 5
FRAME = 16
TOKENS = SIDE * FRAME
LOCAL_HEADS = HEADS // 2
WIRE_TOP = 32768.0


def silu_slope(values):
    logistic = jax.nn.sigmoid(values)
    return logistic * (1.0 + values * (1.0 - logistic))


def dot(left, right):
    return jnp.dot(left, right, preferred_element_type=jnp.float32)


def dot_t(left, right):
    return lax.dot_general(
        left, right, (((1,), (1,)), ((), ())), preferred_element_type=jnp.float32
    )


def t_dot(left, right):
    return lax.dot_general(
        left, right, (((0,), (0,)), ((), ())), preferred_element_type=jnp.float32
    )


def low(values):
    return values.astype(jnp.bfloat16)


class Place:
    def __init__(self):
        self.dp, self.rows = (lax.axis_size("dp"), lax.axis_size("rows"))
        self.count = self.dp * self.rows
        self.index = lax.axis_index("dp") * self.rows + lax.axis_index("rows")
        self.side = self.index % 2
        self.slot = (self.index // 2) % 2
        digits, left = ([], self.dp)
        while left > 4:
            digits.append(4)
            left //= 4
        digits.append(left)
        self.digits = digits + [2]
        strides, step = ([], 2)
        for size in reversed(self.digits):
            strides.insert(0, step)
            step *= size
        self.strides = strides
        self.coords = [(self.index // s) % n for s, n in zip(strides, self.digits)]

    def move(self, value, pairs):
        return lax.ppermute(value, ("dp", "rows"), pairs)

    def swap(self, value, stride=1):
        return self.move(value, [(k, k ^ stride) for k in range(self.count)])

    def shift(self, value, by):
        return self.move(
            value, [(k, k + by) for k in range(self.count) if 0 <= k + by < self.count]
        )

    def rotate(self, value, axis, by):
        stride, size = (self.strides[axis], self.digits[axis])
        pairs = []
        for k in range(self.count):
            at = (k // stride) % size
            pairs.append((k, k + ((at + by) % size - at) * stride))
        return self.move(value, pairs)

    def step(self, value, axis, direction, hops):
        stride, size = (self.strides[axis], self.digits[axis])
        pairs = []
        for k in range(self.count):
            at = (k // stride) % size
            rank = at if direction > 0 else size - 1 - at
            if rank <= hops and rank < size - 1:
                pairs.append((k, k + direction * stride))
        return self.move(value, pairs)

    def half(self, value, axis=-1):
        axis = axis % value.ndim
        return lax.dynamic_slice_in_dim(value, self.side * HALF, HALF, axis)

    def join(self, mine, other):
        first = jnp.where(self.side == 0, mine, other)
        second = jnp.where(self.side == 0, other, mine)
        return jnp.concatenate([first, second], axis=-1)

    def full(self, mine):
        return self.join(mine, self.swap(mine))

    def chip_sum(self, value):
        stride = 2
        while stride < self.count:
            value = value + self.swap(value, stride)
            stride *= 2
        return value


def shard_rows(flat_len, count):
    length = flat_len // count
    rows = -(-(LEAD * WIDE + flat_len) // (WIDE * count))
    rows = -(-rows // 8) * 8
    while rows * WIDE - length < LEAD * WIDE:
        rows += 8
    return rows


def to_blocks(place, shard, rows):
    length, block = (shard.shape[0], rows * WIDE)
    drift = block - length
    reach = drift * (place.count - 1) - LEAD * WIDE + block
    parts, hop = ([jnp.zeros((LEAD * WIDE,), shard.dtype), shard], 1)
    while hop * length < reach:
        take = min(length, reach - hop * length)
        take = min(length, -(-take // 1024) * 1024)
        parts.append(place.shift(shard[:take], -hop))
        hop += 1
    joined = jnp.concatenate(parts)
    lack = drift * (place.count - 1) + block - joined.shape[0]
    if lack > 0:
        joined = jnp.pad(joined, (0, lack))
    return lax.dynamic_slice(joined, (drift * place.index,), (block,)).reshape(rows, WIDE)


def from_blocks(place, block, length):
    flat = block.reshape(-1)
    drift = flat.shape[0] - length
    reach = drift * (place.count - 1) - LEAD * WIDE
    parts, hop, lead = ([flat], 1, 0)
    while lead < reach:
        take = min(flat.shape[0], -(-(reach - lead) // 1024) * 1024)
        parts.insert(0, place.shift(flat[flat.shape[0] - take :], hop))
        lead += take
        hop += 1
    joined = jnp.concatenate(parts)
    start = lead + LEAD * WIDE - drift * place.index
    return lax.dynamic_slice(joined, (start,), (length,))


def pick(values, index, axis):
    return lax.dynamic_index_in_dim(values, index, axis, keepdims=False)


def wire(values):
    return values.astype(jnp.float16)


def plain(values):
    return values.astype(jnp.float32)


SQUARE_AT = 8


class Largest:
    def __init__(self, place, values):
        self.place, self.values, self.stride = (place, values, 1)

    def exchange(self, beside=None):
        if self.stride < self.place.count:
            got = self.place.swap(self.values, self.stride)
            if beside is not None:
                got, beside = lax.optimization_barrier((got, beside))
            self.values = lax.optimization_barrier(jnp.maximum(self.values, got))
            self.stride *= 2
        return beside

    def finish(self):
        while self.stride < self.place.count:
            self.exchange()
        return self.values


def scatter_part(place, grads, low_row, rows, order, scale, after=(), ahead=None):
    held, left, first, factor = (grads, list(range(len(place.digits))), low_row, scale)

    def part_of(dim, index):
        starts, sizes, shape = ([], [], [])
        for at, axis in enumerate(left):
            starts.append(index if at == dim else 0)
            sizes.append(1 if at == dim else place.digits[axis])
            if at != dim:
                shape.append(place.digits[axis])
        out = lax.dynamic_slice(held, starts + [first, 0], sizes + [rows, HALF])
        return out.reshape(shape + [rows, HALF]) * factor

    for axis in order:
        dim = left.index(axis)
        me, size = (place.coords[axis], place.digits[axis])
        total = part_of(dim, me)
        if size == 2 or axis != order[0]:
            for away in range(1, size):
                sent = wire(part_of(dim, (me + away) % size))
                if ahead is not None and axis == order[0] and away == 1:
                    sent = ahead
                got = place.rotate(sent, axis, away)
                if axis == order[0] and after:
                    got = lax.optimization_barrier((got, *after))[0]
                total = total + plain(got)
                last = (sent,)
        else:
            flows, sent = ({1: None, -1: None}, {})
            for hops in range(size - 1):
                for direction in (1, -1):
                    rank = me if direction > 0 else size - 1 - me
                    aim = jnp.minimum(size - 1 - hops + rank, size - 1)
                    aim = aim if direction > 0 else size - 1 - aim
                    value = part_of(dim, aim)
                    if hops == 1 and axis == order[0] and after:
                        flows[direction] = lax.optimization_barrier((flows[direction], *after))[0]
                    if flows[direction] is not None:
                        value = value + plain(flows[direction])
                    sent[direction] = wire(value)
                    flows[direction] = place.step(sent[direction], axis, direction, hops)
            total = total + plain(flows[1]) + plain(flows[-1])
            last = (sent[1], sent[-1])
        if axis == order[0]:
            leaving = last
        held, first, factor = (total, 0, 1.0)
        left.remove(axis)
    return (held, leaving)


SHARES = (0.42, 0.33)


def scatter_sum(place, grads, scale, rows):
    held = grads.reshape(*place.digits, 2 * rows, HALF)
    axes = list(range(len(place.digits)))[::-1]
    total = 2 * rows
    cuts = [0] + [int(total * sum(SHARES[: i + 1]) / 8 + 0.5) * 8 for i in range(2)] + [total]
    orders = [axes[i:] + axes[:i] for i in range(3)]
    parts, after, ahead = ([None] * 3, (), [None] * 3)
    for i in range(2):
        axis = orders[i][0]
        if place.digits[axis] == 2:
            starts = [0] * len(axes) + [cuts[i], 0]
            starts[axis] = 1 - place.coords[axis]
            sizes = [1 if at == axis else size for at, size in enumerate(place.digits)]
            sent = lax.dynamic_slice(held, starts, sizes + [cuts[i + 1] - cuts[i], HALF])
            ahead[i] = wire(jnp.squeeze(sent, axis) * scale)
            after = (*after, ahead[i])
    for i in (2, 0, 1):
        span = (cuts[i], cuts[i + 1] - cuts[i])
        hold = () if i == 0 else after
        parts[i], leaving = scatter_part(place, held, *span, orders[i], scale, hold, ahead[i])
        after = leaving if i == 2 else after
    unit = 1.0 / scale
    parts = [part * unit for part in parts]
    square = sum(jnp.sum(part * part) for part in parts).reshape(1, 1)
    chip = jnp.concatenate(parts, axis=0).reshape(2, rows, HALF)
    mine = pick(chip, place.side, 0)
    other = place.swap(pick(chip, 1 - place.side, 0))
    return (place.join(mine, other), square)


class Store:
    def __init__(self, place, rows):
        self.total = place.count * rows
        self.buffer = None
        self.top = jnp.zeros((1, 1), jnp.float32)
        self.places, at = ({}, LEAD)
        for name, depth, width in mat_layout():
            self.places[name] = at
            at += depth * width // WIDE

    def write(self, out, top):
        self.buffer = out
        if top is not None:
            self.top = jnp.maximum(self.top, top)

    def add(self, name, inputs, gradient):
        if inputs.shape[0] < 16:
            spare = ((0, 16 - inputs.shape[0]), (0, 0))
            inputs, gradient = (jnp.pad(inputs, spare), jnp.pad(gradient, spare))
        grad_into(self, inputs, gradient, self.places[name])

    def put(self, at, values):
        self.buffer = lax.dynamic_update_slice(self.buffer, values, (at, 0))


def store_specs(store, at, tile):
    old = [] if store.buffer is None else [store.buffer]
    out = pl.BlockSpec(
        (pl.Element(tile), pl.Element(HALF)), lambda i, *_: (pl.multiple_of(at + tile * i, 8), 0)
    )
    shape = jax.ShapeDtypeStruct((store.total, HALF), jnp.float32)
    return (old, [pl.BlockSpec(memory_space=pl.ANY) for _ in old], out, shape)


def grad_into(store, inputs, gradient, at):
    tokens, depth = inputs.shape
    pieces = gradient.shape[1] // HALF
    tile = min(depth, 512 if pieces == 1 else 256 if pieces < 8 else 128)
    rows, tiles = (tile * pieces, depth // tile)
    old, old_specs, out_spec, out_shape = store_specs(store, at, rows)

    def body(*refs):
        refs = refs[len(old) :]
        input_ref, gradient_ref, out_ref, top_out = refs[:4]
        step = pl.program_id(0)
        part = t_dot(input_ref[...], gradient_ref[...])
        if pieces == 1:
            out_ref[...] = part
        else:
            mixed = refs[-1]
            for side in range(HALF // 128):
                for j in range(pieces):
                    column = j * HALF + side * 128
                    mixed[pl.ds(j, tile, stride=pieces), :] = part[:, column : column + 128]
                out_ref[:, side * 128 : (side + 1) * 128] = mixed[...]
        largest = jnp.max(jnp.abs(part))

        @pl.when(step == 0)
        def _():
            top_out[0, 0] = largest

        @pl.when(step > 0)
        def _():
            top_out[0, 0] = jnp.maximum(top_out[0, 0], largest)

    out, top = pl.pallas_call(
        body,
        grid=(tiles,),
        in_specs=old_specs
        + [
            pl.BlockSpec((tokens, tile), lambda i: (0, i)),
            pl.BlockSpec(gradient.shape, lambda i: (0, 0)),
        ],
        out_specs=[out_spec, pl.BlockSpec(memory_space=pltpu.SMEM)],
        out_shape=[out_shape, jax.ShapeDtypeStruct((1, 1), jnp.float32)],
        scratch_shapes=[] if pieces == 1 else [pltpu.VMEM((rows, 128), jnp.float32)],
        input_output_aliases={k: k for k in range(len(old))},
        compiler_params=params(),
        cost_estimate=cost(
            2 * tokens * depth * gradient.shape[1],
            depth * gradient.shape[1] * 4 + tokens * depth * 2,
        ),
    )(*old, inputs, gradient)
    store.write(out, top)


VMEM_LIMIT = 50 * 1024 * 1024
PADDED = TOKENS + 2 * FRAME


def params():
    return pltpu.CompilerParams(vmem_limit_bytes=VMEM_LIMIT)


def whole(shape):
    return pl.BlockSpec(shape, lambda *_: (0,) * len(shape))


def cost(flops, nbytes):
    return pl.CostEstimate(flops=flops, bytes_accessed=nbytes, transcendentals=0)


def token_mask(limit):
    return (lax.broadcasted_iota(jnp.int32, (TOKENS, 1), 0) < limit).astype(jnp.float32)


def columns_moved(values, col_off):
    if col_off == 0:
        return values
    col = lax.broadcasted_iota(jnp.int32, (TOKENS, 1), 0) % FRAME
    keep = col > 0 if col_off < 0 else col < FRAME - 1
    return jnp.where(keep, pltpu.roll(values, (-col_off) % TOKENS, 0), 0.0)


def two_sides(side, mine, other):
    first = jnp.where(side == 0, mine, other)
    second = jnp.where(side == 0, other, mine)
    return jnp.concatenate([first, second], axis=1)


def fill_moved(moved, values):
    width = moved.shape[2]
    empty = jnp.zeros((FRAME, width), moved.dtype)
    for slab in range(3):
        moved[slab, 0:FRAME, :] = empty
        moved[slab, FRAME : FRAME + TOKENS, :] = columns_moved(values, slab - 1).astype(moved.dtype)
        moved[slab, FRAME + TOKENS : PADDED, :] = empty


def tap_of(step, turned):
    row_off, col_off = (step // 3 - 1, step % 3 - 1)
    return (
        jnp.where(turned == 1, col_off, row_off),
        jnp.where(turned == 1, row_off, col_off),
    )


def rows_from(row_off):
    return pl.ds(pl.multiple_of(FRAME * (1 + row_off), FRAME), TOKENS)


def group_same():
    left = lax.broadcasted_iota(jnp.int32, (HALF, HALF), 0) // (C // GROUPS)
    right = lax.broadcasted_iota(jnp.int32, (HALF, HALF), 1) // (C // GROUPS)
    return (left == right).astype(jnp.float32)


def spread_in(sums, same):
    wide = jnp.broadcast_to(sums, (8, HALF))
    return jnp.dot(
        wide, same, precision=lax.Precision.HIGHEST, preferred_element_type=jnp.float32
    )[0:1]


def norm_in(value, mask, limit, gain, bias):
    same = group_same()
    share = 1.0 / (limit.astype(jnp.float32) * (C // GROUPS))
    mean_val = spread_in(jnp.sum(value * mask, axis=0, keepdims=True), same) * share
    centered = value - mean_val
    var_val = spread_in(jnp.sum(centered * centered * mask, axis=0, keepdims=True), same) * share
    inv_std = lax.rsqrt(var_val + eps_group)
    normed = centered * inv_std
    return (normed * gain + bias, normed, inv_std)


def silu_in(values):
    return values / (1.0 + jnp.exp(-values))


def finish_forward(total, limit, base, rows, act, act_out, normed_out, inv_out, value_out):
    mask = token_mask(limit)
    value = mask * (total + rows[0:1])
    if base is not None:
        value = value + base
    norm, normed, inv_std = norm_in(value, mask, limit, rows[1:2], rows[2:3])
    result = mask * silu_in(norm) if act else norm
    low_result = result.astype(jnp.bfloat16)
    act_out[...] = low_result
    normed_out[...] = normed
    inv_out[0:1] = inv_std
    inv_out[1:2] = column_squares(low_result)
    if value_out is not None:
        value_out[...] = value


def forward_outs(with_value):
    shapes = [
        jax.ShapeDtypeStruct((TOKENS, HALF), jnp.bfloat16),
        jax.ShapeDtypeStruct((TOKENS, HALF), jnp.float32),
        jax.ShapeDtypeStruct((8, HALF), jnp.float32),
    ]
    if with_value:
        shapes.append(jax.ShapeDtypeStruct((TOKENS, HALF), jnp.float32))
    return shapes


def first_forward(info, inputs, weight, rows):
    def body(info_ref, input_ref, weight_ref, rows_ref, *outs):
        total = dot(input_ref[...], weight_ref[...])
        finish_forward(total, info_ref[2], None, rows_ref[...], True, *outs)

    outs = forward_outs(True)
    return pl.pallas_call(
        body,
        grid_spec=pltpu.PrefetchScalarGridSpec(
            num_scalar_prefetch=1,
            grid=(1,),
            in_specs=[whole(inputs.shape), whole(weight.shape), whole(rows.shape)],
            out_specs=[whole(one.shape) for one in outs],
        ),
        out_shape=outs,
        compiler_params=params(),
        cost_estimate=cost(2 * TOKENS * 27 * HALF, 3 * TOKENS * HALF * 4),
    )(info, inputs, weight, rows)


def conv_forward(info, mine, other, table, at, base, rows, act):
    with_base = base is not None

    def body(info_ref, mine_ref, other_ref, weight_ref, rows_ref, *rest):
        base_ref = rest[0] if with_base else None
        outs, (moved, total) = (rest[int(with_base) : -2], rest[-2:])
        step = pl.program_id(0)

        @pl.when(step == 0)
        def _():
            both = two_sides(info_ref[0], mine_ref[...], other_ref[...])
            fill_moved(moved, both.astype(jnp.float32))
            total[...] = jnp.zeros_like(total)

        part = None
        for j in range(3):
            row_off, col_off = tap_of(3 * step + j, info_ref[1])
            one = dot(moved[col_off + 1, rows_from(row_off), :], weight_ref[C * j : C * (j + 1), :])
            part = one if part is None else part + one
        total[...] += part

        @pl.when(step == 2)
        def _():
            value_out = outs[3] if with_base else None
            held = base_ref[...] if with_base else None
            finish_forward(
                total[...], info_ref[2], held, rows_ref[...], act, *outs[:3], value_out
            )

    outs = forward_outs(with_base)
    extra = [base] if with_base else []
    return pl.pallas_call(
        body,
        grid_spec=pltpu.PrefetchScalarGridSpec(
            num_scalar_prefetch=1,
            grid=(3,),
            in_specs=[
                whole(mine.shape),
                whole(other.shape),
                pl.BlockSpec(
                    (pl.Element(3 * C), pl.Element(HALF)),
                    lambda i, info_ref: (
                        pl.multiple_of(at + 3 * C * i, 8),
                        pl.multiple_of(HALF * info_ref[0], HALF),
                    ),
                ),
                whole(rows.shape),
            ]
            + [whole(one.shape) for one in extra],
            out_specs=[whole(one.shape) for one in outs],
            scratch_shapes=[
                pltpu.VMEM((3, PADDED, C), jnp.bfloat16),
                pltpu.VMEM((TOKENS, HALF), jnp.float32),
            ],
        ),
        out_shape=outs,
        compiler_params=params(),
        cost_estimate=cost(18 * TOKENS * C * HALF, 9 * C * HALF * 2 + 6 * TOKENS * HALF * 4),
    )(info, mine, other, table, rows, *extra)


def conv_backward(info, grad_mine, grad_other, act_mine, act_other, table, store, at, saved, rows, base):
    with_base = base is not None
    old, old_specs, out_spec, out_shape = store_specs(store, at, 3 * C)

    def body(info_ref, *refs):
        refs = refs[len(old) :]
        gm_ref, go_ref, am_ref, ao_ref = refs[:4]
        weight_refs, (normed_ref, inv_ref, rows_ref) = (refs[4:7], refs[7:10])
        base_ref = refs[10] if with_base else None
        refs = refs[10 + int(with_base) :]
        out_ref, low_out, sums_out = refs[:3]
        moved, turned_act, shifted, total = refs[-4:]
        step = pl.program_id(0)

        @pl.when(step == 0)
        def _():
            both = two_sides(info_ref[0], gm_ref[...], go_ref[...])
            fill_moved(moved, both.astype(jnp.float32))
            act = two_sides(info_ref[0], am_ref[...], ao_ref[...]).astype(jnp.float32)
            for slab in range(3):
                turned_act[slab] = columns_moved(act, slab - 1).T.astype(jnp.bfloat16)
            empty = jnp.zeros((FRAME, HALF), jnp.bfloat16)
            shifted[0:FRAME, :] = empty
            shifted[FRAME : FRAME + TOKENS, :] = gm_ref[...]
            shifted[FRAME + TOKENS : PADDED, :] = empty
            total[...] = jnp.zeros_like(total)

        part = None
        for j in range(3):
            row_off, col_off = tap_of(3 * step + j, info_ref[1])
            rows_at = rows_from(-row_off)
            out_ref[C * j : C * (j + 1), :] = dot(turned_act[col_off + 1], shifted[rows_at, :])
            one = dot_t(moved[1 - col_off, rows_at, :], weight_refs[j][...])
            part = one if part is None else part + one
        total[...] += part

        @pl.when(step == 2)
        def _():
            mask = token_mask(info_ref[2])
            gain, normed, inv_std = (rows_ref[0:1], normed_ref[...], inv_ref[0:1])
            norm = normed * gain + rows_ref[1:2]
            logistic = 1.0 / (1.0 + jnp.exp(-norm))
            gradient = mask * total[...] * (logistic * (1.0 + norm * (1.0 - logistic)))
            result, gain_grad, bias_grad = norm_back(
                gradient, normed, inv_std, mask, info_ref[2], gain
            )
            if with_base:
                result = mask * (result + base_ref[...])
            low_result = result.astype(jnp.bfloat16)
            low_out[...] = low_result
            sums_out[3:4] = column_squares(low_result)
            sums_out[0:1] = jnp.sum(result, axis=0, keepdims=True)
            sums_out[1:2] = gain_grad
            sums_out[2:3] = bias_grad

    def tap_rows(j):
        return pl.BlockSpec(
            (pl.Element(HALF), pl.Element(C)),
            lambda i, info_ref: (pl.multiple_of(at + C * (3 * i + j) + HALF * info_ref[0], 8), 0),
        )

    extra = [base] if with_base else []
    operands = [grad_mine, grad_other, act_mine, act_other]
    result = pl.pallas_call(
        body,
        grid_spec=pltpu.PrefetchScalarGridSpec(
            num_scalar_prefetch=1,
            grid=(3,),
            in_specs=old_specs
            + [whole(one.shape) for one in operands]
            + [
                tap_rows(j) for j in range(3)
            ]
            + [
                whole((TOKENS, HALF)),
                whole((8, HALF)),
                whole(rows.shape),
            ]
            + [whole(one.shape) for one in extra],
            out_specs=[
                out_spec,
                whole((TOKENS, HALF)),
                whole((8, HALF)),
            ],
            scratch_shapes=[
                pltpu.VMEM((3, PADDED, C), jnp.bfloat16),
                pltpu.VMEM((3, C, TOKENS), jnp.bfloat16),
                pltpu.VMEM((PADDED, HALF), jnp.bfloat16),
                pltpu.VMEM((TOKENS, HALF), jnp.float32),
            ],
        ),
        out_shape=[
            out_shape,
            jax.ShapeDtypeStruct((TOKENS, HALF), jnp.bfloat16),
            jax.ShapeDtypeStruct((8, HALF), jnp.float32),
        ],
        input_output_aliases={1 + k: k for k in range(len(old))},
        compiler_params=params(),
        cost_estimate=cost(36 * TOKENS * C * HALF, 9 * C * HALF * 6 + 6 * TOKENS * HALF * 4),
    )(info, *old, *operands, table, table, table, *saved, rows, *extra)
    store.write(result[0], None)
    return (result[1], result[2])


def column_squares(values):
    wide = values.astype(jnp.float32)
    return jnp.sum(wide * wide, axis=0, keepdims=True)


def norm_back(gradient, normed, inv_std, mask, limit, gain):
    same = group_same()
    share = 1.0 / (limit.astype(jnp.float32) * (C // GROUPS))
    scaled = gradient * gain
    first = spread_in(jnp.sum(scaled * mask, axis=0, keepdims=True), same) * share
    second = spread_in(jnp.sum(scaled * normed * mask, axis=0, keepdims=True), same) * share
    result = mask * inv_std * (scaled - first - normed * second)
    return (
        result,
        jnp.sum(gradient * normed, axis=0, keepdims=True),
        jnp.sum(gradient, axis=0, keepdims=True),
    )


def unmix(info, table, at, depth, pieces, columns):
    tile = min(depth, 128 if pieces > 4 else 256)

    def body(info_ref, rows_ref, out_ref, mixed):
        for side in range(columns // 128):
            mixed[...] = rows_ref[:, side * 128 : (side + 1) * 128].astype(jnp.float32)
            for j in range(pieces):
                column = j * columns + side * 128
                out_ref[:, column : column + 128] = low(mixed[pl.ds(j, tile, stride=pieces), :])

    return pl.pallas_call(
        body,
        grid_spec=pltpu.PrefetchScalarGridSpec(
            num_scalar_prefetch=1,
            grid=(depth // tile,),
            in_specs=[
                pl.BlockSpec(
                    (pl.Element(tile * pieces), pl.Element(columns)),
                    lambda i, info_ref: (
                        pl.multiple_of(at + tile * pieces * i, 8),
                        pl.multiple_of(HALF * info_ref[0] * int(columns == HALF), HALF),
                    ),
                )
            ],
            out_specs=pl.BlockSpec((tile, pieces * columns), lambda i, info_ref: (i, 0)),
            scratch_shapes=[pltpu.VMEM((tile * pieces, 128), jnp.float32)],
        ),
        out_shape=jax.ShapeDtypeStruct((depth, pieces * columns), jnp.bfloat16),
        compiler_params=params(),
        cost_estimate=cost(0, 4 * depth * pieces * columns),
    )(info, table)


class Rows:
    def __init__(self, at, count, side_columns=False, side_rows=False):
        self.at, self.count = (at, count)
        self.side_columns, self.side_rows = (side_columns, side_rows)

    def spec(self):
        at, columns, rows = (self.at, int(self.side_columns), int(self.side_rows))
        return pl.BlockSpec(
            (pl.Element(self.count), pl.Element(HALF if columns else WIDE)),
            lambda i, info_ref: (
                pl.multiple_of(at + HALF * info_ref[0] * rows, 8),
                pl.multiple_of(HALF * info_ref[0] * columns, HALF),
            ),
        )


def one_step(body, info, table, operands, outs, flops):
    arrays = [table if isinstance(one, Rows) else one for one in operands]
    specs = [one.spec() if isinstance(one, Rows) else whole(one.shape) for one in operands]
    shapes = [jax.ShapeDtypeStruct(shape, kind) for shape, kind in outs]
    nbytes = sum(math.prod(one.shape) * one.dtype.itemsize for one in shapes)
    return pl.pallas_call(
        body,
        grid_spec=pltpu.PrefetchScalarGridSpec(
            num_scalar_prefetch=1,
            grid=(1,),
            in_specs=specs,
            out_specs=[whole(one.shape) for one in shapes],
        ),
        out_shape=shapes,
        compiler_params=params(),
        cost_estimate=cost(flops, 2 * nbytes),
    )(info, *arrays)


f32, bf16 = (jnp.float32, jnp.bfloat16)


def side_of(side, values):
    return jnp.where(side == 0, values[:, :HALF], values[:, HALF:])


def layer_parts(values):
    centered = values - jnp.mean(values, axis=-1, keepdims=True)
    var_val = jnp.mean(centered * centered, axis=-1, keepdims=True)
    inv_std = lax.rsqrt(var_val + eps_layer)
    return (centered * inv_std, inv_std)


def layer_back(gradient, values, gain, base, side, sums_ref):
    normed, inv_std = layer_parts(values)
    scaled = gradient * gain
    first = jnp.mean(scaled, axis=-1, keepdims=True)
    second = jnp.mean(scaled * normed, axis=-1, keepdims=True)
    result = base + inv_std * (scaled - first - normed * second)
    sums_ref[0:1] = side_of(side, jnp.sum(result, axis=0, keepdims=True))
    sums_ref[1:2] = side_of(side, jnp.sum(gradient * normed, axis=0, keepdims=True))
    sums_ref[2:3] = side_of(side, jnp.sum(gradient, axis=0, keepdims=True))
    return result


def head_lanes(head):
    return lax.broadcasted_iota(jnp.int32, (1, HALF), 1) // DHEAD == head


def head_probs(query, key, head, limit):
    mine = jnp.where(head_lanes(head), query, jnp.zeros((), bf16))
    scores = dot_t(mine, key) * 0.125
    seen = lax.broadcasted_iota(jnp.int32, (1, TOKENS), 1) < limit
    scores = jnp.where(seen, scores, -1e30)
    exponent = jnp.exp(scores - jnp.max(scores, axis=-1, keepdims=True))
    return exponent / jnp.sum(exponent, axis=-1, keepdims=True)


def self_front(info, table, mine, other, weight, rows, qkv):
    def body(info_ref, mine_ref, other_ref, weight_ref, rows_ref, qkv_ref, *outs):
        token_ref, resid_ref, ln_ref, packed_ref, out_ref = outs
        token = two_sides(info_ref[0], mine_ref[...], other_ref[...])
        token_ref[...] = token
        resid = dot(token, weight_ref[...]) + rows_ref[0:1]
        resid_ref[...] = resid
        ln = low(layer_parts(resid)[0] * rows_ref[1:2] + rows_ref[2:3])
        ln_ref[...] = ln
        packed_ref[...] = low(dot(ln, qkv_ref[...]))
        query, key = (packed_ref[:, 0:HALF], packed_ref[:, HALF : 2 * HALF])
        value = packed_ref[:, 2 * HALF : 3 * HALF]
        total = jnp.zeros((TOKENS, HALF), f32)
        for head in range(LOCAL_HEADS):
            probs = head_probs(query, key, head, info_ref[2])
            total = jnp.where(head_lanes(head), dot(low(probs), value), total)
        out_ref[...] = low(total)

    outs = [
        ((TOKENS, C), bf16),
        ((TOKENS, C), f32),
        ((TOKENS, C), bf16),
        ((TOKENS, 3 * HALF), bf16),
        ((TOKENS, HALF), bf16),
    ]
    flops = 2 * TOKENS * C * (C + 3 * HALF) + 4 * LOCAL_HEADS * TOKENS * TOKENS * HALF
    return one_step(body, info, table, [mine, other, weight, rows, qkv], outs, flops)


def same_head():
    left = lax.broadcasted_iota(jnp.int32, (HALF, HALF), 0) // DHEAD
    right = lax.broadcasted_iota(jnp.int32, (HALF, HALF), 1) // DHEAD
    return (left == right).astype(f32)


def head_sums(values, same):
    return jnp.dot(values, same, precision=lax.Precision.HIGHEST, preferred_element_type=f32)


def cross_probs(query, context, same):
    first = head_sums(query * context[0:1, :HALF], same) * 0.125
    second = head_sums(query * context[1:2, :HALF], same) * 0.125
    top = jnp.maximum(first, second)
    first, second = (jnp.exp(first - top), jnp.exp(second - top))
    total = first + second
    return (first / total, second / total)


def cross_front(info, table, mine, other, weight, rows, resid, query_weight, context):
    def body(info_ref, mine_ref, other_ref, weight_ref, rows_ref, old_ref, qw_ref, kv_ref, *outs):
        full_ref, resid_ref, ln_ref, query_ref, out_ref = outs
        joined = two_sides(info_ref[0], mine_ref[...], other_ref[...])
        full_ref[...] = joined
        resid_now = old_ref[...] + dot(joined, weight_ref[...]) + rows_ref[0:1]
        resid_ref[...] = resid_now
        ln = low(layer_parts(resid_now)[0] * rows_ref[1:2] + rows_ref[2:3])
        ln_ref[...] = ln
        query = low(dot(ln, qw_ref[...]))
        query_ref[...] = query
        both = kv_ref[...].astype(f32)
        first, second = cross_probs(query.astype(f32), both, same_head())
        out_ref[...] = low(first * both[0:1, HALF:] + second * both[1:2, HALF:])

    outs = [
        ((TOKENS, C), bf16),
        ((TOKENS, C), f32),
        ((TOKENS, C), bf16),
        ((TOKENS, HALF), bf16),
        ((TOKENS, HALF), bf16),
    ]
    operands = [mine, other, weight, rows, resid, query_weight, context]
    return one_step(body, info, table, operands, outs, 2 * TOKENS * C * (C + 13 * HALF))


def gelu_parts(gate):
    return 0.5 * (1.0 + lax.erf(gate * math.sqrt(0.5)))


WIDE_FF = FFI // 2


def ff_front(info, table, mine, other, weight, rows, resid, ff_weight, ff_bias):
    def body(info_ref, mine_ref, other_ref, weight_ref, rows_ref, old_ref, fw_ref, fb_ref, *outs):
        full_ref, resid_ref, ln_ref, proj_ref, out_ref = outs
        joined = two_sides(info_ref[0], mine_ref[...], other_ref[...])
        full_ref[...] = joined
        resid_now = old_ref[...] + dot(joined, weight_ref[...]) + rows_ref[0:1]
        resid_ref[...] = resid_now
        ln = low(layer_parts(resid_now)[0] * rows_ref[1:2] + rows_ref[2:3])
        ln_ref[...] = ln
        for at in range(0, WIDE_FF, HALF):
            gate_at = WIDE_FF + at
            lift = dot(ln, fw_ref[:, at : at + HALF]) + fb_ref[:, at : at + HALF]
            gate = dot(ln, fw_ref[:, gate_at : gate_at + HALF]) + fb_ref[:, gate_at : gate_at + HALF]
            proj_ref[:, at : at + HALF] = lift
            proj_ref[:, gate_at : gate_at + HALF] = gate
            out_ref[:, at : at + HALF] = low(lift * gate * gelu_parts(gate))

    outs = [
        ((TOKENS, C), bf16),
        ((TOKENS, C), f32),
        ((TOKENS, C), bf16),
        ((TOKENS, FFI), f32),
        ((TOKENS, WIDE_FF), bf16),
    ]
    operands = [mine, other, weight, rows, resid, ff_weight, ff_bias]
    return one_step(body, info, table, operands, outs, 2 * TOKENS * C * (C + FFI))


def ff_finish(info, table, mine, other, weight, rows, resid, out_weight, out_bias, state):
    def body(info_ref, mine_ref, other_ref, weight_ref, rows_ref, old_ref, ow_ref, ob_ref, state_ref, *outs):
        full_ref, resid_ref, out_ref = outs
        side = info_ref[0]
        for at in range(0, WIDE_FF, HALF):
            own, peer = (mine_ref[:, at : at + HALF], other_ref[:, at : at + HALF])
            full_ref[:, 2 * at : 2 * at + WIDE] = two_sides(side, own, peer)
        resid_now = old_ref[...] + dot(full_ref[...], weight_ref[...]) + rows_ref[0:1]
        inner = low(resid_now)
        resid_ref[...] = inner
        branch = dot(inner, ow_ref[...]) + ob_ref[0:1]
        out_ref[...] = low(state_ref[...] + token_mask(info_ref[2]) * branch)

    outs = [((TOKENS, FFI), bf16), ((TOKENS, C), bf16), ((TOKENS, HALF), bf16)]
    operands = [mine, other, weight, rows, resid, out_weight, out_bias, state]
    return one_step(body, info, table, operands, outs, 2 * TOKENS * C * (FFI + HALF))


def lanes_moved(values, row_off, col_off):
    token = lax.broadcasted_iota(jnp.int32, (1, TOKENS), 1)
    row, col = (token // FRAME + row_off, token % FRAME + col_off)
    keep = (row >= 0) & (row < SIDE) & (col >= 0) & (col < FRAME)
    away = FRAME * row_off + col_off
    return jnp.where(keep, pltpu.roll(values, lax.rem(TOKENS - away, TOKENS), 1), 0.0)


OUT_ROWS = 8


def loss_back(info, table, mine, other, out_weight, noise, bias, pout, ff2, projected, ff1):
    def body(info_ref, *refs):
        mine_ref, other_ref, ow_ref, noise_ref, bias_ref, pout_ref, ff2_ref, proj_ref, ff1_ref = refs[:9]
        ow_grad, small_out, state_out, pout_low, ff2_low, resid_out, proj_low, ln_out, sums, ff_sums = refs[9:]
        side, turned, limit = (info_ref[0], info_ref[1], info_ref[2])
        state = two_sides(side, mine_ref[...], other_ref[...])
        raw = dot_t(ow_ref[...], state)
        predicted = bias_ref[:, 0:1]
        for tap in range(9):
            row_off, col_off = tap_of(tap, turned)
            part = raw[tap * OUT_ROWS : (tap + 1) * OUT_ROWS]
            predicted = predicted + lanes_moved(part, row_off, col_off)
        token = lax.broadcasted_iota(jnp.int32, (OUT_ROWS, TOKENS), 1)
        channel = lax.broadcasted_iota(jnp.int32, (OUT_ROWS, TOKENS), 0)
        error = jnp.where((token < limit) & (channel < LC), predicted - noise_ref[...], 0.0)
        loss = jnp.sum(jnp.sum(error * error, axis=1, keepdims=True), axis=0, keepdims=True)
        gradient = 2.0 * error
        small_out[:, 0:128] = jnp.broadcast_to(jnp.sum(gradient, axis=1, keepdims=True), (OUT_ROWS, 128))
        small_out[:, 128:256] = jnp.broadcast_to(loss, (OUT_ROWS, 128))
        gradient = low(gradient).astype(f32)
        moved = []
        for tap in range(9):
            row_off, col_off = tap_of(tap, turned)
            moved.append(lanes_moved(gradient, -row_off, -col_off))
        moved = low(jnp.concatenate(moved, axis=0))
        ow_grad[...] = dot(moved, state)
        state_grad = t_dot(moved, ow_ref[...])
        state_out[...] = side_of(side, state_grad)
        branch = token_mask(limit) * state_grad
        sums[1:2] = side_of(side, jnp.sum(branch, axis=0, keepdims=True))
        branch = low(branch)
        pout_low[...] = side_of(side, branch)
        resid_grad = dot_t(branch, pout_ref[...])
        resid_out[...] = resid_grad
        sums[0:1] = side_of(side, jnp.sum(resid_grad, axis=0, keepdims=True))
        resid_low = low(resid_grad)
        ff2_low[...] = side_of(side, resid_low)
        total = jnp.zeros((TOKENS, C), f32)
        for j in range(WIDE_FF // HALF):
            at, gate_at = (j * HALF, WIDE_FF + j * HALF)
            own = pl.ds(pl.multiple_of(WIDE * j + HALF * side, HALF), HALF)
            gated_grad = dot_t(resid_low, ff2_ref[own, :])
            lift, gate = (proj_ref[:, at : at + HALF], proj_ref[:, gate_at : gate_at + HALF])
            cdf = gelu_parts(gate)
            density = jnp.exp(-0.5 * gate * gate) * (1.0 / math.sqrt(2.0 * math.pi))
            lift_grad = gated_grad * gate * cdf
            gate_grad = gated_grad * lift * (cdf + gate * density)
            ff_sums[j : j + 1] = jnp.sum(lift_grad, axis=0, keepdims=True)
            ff_sums[4 + j : 5 + j] = jnp.sum(gate_grad, axis=0, keepdims=True)
            lift_grad, gate_grad = (low(lift_grad), low(gate_grad))
            proj_low[:, at : at + HALF] = lift_grad
            proj_low[:, gate_at : gate_at + HALF] = gate_grad
            total = total + dot_t(lift_grad, ff1_ref[:, at : at + HALF])
            total = total + dot_t(gate_grad, ff1_ref[:, gate_at : gate_at + HALF])
        ln_out[...] = total

    outs = [
        ((9 * OUT_ROWS, C), f32),
        ((OUT_ROWS, HALF), f32),
        ((TOKENS, HALF), f32),
        ((TOKENS, HALF), bf16),
        ((TOKENS, HALF), bf16),
        ((TOKENS, C), f32),
        ((TOKENS, FFI), bf16),
        ((TOKENS, C), f32),
        ((8, HALF), f32),
        ((8, HALF), f32),
    ]
    operands = [mine, other, out_weight, noise, bias, pout, ff2, projected, ff1]
    return one_step(body, info, table, operands, outs, 2 * TOKENS * C * (C + FFI + WIDE_FF))


def cross_back(info, table, mine, other, resid, gain, base, weight, query, context, ckv):
    def body(info_ref, mine_ref, other_ref, resid_ref, gain_ref, base_ref, weight_ref, query_ref, kv_ref, ckv_ref, *outs):
        resid_out, co_low, query_low, kv_grad, sums, context_out = outs
        side = info_ref[0]
        result = layer_back(
            mine_ref[...] + other_ref[...], resid_ref[...], gain_ref[0:1], base_ref[...], side, sums
        )
        resid_out[...] = result
        result = low(result)
        co_low[...] = side_of(side, result)
        out_grad = low(dot_t(result, weight_ref[...])).astype(f32)
        same, both, query_now = (same_head(), kv_ref[...].astype(f32), query_ref[...].astype(f32))
        first, second = cross_probs(query_now, both, same)
        first_grad = head_sums(out_grad * both[0:1, HALF:], same)
        second_grad = head_sums(out_grad * both[1:2, HALF:], same)
        inner = first * first_grad + second * second_grad
        first_grad = first * (first_grad - inner) * 0.125
        second_grad = second * (second_grad - inner) * 0.125
        query_low[...] = low(first_grad * both[0:1, :HALF] + second_grad * both[1:2, :HALF])
        for row, (prob, score) in enumerate(((first, first_grad), (second, second_grad))):
            kv_grad[row : row + 1, :HALF] = jnp.sum(score * query_now, axis=0, keepdims=True)
            kv_grad[row : row + 1, HALF:] = jnp.sum(prob * out_grad, axis=0, keepdims=True)
        kv_grad[2:8, :] = jnp.zeros((6, WIDE), f32)
        halves = [low(kv_grad[:, HALF * j : HALF * (j + 1)]) for j in range(2)]
        context_out[...] = unstuffed([dot_t(one, ckv_ref[...]) for one in halves])

    outs = [
        ((TOKENS, C), f32),
        ((TOKENS, HALF), bf16),
        ((TOKENS, HALF), bf16),
        ((8, WIDE), f32),
        ((8, HALF), f32),
        ((8, WIDE), f32),
    ]
    operands = [mine, other, resid, gain, base, weight, query, context, ckv]
    return one_step(body, info, table, operands, outs, 2 * TOKENS * C * 14 * HALF)


def self_back(info, table, mine, other, query_weight, resid, gain, base, weight, packed, qkv):
    def body(info_ref, mine_ref, other_ref, qw_ref, resid_ref, gain_ref, base_ref, weight_ref, packed_ref, qkv_ref, *outs):
        resid_out, o_low, packed_low, ln_out, sums = outs
        side, limit = (info_ref[0], info_ref[2])
        joined = two_sides(side, mine_ref[...], other_ref[...])
        result = layer_back(
            dot_t(joined, qw_ref[...]), resid_ref[...], gain_ref[0:1], base_ref[...], side, sums
        )
        resid_out[...] = result
        result = low(result)
        o_low[...] = side_of(side, result)
        out_grad = low(dot_t(result, weight_ref[...]))
        query, key = (packed_ref[:, 0:HALF], packed_ref[:, HALF : 2 * HALF])
        value = packed_ref[:, 2 * HALF : 3 * HALF]
        parts = [jnp.zeros((TOKENS, HALF), f32) for _ in range(3)]
        for head in range(LOCAL_HEADS):
            lanes = head_lanes(head)
            probs = head_probs(query, key, head, limit)
            mine_grad = jnp.where(lanes, out_grad, jnp.zeros((), bf16))
            prob_grad = dot_t(mine_grad, value)
            inner = jnp.sum(probs * prob_grad, axis=-1, keepdims=True)
            score_grad = low(probs * (prob_grad - inner) * 0.125)
            parts[0] = jnp.where(lanes, dot(score_grad, key), parts[0])
            parts[1] = jnp.where(lanes, t_dot(score_grad, query), parts[1])
            parts[2] = jnp.where(lanes, t_dot(low(probs), out_grad), parts[2])
        joined = low(jnp.concatenate(parts, axis=1))
        packed_low[...] = joined
        ln_out[...] = dot_t(joined, qkv_ref[...])

    outs = [
        ((TOKENS, C), f32),
        ((TOKENS, HALF), bf16),
        ((TOKENS, 3 * HALF), bf16),
        ((TOKENS, C), f32),
        ((8, HALF), f32),
    ]
    operands = [mine, other, query_weight, resid, gain, base, weight, packed, qkv]
    flops = 2 * TOKENS * C * 6 * HALF + 10 * LOCAL_HEADS * TOKENS * TOKENS * HALF
    return one_step(body, info, table, operands, outs, flops)


def token_back(info, table, mine, other, resid, gain, base, weight, normed, rows, gain_three, state):
    def body(info_ref, mine_ref, other_ref, resid_ref, gain_ref, base_ref, weight_ref, normed_ref, inv_ref, g3_ref, state_ref, *outs):
        pin_low, state_out, conv_low, sums, sums_three = outs
        side, limit = (info_ref[0], info_ref[2])
        result = layer_back(
            mine_ref[...] + other_ref[...], resid_ref[...], gain_ref[0:1], base_ref[...], side, sums
        )
        result = low(result)
        pin_low[...] = side_of(side, result)
        token_grad = dot_t(result, weight_ref[...])
        mask = token_mask(limit)
        norm_grad, gain_grad, bias_grad = norm_back(
            token_grad, normed_ref[...], inv_ref[0:1], mask, limit, g3_ref[0:1]
        )
        state_now = state_ref[...] + norm_grad
        state_out[...] = state_now
        conv_grad = mask * state_now
        low_grad = low(conv_grad)
        conv_low[...] = low_grad
        sums_three[0:1] = jnp.sum(conv_grad, axis=0, keepdims=True)
        sums_three[1:2] = gain_grad
        sums_three[2:3] = bias_grad
        sums_three[3:4] = column_squares(low_grad)

    outs = [
        ((TOKENS, HALF), bf16),
        ((TOKENS, HALF), f32),
        ((TOKENS, HALF), bf16),
        ((8, HALF), f32),
        ((8, HALF), f32),
    ]
    operands = [mine, other, resid, gain, base, weight, normed, rows, gain_three, state]
    return one_step(body, info, table, operands, outs, 2 * TOKENS * C * HALF)


class LabelRows(Rows):
    def spec(self):
        at = self.at
        return pl.BlockSpec(
            (pl.Element(8), pl.Element(WIDE)),
            lambda i, info_ref: (pl.multiple_of(at + info_ref[3] // 8 * 8, 8), 0),
        )


def stuffing(parity, kind):
    row = lax.broadcasted_iota(jnp.int32, (WIDE, 2 * WIDE), 0)
    column = lax.broadcasted_iota(jnp.int32, (WIDE, 2 * WIDE), 1)
    return (column == 2 * row + parity).astype(f32).astype(kind)


def unstuffed(parts):
    total = None
    for parity, part in enumerate(parts):
        thirds, left = ([], part)
        for _ in range(3):
            thirds.append(low(left).astype(f32))
            left = left - thirds[-1]
        one = dot_t(low(jnp.concatenate(thirds, axis=0)), stuffing(parity, bf16))
        one = one[0:8] + one[8:16] + one[16:24]
        total = one if total is None else total + one
    return total


def first_row(values):
    row = lax.broadcasted_iota(jnp.int32, values.shape, 0)
    return jnp.where(row == 0, values, 0.0)


def time_front(info, table, at, embed, biases):
    def body(info_ref, embed_ref, bias_ref, one_ref, two_ref, out_ref, class_ref, kv_ref, *outs):
        inner, both, context_kv = outs
        spread = [stuffing(parity, bf16) for parity in range(2)]
        inner[...] = jnp.zeros_like(inner)
        hidden = []
        for j in range(2):
            pre = dot(low(embed_ref[8 * j : 8 * j + 8, :]), one_ref[...]) + bias_ref[j : j + 1]
            act = low(silu_in(pre))
            inner[0:1, WIDE * j : WIDE * (j + 1)] = pre[0:1]
            inner[2:3, WIDE * j : WIDE * (j + 1)] = act.astype(f32)[0:1]
            hidden.append(act)
        last = []
        for j in range(2):
            pre = bias_ref[2 + j : 3 + j]
            for p in range(2):
                wide = low(dot(hidden[p], spread[j]))
                pre = pre + dot(wide, two_ref[2 * WIDE * p : 2 * WIDE * (p + 1), :])
            act = low(silu_in(pre))
            inner[1:2, WIDE * j : WIDE * (j + 1)] = pre[0:1]
            inner[3:4, WIDE * j : WIDE * (j + 1)] = act.astype(f32)[0:1]
            last.append(act)
        time_vec = bias_ref[4:5]
        for p in range(2):
            time_vec = time_vec + dot(last[p], out_ref[WIDE * p : WIDE * (p + 1), :])
        row = lax.broadcasted_iota(jnp.int32, (8, WIDE), 0)
        rows = class_ref[...].astype(f32)
        class_vec = jnp.sum(jnp.where(row == lax.rem(info_ref[3], 8), rows, 0.0), axis=0, keepdims=True)
        context = jnp.where(row == 0, class_vec, jnp.where(row == 1, time_vec[0:1], 0.0))
        both[...] = context
        context = low(context)
        for j in range(2):
            wide = low(dot(context, spread[j]))
            context_kv[:, HALF * j : HALF * (j + 1)] = low(dot(wide, kv_ref[...]))

    operands = [
        embed,
        biases,
        Rows(at["w_t1"], 2 * TE),
        Rows(at["w_t2"], 2 * TD),
        Rows(at["w_tp"], TD),
        LabelRows(at["table"], 8),
        Rows(at["w_ckv"], 2 * C, side_columns=True),
    ]
    outs = [((8, 2 * WIDE), f32), ((8, WIDE), f32), ((8, WIDE), bf16)]
    return one_step(body, info, table, operands, outs, 2 * 8 * 4096 * WIDE)


def time_back(info, table, at, time_grad, inner, top, context_grad, squares):
    def body(info_ref, grad_ref, inner_ref, two_ref, out_ref, top_ref, context_ref, *rest):
        square_refs, (outs, bound_out) = (rest[:-2], rest[-2:])
        time_low = low(grad_ref[...])
        largest = lambda value: jnp.max(jnp.max(jnp.abs(value), axis=1, keepdims=True), axis=0, keepdims=True)

        def slope(values):
            logistic = 1.0 / (1.0 + jnp.exp(-values))
            return logistic * (1.0 + values * (1.0 - logistic))

        outs[...] = jnp.zeros_like(outs)
        two = []
        for p in range(2):
            cols = slice(WIDE * p, WIDE * (p + 1))
            grad = dot_t(time_low, out_ref[WIDE * p : WIDE * (p + 1), :])
            grad = first_row(grad * slope(inner_ref[1:2, cols]))
            outs[0:1, cols] = grad[0:1]
            two.append(low(grad))
        for p in range(2):
            cols = slice(WIDE * p, WIDE * (p + 1))
            rows = two_ref[2 * WIDE * p : 2 * WIDE * (p + 1), :]
            grad = unstuffed([dot_t(two[j], rows) for j in range(2)])
            outs[1:2, cols] = grad[0:1] * slope(inner_ref[0:1, cols])
        bound = largest(inner_ref[3:4, :]) * largest(time_low.astype(f32))
        bound = jnp.maximum(bound, largest(inner_ref[2:3, :]) * largest(outs[0:1, :]))
        bound = jnp.maximum(bound, largest(outs[1:2, :]))
        bound = jnp.maximum(1.02 * bound, largest(context_ref[0:1, :]))
        bound = jnp.maximum(bound, top_ref[...])
        lane = lax.broadcasted_iota(jnp.int32, (8, 128), 1)
        row = jnp.broadcast_to(bound, (8, 128))
        for i, (ref, (_, at_row)) in enumerate(zip(square_refs, squares)):
            row = jnp.where(lane == i + 1, largest(ref[at_row : at_row + 1, :]), row)
        bound_out[...] = row

    operands = [time_grad, inner, Rows(at["w_t2"], 2 * TD), Rows(at["w_tp"], TD), top, context_grad]
    operands += [one for one, _ in squares]
    outs = [((8, 2 * WIDE), f32), ((8, 128), f32)]
    return one_step(body, info, table, operands, outs, 2 * 8 * 3072 * WIDE)


def channel_mix():
    flat = np.arange(LC * C)[:, None]
    split = np.arange(LC * C)[None]
    return jnp.asarray((flat == LC * (split % C) + split // C).astype(ml_dtypes.bfloat16))


def gather_small(place, value):
    stride, joined = (1, value[None])
    while stride < place.count:
        other = place.swap(joined, stride)
        upper = (place.index // stride) % 2 == 1
        joined = jnp.where(
            upper,
            jnp.concatenate([other, joined], axis=0),
            jnp.concatenate([joined, other], axis=0),
        )
        stride *= 2
    return joined


def windows(values, turned, sign):
    width = values.shape[1]
    col = (lax.iota(jnp.int32, TOKENS) % FRAME)[:, None]
    zero_one = jnp.zeros((1, width), values.dtype)
    zero_row = jnp.zeros((FRAME, width), values.dtype)
    none = jnp.zeros((), values.dtype)
    across = {
        -1: jnp.where(col > 0, jnp.concatenate([zero_one, values[:-1]], axis=0), none),
        0: values,
        1: jnp.where(col < FRAME - 1, jnp.concatenate([values[1:], zero_one], axis=0), none),
    }
    moved = {}
    for col_off, value in across.items():
        moved[-1, col_off] = jnp.concatenate([zero_row, value[:-FRAME]], axis=0)
        moved[0, col_off] = value
        moved[1, col_off] = jnp.concatenate([value[FRAME:], zero_row], axis=0)
    out = []
    for row_off, col_off in tap_offsets:
        plain = moved[sign * row_off, sign * col_off]
        other = moved[sign * col_off, sign * row_off]
        out.append(plain if row_off == col_off else jnp.where(turned, other, plain))
    return jnp.concatenate(out, axis=1)


def frame_of(place, latents, target_noise, turned):
    both = jnp.concatenate([latents, target_noise], axis=-1)
    stride, joined = (1, both[None])
    while stride < place.rows:
        other = place.swap(joined, stride)
        upper = (place.index // stride) % 2 == 1
        joined = jnp.where(
            upper,
            jnp.concatenate([other, joined], axis=0),
            jnp.concatenate([joined, other], axis=0),
        )
        stride *= 2
    image = pick(joined, place.slot, 1).reshape(SIDE, SIDE, 2 * LC)
    portrait = image[:, :FRAME]
    landscape = jnp.transpose(image[:FRAME], (1, 0, 2))
    return jnp.where(turned, landscape, portrait).reshape(TOKENS, 2 * LC)


def train_step(place, store, table, vecs, latents, target_noise, label, step_value, orient, extent):
    half, at = (place.half, store.places)
    turned = orient != 1
    info = jnp.stack([place.side, turned.astype(jnp.int32), extent * FRAME, label]).astype(jnp.int32)
    mask = (lax.iota(jnp.int32, TOKENS) < extent * FRAME).astype(jnp.float32)[:, None]
    frame = frame_of(place, latents, target_noise, turned)
    share = noise_level(step_value)
    noisy = mask * (jnp.sqrt(share) * frame[:, :LC] + jnp.sqrt(1.0 - share) * frame[:, LC:])
    pad_in = windows(low(noisy), turned, 1)
    noise_rows = jnp.pad(frame[:, LC:].T, ((0, OUT_ROWS - LC), (0, 0)))
    embed_in = low(time_embed(step_value))[None]
    mix = channel_mix()
    row = lambda *names: jnp.stack([vecs[name] for name in names])
    side_rows = lambda *names: half(row(*names))

    def part(name, depth=C, **kind):
        return Rows(at[name], depth, **kind)

    def own_rows(name):
        return Rows(at[name], HALF, side_rows=True)

    qkv = unmix(info, table, at["w_qkv"], C, 3, HALF)
    ff1 = unmix(info, table, at["w_ff1"], C, 2 * FFI // WIDE, HALF)
    w_in = half(table[at["w_in"] : at["w_in"] + 9 * LC])
    w_out = dot(table[at["w_out"] : at["w_out"] + 9 * LC].reshape(9, LC * C), mix)
    w_out = low(jnp.pad(w_out.reshape(9, LC, C), ((0, 0), (0, OUT_ROWS - LC), (0, 0))))
    w_out = w_out.reshape(9 * OUT_ROWS, C)

    twice = jnp.repeat(embed_in.astype(jnp.float32), 2, axis=1)
    parity = lax.iota(jnp.int32, 2 * TE)[None] % 2
    stuffed = [jnp.pad(jnp.where(parity == j, twice, 0.0), ((0, 7), (0, 0))) for j in range(2)]
    biases = [vecs["b_t1"].reshape(2, WIDE), vecs["b_t2"].reshape(2, WIDE), vecs["b_tp"][None]]
    biases = jnp.pad(jnp.concatenate(biases, axis=0), ((0, 3), (0, 0)))
    inner, both, context_kv = time_front(info, table, at, jnp.concatenate(stuffed, axis=0), biases)
    context, time_vec = (low(both[:2]), both[1:2])
    hidden_one, hidden_two = (low(inner[2:3]), low(inner[3:4]))

    act_one, normed_one, inv_one, state_zero = first_forward(
        info, pad_in, w_in, side_rows("b_in", "g1", "bb1")
    )
    act_one_peer = place.swap(act_one)
    rows_two = side_rows("b_c1", "g2", "bb2")
    rows_two = jnp.concatenate([rows_two[0:1] + half(time_vec), rows_two[1:]], axis=0)
    act_two, normed_two, inv_two = conv_forward(
        info, act_one, act_one_peer, table, at["w_c1"], None, rows_two, True
    )
    act_two_peer = place.swap(act_two)
    token_own, normed_three, inv_three, state_one = conv_forward(
        info, act_two, act_two_peer, table, at["w_c2"], state_zero, side_rows("b_c2", "g3", "bb3"), False
    )
    token_in, resid_zero, ln_one, packed, attended_own = self_front(
        info, table, token_own, place.swap(token_own), part("w_pin"), row("b_pin", "n1g", "n1b"), qkv
    )
    attended, resid_one, ln_two, cross_query, cross_own = cross_front(
        info,
        table,
        attended_own,
        place.swap(attended_own),
        part("w_o"),
        row("b_o", "n2g", "n2b"),
        resid_zero,
        part("w_cq", side_columns=True),
        context_kv,
    )
    b_ff1 = half(vecs["b_ff1"].reshape(-1, WIDE)).reshape(1, FFI)
    cross_out, resid_two, ln_three, projected, gated_own = ff_front(
        info,
        table,
        cross_own,
        place.swap(cross_own),
        part("w_co"),
        row("b_co", "n3g", "n3b"),
        resid_one,
        ff1,
        b_ff1,
    )
    gated, out_in, state_own = ff_finish(
        info,
        table,
        gated_own,
        place.swap(gated_own),
        part("w_ff2", FFI),
        row("b_ff2"),
        resid_two,
        part("w_pout", side_columns=True),
        side_rows("b_pout"),
        state_one,
    )
    b_out = jnp.broadcast_to(jnp.pad(vecs["b_out"], (0, OUT_ROWS - LC))[:, None], (OUT_ROWS, 128))
    (
        w_out_grad,
        small_out,
        state_grad,
        pout_low,
        ff2_low,
        resid_grad,
        proj_low,
        ln_part,
        sums_out,
        sums_ff,
    ) = loss_back(
        info,
        table,
        state_own,
        place.swap(state_own),
        w_out,
        noise_rows,
        b_out,
        part("w_pout"),
        part("w_ff2", FFI),
        projected,
        ff1,
    )
    ln_peer = place.swap(ln_part)
    store.add("w_pout", out_in, pout_low)
    store.add("w_ff2", gated, ff2_low)
    store.add("w_ff1", ln_three, proj_low)
    w_out_grad = w_out_grad.reshape(9, OUT_ROWS, C)[:, :LC].reshape(9, LC * C)
    thirds, left = ([], w_out_grad)
    for _ in range(3):
        thirds.append(lax.reduce_precision(left, 8, 7))
        left = left - thirds[-1]
    thirds = dot_t(low(jnp.concatenate(thirds, axis=0)), mix)
    w_out_grad = thirds[:9] + thirds[9:18] + thirds[18:]
    w_out_grad = half(w_out_grad.reshape(9 * LC, C))
    store.put(at["w_out"], jnp.zeros((store.total - at["w_out"], HALF), jnp.float32))
    resid_grad, co_low, query_low, kv_grad, sums_co, context_grad = cross_back(
        info,
        table,
        ln_part,
        ln_peer,
        resid_two,
        row("n3g"),
        resid_grad,
        own_rows("w_co"),
        cross_query,
        context_kv,
        Rows(at["w_ckv"], 2 * C, side_columns=True),
    )
    query_peer = place.swap(query_low)
    kv_low = low(kv_grad[:2])
    context_grad = context_grad + place.swap(context_grad)
    store.add("w_co", cross_out, co_low)
    store.add("w_cq", ln_two, query_low)
    store.add("w_ckv", context, kv_low)
    resid_grad, o_low, packed_low, ln_part, sums_o = self_back(
        info,
        table,
        query_low,
        query_peer,
        part("w_cq"),
        resid_one,
        row("n2g"),
        resid_grad,
        own_rows("w_o"),
        packed,
        qkv,
    )
    ln_peer = place.swap(ln_part)
    store.add("w_o", attended, o_low)
    store.add("w_qkv", ln_one, packed_low)
    pin_low, state_grad, conv_low, sums_pin, sums_two = token_back(
        info,
        table,
        ln_part,
        ln_peer,
        resid_zero,
        row("n1g"),
        resid_grad,
        own_rows("w_pin"),
        normed_three,
        inv_three,
        side_rows("g3"),
        state_grad,
    )
    conv_peer = place.swap(conv_low)
    store.add("w_pin", token_in, pin_low)
    conv_low, sums_one = conv_backward(
        info,
        conv_low,
        conv_peer,
        act_two,
        act_two_peer,
        table,
        store,
        at["w_c2"],
        (normed_two, inv_two),
        side_rows("g2", "bb2"),
        None,
    )
    conv_peer = place.swap(conv_low)
    time_grad = place.full(sums_one[0:1]) + context_grad[1:2]
    b_tp = half(time_grad)
    time_low = low(time_grad)
    outer, bounds = time_back(
        info,
        table,
        at,
        jnp.pad(time_grad, ((0, 7), (0, 0))),
        inner,
        store.top,
        context_grad,
        ((inv_one, 1), (inv_two, 1), (sums_two, 3), (sums_one, 3)),
    )
    b_t2, b_t1 = (half(outer[0].reshape(-1, WIDE)), half(outer[1].reshape(-1, WIDE)))
    two_low, one_low = (low(b_t2), low(b_t1))
    largest = Largest(place, bounds)
    store.add("w_tp", hidden_two, half(time_low))
    store.buffer = largest.exchange(store.buffer)
    store.add("w_t2", hidden_one, two_low.reshape(1, -1))
    store.buffer = largest.exchange(store.buffer)
    store.add("w_t1", embed_in, one_low.reshape(1, -1))
    chosen = lax.iota(jnp.int32, NCLS)[:, None] == label
    store.put(at["table"], jnp.where(chosen, half(context_grad[0:1]), 0.0))
    store.put(0, jnp.zeros((at["w_t1"], HALF), jnp.float32))
    store.buffer = largest.exchange(store.buffer)
    in_low, sums_in = conv_backward(
        info,
        conv_low,
        conv_peer,
        act_one,
        act_one_peer,
        table,
        store,
        at["w_c1"],
        (normed_one, inv_one),
        side_rows("g1", "bb1"),
        state_grad,
    )
    store.buffer = largest.exchange(store.buffer)
    tops = largest.finish()[0]
    bound = jnp.maximum(tops[0], 1.01 * jnp.sqrt(tops[1] * tops[4]))
    bound = jnp.maximum(bound, 1.01 * jnp.sqrt(tops[2] * tops[3]))
    scale = (WIRE_TOP / (place.count // 2)) / jnp.maximum(bound, 1e-30)
    w_in_grad = t_dot(pad_in, in_low)
    small = [b_t1, b_t2, b_tp, sums_in[:3], sums_one[:3], sums_two[:3], sums_pin[:3], sums_o[:3]]
    small += [sums_co[:3], sums_ff, sums_out[:2]]
    extra = [small_out[:LC, 0], small_out[0:1, 128], (extent * FRAME).astype(jnp.float32)[None]]
    extra = jnp.pad(jnp.concatenate(extra), (0, HALF - LC - 2))[None]
    return (jnp.concatenate(small + [extra, w_in_grad, w_out_grad], axis=0), scale)


def adam_update(params, first_mom, second, gradient, decay_rate):
    first_new = adam_one * first_mom + (1.0 - adam_one) * gradient
    second_new = adam_two * second + (1.0 - adam_two) * gradient * gradient
    step_size = (
        first_new
        / (1.0 - adam_one**STEP)
        / (jnp.sqrt(second_new / (1.0 - adam_two**STEP)) + adam_eps)
    )
    return (params - learn_rate * (step_size + decay_rate * params), first_new, second_new)


def local(
    latents,
    target_noise,
    labels,
    timesteps,
    orient,
    extent,
    mat_params,
    mat_first,
    mat_second,
    mat_ema,
    vec_params,
    vec_first,
    vec_second,
    vec_ema,
):
    place = Place()
    length = mat_params.shape[0]
    rows = shard_rows(length * place.count, place.count)
    block = to_blocks(place, mat_params.astype(jnp.bfloat16), rows)
    table = lax.all_gather(block, ("dp", "rows"), axis=0, tiled=True)
    vec_len = vec_params.shape[0]
    vec_wide = -(-vec_len // 128) * 128
    padded = jnp.pad(vec_params, (0, vec_wide - vec_len)).reshape(-1, 128)
    vec_all = gather_small(place, padded).reshape(place.count, vec_wide)[:, :vec_len]
    vec_all = vec_all.reshape(-1).astype(jnp.bfloat16).astype(jnp.float32)
    vecs = unpack(vec_all, vec_layout())
    own = lambda values: pick(values, place.slot, 0)
    store = Store(place, rows)
    small, scale = train_step(
        place,
        store,
        table,
        vecs,
        latents,
        target_noise,
        own(labels),
        own(timesteps),
        own(orient),
        own(extent),
    )
    block_grad, square = scatter_sum(place, store.buffer, scale, rows)
    small = jnp.pad(small, ((0, -small.shape[0] % 8), (0, 0)))
    body = sum(record[1] for record in vec_layout()[:-1]) // WIDE
    lane = lax.broadcasted_iota(jnp.int32, small.shape, 1)
    line = lax.broadcasted_iota(jnp.int32, small.shape, 0)
    small = jnp.where((lane == SQUARE_AT) & (line == body), square, small)
    small = place.full(place.chip_sum(small))
    loss_sum, pixel_count = (small[body, LC], small[body, LC + 1])
    vec_flat = jnp.concatenate([small[:body].reshape(-1), small[body, :LC]])
    vec_flat = jnp.pad(vec_flat, (0, vec_len * place.count - vec_flat.shape[0]))
    shard_vec = lax.dynamic_slice(vec_flat, (vec_len * place.index,), (vec_len,))
    square = small[body, SQUARE_AT] + small[body, HALF + SQUARE_AT] + jnp.sum(vec_flat * vec_flat)
    shard_mat = from_blocks(place, block_grad, length)
    for i, name in enumerate(("w_in", "w_out")):
        values = small[body + 1 + 9 * LC * i : body + 1 + 9 * LC * (i + 1)]
        square = square + jnp.sum(values * values)
        owner, offset = divmod((store.places[name] - LEAD) * WIDE, length)
        old = lax.dynamic_slice(shard_mat, (offset,), (9 * LC * C,))
        new = jnp.where(place.index == owner, values.reshape(-1), old)
        shard_mat = lax.dynamic_update_slice(shard_mat, new, (offset,))
    inverse = 1.0 / pixel_count
    grad_norm = jnp.sqrt(square) * inverse
    factor = clip_norm / jnp.maximum(grad_norm, clip_norm) * inverse
    new_mat, mat_first_new, mat_second_new = adam_update(
        mat_params, mat_first, mat_second, shard_mat * factor, weight_decay
    )
    new_vec, vec_first_new, vec_second_new = adam_update(
        vec_params, vec_first, vec_second, shard_vec * factor, 0.0
    )
    ema_rate = min(ema_ceiling, (1.0 + STEP) / (10.0 + STEP))
    mat_ema_new = ema_rate * mat_ema + (1.0 - ema_rate) * new_mat
    vec_ema_new = ema_rate * vec_ema + (1.0 - ema_rate) * new_vec
    return (
        new_mat,
        mat_first_new,
        mat_second_new,
        mat_ema_new,
        new_vec,
        vec_first_new,
        vec_second_new,
        vec_ema_new,
        grad_norm,
        loss_sum,
        pixel_count,
    )


def solution(mesh):
    return jax.shard_map(
        local,
        mesh=mesh,
        in_specs=(
            P("dp", "rows", None, None),
            P("dp", "rows", None, None),
            P("dp"),
            P("dp"),
            P("dp"),
            P("dp"),
            P(("dp", "rows")),
            P(("dp", "rows")),
            P(("dp", "rows")),
            P(("dp", "rows")),
            P(("dp", "rows")),
            P(("dp", "rows")),
            P(("dp", "rows")),
            P(("dp", "rows")),
        ),
        out_specs=(
            P(("dp", "rows")),
            P(("dp", "rows")),
            P(("dp", "rows")),
            P(("dp", "rows")),
            P(("dp", "rows")),
            P(("dp", "rows")),
            P(("dp", "rows")),
            P(("dp", "rows")),
            P(),
            P(),
            P(),
        ),
        check_vma=False,
    )
```

```python
import math

import jax
import jax.numpy as jnp
import ml_dtypes
import numpy as np
from jax import lax
from jax.experimental import pallas as pl
from jax.experimental.pallas import tpu as pltpu
from jax.sharding import PartitionSpec as P

C = 512
HEADS = 8
DHEAD = 64
FFI = 2048
TE = 256
TD = 1024
NCLS = 1000
LC = 3
GROUPS = 32
SIDE = 32
NT = 1000
STEP = 10


tap_offsets = [(-1, -1), (-1, 0), (-1, 1), (0, -1), (0, 0), (0, 1), (1, -1), (1, 0), (1, 1)]
eps_group = 1e-06
eps_layer = 1e-05
beta_first = 0.00085
beta_last = 0.012
adam_one = 0.9
adam_two = 0.999
adam_eps = 1e-08
learn_rate = 0.05
weight_decay = 0.01
ema_ceiling = 0.9999
clip_norm = 0.1


def mat_layout():
    return [
        ("w_in", 9 * LC, C),
        ("w_t1", TE, TD),
        ("w_t2", TD, TD),
        ("w_tp", TD, C),
        ("table", NCLS, C),
        ("w_c1", 9 * C, C),
        ("w_c2", 9 * C, C),
        ("w_pin", C, C),
        ("w_qkv", C, 3 * C),
        ("w_o", C, C),
        ("w_cq", C, C),
        ("w_ckv", C, 2 * C),
        ("w_co", C, C),
        ("w_ff1", C, 2 * FFI),
        ("w_ff2", FFI, C),
        ("w_pout", C, C),
        ("w_out", 9 * C, LC),
    ]


def vec_layout():
    names = [
        "b_tp",
        "b_in",
        "g1",
        "bb1",
        "b_c1",
        "g2",
        "bb2",
        "b_c2",
        "g3",
        "bb3",
        "b_pin",
        "n1g",
        "n1b",
        "b_o",
        "n2g",
        "n2b",
        "b_co",
        "n3g",
        "n3b",
    ]
    return (
        [("b_t1", TD), ("b_t2", TD)]
        + [(name_one, C) for name_one in names]
        + [("b_ff1", 2 * FFI), ("b_ff2", C), ("b_pout", C), ("b_out", LC)]
    )


def unpack(joined, layout):
    pieces = {}
    start_at = 0
    for record in layout:
        length = 1
        for extent_one in record[1:]:
            length = length * extent_one
        pieces[record[0]] = joined[start_at : start_at + length].reshape(record[1:])
        start_at = start_at + length
    return pieces


def noise_level(step_value):
    steps_idx = jnp.arange(NT).astype(jnp.float32)
    root_beta = math.sqrt(beta_first) + (
        math.sqrt(beta_last) - math.sqrt(beta_first)
    ) * steps_idx / (NT - 1)
    log_keep = jnp.log1p(-root_beta * root_beta)
    return jnp.exp(jnp.sum(jnp.where(jnp.arange(NT) <= step_value, log_keep, 0.0)))


def time_embed(step_value):
    frequency = jnp.exp(-math.log(10000.0) * jnp.arange(TE // 2).astype(jnp.float32) / (TE // 2))
    angles = step_value.astype(jnp.float32) * frequency
    return jnp.concatenate([jnp.cos(angles), jnp.sin(angles)])


WIDE = 512
HALF = 256
LEAD = 5
FRAME = 16
TOKENS = SIDE * FRAME
LOCAL_HEADS = HEADS // 2
WIRE_TOP = 32768.0


def silu_slope(values):
    logistic = jax.nn.sigmoid(values)
    return logistic * (1.0 + values * (1.0 - logistic))


def dot(left, right):
    return jnp.dot(left, right, preferred_element_type=jnp.float32)


def dot_t(left, right):
    return lax.dot_general(
        left, right, (((1,), (1,)), ((), ())), preferred_element_type=jnp.float32
    )


def t_dot(left, right):
    return lax.dot_general(
        left, right, (((0,), (0,)), ((), ())), preferred_element_type=jnp.float32
    )


def low(values):
    return values.astype(jnp.bfloat16)


class Place:
    def __init__(self):
        self.dp, self.rows = (lax.axis_size("dp"), lax.axis_size("rows"))
        self.count = self.dp * self.rows
        self.index = lax.axis_index("dp") * self.rows + lax.axis_index("rows")
        self.side = self.index % 2
        self.slot = (self.index // 2) % 2
        digits, left = ([], self.dp)
        while left > 4:
            digits.append(4)
            left //= 4
        digits.append(left)
        self.digits = digits + [2]
        strides, step = ([], 2)
        for size in reversed(self.digits):
            strides.insert(0, step)
            step *= size
        self.strides = strides
        self.coords = [(self.index // s) % n for s, n in zip(strides, self.digits)]

    def move(self, value, pairs):
        return lax.ppermute(value, ("dp", "rows"), pairs)

    def swap(self, value, stride=1):
        return self.move(value, [(k, k ^ stride) for k in range(self.count)])

    def shift(self, value, by):
        return self.move(
            value, [(k, k + by) for k in range(self.count) if 0 <= k + by < self.count]
        )

    def rotate(self, value, axis, by):
        stride, size = (self.strides[axis], self.digits[axis])
        pairs = []
        for k in range(self.count):
            at = (k // stride) % size
            pairs.append((k, k + ((at + by) % size - at) * stride))
        return self.move(value, pairs)

    def step(self, value, axis, direction, hops):
        stride, size = (self.strides[axis], self.digits[axis])
        pairs = []
        for k in range(self.count):
            at = (k // stride) % size
            rank = at if direction > 0 else size - 1 - at
            if rank <= hops and rank < size - 1:
                pairs.append((k, k + direction * stride))
        return self.move(value, pairs)

    def half(self, value, axis=-1):
        axis = axis % value.ndim
        return lax.dynamic_slice_in_dim(value, self.side * HALF, HALF, axis)

    def join(self, mine, other):
        first = jnp.where(self.side == 0, mine, other)
        second = jnp.where(self.side == 0, other, mine)
        return jnp.concatenate([first, second], axis=-1)

    def full(self, mine):
        return self.join(mine, self.swap(mine))

    def chip_sum(self, value):
        stride = 2
        while stride < self.count:
            if 2 * stride < self.count:
                near, far, both = [self.swap(value, stride * n) for n in (1, 2, 3)]
                value = (value + near) + (far + both)
            else:
                value = value + self.swap(value, stride)
            stride *= 4
        return value


def shard_rows(flat_len, count):
    length = flat_len // count
    rows = -(-(LEAD * WIDE + flat_len) // (WIDE * count))
    rows = -(-rows // 8) * 8
    while rows * WIDE - length < LEAD * WIDE:
        rows += 8
    return rows


def to_blocks(place, shard, rows):
    length, block = (shard.shape[0], rows * WIDE)
    drift = block - length
    reach = drift * (place.count - 1) - LEAD * WIDE + block
    parts, hop = ([jnp.zeros((LEAD * WIDE,), shard.dtype), shard], 1)
    while hop * length < reach:
        take = min(length, reach - hop * length)
        take = min(length, -(-take // 1024) * 1024)
        parts.append(place.shift(shard[:take], -hop))
        hop += 1
    joined = jnp.concatenate(parts)
    lack = drift * (place.count - 1) + block - joined.shape[0]
    if lack > 0:
        joined = jnp.pad(joined, (0, lack))
    return lax.dynamic_slice(joined, (drift * place.index,), (block,)).reshape(rows, WIDE)


def from_blocks(place, block, length):
    flat = block.reshape(-1)
    drift = flat.shape[0] - length
    reach = drift * (place.count - 1) - LEAD * WIDE
    parts, hop, lead = ([flat], 1, 0)
    while lead < reach:
        take = min(flat.shape[0], -(-(reach - lead) // 1024) * 1024)
        parts.insert(0, place.shift(flat[flat.shape[0] - take :], hop))
        lead += take
        hop += 1
    joined = jnp.concatenate(parts)
    start = lead + LEAD * WIDE - drift * place.index
    return lax.dynamic_slice(joined, (start,), (length,))


def pick(values, index, axis):
    return lax.dynamic_index_in_dim(values, index, axis, keepdims=False)


def wire(values):
    return values.astype(jnp.float16)


def plain(values):
    return values.astype(jnp.float32)


SQUARE_AT = 8


class Largest:
    def __init__(self, place, values):
        self.place, self.values, self.stride = (place, values, 1)

    def exchange(self, beside=None):
        if self.stride < self.place.count:
            several = self.stride > 1 and 2 * self.stride < self.place.count
            times = (1, 2, 3) if several else (1,)
            got = [self.place.swap(self.values, self.stride * n) for n in times]
            if beside is not None:
                *got, beside = lax.optimization_barrier((*got, beside))
            values = self.values
            for one in got:
                values = jnp.maximum(values, one)
            self.values = lax.optimization_barrier(values)
            self.stride *= 4 if several else 2
        return beside

    def finish(self):
        while self.stride < self.place.count:
            self.exchange()
        return self.values


def scatter_part(place, grads, low_row, rows, order, scale, after=(), ahead=None):
    held, left, first, factor = (grads, list(range(len(place.digits))), low_row, scale)

    def part_of(dim, index):
        starts, sizes, shape = ([], [], [])
        for at, axis in enumerate(left):
            starts.append(index if at == dim else 0)
            sizes.append(1 if at == dim else place.digits[axis])
            if at != dim:
                shape.append(place.digits[axis])
        out = lax.dynamic_slice(held, starts + [first, 0], sizes + [rows, HALF])
        return out.reshape(shape + [rows, HALF]) * factor

    for axis in order:
        dim = left.index(axis)
        me, size = (place.coords[axis], place.digits[axis])
        total = part_of(dim, me)
        if size == 2 or axis != order[0]:
            for away in range(1, size):
                sent = wire(part_of(dim, (me + away) % size))
                if ahead is not None and axis == order[0] and away == 1:
                    sent = ahead
                got = place.rotate(sent, axis, away)
                if axis == order[0] and after:
                    got = lax.optimization_barrier((got, *after))[0]
                total = total + plain(got)
                last = (sent,)
        else:
            flows, sent = ({1: None, -1: None}, {})
            for hops in range(size - 1):
                for direction in (1, -1):
                    rank = me if direction > 0 else size - 1 - me
                    aim = jnp.minimum(size - 1 - hops + rank, size - 1)
                    aim = aim if direction > 0 else size - 1 - aim
                    value = part_of(dim, aim)
                    if hops == 1 and axis == order[0] and after:
                        flows[direction] = lax.optimization_barrier((flows[direction], *after))[0]
                    if flows[direction] is not None:
                        value = value + plain(flows[direction])
                    sent[direction] = wire(value)
                    flows[direction] = place.step(sent[direction], axis, direction, hops)
            total = total + plain(flows[1]) + plain(flows[-1])
            last = (sent[1], sent[-1])
        if axis == order[0]:
            leaving = last
        held, first, factor = (total, 0, 1.0)
        left.remove(axis)
    return (held, leaving)


SHARES = (0.42, 0.33)


def scatter_sum(place, grads, scale, rows):
    held = grads.reshape(*place.digits, 2 * rows, HALF)
    axes = list(range(len(place.digits)))[::-1]
    total = 2 * rows
    cuts = [0] + [int(total * sum(SHARES[: i + 1]) / 8 + 0.5) * 8 for i in range(2)] + [total]
    orders = [axes[i:] + axes[:i] for i in range(3)]
    parts, after, ahead = ([None] * 3, (), [None] * 3)
    for i in range(2):
        axis = orders[i][0]
        if place.digits[axis] == 2:
            starts = [0] * len(axes) + [cuts[i], 0]
            starts[axis] = 1 - place.coords[axis]
            sizes = [1 if at == axis else size for at, size in enumerate(place.digits)]
            sent = lax.dynamic_slice(held, starts, sizes + [cuts[i + 1] - cuts[i], HALF])
            ahead[i] = wire(jnp.squeeze(sent, axis) * scale)
            after = (*after, ahead[i])
    for i in (2, 0, 1):
        span = (cuts[i], cuts[i + 1] - cuts[i])
        hold = () if i == 0 else after
        parts[i], leaving = scatter_part(place, held, *span, orders[i], scale, hold, ahead[i])
        after = leaving if i == 2 else after
    unit = 1.0 / scale
    parts = [part * unit for part in parts]
    square = sum(jnp.sum(part * part) for part in parts).reshape(1, 1)
    chip = jnp.concatenate(parts, axis=0).reshape(2, rows, HALF)
    mine = pick(chip, place.side, 0)
    other = place.swap(pick(chip, 1 - place.side, 0))
    return (place.join(mine, other), square)


class Store:
    def __init__(self, place, rows):
        self.total = place.count * rows
        self.buffer = None
        self.top = jnp.zeros((1, 1), jnp.float32)
        self.places, at = ({}, LEAD)
        for name, depth, width in mat_layout():
            self.places[name] = at
            at += depth * width // WIDE

    def write(self, out, top):
        self.buffer = out
        if top is not None:
            self.top = jnp.maximum(self.top, top)

    def add(self, name, inputs, gradient):
        if inputs.shape[0] < 16:
            spare = ((0, 16 - inputs.shape[0]), (0, 0))
            inputs, gradient = (jnp.pad(inputs, spare), jnp.pad(gradient, spare))
        grad_into(self, inputs, gradient, self.places[name])

    def put(self, at, values):
        self.buffer = lax.dynamic_update_slice(self.buffer, values, (at, 0))


def store_specs(store, at, tile):
    old = [] if store.buffer is None else [store.buffer]
    out = pl.BlockSpec(
        (pl.Element(tile), pl.Element(HALF)), lambda i, *_: (pl.multiple_of(at + tile * i, 8), 0)
    )
    shape = jax.ShapeDtypeStruct((store.total, HALF), jnp.float32)
    return (old, [pl.BlockSpec(memory_space=pl.ANY) for _ in old], out, shape)


def grad_into(store, inputs, gradient, at):
    tokens, depth = inputs.shape
    pieces = gradient.shape[1] // HALF
    tile = min(depth, 512 if pieces == 1 else 256 if pieces < 8 else 128)
    rows, tiles = (tile * pieces, depth // tile)
    old, old_specs, out_spec, out_shape = store_specs(store, at, rows)

    def body(*refs):
        refs = refs[len(old) :]
        input_ref, gradient_ref, out_ref, top_out = refs[:4]
        step = pl.program_id(0)
        part = t_dot(input_ref[...], gradient_ref[...])
        if pieces == 1:
            out_ref[...] = part
        else:
            mixed = refs[-1]
            for side in range(HALF // 128):
                for j in range(pieces):
                    column = j * HALF + side * 128
                    mixed[pl.ds(j, tile, stride=pieces), :] = part[:, column : column + 128]
                out_ref[:, side * 128 : (side + 1) * 128] = mixed[...]
        largest = jnp.max(jnp.abs(part))

        @pl.when(step == 0)
        def _():
            top_out[0, 0] = largest

        @pl.when(step > 0)
        def _():
            top_out[0, 0] = jnp.maximum(top_out[0, 0], largest)

    out, top = pl.pallas_call(
        body,
        grid=(tiles,),
        in_specs=old_specs
        + [
            pl.BlockSpec((tokens, tile), lambda i: (0, i)),
            pl.BlockSpec(gradient.shape, lambda i: (0, 0)),
        ],
        out_specs=[out_spec, pl.BlockSpec(memory_space=pltpu.SMEM)],
        out_shape=[out_shape, jax.ShapeDtypeStruct((1, 1), jnp.float32)],
        scratch_shapes=[] if pieces == 1 else [pltpu.VMEM((rows, 128), jnp.float32)],
        input_output_aliases={k: k for k in range(len(old))},
        compiler_params=params(),
        cost_estimate=cost(
            2 * tokens * depth * gradient.shape[1],
            depth * gradient.shape[1] * 4 + tokens * depth * 2,
        ),
    )(*old, inputs, gradient)
    store.write(out, top)


VMEM_LIMIT = 50 * 1024 * 1024
PADDED = TOKENS + 2 * FRAME


def params():
    return pltpu.CompilerParams(vmem_limit_bytes=VMEM_LIMIT)


def whole(shape):
    return pl.BlockSpec(shape, lambda *_: (0,) * len(shape))


def cost(flops, nbytes):
    return pl.CostEstimate(flops=flops, bytes_accessed=nbytes, transcendentals=0)


def token_mask(limit):
    return (lax.broadcasted_iota(jnp.int32, (TOKENS, 1), 0) < limit).astype(jnp.float32)


def columns_moved(values, col_off):
    if col_off == 0:
        return values
    col = lax.broadcasted_iota(jnp.int32, (TOKENS, 1), 0) % FRAME
    keep = col > 0 if col_off < 0 else col < FRAME - 1
    return jnp.where(keep, pltpu.roll(values, (-col_off) % TOKENS, 0), 0.0)


def two_sides(side, mine, other):
    first = jnp.where(side == 0, mine, other)
    second = jnp.where(side == 0, other, mine)
    return jnp.concatenate([first, second], axis=1)


def fill_moved(moved, values):
    width = moved.shape[2]
    empty = jnp.zeros((FRAME, width), moved.dtype)
    for slab in range(3):
        moved[slab, 0:FRAME, :] = empty
        moved[slab, FRAME : FRAME + TOKENS, :] = columns_moved(values, slab - 1).astype(moved.dtype)
        moved[slab, FRAME + TOKENS : PADDED, :] = empty


def tap_of(step, turned):
    row_off, col_off = (step // 3 - 1, step % 3 - 1)
    return (
        jnp.where(turned == 1, col_off, row_off),
        jnp.where(turned == 1, row_off, col_off),
    )


def rows_from(row_off):
    return pl.ds(pl.multiple_of(FRAME * (1 + row_off), FRAME), TOKENS)


def group_same():
    left = lax.broadcasted_iota(jnp.int32, (HALF, HALF), 0) // (C // GROUPS)
    right = lax.broadcasted_iota(jnp.int32, (HALF, HALF), 1) // (C // GROUPS)
    return (left == right).astype(jnp.float32)


def spread_in(sums, same):
    wide = jnp.broadcast_to(sums, (8, HALF))
    return jnp.dot(
        wide, same, precision=lax.Precision.HIGHEST, preferred_element_type=jnp.float32
    )[0:1]


def norm_in(value, mask, limit, gain, bias):
    same = group_same()
    share = 1.0 / (limit.astype(jnp.float32) * (C // GROUPS))
    mean_val = spread_in(jnp.sum(value * mask, axis=0, keepdims=True), same) * share
    centered = value - mean_val
    var_val = spread_in(jnp.sum(centered * centered * mask, axis=0, keepdims=True), same) * share
    inv_std = lax.rsqrt(var_val + eps_group)
    normed = centered * inv_std
    return (normed * gain + bias, normed, inv_std)


def silu_in(values):
    return values / (1.0 + jnp.exp(-values))


def finish_forward(total, limit, base, rows, act, act_out, normed_out, inv_out, value_out):
    mask = token_mask(limit)
    value = mask * (total + rows[0:1])
    if base is not None:
        value = value + base
    norm, normed, inv_std = norm_in(value, mask, limit, rows[1:2], rows[2:3])
    result = mask * silu_in(norm) if act else norm
    low_result = result.astype(jnp.bfloat16)
    act_out[...] = low_result
    normed_out[...] = normed
    inv_out[0:1] = inv_std
    inv_out[1:2] = column_squares(low_result)
    if value_out is not None:
        value_out[...] = value


def forward_outs(with_value):
    shapes = [
        jax.ShapeDtypeStruct((TOKENS, HALF), jnp.bfloat16),
        jax.ShapeDtypeStruct((TOKENS, HALF), jnp.float32),
        jax.ShapeDtypeStruct((8, HALF), jnp.float32),
    ]
    if with_value:
        shapes.append(jax.ShapeDtypeStruct((TOKENS, HALF), jnp.float32))
    return shapes


def first_forward(info, inputs, weight, rows):
    def body(info_ref, input_ref, weight_ref, rows_ref, *outs):
        total = dot(input_ref[...], weight_ref[...])
        finish_forward(total, info_ref[2], None, rows_ref[...], True, *outs)

    outs = forward_outs(True)
    return pl.pallas_call(
        body,
        grid_spec=pltpu.PrefetchScalarGridSpec(
            num_scalar_prefetch=1,
            grid=(1,),
            in_specs=[whole(inputs.shape), whole(weight.shape), whole(rows.shape)],
            out_specs=[whole(one.shape) for one in outs],
        ),
        out_shape=outs,
        compiler_params=params(),
        cost_estimate=cost(2 * TOKENS * 27 * HALF, 3 * TOKENS * HALF * 4),
    )(info, inputs, weight, rows)


def conv_forward(info, mine, other, table, at, base, rows, act):
    with_base = base is not None

    def body(info_ref, mine_ref, other_ref, weight_ref, rows_ref, *rest):
        base_ref = rest[0] if with_base else None
        outs, (moved, total) = (rest[int(with_base) : -2], rest[-2:])
        step = pl.program_id(0)

        @pl.when(step == 0)
        def _():
            both = two_sides(info_ref[0], mine_ref[...], other_ref[...])
            fill_moved(moved, both.astype(jnp.float32))
            total[...] = jnp.zeros_like(total)

        part = None
        for j in range(3):
            row_off, col_off = tap_of(3 * step + j, info_ref[1])
            one = dot(moved[col_off + 1, rows_from(row_off), :], weight_ref[C * j : C * (j + 1), :])
            part = one if part is None else part + one
        total[...] += part

        @pl.when(step == 2)
        def _():
            value_out = outs[3] if with_base else None
            held = base_ref[...] if with_base else None
            finish_forward(
                total[...], info_ref[2], held, rows_ref[...], act, *outs[:3], value_out
            )

    outs = forward_outs(with_base)
    extra = [base] if with_base else []
    return pl.pallas_call(
        body,
        grid_spec=pltpu.PrefetchScalarGridSpec(
            num_scalar_prefetch=1,
            grid=(3,),
            in_specs=[
                whole(mine.shape),
                whole(other.shape),
                pl.BlockSpec(
                    (pl.Element(3 * C), pl.Element(HALF)),
                    lambda i, info_ref: (
                        pl.multiple_of(at + 3 * C * i, 8),
                        pl.multiple_of(HALF * info_ref[0], HALF),
                    ),
                ),
                whole(rows.shape),
            ]
            + [whole(one.shape) for one in extra],
            out_specs=[whole(one.shape) for one in outs],
            scratch_shapes=[
                pltpu.VMEM((3, PADDED, C), jnp.bfloat16),
                pltpu.VMEM((TOKENS, HALF), jnp.float32),
            ],
        ),
        out_shape=outs,
        compiler_params=params(),
        cost_estimate=cost(18 * TOKENS * C * HALF, 9 * C * HALF * 2 + 6 * TOKENS * HALF * 4),
    )(info, mine, other, table, rows, *extra)


def conv_backward(info, grad_mine, grad_other, act_mine, act_other, table, store, at, saved, rows, base):
    with_base = base is not None
    old, old_specs, out_spec, out_shape = store_specs(store, at, 3 * C)

    def body(info_ref, *refs):
        refs = refs[len(old) :]
        gm_ref, go_ref, am_ref, ao_ref = refs[:4]
        weight_refs, (normed_ref, inv_ref, rows_ref) = (refs[4:7], refs[7:10])
        base_ref = refs[10] if with_base else None
        refs = refs[10 + int(with_base) :]
        out_ref, low_out, sums_out = refs[:3]
        moved, turned_act, shifted, total = refs[-4:]
        step = pl.program_id(0)

        @pl.when(step == 0)
        def _():
            both = two_sides(info_ref[0], gm_ref[...], go_ref[...])
            fill_moved(moved, both.astype(jnp.float32))
            act = two_sides(info_ref[0], am_ref[...], ao_ref[...]).astype(jnp.float32)
            for slab in range(3):
                turned_act[slab] = columns_moved(act, slab - 1).T.astype(jnp.bfloat16)
            empty = jnp.zeros((FRAME, HALF), jnp.bfloat16)
            shifted[0:FRAME, :] = empty
            shifted[FRAME : FRAME + TOKENS, :] = gm_ref[...]
            shifted[FRAME + TOKENS : PADDED, :] = empty
            total[...] = jnp.zeros_like(total)

        part = None
        for j in range(3):
            row_off, col_off = tap_of(3 * step + j, info_ref[1])
            rows_at = rows_from(-row_off)
            out_ref[C * j : C * (j + 1), :] = dot(turned_act[col_off + 1], shifted[rows_at, :])
            one = dot_t(moved[1 - col_off, rows_at, :], weight_refs[j][...])
            part = one if part is None else part + one
        total[...] += part

        @pl.when(step == 2)
        def _():
            mask = token_mask(info_ref[2])
            gain, normed, inv_std = (rows_ref[0:1], normed_ref[...], inv_ref[0:1])
            norm = normed * gain + rows_ref[1:2]
            logistic = 1.0 / (1.0 + jnp.exp(-norm))
            gradient = mask * total[...] * (logistic * (1.0 + norm * (1.0 - logistic)))
            result, gain_grad, bias_grad = norm_back(
                gradient, normed, inv_std, mask, info_ref[2], gain
            )
            if with_base:
                result = mask * (result + base_ref[...])
            low_result = result.astype(jnp.bfloat16)
            low_out[...] = low_result
            sums_out[3:4] = column_squares(low_result)
            sums_out[0:1] = jnp.sum(result, axis=0, keepdims=True)
            sums_out[1:2] = gain_grad
            sums_out[2:3] = bias_grad

    def tap_rows(j):
        return pl.BlockSpec(
            (pl.Element(HALF), pl.Element(C)),
            lambda i, info_ref: (pl.multiple_of(at + C * (3 * i + j) + HALF * info_ref[0], 8), 0),
        )

    extra = [base] if with_base else []
    operands = [grad_mine, grad_other, act_mine, act_other]
    result = pl.pallas_call(
        body,
        grid_spec=pltpu.PrefetchScalarGridSpec(
            num_scalar_prefetch=1,
            grid=(3,),
            in_specs=old_specs
            + [whole(one.shape) for one in operands]
            + [
                tap_rows(j) for j in range(3)
            ]
            + [
                whole((TOKENS, HALF)),
                whole((8, HALF)),
                whole(rows.shape),
            ]
            + [whole(one.shape) for one in extra],
            out_specs=[
                out_spec,
                whole((TOKENS, HALF)),
                whole((8, HALF)),
            ],
            scratch_shapes=[
                pltpu.VMEM((3, PADDED, C), jnp.bfloat16),
                pltpu.VMEM((3, C, TOKENS), jnp.bfloat16),
                pltpu.VMEM((PADDED, HALF), jnp.bfloat16),
                pltpu.VMEM((TOKENS, HALF), jnp.float32),
            ],
        ),
        out_shape=[
            out_shape,
            jax.ShapeDtypeStruct((TOKENS, HALF), jnp.bfloat16),
            jax.ShapeDtypeStruct((8, HALF), jnp.float32),
        ],
        input_output_aliases={1 + k: k for k in range(len(old))},
        compiler_params=params(),
        cost_estimate=cost(36 * TOKENS * C * HALF, 9 * C * HALF * 6 + 6 * TOKENS * HALF * 4),
    )(info, *old, *operands, table, table, table, *saved, rows, *extra)
    store.write(result[0], None)
    return (result[1], result[2])


def column_squares(values):
    wide = values.astype(jnp.float32)
    return jnp.sum(wide * wide, axis=0, keepdims=True)


def norm_back(gradient, normed, inv_std, mask, limit, gain):
    same = group_same()
    share = 1.0 / (limit.astype(jnp.float32) * (C // GROUPS))
    scaled = gradient * gain
    first = spread_in(jnp.sum(scaled * mask, axis=0, keepdims=True), same) * share
    second = spread_in(jnp.sum(scaled * normed * mask, axis=0, keepdims=True), same) * share
    result = mask * inv_std * (scaled - first - normed * second)
    return (
        result,
        jnp.sum(gradient * normed, axis=0, keepdims=True),
        jnp.sum(gradient, axis=0, keepdims=True),
    )


def unmix(info, table, at, depth, pieces, columns):
    tile = min(depth, 128 if pieces > 4 else 256)

    def body(info_ref, rows_ref, out_ref, mixed):
        for side in range(columns // 128):
            mixed[...] = rows_ref[:, side * 128 : (side + 1) * 128].astype(jnp.float32)
            for j in range(pieces):
                column = j * columns + side * 128
                out_ref[:, column : column + 128] = low(mixed[pl.ds(j, tile, stride=pieces), :])

    return pl.pallas_call(
        body,
        grid_spec=pltpu.PrefetchScalarGridSpec(
            num_scalar_prefetch=1,
            grid=(depth // tile,),
            in_specs=[
                pl.BlockSpec(
                    (pl.Element(tile * pieces), pl.Element(columns)),
                    lambda i, info_ref: (
                        pl.multiple_of(at + tile * pieces * i, 8),
                        pl.multiple_of(HALF * info_ref[0] * int(columns == HALF), HALF),
                    ),
                )
            ],
            out_specs=pl.BlockSpec((tile, pieces * columns), lambda i, info_ref: (i, 0)),
            scratch_shapes=[pltpu.VMEM((tile * pieces, 128), jnp.float32)],
        ),
        out_shape=jax.ShapeDtypeStruct((depth, pieces * columns), jnp.bfloat16),
        compiler_params=params(),
        cost_estimate=cost(0, 4 * depth * pieces * columns),
    )(info, table)


class Rows:
    def __init__(self, at, count, side_columns=False, side_rows=False):
        self.at, self.count = (at, count)
        self.side_columns, self.side_rows = (side_columns, side_rows)

    def spec(self):
        at, columns, rows = (self.at, int(self.side_columns), int(self.side_rows))
        return pl.BlockSpec(
            (pl.Element(self.count), pl.Element(HALF if columns else WIDE)),
            lambda i, info_ref: (
                pl.multiple_of(at + HALF * info_ref[0] * rows, 8),
                pl.multiple_of(HALF * info_ref[0] * columns, HALF),
            ),
        )


def one_step(body, info, table, operands, outs, flops):
    arrays = [table if isinstance(one, Rows) else one for one in operands]
    specs = [one.spec() if isinstance(one, Rows) else whole(one.shape) for one in operands]
    shapes = [jax.ShapeDtypeStruct(shape, kind) for shape, kind in outs]
    nbytes = sum(math.prod(one.shape) * one.dtype.itemsize for one in shapes)
    return pl.pallas_call(
        body,
        grid_spec=pltpu.PrefetchScalarGridSpec(
            num_scalar_prefetch=1,
            grid=(1,),
            in_specs=specs,
            out_specs=[whole(one.shape) for one in shapes],
        ),
        out_shape=shapes,
        compiler_params=params(),
        cost_estimate=cost(flops, 2 * nbytes),
    )(info, *arrays)


f32, bf16 = (jnp.float32, jnp.bfloat16)


def side_of(side, values):
    return jnp.where(side == 0, values[:, :HALF], values[:, HALF:])


def layer_parts(values):
    centered = values - jnp.mean(values, axis=-1, keepdims=True)
    var_val = jnp.mean(centered * centered, axis=-1, keepdims=True)
    inv_std = lax.rsqrt(var_val + eps_layer)
    return (centered * inv_std, inv_std)


def layer_back(gradient, values, gain, base, side, sums_ref):
    normed, inv_std = layer_parts(values)
    scaled = gradient * gain
    first = jnp.mean(scaled, axis=-1, keepdims=True)
    second = jnp.mean(scaled * normed, axis=-1, keepdims=True)
    result = base + inv_std * (scaled - first - normed * second)
    sums_ref[0:1] = side_of(side, jnp.sum(result, axis=0, keepdims=True))
    sums_ref[1:2] = side_of(side, jnp.sum(gradient * normed, axis=0, keepdims=True))
    sums_ref[2:3] = side_of(side, jnp.sum(gradient, axis=0, keepdims=True))
    return result


def head_lanes(head):
    return lax.broadcasted_iota(jnp.int32, (1, HALF), 1) // DHEAD == head


def head_probs(query, key, head, limit):
    mine = jnp.where(head_lanes(head), query, jnp.zeros((), bf16))
    scores = dot_t(mine, key) * 0.125
    seen = lax.broadcasted_iota(jnp.int32, (1, TOKENS), 1) < limit
    scores = jnp.where(seen, scores, -1e30)
    exponent = jnp.exp(scores - jnp.max(scores, axis=-1, keepdims=True))
    return exponent / jnp.sum(exponent, axis=-1, keepdims=True)


def self_front(info, table, mine, other, weight, rows, qkv):
    def body(info_ref, mine_ref, other_ref, weight_ref, rows_ref, qkv_ref, *outs):
        token_ref, resid_ref, ln_ref, packed_ref, out_ref = outs
        token = two_sides(info_ref[0], mine_ref[...], other_ref[...])
        token_ref[...] = token
        resid = dot(token, weight_ref[...]) + rows_ref[0:1]
        resid_ref[...] = resid
        ln = low(layer_parts(resid)[0] * rows_ref[1:2] + rows_ref[2:3])
        ln_ref[...] = ln
        packed_ref[...] = low(dot(ln, qkv_ref[...]))
        query, key = (packed_ref[:, 0:HALF], packed_ref[:, HALF : 2 * HALF])
        value = packed_ref[:, 2 * HALF : 3 * HALF]
        total = jnp.zeros((TOKENS, HALF), f32)
        for head in range(LOCAL_HEADS):
            probs = head_probs(query, key, head, info_ref[2])
            total = jnp.where(head_lanes(head), dot(low(probs), value), total)
        out_ref[...] = low(total)

    outs = [
        ((TOKENS, C), bf16),
        ((TOKENS, C), f32),
        ((TOKENS, C), bf16),
        ((TOKENS, 3 * HALF), bf16),
        ((TOKENS, HALF), bf16),
    ]
    flops = 2 * TOKENS * C * (C + 3 * HALF) + 4 * LOCAL_HEADS * TOKENS * TOKENS * HALF
    return one_step(body, info, table, [mine, other, weight, rows, qkv], outs, flops)


def same_head():
    left = lax.broadcasted_iota(jnp.int32, (HALF, HALF), 0) // DHEAD
    right = lax.broadcasted_iota(jnp.int32, (HALF, HALF), 1) // DHEAD
    return (left == right).astype(f32)


def head_sums(values, same):
    return jnp.dot(values, same, precision=lax.Precision.HIGHEST, preferred_element_type=f32)


def cross_probs(query, context, same):
    first = head_sums(query * context[0:1, :HALF], same) * 0.125
    second = head_sums(query * context[1:2, :HALF], same) * 0.125
    top = jnp.maximum(first, second)
    first, second = (jnp.exp(first - top), jnp.exp(second - top))
    total = first + second
    return (first / total, second / total)


def cross_front(info, table, mine, other, weight, rows, resid, query_weight, context):
    def body(info_ref, mine_ref, other_ref, weight_ref, rows_ref, old_ref, qw_ref, kv_ref, *outs):
        full_ref, resid_ref, ln_ref, query_ref, out_ref = outs
        joined = two_sides(info_ref[0], mine_ref[...], other_ref[...])
        full_ref[...] = joined
        resid_now = old_ref[...] + dot(joined, weight_ref[...]) + rows_ref[0:1]
        resid_ref[...] = resid_now
        ln = low(layer_parts(resid_now)[0] * rows_ref[1:2] + rows_ref[2:3])
        ln_ref[...] = ln
        query = low(dot(ln, qw_ref[...]))
        query_ref[...] = query
        both = kv_ref[...].astype(f32)
        first, second = cross_probs(query.astype(f32), both, same_head())
        out_ref[...] = low(first * both[0:1, HALF:] + second * both[1:2, HALF:])

    outs = [
        ((TOKENS, C), bf16),
        ((TOKENS, C), f32),
        ((TOKENS, C), bf16),
        ((TOKENS, HALF), bf16),
        ((TOKENS, HALF), bf16),
    ]
    operands = [mine, other, weight, rows, resid, query_weight, context]
    return one_step(body, info, table, operands, outs, 2 * TOKENS * C * (C + 13 * HALF))


def gelu_parts(gate):
    return 0.5 * (1.0 + lax.erf(gate * math.sqrt(0.5)))


WIDE_FF = FFI // 2


def ff_front(info, table, mine, other, weight, rows, resid, ff_weight, ff_bias):
    def body(info_ref, mine_ref, other_ref, weight_ref, rows_ref, old_ref, fw_ref, fb_ref, *outs):
        full_ref, resid_ref, ln_ref, proj_ref, out_ref = outs
        joined = two_sides(info_ref[0], mine_ref[...], other_ref[...])
        full_ref[...] = joined
        resid_now = old_ref[...] + dot(joined, weight_ref[...]) + rows_ref[0:1]
        resid_ref[...] = resid_now
        ln = low(layer_parts(resid_now)[0] * rows_ref[1:2] + rows_ref[2:3])
        ln_ref[...] = ln
        for at in range(0, WIDE_FF, HALF):
            gate_at = WIDE_FF + at
            lift = dot(ln, fw_ref[:, at : at + HALF]) + fb_ref[:, at : at + HALF]
            gate = dot(ln, fw_ref[:, gate_at : gate_at + HALF]) + fb_ref[:, gate_at : gate_at + HALF]
            proj_ref[:, at : at + HALF] = lift
            proj_ref[:, gate_at : gate_at + HALF] = gate
            out_ref[:, at : at + HALF] = low(lift * gate * gelu_parts(gate))

    outs = [
        ((TOKENS, C), bf16),
        ((TOKENS, C), f32),
        ((TOKENS, C), bf16),
        ((TOKENS, FFI), f32),
        ((TOKENS, WIDE_FF), bf16),
    ]
    operands = [mine, other, weight, rows, resid, ff_weight, ff_bias]
    return one_step(body, info, table, operands, outs, 2 * TOKENS * C * (C + FFI))


def ff_finish(info, table, mine, other, weight, rows, resid, out_weight, out_bias, state):
    def body(info_ref, mine_ref, other_ref, weight_ref, rows_ref, old_ref, ow_ref, ob_ref, state_ref, *outs):
        full_ref, resid_ref, out_ref = outs
        side = info_ref[0]
        for at in range(0, WIDE_FF, HALF):
            own, peer = (mine_ref[:, at : at + HALF], other_ref[:, at : at + HALF])
            full_ref[:, 2 * at : 2 * at + WIDE] = two_sides(side, own, peer)
        resid_now = old_ref[...] + dot(full_ref[...], weight_ref[...]) + rows_ref[0:1]
        inner = low(resid_now)
        resid_ref[...] = inner
        branch = dot(inner, ow_ref[...]) + ob_ref[0:1]
        out_ref[...] = low(state_ref[...] + token_mask(info_ref[2]) * branch)

    outs = [((TOKENS, FFI), bf16), ((TOKENS, C), bf16), ((TOKENS, HALF), bf16)]
    operands = [mine, other, weight, rows, resid, out_weight, out_bias, state]
    return one_step(body, info, table, operands, outs, 2 * TOKENS * C * (FFI + HALF))


def lanes_moved(values, row_off, col_off):
    token = lax.broadcasted_iota(jnp.int32, (1, TOKENS), 1)
    row, col = (token // FRAME + row_off, token % FRAME + col_off)
    keep = (row >= 0) & (row < SIDE) & (col >= 0) & (col < FRAME)
    away = FRAME * row_off + col_off
    return jnp.where(keep, pltpu.roll(values, lax.rem(TOKENS - away, TOKENS), 1), 0.0)


OUT_ROWS = 8


def loss_back(info, table, mine, other, out_weight, noise, bias, pout, ff2, projected, ff1):
    def body(info_ref, *refs):
        mine_ref, other_ref, ow_ref, noise_ref, bias_ref, pout_ref, ff2_ref, proj_ref, ff1_ref = refs[:9]
        ow_grad, small_out, state_out, pout_low, ff2_low, resid_out, proj_low, ln_out, sums, ff_sums = refs[9:]
        side, turned, limit = (info_ref[0], info_ref[1], info_ref[2])
        state = two_sides(side, mine_ref[...], other_ref[...])
        raw = dot_t(ow_ref[...], state)
        predicted = bias_ref[:, 0:1]
        for tap in range(9):
            row_off, col_off = tap_of(tap, turned)
            part = raw[tap * OUT_ROWS : (tap + 1) * OUT_ROWS]
            predicted = predicted + lanes_moved(part, row_off, col_off)
        token = lax.broadcasted_iota(jnp.int32, (OUT_ROWS, TOKENS), 1)
        channel = lax.broadcasted_iota(jnp.int32, (OUT_ROWS, TOKENS), 0)
        error = jnp.where((token < limit) & (channel < LC), predicted - noise_ref[...], 0.0)
        loss = jnp.sum(jnp.sum(error * error, axis=1, keepdims=True), axis=0, keepdims=True)
        gradient = 2.0 * error
        small_out[:, 0:128] = jnp.broadcast_to(jnp.sum(gradient, axis=1, keepdims=True), (OUT_ROWS, 128))
        small_out[:, 128:256] = jnp.broadcast_to(loss, (OUT_ROWS, 128))
        gradient = low(gradient).astype(f32)
        moved = []
        for tap in range(9):
            row_off, col_off = tap_of(tap, turned)
            moved.append(lanes_moved(gradient, -row_off, -col_off))
        moved = low(jnp.concatenate(moved, axis=0))
        ow_grad[...] = dot(moved, state)
        state_grad = t_dot(moved, ow_ref[...])
        state_out[...] = side_of(side, state_grad)
        branch = token_mask(limit) * state_grad
        sums[1:2] = side_of(side, jnp.sum(branch, axis=0, keepdims=True))
        branch = low(branch)
        pout_low[...] = side_of(side, branch)
        resid_grad = dot_t(branch, pout_ref[...])
        resid_out[...] = resid_grad
        sums[0:1] = side_of(side, jnp.sum(resid_grad, axis=0, keepdims=True))
        resid_low = low(resid_grad)
        ff2_low[...] = side_of(side, resid_low)
        total = jnp.zeros((TOKENS, C), f32)
        for j in range(WIDE_FF // HALF):
            at, gate_at = (j * HALF, WIDE_FF + j * HALF)
            own = pl.ds(pl.multiple_of(WIDE * j + HALF * side, HALF), HALF)
            gated_grad = dot_t(resid_low, ff2_ref[own, :])
            lift, gate = (proj_ref[:, at : at + HALF], proj_ref[:, gate_at : gate_at + HALF])
            cdf = gelu_parts(gate)
            density = jnp.exp(-0.5 * gate * gate) * (1.0 / math.sqrt(2.0 * math.pi))
            lift_grad = gated_grad * gate * cdf
            gate_grad = gated_grad * lift * (cdf + gate * density)
            ff_sums[j : j + 1] = jnp.sum(lift_grad, axis=0, keepdims=True)
            ff_sums[4 + j : 5 + j] = jnp.sum(gate_grad, axis=0, keepdims=True)
            lift_grad, gate_grad = (low(lift_grad), low(gate_grad))
            proj_low[:, at : at + HALF] = lift_grad
            proj_low[:, gate_at : gate_at + HALF] = gate_grad
            total = total + dot_t(lift_grad, ff1_ref[:, at : at + HALF])
            total = total + dot_t(gate_grad, ff1_ref[:, gate_at : gate_at + HALF])
        ln_out[...] = total

    outs = [
        ((9 * OUT_ROWS, C), f32),
        ((OUT_ROWS, HALF), f32),
        ((TOKENS, HALF), f32),
        ((TOKENS, HALF), bf16),
        ((TOKENS, HALF), bf16),
        ((TOKENS, C), f32),
        ((TOKENS, FFI), bf16),
        ((TOKENS, C), f32),
        ((8, HALF), f32),
        ((8, HALF), f32),
    ]
    operands = [mine, other, out_weight, noise, bias, pout, ff2, projected, ff1]
    return one_step(body, info, table, operands, outs, 2 * TOKENS * C * (C + FFI + WIDE_FF))


def cross_back(info, table, mine, other, resid, gain, base, weight, query, context, ckv):
    def body(info_ref, mine_ref, other_ref, resid_ref, gain_ref, base_ref, weight_ref, query_ref, kv_ref, ckv_ref, *outs):
        resid_out, co_low, query_low, kv_grad, sums, context_out = outs
        side = info_ref[0]
        result = layer_back(
            mine_ref[...] + other_ref[...], resid_ref[...], gain_ref[0:1], base_ref[...], side, sums
        )
        resid_out[...] = result
        result = low(result)
        co_low[...] = side_of(side, result)
        out_grad = low(dot_t(result, weight_ref[...])).astype(f32)
        same, both, query_now = (same_head(), kv_ref[...].astype(f32), query_ref[...].astype(f32))
        first, second = cross_probs(query_now, both, same)
        first_grad = head_sums(out_grad * both[0:1, HALF:], same)
        second_grad = head_sums(out_grad * both[1:2, HALF:], same)
        inner = first * first_grad + second * second_grad
        first_grad = first * (first_grad - inner) * 0.125
        second_grad = second * (second_grad - inner) * 0.125
        query_low[...] = low(first_grad * both[0:1, :HALF] + second_grad * both[1:2, :HALF])
        for row, (prob, score) in enumerate(((first, first_grad), (second, second_grad))):
            kv_grad[row : row + 1, :HALF] = jnp.sum(score * query_now, axis=0, keepdims=True)
            kv_grad[row : row + 1, HALF:] = jnp.sum(prob * out_grad, axis=0, keepdims=True)
        kv_grad[2:8, :] = jnp.zeros((6, WIDE), f32)
        halves = [low(kv_grad[:, HALF * j : HALF * (j + 1)]) for j in range(2)]
        context_out[...] = unstuffed([dot_t(one, ckv_ref[...]) for one in halves])

    outs = [
        ((TOKENS, C), f32),
        ((TOKENS, HALF), bf16),
        ((TOKENS, HALF), bf16),
        ((8, WIDE), f32),
        ((8, HALF), f32),
        ((8, WIDE), f32),
    ]
    operands = [mine, other, resid, gain, base, weight, query, context, ckv]
    return one_step(body, info, table, operands, outs, 2 * TOKENS * C * 14 * HALF)


def self_back(info, table, mine, other, query_weight, resid, gain, base, weight, packed, qkv):
    def body(info_ref, mine_ref, other_ref, qw_ref, resid_ref, gain_ref, base_ref, weight_ref, packed_ref, qkv_ref, *outs):
        resid_out, o_low, packed_low, ln_out, sums = outs
        side, limit = (info_ref[0], info_ref[2])
        joined = two_sides(side, mine_ref[...], other_ref[...])
        result = layer_back(
            dot_t(joined, qw_ref[...]), resid_ref[...], gain_ref[0:1], base_ref[...], side, sums
        )
        resid_out[...] = result
        result = low(result)
        o_low[...] = side_of(side, result)
        out_grad = low(dot_t(result, weight_ref[...]))
        query, key = (packed_ref[:, 0:HALF], packed_ref[:, HALF : 2 * HALF])
        value = packed_ref[:, 2 * HALF : 3 * HALF]
        parts = [jnp.zeros((TOKENS, HALF), f32) for _ in range(3)]
        for head in range(LOCAL_HEADS):
            lanes = head_lanes(head)
            probs = head_probs(query, key, head, limit)
            mine_grad = jnp.where(lanes, out_grad, jnp.zeros((), bf16))
            prob_grad = dot_t(mine_grad, value)
            inner = jnp.sum(probs * prob_grad, axis=-1, keepdims=True)
            score_grad = low(probs * (prob_grad - inner) * 0.125)
            parts[0] = jnp.where(lanes, dot(score_grad, key), parts[0])
            parts[1] = jnp.where(lanes, t_dot(score_grad, query), parts[1])
            parts[2] = jnp.where(lanes, t_dot(low(probs), out_grad), parts[2])
        joined = low(jnp.concatenate(parts, axis=1))
        packed_low[...] = joined
        ln_out[...] = dot_t(joined, qkv_ref[...])

    outs = [
        ((TOKENS, C), f32),
        ((TOKENS, HALF), bf16),
        ((TOKENS, 3 * HALF), bf16),
        ((TOKENS, C), f32),
        ((8, HALF), f32),
    ]
    operands = [mine, other, query_weight, resid, gain, base, weight, packed, qkv]
    flops = 2 * TOKENS * C * 6 * HALF + 10 * LOCAL_HEADS * TOKENS * TOKENS * HALF
    return one_step(body, info, table, operands, outs, flops)


def token_back(info, table, mine, other, resid, gain, base, weight, normed, rows, gain_three, state):
    def body(info_ref, mine_ref, other_ref, resid_ref, gain_ref, base_ref, weight_ref, normed_ref, inv_ref, g3_ref, state_ref, *outs):
        pin_low, state_out, conv_low, sums, sums_three = outs
        side, limit = (info_ref[0], info_ref[2])
        result = layer_back(
            mine_ref[...] + other_ref[...], resid_ref[...], gain_ref[0:1], base_ref[...], side, sums
        )
        result = low(result)
        pin_low[...] = side_of(side, result)
        token_grad = dot_t(result, weight_ref[...])
        mask = token_mask(limit)
        norm_grad, gain_grad, bias_grad = norm_back(
            token_grad, normed_ref[...], inv_ref[0:1], mask, limit, g3_ref[0:1]
        )
        state_now = state_ref[...] + norm_grad
        state_out[...] = state_now
        conv_grad = mask * state_now
        low_grad = low(conv_grad)
        conv_low[...] = low_grad
        sums_three[0:1] = jnp.sum(conv_grad, axis=0, keepdims=True)
        sums_three[1:2] = gain_grad
        sums_three[2:3] = bias_grad
        sums_three[3:4] = column_squares(low_grad)

    outs = [
        ((TOKENS, HALF), bf16),
        ((TOKENS, HALF), f32),
        ((TOKENS, HALF), bf16),
        ((8, HALF), f32),
        ((8, HALF), f32),
    ]
    operands = [mine, other, resid, gain, base, weight, normed, rows, gain_three, state]
    return one_step(body, info, table, operands, outs, 2 * TOKENS * C * HALF)


class LabelRows(Rows):
    def spec(self):
        at = self.at
        return pl.BlockSpec(
            (pl.Element(8), pl.Element(WIDE)),
            lambda i, info_ref: (pl.multiple_of(at + info_ref[3] // 8 * 8, 8), 0),
        )


def stuffing(parity, kind):
    row = lax.broadcasted_iota(jnp.int32, (WIDE, 2 * WIDE), 0)
    column = lax.broadcasted_iota(jnp.int32, (WIDE, 2 * WIDE), 1)
    return (column == 2 * row + parity).astype(f32).astype(kind)


def unstuffed(parts):
    total = None
    for parity, part in enumerate(parts):
        thirds, left = ([], part)
        for _ in range(3):
            thirds.append(low(left).astype(f32))
            left = left - thirds[-1]
        one = dot_t(low(jnp.concatenate(thirds, axis=0)), stuffing(parity, bf16))
        one = one[0:8] + one[8:16] + one[16:24]
        total = one if total is None else total + one
    return total


def first_row(values):
    row = lax.broadcasted_iota(jnp.int32, values.shape, 0)
    return jnp.where(row == 0, values, 0.0)


def time_front(info, table, at, embed, biases):
    def body(info_ref, embed_ref, bias_ref, one_ref, two_ref, out_ref, class_ref, kv_ref, *outs):
        inner, both, context_kv = outs
        spread = [stuffing(parity, bf16) for parity in range(2)]
        inner[...] = jnp.zeros_like(inner)
        hidden = []
        for j in range(2):
            pre = dot(low(embed_ref[8 * j : 8 * j + 8, :]), one_ref[...]) + bias_ref[j : j + 1]
            act = low(silu_in(pre))
            inner[0:1, WIDE * j : WIDE * (j + 1)] = pre[0:1]
            inner[2:3, WIDE * j : WIDE * (j + 1)] = act.astype(f32)[0:1]
            hidden.append(act)
        last = []
        for j in range(2):
            pre = bias_ref[2 + j : 3 + j]
            for p in range(2):
                wide = low(dot(hidden[p], spread[j]))
                pre = pre + dot(wide, two_ref[2 * WIDE * p : 2 * WIDE * (p + 1), :])
            act = low(silu_in(pre))
            inner[1:2, WIDE * j : WIDE * (j + 1)] = pre[0:1]
            inner[3:4, WIDE * j : WIDE * (j + 1)] = act.astype(f32)[0:1]
            last.append(act)
        time_vec = bias_ref[4:5]
        for p in range(2):
            time_vec = time_vec + dot(last[p], out_ref[WIDE * p : WIDE * (p + 1), :])
        row = lax.broadcasted_iota(jnp.int32, (8, WIDE), 0)
        rows = class_ref[...].astype(f32)
        class_vec = jnp.sum(jnp.where(row == lax.rem(info_ref[3], 8), rows, 0.0), axis=0, keepdims=True)
        context = jnp.where(row == 0, class_vec, jnp.where(row == 1, time_vec[0:1], 0.0))
        both[...] = context
        context = low(context)
        for j in range(2):
            wide = low(dot(context, spread[j]))
            context_kv[:, HALF * j : HALF * (j + 1)] = low(dot(wide, kv_ref[...]))

    operands = [
        embed,
        biases,
        Rows(at["w_t1"], 2 * TE),
        Rows(at["w_t2"], 2 * TD),
        Rows(at["w_tp"], TD),
        LabelRows(at["table"], 8),
        Rows(at["w_ckv"], 2 * C, side_columns=True),
    ]
    outs = [((8, 2 * WIDE), f32), ((8, WIDE), f32), ((8, WIDE), bf16)]
    return one_step(body, info, table, operands, outs, 2 * 8 * 4096 * WIDE)


def time_back(info, table, at, time_grad, inner, top, context_grad, squares):
    def body(info_ref, grad_ref, inner_ref, two_ref, out_ref, top_ref, context_ref, *rest):
        square_refs, (outs, bound_out) = (rest[:-2], rest[-2:])
        time_low = low(grad_ref[...])
        largest = lambda value: jnp.max(jnp.max(jnp.abs(value), axis=1, keepdims=True), axis=0, keepdims=True)

        def slope(values):
            logistic = 1.0 / (1.0 + jnp.exp(-values))
            return logistic * (1.0 + values * (1.0 - logistic))

        outs[...] = jnp.zeros_like(outs)
        two = []
        for p in range(2):
            cols = slice(WIDE * p, WIDE * (p + 1))
            grad = dot_t(time_low, out_ref[WIDE * p : WIDE * (p + 1), :])
            grad = first_row(grad * slope(inner_ref[1:2, cols]))
            outs[0:1, cols] = grad[0:1]
            two.append(low(grad))
        for p in range(2):
            cols = slice(WIDE * p, WIDE * (p + 1))
            rows = two_ref[2 * WIDE * p : 2 * WIDE * (p + 1), :]
            grad = unstuffed([dot_t(two[j], rows) for j in range(2)])
            outs[1:2, cols] = grad[0:1] * slope(inner_ref[0:1, cols])
        bound = largest(inner_ref[3:4, :]) * largest(time_low.astype(f32))
        bound = jnp.maximum(bound, largest(inner_ref[2:3, :]) * largest(outs[0:1, :]))
        bound = jnp.maximum(bound, largest(outs[1:2, :]))
        bound = jnp.maximum(1.02 * bound, largest(context_ref[0:1, :]))
        bound = jnp.maximum(bound, top_ref[...])
        lane = lax.broadcasted_iota(jnp.int32, (8, 128), 1)
        row = jnp.broadcast_to(bound, (8, 128))
        for i, (ref, (_, at_row)) in enumerate(zip(square_refs, squares)):
            row = jnp.where(lane == i + 1, largest(ref[at_row : at_row + 1, :]), row)
        bound_out[...] = row

    operands = [time_grad, inner, Rows(at["w_t2"], 2 * TD), Rows(at["w_tp"], TD), top, context_grad]
    operands += [one for one, _ in squares]
    outs = [((8, 2 * WIDE), f32), ((8, 128), f32)]
    return one_step(body, info, table, operands, outs, 2 * 8 * 3072 * WIDE)


def channel_mix():
    flat = np.arange(LC * C)[:, None]
    split = np.arange(LC * C)[None]
    return jnp.asarray((flat == LC * (split % C) + split // C).astype(ml_dtypes.bfloat16))


def gather_small(place, value):
    stride, joined = (1, value[None])
    while stride < place.count:
        other = place.swap(joined, stride)
        upper = (place.index // stride) % 2 == 1
        joined = jnp.where(
            upper,
            jnp.concatenate([other, joined], axis=0),
            jnp.concatenate([joined, other], axis=0),
        )
        stride *= 2
    return joined


def windows(values, turned, sign):
    width = values.shape[1]
    col = (lax.iota(jnp.int32, TOKENS) % FRAME)[:, None]
    zero_one = jnp.zeros((1, width), values.dtype)
    zero_row = jnp.zeros((FRAME, width), values.dtype)
    none = jnp.zeros((), values.dtype)
    across = {
        -1: jnp.where(col > 0, jnp.concatenate([zero_one, values[:-1]], axis=0), none),
        0: values,
        1: jnp.where(col < FRAME - 1, jnp.concatenate([values[1:], zero_one], axis=0), none),
    }
    moved = {}
    for col_off, value in across.items():
        moved[-1, col_off] = jnp.concatenate([zero_row, value[:-FRAME]], axis=0)
        moved[0, col_off] = value
        moved[1, col_off] = jnp.concatenate([value[FRAME:], zero_row], axis=0)
    out = []
    for row_off, col_off in tap_offsets:
        plain = moved[sign * row_off, sign * col_off]
        other = moved[sign * col_off, sign * row_off]
        out.append(plain if row_off == col_off else jnp.where(turned, other, plain))
    return jnp.concatenate(out, axis=1)


def frame_of(place, latents, target_noise, turned):
    both = jnp.concatenate([latents, target_noise], axis=-1)
    stride, joined = (1, both[None])
    while stride < place.rows:
        other = place.swap(joined, stride)
        upper = (place.index // stride) % 2 == 1
        joined = jnp.where(
            upper,
            jnp.concatenate([other, joined], axis=0),
            jnp.concatenate([joined, other], axis=0),
        )
        stride *= 2
    image = pick(joined, place.slot, 1).reshape(SIDE, SIDE, 2 * LC)
    portrait = image[:, :FRAME]
    landscape = jnp.transpose(image[:FRAME], (1, 0, 2))
    return jnp.where(turned, landscape, portrait).reshape(TOKENS, 2 * LC)


def train_step(place, store, table, vecs, latents, target_noise, label, step_value, orient, extent):
    half, at = (place.half, store.places)
    turned = orient != 1
    info = jnp.stack([place.side, turned.astype(jnp.int32), extent * FRAME, label]).astype(jnp.int32)
    mask = (lax.iota(jnp.int32, TOKENS) < extent * FRAME).astype(jnp.float32)[:, None]
    frame = frame_of(place, latents, target_noise, turned)
    share = noise_level(step_value)
    noisy = mask * (jnp.sqrt(share) * frame[:, :LC] + jnp.sqrt(1.0 - share) * frame[:, LC:])
    pad_in = windows(low(noisy), turned, 1)
    noise_rows = jnp.pad(frame[:, LC:].T, ((0, OUT_ROWS - LC), (0, 0)))
    embed_in = low(time_embed(step_value))[None]
    mix = channel_mix()
    row = lambda *names: jnp.stack([vecs[name] for name in names])
    side_rows = lambda *names: half(row(*names))

    def part(name, depth=C, **kind):
        return Rows(at[name], depth, **kind)

    def own_rows(name):
        return Rows(at[name], HALF, side_rows=True)

    qkv = unmix(info, table, at["w_qkv"], C, 3, HALF)
    ff1 = unmix(info, table, at["w_ff1"], C, 2 * FFI // WIDE, HALF)
    w_in = half(table[at["w_in"] : at["w_in"] + 9 * LC])
    w_out = dot(table[at["w_out"] : at["w_out"] + 9 * LC].reshape(9, LC * C), mix)
    w_out = low(jnp.pad(w_out.reshape(9, LC, C), ((0, 0), (0, OUT_ROWS - LC), (0, 0))))
    w_out = w_out.reshape(9 * OUT_ROWS, C)

    twice = jnp.repeat(embed_in.astype(jnp.float32), 2, axis=1)
    parity = lax.iota(jnp.int32, 2 * TE)[None] % 2
    stuffed = [jnp.pad(jnp.where(parity == j, twice, 0.0), ((0, 7), (0, 0))) for j in range(2)]
    biases = [vecs["b_t1"].reshape(2, WIDE), vecs["b_t2"].reshape(2, WIDE), vecs["b_tp"][None]]
    biases = jnp.pad(jnp.concatenate(biases, axis=0), ((0, 3), (0, 0)))
    inner, both, context_kv = time_front(info, table, at, jnp.concatenate(stuffed, axis=0), biases)
    context, time_vec = (low(both[:2]), both[1:2])
    hidden_one, hidden_two = (low(inner[2:3]), low(inner[3:4]))

    act_one, normed_one, inv_one, state_zero = first_forward(
        info, pad_in, w_in, side_rows("b_in", "g1", "bb1")
    )
    act_one_peer = place.swap(act_one)
    rows_two = side_rows("b_c1", "g2", "bb2")
    rows_two = jnp.concatenate([rows_two[0:1] + half(time_vec), rows_two[1:]], axis=0)
    act_two, normed_two, inv_two = conv_forward(
        info, act_one, act_one_peer, table, at["w_c1"], None, rows_two, True
    )
    act_two_peer = place.swap(act_two)
    token_own, normed_three, inv_three, state_one = conv_forward(
        info, act_two, act_two_peer, table, at["w_c2"], state_zero, side_rows("b_c2", "g3", "bb3"), False
    )
    token_in, resid_zero, ln_one, packed, attended_own = self_front(
        info, table, token_own, place.swap(token_own), part("w_pin"), row("b_pin", "n1g", "n1b"), qkv
    )
    attended, resid_one, ln_two, cross_query, cross_own = cross_front(
        info,
        table,
        attended_own,
        place.swap(attended_own),
        part("w_o"),
        row("b_o", "n2g", "n2b"),
        resid_zero,
        part("w_cq", side_columns=True),
        context_kv,
    )
    b_ff1 = half(vecs["b_ff1"].reshape(-1, WIDE)).reshape(1, FFI)
    cross_out, resid_two, ln_three, projected, gated_own = ff_front(
        info,
        table,
        cross_own,
        place.swap(cross_own),
        part("w_co"),
        row("b_co", "n3g", "n3b"),
        resid_one,
        ff1,
        b_ff1,
    )
    gated, out_in, state_own = ff_finish(
        info,
        table,
        gated_own,
        place.swap(gated_own),
        part("w_ff2", FFI),
        row("b_ff2"),
        resid_two,
        part("w_pout", side_columns=True),
        side_rows("b_pout"),
        state_one,
    )
    b_out = jnp.broadcast_to(jnp.pad(vecs["b_out"], (0, OUT_ROWS - LC))[:, None], (OUT_ROWS, 128))
    (
        w_out_grad,
        small_out,
        state_grad,
        pout_low,
        ff2_low,
        resid_grad,
        proj_low,
        ln_part,
        sums_out,
        sums_ff,
    ) = loss_back(
        info,
        table,
        state_own,
        place.swap(state_own),
        w_out,
        noise_rows,
        b_out,
        part("w_pout"),
        part("w_ff2", FFI),
        projected,
        ff1,
    )
    ln_peer = place.swap(ln_part)
    store.add("w_pout", out_in, pout_low)
    store.add("w_ff2", gated, ff2_low)
    store.add("w_ff1", ln_three, proj_low)
    w_out_grad = w_out_grad.reshape(9, OUT_ROWS, C)[:, :LC].reshape(9, LC * C)
    thirds, left = ([], w_out_grad)
    for _ in range(3):
        thirds.append(lax.reduce_precision(left, 8, 7))
        left = left - thirds[-1]
    thirds = dot_t(low(jnp.concatenate(thirds, axis=0)), mix)
    w_out_grad = thirds[:9] + thirds[9:18] + thirds[18:]
    w_out_grad = half(w_out_grad.reshape(9 * LC, C))
    store.put(at["w_out"], jnp.zeros((store.total - at["w_out"], HALF), jnp.float32))
    resid_grad, co_low, query_low, kv_grad, sums_co, context_grad = cross_back(
        info,
        table,
        ln_part,
        ln_peer,
        resid_two,
        row("n3g"),
        resid_grad,
        own_rows("w_co"),
        cross_query,
        context_kv,
        Rows(at["w_ckv"], 2 * C, side_columns=True),
    )
    query_peer = place.swap(query_low)
    kv_low = low(kv_grad[:2])
    context_grad = context_grad + place.swap(context_grad)
    store.add("w_co", cross_out, co_low)
    store.add("w_cq", ln_two, query_low)
    store.add("w_ckv", context, kv_low)
    resid_grad, o_low, packed_low, ln_part, sums_o = self_back(
        info,
        table,
        query_low,
        query_peer,
        part("w_cq"),
        resid_one,
        row("n2g"),
        resid_grad,
        own_rows("w_o"),
        packed,
        qkv,
    )
    ln_peer = place.swap(ln_part)
    store.add("w_o", attended, o_low)
    store.add("w_qkv", ln_one, packed_low)
    pin_low, state_grad, conv_low, sums_pin, sums_two = token_back(
        info,
        table,
        ln_part,
        ln_peer,
        resid_zero,
        row("n1g"),
        resid_grad,
        own_rows("w_pin"),
        normed_three,
        inv_three,
        side_rows("g3"),
        state_grad,
    )
    conv_peer = place.swap(conv_low)
    store.add("w_pin", token_in, pin_low)
    conv_low, sums_one = conv_backward(
        info,
        conv_low,
        conv_peer,
        act_two,
        act_two_peer,
        table,
        store,
        at["w_c2"],
        (normed_two, inv_two),
        side_rows("g2", "bb2"),
        None,
    )
    conv_peer = place.swap(conv_low)
    time_grad = place.full(sums_one[0:1]) + context_grad[1:2]
    b_tp = half(time_grad)
    time_low = low(time_grad)
    outer, bounds = time_back(
        info,
        table,
        at,
        jnp.pad(time_grad, ((0, 7), (0, 0))),
        inner,
        store.top,
        context_grad,
        ((inv_one, 1), (inv_two, 1), (sums_two, 3), (sums_one, 3)),
    )
    b_t2, b_t1 = (half(outer[0].reshape(-1, WIDE)), half(outer[1].reshape(-1, WIDE)))
    two_low, one_low = (low(b_t2), low(b_t1))
    largest = Largest(place, bounds)
    store.add("w_tp", hidden_two, half(time_low))
    store.buffer = largest.exchange(store.buffer)
    store.add("w_t2", hidden_one, two_low.reshape(1, -1))
    store.buffer = largest.exchange(store.buffer)
    store.add("w_t1", embed_in, one_low.reshape(1, -1))
    chosen = lax.iota(jnp.int32, NCLS)[:, None] == label
    store.put(at["table"], jnp.where(chosen, half(context_grad[0:1]), 0.0))
    store.put(0, jnp.zeros((at["w_t1"], HALF), jnp.float32))
    store.buffer = largest.exchange(store.buffer)
    in_low, sums_in = conv_backward(
        info,
        conv_low,
        conv_peer,
        act_one,
        act_one_peer,
        table,
        store,
        at["w_c1"],
        (normed_one, inv_one),
        side_rows("g1", "bb1"),
        state_grad,
    )
    store.buffer = largest.exchange(store.buffer)
    tops = largest.finish()[0]
    bound = jnp.maximum(tops[0], 1.01 * jnp.sqrt(tops[1] * tops[4]))
    bound = jnp.maximum(bound, 1.01 * jnp.sqrt(tops[2] * tops[3]))
    scale = (WIRE_TOP / (place.count // 2)) / jnp.maximum(bound, 1e-30)
    w_in_grad = t_dot(pad_in, in_low)
    small = [b_t1, b_t2, b_tp, sums_in[:3], sums_one[:3], sums_two[:3], sums_pin[:3], sums_o[:3]]
    small += [sums_co[:3], sums_ff, sums_out[:2]]
    extra = [small_out[:LC, 0], small_out[0:1, 128], (extent * FRAME).astype(jnp.float32)[None]]
    extra = jnp.pad(jnp.concatenate(extra), (0, HALF - LC - 2))[None]
    return (jnp.concatenate(small + [extra, w_in_grad, w_out_grad], axis=0), scale)


def adam_update(params, first_mom, second, gradient, decay_rate):
    first_new = adam_one * first_mom + (1.0 - adam_one) * gradient
    second_new = adam_two * second + (1.0 - adam_two) * gradient * gradient
    step_size = (
        first_new
        / (1.0 - adam_one**STEP)
        / (jnp.sqrt(second_new / (1.0 - adam_two**STEP)) + adam_eps)
    )
    return (params - learn_rate * (step_size + decay_rate * params), first_new, second_new)


def local(
    latents,
    target_noise,
    labels,
    timesteps,
    orient,
    extent,
    mat_params,
    mat_first,
    mat_second,
    mat_ema,
    vec_params,
    vec_first,
    vec_second,
    vec_ema,
):
    place = Place()
    length = mat_params.shape[0]
    rows = shard_rows(length * place.count, place.count)
    block = to_blocks(place, mat_params.astype(jnp.bfloat16), rows)
    table = lax.all_gather(block, ("dp", "rows"), axis=0, tiled=True)
    vec_len = vec_params.shape[0]
    vec_wide = -(-vec_len // 128) * 128
    padded = jnp.pad(vec_params, (0, vec_wide - vec_len)).reshape(-1, 128)
    vec_all = gather_small(place, padded).reshape(place.count, vec_wide)[:, :vec_len]
    vec_all = vec_all.reshape(-1).astype(jnp.bfloat16).astype(jnp.float32)
    vecs = unpack(vec_all, vec_layout())
    own = lambda values: pick(values, place.slot, 0)
    store = Store(place, rows)
    small, scale = train_step(
        place,
        store,
        table,
        vecs,
        latents,
        target_noise,
        own(labels),
        own(timesteps),
        own(orient),
        own(extent),
    )
    block_grad, square = scatter_sum(place, store.buffer, scale, rows)
    small = jnp.pad(small, ((0, -small.shape[0] % 8), (0, 0)))
    body = sum(record[1] for record in vec_layout()[:-1]) // WIDE
    lane = lax.broadcasted_iota(jnp.int32, small.shape, 1)
    line = lax.broadcasted_iota(jnp.int32, small.shape, 0)
    small = jnp.where((lane == SQUARE_AT) & (line == body), square, small)
    small = place.full(place.chip_sum(small))
    loss_sum, pixel_count = (small[body, LC], small[body, LC + 1])
    vec_flat = jnp.concatenate([small[:body].reshape(-1), small[body, :LC]])
    vec_flat = jnp.pad(vec_flat, (0, vec_len * place.count - vec_flat.shape[0]))
    shard_vec = lax.dynamic_slice(vec_flat, (vec_len * place.index,), (vec_len,))
    square = small[body, SQUARE_AT] + small[body, HALF + SQUARE_AT] + jnp.sum(vec_flat * vec_flat)
    shard_mat = from_blocks(place, block_grad, length)
    for i, name in enumerate(("w_in", "w_out")):
        values = small[body + 1 + 9 * LC * i : body + 1 + 9 * LC * (i + 1)]
        square = square + jnp.sum(values * values)
        owner, offset = divmod((store.places[name] - LEAD) * WIDE, length)
        old = lax.dynamic_slice(shard_mat, (offset,), (9 * LC * C,))
        new = jnp.where(place.index == owner, values.reshape(-1), old)
        shard_mat = lax.dynamic_update_slice(shard_mat, new, (offset,))
    inverse = 1.0 / pixel_count
    grad_norm = jnp.sqrt(square) * inverse
    factor = clip_norm / jnp.maximum(grad_norm, clip_norm) * inverse
    new_mat, mat_first_new, mat_second_new = adam_update(
        mat_params, mat_first, mat_second, shard_mat * factor, weight_decay
    )
    new_vec, vec_first_new, vec_second_new = adam_update(
        vec_params, vec_first, vec_second, shard_vec * factor, 0.0
    )
    ema_rate = min(ema_ceiling, (1.0 + STEP) / (10.0 + STEP))
    mat_ema_new = ema_rate * mat_ema + (1.0 - ema_rate) * new_mat
    vec_ema_new = ema_rate * vec_ema + (1.0 - ema_rate) * new_vec
    return (
        new_mat,
        mat_first_new,
        mat_second_new,
        mat_ema_new,
        new_vec,
        vec_first_new,
        vec_second_new,
        vec_ema_new,
        grad_norm,
        loss_sum,
        pixel_count,
    )


def solution(mesh):
    return jax.shard_map(
        local,
        mesh=mesh,
        in_specs=(
            P("dp", "rows", None, None),
            P("dp", "rows", None, None),
            P("dp"),
            P("dp"),
            P("dp"),
            P("dp"),
            P(("dp", "rows")),
            P(("dp", "rows")),
            P(("dp", "rows")),
            P(("dp", "rows")),
            P(("dp", "rows")),
            P(("dp", "rows")),
            P(("dp", "rows")),
            P(("dp", "rows")),
        ),
        out_specs=(
            P(("dp", "rows")),
            P(("dp", "rows")),
            P(("dp", "rows")),
            P(("dp", "rows")),
            P(("dp", "rows")),
            P(("dp", "rows")),
            P(("dp", "rows")),
            P(("dp", "rows")),
            P(),
            P(),
            P(),
        ),
        check_vma=False,
    )
```

```python
import math

import jax
import jax.numpy as jnp
import ml_dtypes
import numpy as np
from jax import lax
from jax.experimental import pallas as pl
from jax.experimental.pallas import tpu as pltpu
from jax.sharding import PartitionSpec as P

C = 512
HEADS = 8
DHEAD = 64
FFI = 2048
TE = 256
TD = 1024
NCLS = 1000
LC = 3
GROUPS = 32
SIDE = 32
NT = 1000
STEP = 10


tap_offsets = [(-1, -1), (-1, 0), (-1, 1), (0, -1), (0, 0), (0, 1), (1, -1), (1, 0), (1, 1)]
eps_group = 1e-06
eps_layer = 1e-05
beta_first = 0.00085
beta_last = 0.012
adam_one = 0.9
adam_two = 0.999
adam_eps = 1e-08
learn_rate = 0.05
weight_decay = 0.01
ema_ceiling = 0.9999
clip_norm = 0.1


def mat_layout():
    return [
        ("w_in", 9 * LC, C),
        ("w_t1", TE, TD),
        ("w_t2", TD, TD),
        ("w_tp", TD, C),
        ("table", NCLS, C),
        ("w_c1", 9 * C, C),
        ("w_c2", 9 * C, C),
        ("w_pin", C, C),
        ("w_qkv", C, 3 * C),
        ("w_o", C, C),
        ("w_cq", C, C),
        ("w_ckv", C, 2 * C),
        ("w_co", C, C),
        ("w_ff1", C, 2 * FFI),
        ("w_ff2", FFI, C),
        ("w_pout", C, C),
        ("w_out", 9 * C, LC),
    ]


def vec_layout():
    names = [
        "b_tp",
        "b_in",
        "g1",
        "bb1",
        "b_c1",
        "g2",
        "bb2",
        "b_c2",
        "g3",
        "bb3",
        "b_pin",
        "n1g",
        "n1b",
        "b_o",
        "n2g",
        "n2b",
        "b_co",
        "n3g",
        "n3b",
    ]
    return (
        [("b_t1", TD), ("b_t2", TD)]
        + [(name_one, C) for name_one in names]
        + [("b_ff1", 2 * FFI), ("b_ff2", C), ("b_pout", C), ("b_out", LC)]
    )


def unpack(joined, layout):
    pieces = {}
    start_at = 0
    for record in layout:
        length = 1
        for extent_one in record[1:]:
            length = length * extent_one
        pieces[record[0]] = joined[start_at : start_at + length].reshape(record[1:])
        start_at = start_at + length
    return pieces


def noise_level(step_value):
    steps_idx = jnp.arange(NT).astype(jnp.float32)
    root_beta = math.sqrt(beta_first) + (
        math.sqrt(beta_last) - math.sqrt(beta_first)
    ) * steps_idx / (NT - 1)
    log_keep = jnp.log1p(-root_beta * root_beta)
    return jnp.exp(jnp.sum(jnp.where(jnp.arange(NT) <= step_value, log_keep, 0.0)))


def time_embed(step_value):
    frequency = jnp.exp(-math.log(10000.0) * jnp.arange(TE // 2).astype(jnp.float32) / (TE // 2))
    angles = step_value.astype(jnp.float32) * frequency
    return jnp.concatenate([jnp.cos(angles), jnp.sin(angles)])


WIDE = 512
HALF = 256
LEAD = 5
FRAME = 16
TOKENS = SIDE * FRAME
LOCAL_HEADS = HEADS // 2
WIRE_TOP = 32768.0


def silu_slope(values):
    logistic = jax.nn.sigmoid(values)
    return logistic * (1.0 + values * (1.0 - logistic))


def dot(left, right):
    return jnp.dot(left, right, preferred_element_type=jnp.float32)


def dot_t(left, right):
    return lax.dot_general(
        left, right, (((1,), (1,)), ((), ())), preferred_element_type=jnp.float32
    )


def t_dot(left, right):
    return lax.dot_general(
        left, right, (((0,), (0,)), ((), ())), preferred_element_type=jnp.float32
    )


def low(values):
    return values.astype(jnp.bfloat16)


class Place:
    def __init__(self):
        self.dp, self.rows = (lax.axis_size("dp"), lax.axis_size("rows"))
        self.count = self.dp * self.rows
        self.index = lax.axis_index("dp") * self.rows + lax.axis_index("rows")
        self.side = self.index % 2
        self.slot = (self.index // 2) % 2
        digits, left = ([], self.dp)
        while left > 4:
            digits.append(4)
            left //= 4
        digits.append(left)
        self.digits = digits + [2]
        strides, step = ([], 2)
        for size in reversed(self.digits):
            strides.insert(0, step)
            step *= size
        self.strides = strides
        self.coords = [(self.index // s) % n for s, n in zip(strides, self.digits)]

    def move(self, value, pairs):
        return lax.ppermute(value, ("dp", "rows"), pairs)

    def swap(self, value, stride=1):
        return self.move(value, [(k, k ^ stride) for k in range(self.count)])

    def shift(self, value, by):
        return self.move(
            value, [(k, k + by) for k in range(self.count) if 0 <= k + by < self.count]
        )

    def rotate(self, value, axis, by):
        stride, size = (self.strides[axis], self.digits[axis])
        pairs = []
        for k in range(self.count):
            at = (k // stride) % size
            pairs.append((k, k + ((at + by) % size - at) * stride))
        return self.move(value, pairs)

    def step(self, value, axis, direction, hops):
        stride, size = (self.strides[axis], self.digits[axis])
        pairs = []
        for k in range(self.count):
            at = (k // stride) % size
            rank = at if direction > 0 else size - 1 - at
            if rank <= hops and rank < size - 1:
                pairs.append((k, k + direction * stride))
        return self.move(value, pairs)

    def half(self, value, axis=-1):
        axis = axis % value.ndim
        return lax.dynamic_slice_in_dim(value, self.side * HALF, HALF, axis)

    def join(self, mine, other):
        first = jnp.where(self.side == 0, mine, other)
        second = jnp.where(self.side == 0, other, mine)
        return jnp.concatenate([first, second], axis=-1)

    def full(self, mine):
        return self.join(mine, self.swap(mine))

    def chip_sum(self, value):
        stride = 2
        while stride < self.count:
            if 2 * stride < self.count:
                near, far, both = [self.swap(value, stride * n) for n in (1, 2, 3)]
                value = (value + near) + (far + both)
            else:
                value = value + self.swap(value, stride)
            stride *= 4
        return value


def shard_rows(flat_len, count):
    length = flat_len // count
    rows = -(-(LEAD * WIDE + flat_len) // (WIDE * count))
    rows = -(-rows // 8) * 8
    while rows * WIDE - length < LEAD * WIDE:
        rows += 8
    return rows


def to_blocks(place, shard, rows):
    length, block = (shard.shape[0], rows * WIDE)
    drift = block - length
    reach = drift * (place.count - 1) - LEAD * WIDE + block
    parts, hop = ([jnp.zeros((LEAD * WIDE,), shard.dtype), shard], 1)
    while hop * length < reach:
        take = min(length, reach - hop * length)
        take = min(length, -(-take // 1024) * 1024)
        parts.append(place.shift(shard[:take], -hop))
        hop += 1
    joined = jnp.concatenate(parts)
    lack = drift * (place.count - 1) + block - joined.shape[0]
    if lack > 0:
        joined = jnp.pad(joined, (0, lack))
    return lax.dynamic_slice(joined, (drift * place.index,), (block,)).reshape(rows, WIDE)


def from_blocks(place, block, length):
    flat = block.reshape(-1)
    drift = flat.shape[0] - length
    reach = drift * (place.count - 1) - LEAD * WIDE
    parts, hop, lead = ([flat], 1, 0)
    while lead < reach:
        take = min(flat.shape[0], -(-(reach - lead) // 1024) * 1024)
        parts.insert(0, place.shift(flat[flat.shape[0] - take :], hop))
        lead += take
        hop += 1
    joined = jnp.concatenate(parts)
    start = lead + LEAD * WIDE - drift * place.index
    return lax.dynamic_slice(joined, (start,), (length,))


def pick(values, index, axis):
    return lax.dynamic_index_in_dim(values, index, axis, keepdims=False)


def wire(values):
    return values.astype(jnp.float16)


def plain(values):
    return values.astype(jnp.float32)


SQUARE_AT = 8


class Largest:
    def __init__(self, place, values):
        self.place, self.values, self.stride = (place, values, 1)

    def exchange(self, beside=None):
        if self.stride < self.place.count:
            several = self.stride > 1 and 2 * self.stride < self.place.count
            times = (1, 2, 3) if several else (1,)
            got = [self.place.swap(self.values, self.stride * n) for n in times]
            if beside is not None:
                *got, beside = lax.optimization_barrier((*got, beside))
            values = self.values
            for one in got:
                values = jnp.maximum(values, one)
            self.values = lax.optimization_barrier(values)
            self.stride *= 4 if several else 2
        return beside

    def finish(self):
        while self.stride < self.place.count:
            self.exchange()
        return self.values


def scatter_part(place, grads, low_row, rows, order, scale, after=(), ahead=None):
    held, left, first, factor = (grads, list(range(len(place.digits))), low_row, scale)

    def part_of(dim, index):
        starts, sizes, shape = ([], [], [])
        for at, axis in enumerate(left):
            starts.append(index if at == dim else 0)
            sizes.append(1 if at == dim else place.digits[axis])
            if at != dim:
                shape.append(place.digits[axis])
        out = lax.dynamic_slice(held, starts + [first, 0], sizes + [rows, HALF])
        return out.reshape(shape + [rows, HALF]) * factor

    for axis in order:
        dim = left.index(axis)
        me, size = (place.coords[axis], place.digits[axis])
        total = part_of(dim, me)
        if size == 2 or axis == order[-1]:
            for away in range(1, size):
                sent = wire(part_of(dim, (me + away) % size))
                if ahead is not None and axis == order[0] and away == 1:
                    sent = ahead
                got = place.rotate(sent, axis, away)
                if axis == order[0] and after:
                    got = lax.optimization_barrier((got, *after))[0]
                total = total + plain(got)
                last = (sent,)
        else:
            flows, sent = ({1: None, -1: None}, {})
            for hops in range(size - 1):
                for direction in (1, -1):
                    rank = me if direction > 0 else size - 1 - me
                    aim = jnp.minimum(size - 1 - hops + rank, size - 1)
                    aim = aim if direction > 0 else size - 1 - aim
                    value = part_of(dim, aim)
                    if hops == 1 and axis == order[0] and after:
                        flows[direction] = lax.optimization_barrier((flows[direction], *after))[0]
                    if flows[direction] is not None:
                        value = value + plain(flows[direction])
                    sent[direction] = wire(value)
                    flows[direction] = place.step(sent[direction], axis, direction, hops)
            total = total + plain(flows[1]) + plain(flows[-1])
            last = (sent[1], sent[-1])
        if axis == order[0]:
            leaving = last
        held, first, factor = (total, 0, 1.0)
        left.remove(axis)
    return (held, leaving)


SHARES = (0.42, 0.33)


def scatter_sum(place, grads, scale, rows):
    held = grads.reshape(*place.digits, 2 * rows, HALF)
    axes = list(range(len(place.digits)))[::-1]
    total = 2 * rows
    cuts = [0] + [int(total * sum(SHARES[: i + 1]) / 8 + 0.5) * 8 for i in range(2)] + [total]
    orders = [axes[i:] + axes[:i] for i in range(3)]
    parts, after, ahead = ([None] * 3, (), [None] * 3)
    for i in range(2):
        axis = orders[i][0]
        if place.digits[axis] == 2:
            starts = [0] * len(axes) + [cuts[i], 0]
            starts[axis] = 1 - place.coords[axis]
            sizes = [1 if at == axis else size for at, size in enumerate(place.digits)]
            sent = lax.dynamic_slice(held, starts, sizes + [cuts[i + 1] - cuts[i], HALF])
            ahead[i] = wire(jnp.squeeze(sent, axis) * scale)
            after = (*after, ahead[i])
    for i in (2, 0, 1):
        span = (cuts[i], cuts[i + 1] - cuts[i])
        hold = () if i == 0 else after
        parts[i], leaving = scatter_part(place, held, *span, orders[i], scale, hold, ahead[i])
        after = leaving if i == 2 else after
    unit = 1.0 / scale
    parts = [part * unit for part in parts]
    square = sum(jnp.sum(part * part) for part in parts).reshape(1, 1)
    chip = jnp.concatenate(parts, axis=0).reshape(2, rows, HALF)
    mine = pick(chip, place.side, 0)
    other = place.swap(pick(chip, 1 - place.side, 0))
    return (place.join(mine, other), square)


class Store:
    def __init__(self, place, rows):
        self.total = place.count * rows
        self.buffer = None
        self.top = jnp.zeros((1, 1), jnp.float32)
        self.places, at = ({}, LEAD)
        for name, depth, width in mat_layout():
            self.places[name] = at
            at += depth * width // WIDE

    def write(self, out, top):
        self.buffer = out
        if top is not None:
            self.top = jnp.maximum(self.top, top)

    def add(self, name, inputs, gradient):
        if inputs.shape[0] < 16:
            spare = ((0, 16 - inputs.shape[0]), (0, 0))
            inputs, gradient = (jnp.pad(inputs, spare), jnp.pad(gradient, spare))
        grad_into(self, inputs, gradient, self.places[name])

    def put(self, at, values):
        self.buffer = lax.dynamic_update_slice(self.buffer, values, (at, 0))


def store_specs(store, at, tile):
    old = [] if store.buffer is None else [store.buffer]
    out = pl.BlockSpec(
        (pl.Element(tile), pl.Element(HALF)), lambda i, *_: (pl.multiple_of(at + tile * i, 8), 0)
    )
    shape = jax.ShapeDtypeStruct((store.total, HALF), jnp.float32)
    return (old, [pl.BlockSpec(memory_space=pl.ANY) for _ in old], out, shape)


def grad_into(store, inputs, gradient, at):
    tokens, depth = inputs.shape
    pieces = gradient.shape[1] // HALF
    tile = min(depth, 512 if pieces == 1 else 256 if pieces < 8 else 128)
    rows, tiles = (tile * pieces, depth // tile)
    old, old_specs, out_spec, out_shape = store_specs(store, at, rows)

    def body(*refs):
        refs = refs[len(old) :]
        input_ref, gradient_ref, out_ref, top_out = refs[:4]
        step = pl.program_id(0)
        part = t_dot(input_ref[...], gradient_ref[...])
        if pieces == 1:
            out_ref[...] = part
        else:
            mixed = refs[-1]
            for side in range(HALF // 128):
                for j in range(pieces):
                    column = j * HALF + side * 128
                    mixed[pl.ds(j, tile, stride=pieces), :] = part[:, column : column + 128]
                out_ref[:, side * 128 : (side + 1) * 128] = mixed[...]
        largest = jnp.max(jnp.abs(part))

        @pl.when(step == 0)
        def _():
            top_out[0, 0] = largest

        @pl.when(step > 0)
        def _():
            top_out[0, 0] = jnp.maximum(top_out[0, 0], largest)

    out, top = pl.pallas_call(
        body,
        grid=(tiles,),
        in_specs=old_specs
        + [
            pl.BlockSpec((tokens, tile), lambda i: (0, i)),
            pl.BlockSpec(gradient.shape, lambda i: (0, 0)),
        ],
        out_specs=[out_spec, pl.BlockSpec(memory_space=pltpu.SMEM)],
        out_shape=[out_shape, jax.ShapeDtypeStruct((1, 1), jnp.float32)],
        scratch_shapes=[] if pieces == 1 else [pltpu.VMEM((rows, 128), jnp.float32)],
        input_output_aliases={k: k for k in range(len(old))},
        compiler_params=params(),
        cost_estimate=cost(
            2 * tokens * depth * gradient.shape[1],
            depth * gradient.shape[1] * 4 + tokens * depth * 2,
        ),
    )(*old, inputs, gradient)
    store.write(out, top)


VMEM_LIMIT = 50 * 1024 * 1024
PADDED = TOKENS + 2 * FRAME


def params():
    return pltpu.CompilerParams(vmem_limit_bytes=VMEM_LIMIT)


def whole(shape):
    return pl.BlockSpec(shape, lambda *_: (0,) * len(shape))


def cost(flops, nbytes):
    return pl.CostEstimate(flops=flops, bytes_accessed=nbytes, transcendentals=0)


def token_mask(limit):
    return (lax.broadcasted_iota(jnp.int32, (TOKENS, 1), 0) < limit).astype(jnp.float32)


def columns_moved(values, col_off):
    if col_off == 0:
        return values
    col = lax.broadcasted_iota(jnp.int32, (TOKENS, 1), 0) % FRAME
    keep = col > 0 if col_off < 0 else col < FRAME - 1
    return jnp.where(keep, pltpu.roll(values, (-col_off) % TOKENS, 0), 0.0)


def two_sides(side, mine, other):
    first = jnp.where(side == 0, mine, other)
    second = jnp.where(side == 0, other, mine)
    return jnp.concatenate([first, second], axis=1)


def fill_moved(moved, values):
    width = moved.shape[2]
    empty = jnp.zeros((FRAME, width), moved.dtype)
    for slab in range(3):
        moved[slab, 0:FRAME, :] = empty
        moved[slab, FRAME : FRAME + TOKENS, :] = columns_moved(values, slab - 1).astype(moved.dtype)
        moved[slab, FRAME + TOKENS : PADDED, :] = empty


def tap_of(step, turned):
    row_off, col_off = (step // 3 - 1, step % 3 - 1)
    return (
        jnp.where(turned == 1, col_off, row_off),
        jnp.where(turned == 1, row_off, col_off),
    )


def rows_from(row_off):
    return pl.ds(pl.multiple_of(FRAME * (1 + row_off), FRAME), TOKENS)


def group_same():
    left = lax.broadcasted_iota(jnp.int32, (HALF, HALF), 0) // (C // GROUPS)
    right = lax.broadcasted_iota(jnp.int32, (HALF, HALF), 1) // (C // GROUPS)
    return (left == right).astype(jnp.float32)


def spread_in(sums, same):
    wide = jnp.broadcast_to(sums, (8, HALF))
    return jnp.dot(
        wide, same, precision=lax.Precision.HIGHEST, preferred_element_type=jnp.float32
    )[0:1]


def norm_in(value, mask, limit, gain, bias):
    same = group_same()
    share = 1.0 / (limit.astype(jnp.float32) * (C // GROUPS))
    mean_val = spread_in(jnp.sum(value * mask, axis=0, keepdims=True), same) * share
    centered = value - mean_val
    var_val = spread_in(jnp.sum(centered * centered * mask, axis=0, keepdims=True), same) * share
    inv_std = lax.rsqrt(var_val + eps_group)
    normed = centered * inv_std
    return (normed * gain + bias, normed, inv_std)


def silu_in(values):
    return values / (1.0 + jnp.exp(-values))


def finish_forward(total, limit, base, rows, act, act_out, normed_out, inv_out, value_out):
    mask = token_mask(limit)
    value = mask * (total + rows[0:1])
    if base is not None:
        value = value + base
    norm, normed, inv_std = norm_in(value, mask, limit, rows[1:2], rows[2:3])
    result = mask * silu_in(norm) if act else norm
    low_result = result.astype(jnp.bfloat16)
    act_out[...] = low_result
    normed_out[...] = normed
    inv_out[0:1] = inv_std
    inv_out[1:2] = column_squares(low_result)
    if value_out is not None:
        value_out[...] = value


def forward_outs(with_value):
    shapes = [
        jax.ShapeDtypeStruct((TOKENS, HALF), jnp.bfloat16),
        jax.ShapeDtypeStruct((TOKENS, HALF), jnp.float32),
        jax.ShapeDtypeStruct((8, HALF), jnp.float32),
    ]
    if with_value:
        shapes.append(jax.ShapeDtypeStruct((TOKENS, HALF), jnp.float32))
    return shapes


def first_forward(info, inputs, weight, rows):
    def body(info_ref, input_ref, weight_ref, rows_ref, *outs):
        total = dot(input_ref[...], weight_ref[...])
        finish_forward(total, info_ref[2], None, rows_ref[...], True, *outs)

    outs = forward_outs(True)
    return pl.pallas_call(
        body,
        grid_spec=pltpu.PrefetchScalarGridSpec(
            num_scalar_prefetch=1,
            grid=(1,),
            in_specs=[whole(inputs.shape), whole(weight.shape), whole(rows.shape)],
            out_specs=[whole(one.shape) for one in outs],
        ),
        out_shape=outs,
        compiler_params=params(),
        cost_estimate=cost(2 * TOKENS * 27 * HALF, 3 * TOKENS * HALF * 4),
    )(info, inputs, weight, rows)


def conv_forward(info, mine, other, table, at, base, rows, act):
    with_base = base is not None

    def body(info_ref, mine_ref, other_ref, weight_ref, rows_ref, *rest):
        base_ref = rest[0] if with_base else None
        outs, (moved, total) = (rest[int(with_base) : -2], rest[-2:])
        step = pl.program_id(0)

        @pl.when(step == 0)
        def _():
            both = two_sides(info_ref[0], mine_ref[...], other_ref[...])
            fill_moved(moved, both.astype(jnp.float32))
            total[...] = jnp.zeros_like(total)

        part = None
        for j in range(3):
            row_off, col_off = tap_of(3 * step + j, info_ref[1])
            one = dot(moved[col_off + 1, rows_from(row_off), :], weight_ref[C * j : C * (j + 1), :])
            part = one if part is None else part + one
        total[...] += part

        @pl.when(step == 2)
        def _():
            value_out = outs[3] if with_base else None
            held = base_ref[...] if with_base else None
            finish_forward(
                total[...], info_ref[2], held, rows_ref[...], act, *outs[:3], value_out
            )

    outs = forward_outs(with_base)
    extra = [base] if with_base else []
    return pl.pallas_call(
        body,
        grid_spec=pltpu.PrefetchScalarGridSpec(
            num_scalar_prefetch=1,
            grid=(3,),
            in_specs=[
                whole(mine.shape),
                whole(other.shape),
                pl.BlockSpec(
                    (pl.Element(3 * C), pl.Element(HALF)),
                    lambda i, info_ref: (
                        pl.multiple_of(at + 3 * C * i, 8),
                        pl.multiple_of(HALF * info_ref[0], HALF),
                    ),
                ),
                whole(rows.shape),
            ]
            + [whole(one.shape) for one in extra],
            out_specs=[whole(one.shape) for one in outs],
            scratch_shapes=[
                pltpu.VMEM((3, PADDED, C), jnp.bfloat16),
                pltpu.VMEM((TOKENS, HALF), jnp.float32),
            ],
        ),
        out_shape=outs,
        compiler_params=params(),
        cost_estimate=cost(18 * TOKENS * C * HALF, 9 * C * HALF * 2 + 6 * TOKENS * HALF * 4),
    )(info, mine, other, table, rows, *extra)


def conv_backward(info, grad_mine, grad_other, act_mine, act_other, table, store, at, saved, rows, base):
    with_base = base is not None
    old, old_specs, out_spec, out_shape = store_specs(store, at, 3 * C)

    def body(info_ref, *refs):
        refs = refs[len(old) :]
        gm_ref, go_ref, am_ref, ao_ref = refs[:4]
        weight_refs, (normed_ref, inv_ref, rows_ref) = (refs[4:7], refs[7:10])
        base_ref = refs[10] if with_base else None
        refs = refs[10 + int(with_base) :]
        out_ref, low_out, sums_out = refs[:3]
        moved, turned_act, shifted, total = refs[-4:]
        step = pl.program_id(0)

        @pl.when(step == 0)
        def _():
            both = two_sides(info_ref[0], gm_ref[...], go_ref[...])
            fill_moved(moved, both.astype(jnp.float32))
            act = two_sides(info_ref[0], am_ref[...], ao_ref[...]).astype(jnp.float32)
            for slab in range(3):
                turned_act[slab] = columns_moved(act, slab - 1).T.astype(jnp.bfloat16)
            empty = jnp.zeros((FRAME, HALF), jnp.bfloat16)
            shifted[0:FRAME, :] = empty
            shifted[FRAME : FRAME + TOKENS, :] = gm_ref[...]
            shifted[FRAME + TOKENS : PADDED, :] = empty
            total[...] = jnp.zeros_like(total)

        part = None
        for j in range(3):
            row_off, col_off = tap_of(3 * step + j, info_ref[1])
            rows_at = rows_from(-row_off)
            out_ref[C * j : C * (j + 1), :] = dot(turned_act[col_off + 1], shifted[rows_at, :])
            one = dot_t(moved[1 - col_off, rows_at, :], weight_refs[j][...])
            part = one if part is None else part + one
        total[...] += part

        @pl.when(step == 2)
        def _():
            mask = token_mask(info_ref[2])
            gain, normed, inv_std = (rows_ref[0:1], normed_ref[...], inv_ref[0:1])
            norm = normed * gain + rows_ref[1:2]
            logistic = 1.0 / (1.0 + jnp.exp(-norm))
            gradient = mask * total[...] * (logistic * (1.0 + norm * (1.0 - logistic)))
            result, gain_grad, bias_grad = norm_back(
                gradient, normed, inv_std, mask, info_ref[2], gain
            )
            if with_base:
                result = mask * (result + base_ref[...])
            low_result = result.astype(jnp.bfloat16)
            low_out[...] = low_result
            sums_out[3:4] = column_squares(low_result)
            sums_out[0:1] = jnp.sum(result, axis=0, keepdims=True)
            sums_out[1:2] = gain_grad
            sums_out[2:3] = bias_grad

    def tap_rows(j):
        return pl.BlockSpec(
            (pl.Element(HALF), pl.Element(C)),
            lambda i, info_ref: (pl.multiple_of(at + C * (3 * i + j) + HALF * info_ref[0], 8), 0),
        )

    extra = [base] if with_base else []
    operands = [grad_mine, grad_other, act_mine, act_other]
    result = pl.pallas_call(
        body,
        grid_spec=pltpu.PrefetchScalarGridSpec(
            num_scalar_prefetch=1,
            grid=(3,),
            in_specs=old_specs
            + [whole(one.shape) for one in operands]
            + [
                tap_rows(j) for j in range(3)
            ]
            + [
                whole((TOKENS, HALF)),
                whole((8, HALF)),
                whole(rows.shape),
            ]
            + [whole(one.shape) for one in extra],
            out_specs=[
                out_spec,
                whole((TOKENS, HALF)),
                whole((8, HALF)),
            ],
            scratch_shapes=[
                pltpu.VMEM((3, PADDED, C), jnp.bfloat16),
                pltpu.VMEM((3, C, TOKENS), jnp.bfloat16),
                pltpu.VMEM((PADDED, HALF), jnp.bfloat16),
                pltpu.VMEM((TOKENS, HALF), jnp.float32),
            ],
        ),
        out_shape=[
            out_shape,
            jax.ShapeDtypeStruct((TOKENS, HALF), jnp.bfloat16),
            jax.ShapeDtypeStruct((8, HALF), jnp.float32),
        ],
        input_output_aliases={1 + k: k for k in range(len(old))},
        compiler_params=params(),
        cost_estimate=cost(36 * TOKENS * C * HALF, 9 * C * HALF * 6 + 6 * TOKENS * HALF * 4),
    )(info, *old, *operands, table, table, table, *saved, rows, *extra)
    store.write(result[0], None)
    return (result[1], result[2])


def column_squares(values):
    wide = values.astype(jnp.float32)
    return jnp.sum(wide * wide, axis=0, keepdims=True)


def norm_back(gradient, normed, inv_std, mask, limit, gain):
    same = group_same()
    share = 1.0 / (limit.astype(jnp.float32) * (C // GROUPS))
    scaled = gradient * gain
    first = spread_in(jnp.sum(scaled * mask, axis=0, keepdims=True), same) * share
    second = spread_in(jnp.sum(scaled * normed * mask, axis=0, keepdims=True), same) * share
    result = mask * inv_std * (scaled - first - normed * second)
    return (
        result,
        jnp.sum(gradient * normed, axis=0, keepdims=True),
        jnp.sum(gradient, axis=0, keepdims=True),
    )


def unmix(info, table, at, depth, pieces, columns):
    tile = min(depth, 128 if pieces > 4 else 256)

    def body(info_ref, rows_ref, out_ref, mixed):
        for side in range(columns // 128):
            mixed[...] = rows_ref[:, side * 128 : (side + 1) * 128].astype(jnp.float32)
            for j in range(pieces):
                column = j * columns + side * 128
                out_ref[:, column : column + 128] = low(mixed[pl.ds(j, tile, stride=pieces), :])

    return pl.pallas_call(
        body,
        grid_spec=pltpu.PrefetchScalarGridSpec(
            num_scalar_prefetch=1,
            grid=(depth // tile,),
            in_specs=[
                pl.BlockSpec(
                    (pl.Element(tile * pieces), pl.Element(columns)),
                    lambda i, info_ref: (
                        pl.multiple_of(at + tile * pieces * i, 8),
                        pl.multiple_of(HALF * info_ref[0] * int(columns == HALF), HALF),
                    ),
                )
            ],
            out_specs=pl.BlockSpec((tile, pieces * columns), lambda i, info_ref: (i, 0)),
            scratch_shapes=[pltpu.VMEM((tile * pieces, 128), jnp.float32)],
        ),
        out_shape=jax.ShapeDtypeStruct((depth, pieces * columns), jnp.bfloat16),
        compiler_params=params(),
        cost_estimate=cost(0, 4 * depth * pieces * columns),
    )(info, table)


class Rows:
    def __init__(self, at, count, side_columns=False, side_rows=False):
        self.at, self.count = (at, count)
        self.side_columns, self.side_rows = (side_columns, side_rows)

    def spec(self):
        at, columns, rows = (self.at, int(self.side_columns), int(self.side_rows))
        return pl.BlockSpec(
            (pl.Element(self.count), pl.Element(HALF if columns else WIDE)),
            lambda i, info_ref: (
                pl.multiple_of(at + HALF * info_ref[0] * rows, 8),
                pl.multiple_of(HALF * info_ref[0] * columns, HALF),
            ),
        )


def one_step(body, info, table, operands, outs, flops):
    arrays = [table if isinstance(one, Rows) else one for one in operands]
    specs = [one.spec() if isinstance(one, Rows) else whole(one.shape) for one in operands]
    shapes = [jax.ShapeDtypeStruct(shape, kind) for shape, kind in outs]
    nbytes = sum(math.prod(one.shape) * one.dtype.itemsize for one in shapes)
    return pl.pallas_call(
        body,
        grid_spec=pltpu.PrefetchScalarGridSpec(
            num_scalar_prefetch=1,
            grid=(1,),
            in_specs=specs,
            out_specs=[whole(one.shape) for one in shapes],
        ),
        out_shape=shapes,
        compiler_params=params(),
        cost_estimate=cost(flops, 2 * nbytes),
    )(info, *arrays)


f32, bf16 = (jnp.float32, jnp.bfloat16)


def side_of(side, values):
    return jnp.where(side == 0, values[:, :HALF], values[:, HALF:])


def layer_parts(values):
    centered = values - jnp.mean(values, axis=-1, keepdims=True)
    var_val = jnp.mean(centered * centered, axis=-1, keepdims=True)
    inv_std = lax.rsqrt(var_val + eps_layer)
    return (centered * inv_std, inv_std)


def layer_back(gradient, values, gain, base, side, sums_ref):
    normed, inv_std = layer_parts(values)
    scaled = gradient * gain
    first = jnp.mean(scaled, axis=-1, keepdims=True)
    second = jnp.mean(scaled * normed, axis=-1, keepdims=True)
    result = base + inv_std * (scaled - first - normed * second)
    sums_ref[0:1] = side_of(side, jnp.sum(result, axis=0, keepdims=True))
    sums_ref[1:2] = side_of(side, jnp.sum(gradient * normed, axis=0, keepdims=True))
    sums_ref[2:3] = side_of(side, jnp.sum(gradient, axis=0, keepdims=True))
    return result


def head_lanes(head):
    return lax.broadcasted_iota(jnp.int32, (1, HALF), 1) // DHEAD == head


def head_probs(query, key, head, limit):
    mine = jnp.where(head_lanes(head), query, jnp.zeros((), bf16))
    scores = dot_t(mine, key) * 0.125
    seen = lax.broadcasted_iota(jnp.int32, (1, TOKENS), 1) < limit
    scores = jnp.where(seen, scores, -1e30)
    exponent = jnp.exp(scores - jnp.max(scores, axis=-1, keepdims=True))
    return exponent / jnp.sum(exponent, axis=-1, keepdims=True)


def self_front(info, table, mine, other, weight, rows, qkv):
    def body(info_ref, mine_ref, other_ref, weight_ref, rows_ref, qkv_ref, *outs):
        token_ref, resid_ref, ln_ref, packed_ref, out_ref = outs
        token = two_sides(info_ref[0], mine_ref[...], other_ref[...])
        token_ref[...] = token
        resid = dot(token, weight_ref[...]) + rows_ref[0:1]
        resid_ref[...] = resid
        ln = low(layer_parts(resid)[0] * rows_ref[1:2] + rows_ref[2:3])
        ln_ref[...] = ln
        packed_ref[...] = low(dot(ln, qkv_ref[...]))
        query, key = (packed_ref[:, 0:HALF], packed_ref[:, HALF : 2 * HALF])
        value = packed_ref[:, 2 * HALF : 3 * HALF]
        total = jnp.zeros((TOKENS, HALF), f32)
        for head in range(LOCAL_HEADS):
            probs = head_probs(query, key, head, info_ref[2])
            total = jnp.where(head_lanes(head), dot(low(probs), value), total)
        out_ref[...] = low(total)

    outs = [
        ((TOKENS, C), bf16),
        ((TOKENS, C), f32),
        ((TOKENS, C), bf16),
        ((TOKENS, 3 * HALF), bf16),
        ((TOKENS, HALF), bf16),
    ]
    flops = 2 * TOKENS * C * (C + 3 * HALF) + 4 * LOCAL_HEADS * TOKENS * TOKENS * HALF
    return one_step(body, info, table, [mine, other, weight, rows, qkv], outs, flops)


def same_head():
    left = lax.broadcasted_iota(jnp.int32, (HALF, HALF), 0) // DHEAD
    right = lax.broadcasted_iota(jnp.int32, (HALF, HALF), 1) // DHEAD
    return (left == right).astype(f32)


def head_sums(values, same):
    return jnp.dot(values, same, precision=lax.Precision.HIGHEST, preferred_element_type=f32)


def cross_probs(query, context, same):
    first = head_sums(query * context[0:1, :HALF], same) * 0.125
    second = head_sums(query * context[1:2, :HALF], same) * 0.125
    top = jnp.maximum(first, second)
    first, second = (jnp.exp(first - top), jnp.exp(second - top))
    total = first + second
    return (first / total, second / total)


def cross_front(info, table, mine, other, weight, rows, resid, query_weight, context):
    def body(info_ref, mine_ref, other_ref, weight_ref, rows_ref, old_ref, qw_ref, kv_ref, *outs):
        full_ref, resid_ref, ln_ref, query_ref, out_ref = outs
        joined = two_sides(info_ref[0], mine_ref[...], other_ref[...])
        full_ref[...] = joined
        resid_now = old_ref[...] + dot(joined, weight_ref[...]) + rows_ref[0:1]
        resid_ref[...] = resid_now
        ln = low(layer_parts(resid_now)[0] * rows_ref[1:2] + rows_ref[2:3])
        ln_ref[...] = ln
        query = low(dot(ln, qw_ref[...]))
        query_ref[...] = query
        both = kv_ref[...].astype(f32)
        first, second = cross_probs(query.astype(f32), both, same_head())
        out_ref[...] = low(first * both[0:1, HALF:] + second * both[1:2, HALF:])

    outs = [
        ((TOKENS, C), bf16),
        ((TOKENS, C), f32),
        ((TOKENS, C), bf16),
        ((TOKENS, HALF), bf16),
        ((TOKENS, HALF), bf16),
    ]
    operands = [mine, other, weight, rows, resid, query_weight, context]
    return one_step(body, info, table, operands, outs, 2 * TOKENS * C * (C + 13 * HALF))


def gelu_parts(gate):
    return 0.5 * (1.0 + lax.erf(gate * math.sqrt(0.5)))


WIDE_FF = FFI // 2


def ff_front(info, table, mine, other, weight, rows, resid, ff_weight, ff_bias):
    def body(info_ref, mine_ref, other_ref, weight_ref, rows_ref, old_ref, fw_ref, fb_ref, *outs):
        full_ref, resid_ref, ln_ref, proj_ref, out_ref = outs
        joined = two_sides(info_ref[0], mine_ref[...], other_ref[...])
        full_ref[...] = joined
        resid_now = old_ref[...] + dot(joined, weight_ref[...]) + rows_ref[0:1]
        resid_ref[...] = resid_now
        ln = low(layer_parts(resid_now)[0] * rows_ref[1:2] + rows_ref[2:3])
        ln_ref[...] = ln
        for at in range(0, WIDE_FF, HALF):
            gate_at = WIDE_FF + at
            lift = dot(ln, fw_ref[:, at : at + HALF]) + fb_ref[:, at : at + HALF]
            gate = dot(ln, fw_ref[:, gate_at : gate_at + HALF]) + fb_ref[:, gate_at : gate_at + HALF]
            proj_ref[:, at : at + HALF] = lift
            proj_ref[:, gate_at : gate_at + HALF] = gate
            out_ref[:, at : at + HALF] = low(lift * gate * gelu_parts(gate))

    outs = [
        ((TOKENS, C), bf16),
        ((TOKENS, C), f32),
        ((TOKENS, C), bf16),
        ((TOKENS, FFI), f32),
        ((TOKENS, WIDE_FF), bf16),
    ]
    operands = [mine, other, weight, rows, resid, ff_weight, ff_bias]
    return one_step(body, info, table, operands, outs, 2 * TOKENS * C * (C + FFI))


def ff_finish(info, table, mine, other, weight, rows, resid, out_weight, out_bias, state):
    def body(info_ref, mine_ref, other_ref, weight_ref, rows_ref, old_ref, ow_ref, ob_ref, state_ref, *outs):
        full_ref, resid_ref, out_ref = outs
        side = info_ref[0]
        for at in range(0, WIDE_FF, HALF):
            own, peer = (mine_ref[:, at : at + HALF], other_ref[:, at : at + HALF])
            full_ref[:, 2 * at : 2 * at + WIDE] = two_sides(side, own, peer)
        resid_now = old_ref[...] + dot(full_ref[...], weight_ref[...]) + rows_ref[0:1]
        inner = low(resid_now)
        resid_ref[...] = inner
        branch = dot(inner, ow_ref[...]) + ob_ref[0:1]
        out_ref[...] = low(state_ref[...] + token_mask(info_ref[2]) * branch)

    outs = [((TOKENS, FFI), bf16), ((TOKENS, C), bf16), ((TOKENS, HALF), bf16)]
    operands = [mine, other, weight, rows, resid, out_weight, out_bias, state]
    return one_step(body, info, table, operands, outs, 2 * TOKENS * C * (FFI + HALF))


def lanes_moved(values, row_off, col_off):
    token = lax.broadcasted_iota(jnp.int32, (1, TOKENS), 1)
    row, col = (token // FRAME + row_off, token % FRAME + col_off)
    keep = (row >= 0) & (row < SIDE) & (col >= 0) & (col < FRAME)
    away = FRAME * row_off + col_off
    return jnp.where(keep, pltpu.roll(values, lax.rem(TOKENS - away, TOKENS), 1), 0.0)


OUT_ROWS = 8


def loss_back(info, table, mine, other, out_weight, noise, bias, pout, ff2, projected, ff1):
    def body(info_ref, *refs):
        mine_ref, other_ref, ow_ref, noise_ref, bias_ref, pout_ref, ff2_ref, proj_ref, ff1_ref = refs[:9]
        ow_grad, small_out, state_out, pout_low, ff2_low, resid_out, proj_low, ln_out, sums, ff_sums = refs[9:]
        side, turned, limit = (info_ref[0], info_ref[1], info_ref[2])
        state = two_sides(side, mine_ref[...], other_ref[...])
        raw = dot_t(ow_ref[...], state)
        predicted = bias_ref[:, 0:1]
        for tap in range(9):
            row_off, col_off = tap_of(tap, turned)
            part = raw[tap * OUT_ROWS : (tap + 1) * OUT_ROWS]
            predicted = predicted + lanes_moved(part, row_off, col_off)
        token = lax.broadcasted_iota(jnp.int32, (OUT_ROWS, TOKENS), 1)
        channel = lax.broadcasted_iota(jnp.int32, (OUT_ROWS, TOKENS), 0)
        error = jnp.where((token < limit) & (channel < LC), predicted - noise_ref[...], 0.0)
        loss = jnp.sum(jnp.sum(error * error, axis=1, keepdims=True), axis=0, keepdims=True)
        gradient = 2.0 * error
        small_out[:, 0:128] = jnp.broadcast_to(jnp.sum(gradient, axis=1, keepdims=True), (OUT_ROWS, 128))
        small_out[:, 128:256] = jnp.broadcast_to(loss, (OUT_ROWS, 128))
        gradient = low(gradient).astype(f32)
        moved = []
        for tap in range(9):
            row_off, col_off = tap_of(tap, turned)
            moved.append(lanes_moved(gradient, -row_off, -col_off))
        moved = low(jnp.concatenate(moved, axis=0))
        ow_grad[...] = dot(moved, state)
        state_grad = t_dot(moved, ow_ref[...])
        state_out[...] = side_of(side, state_grad)
        branch = token_mask(limit) * state_grad
        sums[1:2] = side_of(side, jnp.sum(branch, axis=0, keepdims=True))
        branch = low(branch)
        pout_low[...] = side_of(side, branch)
        resid_grad = dot_t(branch, pout_ref[...])
        resid_out[...] = resid_grad
        sums[0:1] = side_of(side, jnp.sum(resid_grad, axis=0, keepdims=True))
        resid_low = low(resid_grad)
        ff2_low[...] = side_of(side, resid_low)
        total = jnp.zeros((TOKENS, C), f32)
        for j in range(WIDE_FF // HALF):
            at, gate_at = (j * HALF, WIDE_FF + j * HALF)
            own = pl.ds(pl.multiple_of(WIDE * j + HALF * side, HALF), HALF)
            gated_grad = dot_t(resid_low, ff2_ref[own, :])
            lift, gate = (proj_ref[:, at : at + HALF], proj_ref[:, gate_at : gate_at + HALF])
            cdf = gelu_parts(gate)
            density = jnp.exp(-0.5 * gate * gate) * (1.0 / math.sqrt(2.0 * math.pi))
            lift_grad = gated_grad * gate * cdf
            gate_grad = gated_grad * lift * (cdf + gate * density)
            ff_sums[j : j + 1] = jnp.sum(lift_grad, axis=0, keepdims=True)
            ff_sums[4 + j : 5 + j] = jnp.sum(gate_grad, axis=0, keepdims=True)
            lift_grad, gate_grad = (low(lift_grad), low(gate_grad))
            proj_low[:, at : at + HALF] = lift_grad
            proj_low[:, gate_at : gate_at + HALF] = gate_grad
            total = total + dot_t(lift_grad, ff1_ref[:, at : at + HALF])
            total = total + dot_t(gate_grad, ff1_ref[:, gate_at : gate_at + HALF])
        ln_out[...] = total

    outs = [
        ((9 * OUT_ROWS, C), f32),
        ((OUT_ROWS, HALF), f32),
        ((TOKENS, HALF), f32),
        ((TOKENS, HALF), bf16),
        ((TOKENS, HALF), bf16),
        ((TOKENS, C), f32),
        ((TOKENS, FFI), bf16),
        ((TOKENS, C), f32),
        ((8, HALF), f32),
        ((8, HALF), f32),
    ]
    operands = [mine, other, out_weight, noise, bias, pout, ff2, projected, ff1]
    return one_step(body, info, table, operands, outs, 2 * TOKENS * C * (C + FFI + WIDE_FF))


def cross_back(info, table, mine, other, resid, gain, base, weight, query, context, ckv):
    def body(info_ref, mine_ref, other_ref, resid_ref, gain_ref, base_ref, weight_ref, query_ref, kv_ref, ckv_ref, *outs):
        resid_out, co_low, query_low, kv_grad, sums, context_out = outs
        side = info_ref[0]
        result = layer_back(
            mine_ref[...] + other_ref[...], resid_ref[...], gain_ref[0:1], base_ref[...], side, sums
        )
        resid_out[...] = result
        result = low(result)
        co_low[...] = side_of(side, result)
        out_grad = low(dot_t(result, weight_ref[...])).astype(f32)
        same, both, query_now = (same_head(), kv_ref[...].astype(f32), query_ref[...].astype(f32))
        first, second = cross_probs(query_now, both, same)
        first_grad = head_sums(out_grad * both[0:1, HALF:], same)
        second_grad = head_sums(out_grad * both[1:2, HALF:], same)
        inner = first * first_grad + second * second_grad
        first_grad = first * (first_grad - inner) * 0.125
        second_grad = second * (second_grad - inner) * 0.125
        query_low[...] = low(first_grad * both[0:1, :HALF] + second_grad * both[1:2, :HALF])
        for row, (prob, score) in enumerate(((first, first_grad), (second, second_grad))):
            kv_grad[row : row + 1, :HALF] = jnp.sum(score * query_now, axis=0, keepdims=True)
            kv_grad[row : row + 1, HALF:] = jnp.sum(prob * out_grad, axis=0, keepdims=True)
        kv_grad[2:8, :] = jnp.zeros((6, WIDE), f32)
        halves = [low(kv_grad[:, HALF * j : HALF * (j + 1)]) for j in range(2)]
        context_out[...] = unstuffed([dot_t(one, ckv_ref[...]) for one in halves])

    outs = [
        ((TOKENS, C), f32),
        ((TOKENS, HALF), bf16),
        ((TOKENS, HALF), bf16),
        ((8, WIDE), f32),
        ((8, HALF), f32),
        ((8, WIDE), f32),
    ]
    operands = [mine, other, resid, gain, base, weight, query, context, ckv]
    return one_step(body, info, table, operands, outs, 2 * TOKENS * C * 14 * HALF)


def self_back(info, table, mine, other, query_weight, resid, gain, base, weight, packed, qkv):
    def body(info_ref, mine_ref, other_ref, qw_ref, resid_ref, gain_ref, base_ref, weight_ref, packed_ref, qkv_ref, *outs):
        resid_out, o_low, packed_low, ln_out, sums = outs
        side, limit = (info_ref[0], info_ref[2])
        joined = two_sides(side, mine_ref[...], other_ref[...])
        result = layer_back(
            dot_t(joined, qw_ref[...]), resid_ref[...], gain_ref[0:1], base_ref[...], side, sums
        )
        resid_out[...] = result
        result = low(result)
        o_low[...] = side_of(side, result)
        out_grad = low(dot_t(result, weight_ref[...]))
        query, key = (packed_ref[:, 0:HALF], packed_ref[:, HALF : 2 * HALF])
        value = packed_ref[:, 2 * HALF : 3 * HALF]
        parts = [jnp.zeros((TOKENS, HALF), f32) for _ in range(3)]
        for head in range(LOCAL_HEADS):
            lanes = head_lanes(head)
            probs = head_probs(query, key, head, limit)
            mine_grad = jnp.where(lanes, out_grad, jnp.zeros((), bf16))
            prob_grad = dot_t(mine_grad, value)
            inner = jnp.sum(probs * prob_grad, axis=-1, keepdims=True)
            score_grad = low(probs * (prob_grad - inner) * 0.125)
            parts[0] = jnp.where(lanes, dot(score_grad, key), parts[0])
            parts[1] = jnp.where(lanes, t_dot(score_grad, query), parts[1])
            parts[2] = jnp.where(lanes, t_dot(low(probs), out_grad), parts[2])
        joined = low(jnp.concatenate(parts, axis=1))
        packed_low[...] = joined
        ln_out[...] = dot_t(joined, qkv_ref[...])

    outs = [
        ((TOKENS, C), f32),
        ((TOKENS, HALF), bf16),
        ((TOKENS, 3 * HALF), bf16),
        ((TOKENS, C), f32),
        ((8, HALF), f32),
    ]
    operands = [mine, other, query_weight, resid, gain, base, weight, packed, qkv]
    flops = 2 * TOKENS * C * 6 * HALF + 10 * LOCAL_HEADS * TOKENS * TOKENS * HALF
    return one_step(body, info, table, operands, outs, flops)


def token_back(info, table, mine, other, resid, gain, base, weight, normed, rows, gain_three, state):
    def body(info_ref, mine_ref, other_ref, resid_ref, gain_ref, base_ref, weight_ref, normed_ref, inv_ref, g3_ref, state_ref, *outs):
        pin_low, state_out, conv_low, sums, sums_three = outs
        side, limit = (info_ref[0], info_ref[2])
        result = layer_back(
            mine_ref[...] + other_ref[...], resid_ref[...], gain_ref[0:1], base_ref[...], side, sums
        )
        result = low(result)
        pin_low[...] = side_of(side, result)
        token_grad = dot_t(result, weight_ref[...])
        mask = token_mask(limit)
        norm_grad, gain_grad, bias_grad = norm_back(
            token_grad, normed_ref[...], inv_ref[0:1], mask, limit, g3_ref[0:1]
        )
        state_now = state_ref[...] + norm_grad
        state_out[...] = state_now
        conv_grad = mask * state_now
        low_grad = low(conv_grad)
        conv_low[...] = low_grad
        sums_three[0:1] = jnp.sum(conv_grad, axis=0, keepdims=True)
        sums_three[1:2] = gain_grad
        sums_three[2:3] = bias_grad
        sums_three[3:4] = column_squares(low_grad)

    outs = [
        ((TOKENS, HALF), bf16),
        ((TOKENS, HALF), f32),
        ((TOKENS, HALF), bf16),
        ((8, HALF), f32),
        ((8, HALF), f32),
    ]
    operands = [mine, other, resid, gain, base, weight, normed, rows, gain_three, state]
    return one_step(body, info, table, operands, outs, 2 * TOKENS * C * HALF)


class LabelRows(Rows):
    def spec(self):
        at = self.at
        return pl.BlockSpec(
            (pl.Element(8), pl.Element(WIDE)),
            lambda i, info_ref: (pl.multiple_of(at + info_ref[3] // 8 * 8, 8), 0),
        )


def stuffing(parity, kind):
    row = lax.broadcasted_iota(jnp.int32, (WIDE, 2 * WIDE), 0)
    column = lax.broadcasted_iota(jnp.int32, (WIDE, 2 * WIDE), 1)
    return (column == 2 * row + parity).astype(f32).astype(kind)


def unstuffed(parts):
    total = None
    for parity, part in enumerate(parts):
        thirds, left = ([], part)
        for _ in range(3):
            thirds.append(low(left).astype(f32))
            left = left - thirds[-1]
        one = dot_t(low(jnp.concatenate(thirds, axis=0)), stuffing(parity, bf16))
        one = one[0:8] + one[8:16] + one[16:24]
        total = one if total is None else total + one
    return total


def first_row(values):
    row = lax.broadcasted_iota(jnp.int32, values.shape, 0)
    return jnp.where(row == 0, values, 0.0)


def time_front(info, table, at, embed, biases):
    def body(info_ref, embed_ref, bias_ref, one_ref, two_ref, out_ref, class_ref, kv_ref, *outs):
        inner, both, context_kv = outs
        spread = [stuffing(parity, bf16) for parity in range(2)]
        inner[...] = jnp.zeros_like(inner)
        hidden = []
        for j in range(2):
            pre = dot(low(embed_ref[8 * j : 8 * j + 8, :]), one_ref[...]) + bias_ref[j : j + 1]
            act = low(silu_in(pre))
            inner[0:1, WIDE * j : WIDE * (j + 1)] = pre[0:1]
            inner[2:3, WIDE * j : WIDE * (j + 1)] = act.astype(f32)[0:1]
            hidden.append(act)
        last = []
        for j in range(2):
            pre = bias_ref[2 + j : 3 + j]
            for p in range(2):
                wide = low(dot(hidden[p], spread[j]))
                pre = pre + dot(wide, two_ref[2 * WIDE * p : 2 * WIDE * (p + 1), :])
            act = low(silu_in(pre))
            inner[1:2, WIDE * j : WIDE * (j + 1)] = pre[0:1]
            inner[3:4, WIDE * j : WIDE * (j + 1)] = act.astype(f32)[0:1]
            last.append(act)
        time_vec = bias_ref[4:5]
        for p in range(2):
            time_vec = time_vec + dot(last[p], out_ref[WIDE * p : WIDE * (p + 1), :])
        row = lax.broadcasted_iota(jnp.int32, (8, WIDE), 0)
        rows = class_ref[...].astype(f32)
        class_vec = jnp.sum(jnp.where(row == lax.rem(info_ref[3], 8), rows, 0.0), axis=0, keepdims=True)
        context = jnp.where(row == 0, class_vec, jnp.where(row == 1, time_vec[0:1], 0.0))
        both[...] = context
        context = low(context)
        for j in range(2):
            wide = low(dot(context, spread[j]))
            context_kv[:, HALF * j : HALF * (j + 1)] = low(dot(wide, kv_ref[...]))

    operands = [
        embed,
        biases,
        Rows(at["w_t1"], 2 * TE),
        Rows(at["w_t2"], 2 * TD),
        Rows(at["w_tp"], TD),
        LabelRows(at["table"], 8),
        Rows(at["w_ckv"], 2 * C, side_columns=True),
    ]
    outs = [((8, 2 * WIDE), f32), ((8, WIDE), f32), ((8, WIDE), bf16)]
    return one_step(body, info, table, operands, outs, 2 * 8 * 4096 * WIDE)


def time_back(info, table, at, time_grad, inner, top, context_grad, squares):
    def body(info_ref, grad_ref, inner_ref, two_ref, out_ref, top_ref, context_ref, *rest):
        square_refs, (outs, bound_out) = (rest[:-2], rest[-2:])
        time_low = low(grad_ref[...])
        largest = lambda value: jnp.max(jnp.max(jnp.abs(value), axis=1, keepdims=True), axis=0, keepdims=True)

        def slope(values):
            logistic = 1.0 / (1.0 + jnp.exp(-values))
            return logistic * (1.0 + values * (1.0 - logistic))

        outs[...] = jnp.zeros_like(outs)
        two = []
        for p in range(2):
            cols = slice(WIDE * p, WIDE * (p + 1))
            grad = dot_t(time_low, out_ref[WIDE * p : WIDE * (p + 1), :])
            grad = first_row(grad * slope(inner_ref[1:2, cols]))
            outs[0:1, cols] = grad[0:1]
            two.append(low(grad))
        for p in range(2):
            cols = slice(WIDE * p, WIDE * (p + 1))
            rows = two_ref[2 * WIDE * p : 2 * WIDE * (p + 1), :]
            grad = unstuffed([dot_t(two[j], rows) for j in range(2)])
            outs[1:2, cols] = grad[0:1] * slope(inner_ref[0:1, cols])
        bound = largest(inner_ref[3:4, :]) * largest(time_low.astype(f32))
        bound = jnp.maximum(bound, largest(inner_ref[2:3, :]) * largest(outs[0:1, :]))
        bound = jnp.maximum(bound, largest(outs[1:2, :]))
        bound = jnp.maximum(1.02 * bound, largest(context_ref[0:1, :]))
        bound = jnp.maximum(bound, top_ref[...])
        lane = lax.broadcasted_iota(jnp.int32, (8, 128), 1)
        row = jnp.broadcast_to(bound, (8, 128))
        for i, (ref, (_, at_row)) in enumerate(zip(square_refs, squares)):
            row = jnp.where(lane == i + 1, largest(ref[at_row : at_row + 1, :]), row)
        bound_out[...] = row

    operands = [time_grad, inner, Rows(at["w_t2"], 2 * TD), Rows(at["w_tp"], TD), top, context_grad]
    operands += [one for one, _ in squares]
    outs = [((8, 2 * WIDE), f32), ((8, 128), f32)]
    return one_step(body, info, table, operands, outs, 2 * 8 * 3072 * WIDE)


def channel_mix():
    flat = np.arange(LC * C)[:, None]
    split = np.arange(LC * C)[None]
    return jnp.asarray((flat == LC * (split % C) + split // C).astype(ml_dtypes.bfloat16))


def gather_small(place, value):
    stride, joined = (1, value[None])
    while stride < place.count:
        other = place.swap(joined, stride)
        upper = (place.index // stride) % 2 == 1
        joined = jnp.where(
            upper,
            jnp.concatenate([other, joined], axis=0),
            jnp.concatenate([joined, other], axis=0),
        )
        stride *= 2
    return joined


def windows(values, turned, sign):
    width = values.shape[1]
    col = (lax.iota(jnp.int32, TOKENS) % FRAME)[:, None]
    zero_one = jnp.zeros((1, width), values.dtype)
    zero_row = jnp.zeros((FRAME, width), values.dtype)
    none = jnp.zeros((), values.dtype)
    across = {
        -1: jnp.where(col > 0, jnp.concatenate([zero_one, values[:-1]], axis=0), none),
        0: values,
        1: jnp.where(col < FRAME - 1, jnp.concatenate([values[1:], zero_one], axis=0), none),
    }
    moved = {}
    for col_off, value in across.items():
        moved[-1, col_off] = jnp.concatenate([zero_row, value[:-FRAME]], axis=0)
        moved[0, col_off] = value
        moved[1, col_off] = jnp.concatenate([value[FRAME:], zero_row], axis=0)
    out = []
    for row_off, col_off in tap_offsets:
        plain = moved[sign * row_off, sign * col_off]
        other = moved[sign * col_off, sign * row_off]
        out.append(plain if row_off == col_off else jnp.where(turned, other, plain))
    return jnp.concatenate(out, axis=1)


def frame_of(place, latents, target_noise, turned):
    both = jnp.concatenate([latents, target_noise], axis=-1)
    stride, joined = (1, both[None])
    while stride < place.rows:
        other = place.swap(joined, stride)
        upper = (place.index // stride) % 2 == 1
        joined = jnp.where(
            upper,
            jnp.concatenate([other, joined], axis=0),
            jnp.concatenate([joined, other], axis=0),
        )
        stride *= 2
    image = pick(joined, place.slot, 1).reshape(SIDE, SIDE, 2 * LC)
    portrait = image[:, :FRAME]
    landscape = jnp.transpose(image[:FRAME], (1, 0, 2))
    return jnp.where(turned, landscape, portrait).reshape(TOKENS, 2 * LC)


def train_step(place, store, table, vecs, latents, target_noise, label, step_value, orient, extent):
    half, at = (place.half, store.places)
    turned = orient != 1
    info = jnp.stack([place.side, turned.astype(jnp.int32), extent * FRAME, label]).astype(jnp.int32)
    mask = (lax.iota(jnp.int32, TOKENS) < extent * FRAME).astype(jnp.float32)[:, None]
    frame = frame_of(place, latents, target_noise, turned)
    share = noise_level(step_value)
    noisy = mask * (jnp.sqrt(share) * frame[:, :LC] + jnp.sqrt(1.0 - share) * frame[:, LC:])
    pad_in = windows(low(noisy), turned, 1)
    noise_rows = jnp.pad(frame[:, LC:].T, ((0, OUT_ROWS - LC), (0, 0)))
    embed_in = low(time_embed(step_value))[None]
    mix = channel_mix()
    row = lambda *names: jnp.stack([vecs[name] for name in names])
    side_rows = lambda *names: half(row(*names))

    def part(name, depth=C, **kind):
        return Rows(at[name], depth, **kind)

    def own_rows(name):
        return Rows(at[name], HALF, side_rows=True)

    qkv = unmix(info, table, at["w_qkv"], C, 3, HALF)
    ff1 = unmix(info, table, at["w_ff1"], C, 2 * FFI // WIDE, HALF)
    w_in = half(table[at["w_in"] : at["w_in"] + 9 * LC])
    w_out = dot(table[at["w_out"] : at["w_out"] + 9 * LC].reshape(9, LC * C), mix)
    w_out = low(jnp.pad(w_out.reshape(9, LC, C), ((0, 0), (0, OUT_ROWS - LC), (0, 0))))
    w_out = w_out.reshape(9 * OUT_ROWS, C)

    twice = jnp.repeat(embed_in.astype(jnp.float32), 2, axis=1)
    parity = lax.iota(jnp.int32, 2 * TE)[None] % 2
    stuffed = [jnp.pad(jnp.where(parity == j, twice, 0.0), ((0, 7), (0, 0))) for j in range(2)]
    biases = [vecs["b_t1"].reshape(2, WIDE), vecs["b_t2"].reshape(2, WIDE), vecs["b_tp"][None]]
    biases = jnp.pad(jnp.concatenate(biases, axis=0), ((0, 3), (0, 0)))
    inner, both, context_kv = time_front(info, table, at, jnp.concatenate(stuffed, axis=0), biases)
    context, time_vec = (low(both[:2]), both[1:2])
    hidden_one, hidden_two = (low(inner[2:3]), low(inner[3:4]))

    act_one, normed_one, inv_one, state_zero = first_forward(
        info, pad_in, w_in, side_rows("b_in", "g1", "bb1")
    )
    act_one_peer = place.swap(act_one)
    rows_two = side_rows("b_c1", "g2", "bb2")
    rows_two = jnp.concatenate([rows_two[0:1] + half(time_vec), rows_two[1:]], axis=0)
    act_two, normed_two, inv_two = conv_forward(
        info, act_one, act_one_peer, table, at["w_c1"], None, rows_two, True
    )
    act_two_peer = place.swap(act_two)
    token_own, normed_three, inv_three, state_one = conv_forward(
        info, act_two, act_two_peer, table, at["w_c2"], state_zero, side_rows("b_c2", "g3", "bb3"), False
    )
    token_in, resid_zero, ln_one, packed, attended_own = self_front(
        info, table, token_own, place.swap(token_own), part("w_pin"), row("b_pin", "n1g", "n1b"), qkv
    )
    attended, resid_one, ln_two, cross_query, cross_own = cross_front(
        info,
        table,
        attended_own,
        place.swap(attended_own),
        part("w_o"),
        row("b_o", "n2g", "n2b"),
        resid_zero,
        part("w_cq", side_columns=True),
        context_kv,
    )
    b_ff1 = half(vecs["b_ff1"].reshape(-1, WIDE)).reshape(1, FFI)
    cross_out, resid_two, ln_three, projected, gated_own = ff_front(
        info,
        table,
        cross_own,
        place.swap(cross_own),
        part("w_co"),
        row("b_co", "n3g", "n3b"),
        resid_one,
        ff1,
        b_ff1,
    )
    gated, out_in, state_own = ff_finish(
        info,
        table,
        gated_own,
        place.swap(gated_own),
        part("w_ff2", FFI),
        row("b_ff2"),
        resid_two,
        part("w_pout", side_columns=True),
        side_rows("b_pout"),
        state_one,
    )
    b_out = jnp.broadcast_to(jnp.pad(vecs["b_out"], (0, OUT_ROWS - LC))[:, None], (OUT_ROWS, 128))
    (
        w_out_grad,
        small_out,
        state_grad,
        pout_low,
        ff2_low,
        resid_grad,
        proj_low,
        ln_part,
        sums_out,
        sums_ff,
    ) = loss_back(
        info,
        table,
        state_own,
        place.swap(state_own),
        w_out,
        noise_rows,
        b_out,
        part("w_pout"),
        part("w_ff2", FFI),
        projected,
        ff1,
    )
    ln_peer = place.swap(ln_part)
    store.add("w_pout", out_in, pout_low)
    store.add("w_ff2", gated, ff2_low)
    store.add("w_ff1", ln_three, proj_low)
    w_out_grad = w_out_grad.reshape(9, OUT_ROWS, C)[:, :LC].reshape(9, LC * C)
    thirds, left = ([], w_out_grad)
    for _ in range(3):
        thirds.append(lax.reduce_precision(left, 8, 7))
        left = left - thirds[-1]
    thirds = dot_t(low(jnp.concatenate(thirds, axis=0)), mix)
    w_out_grad = thirds[:9] + thirds[9:18] + thirds[18:]
    w_out_grad = half(w_out_grad.reshape(9 * LC, C))
    store.put(at["w_out"], jnp.zeros((store.total - at["w_out"], HALF), jnp.float32))
    resid_grad, co_low, query_low, kv_grad, sums_co, context_grad = cross_back(
        info,
        table,
        ln_part,
        ln_peer,
        resid_two,
        row("n3g"),
        resid_grad,
        own_rows("w_co"),
        cross_query,
        context_kv,
        Rows(at["w_ckv"], 2 * C, side_columns=True),
    )
    query_peer = place.swap(query_low)
    kv_low = low(kv_grad[:2])
    context_grad = context_grad + place.swap(context_grad)
    store.add("w_co", cross_out, co_low)
    store.add("w_cq", ln_two, query_low)
    store.add("w_ckv", context, kv_low)
    resid_grad, o_low, packed_low, ln_part, sums_o = self_back(
        info,
        table,
        query_low,
        query_peer,
        part("w_cq"),
        resid_one,
        row("n2g"),
        resid_grad,
        own_rows("w_o"),
        packed,
        qkv,
    )
    ln_peer = place.swap(ln_part)
    store.add("w_o", attended, o_low)
    store.add("w_qkv", ln_one, packed_low)
    pin_low, state_grad, conv_low, sums_pin, sums_two = token_back(
        info,
        table,
        ln_part,
        ln_peer,
        resid_zero,
        row("n1g"),
        resid_grad,
        own_rows("w_pin"),
        normed_three,
        inv_three,
        side_rows("g3"),
        state_grad,
    )
    conv_peer = place.swap(conv_low)
    store.add("w_pin", token_in, pin_low)
    conv_low, sums_one = conv_backward(
        info,
        conv_low,
        conv_peer,
        act_two,
        act_two_peer,
        table,
        store,
        at["w_c2"],
        (normed_two, inv_two),
        side_rows("g2", "bb2"),
        None,
    )
    conv_peer = place.swap(conv_low)
    time_grad = place.full(sums_one[0:1]) + context_grad[1:2]
    b_tp = half(time_grad)
    time_low = low(time_grad)
    outer, bounds = time_back(
        info,
        table,
        at,
        jnp.pad(time_grad, ((0, 7), (0, 0))),
        inner,
        store.top,
        context_grad,
        ((inv_one, 1), (inv_two, 1), (sums_two, 3), (sums_one, 3)),
    )
    b_t2, b_t1 = (half(outer[0].reshape(-1, WIDE)), half(outer[1].reshape(-1, WIDE)))
    two_low, one_low = (low(b_t2), low(b_t1))
    largest = Largest(place, bounds)
    store.add("w_tp", hidden_two, half(time_low))
    store.buffer = largest.exchange(store.buffer)
    store.add("w_t2", hidden_one, two_low.reshape(1, -1))
    store.buffer = largest.exchange(store.buffer)
    store.add("w_t1", embed_in, one_low.reshape(1, -1))
    chosen = lax.iota(jnp.int32, NCLS)[:, None] == label
    store.put(at["table"], jnp.where(chosen, half(context_grad[0:1]), 0.0))
    store.put(0, jnp.zeros((at["w_t1"], HALF), jnp.float32))
    store.buffer = largest.exchange(store.buffer)
    in_low, sums_in = conv_backward(
        info,
        conv_low,
        conv_peer,
        act_one,
        act_one_peer,
        table,
        store,
        at["w_c1"],
        (normed_one, inv_one),
        side_rows("g1", "bb1"),
        state_grad,
    )
    store.buffer = largest.exchange(store.buffer)
    tops = largest.finish()[0]
    bound = jnp.maximum(tops[0], 1.01 * jnp.sqrt(tops[1] * tops[4]))
    bound = jnp.maximum(bound, 1.01 * jnp.sqrt(tops[2] * tops[3]))
    scale = (WIRE_TOP / (place.count // 2)) / jnp.maximum(bound, 1e-30)
    w_in_grad = t_dot(pad_in, in_low)
    small = [b_t1, b_t2, b_tp, sums_in[:3], sums_one[:3], sums_two[:3], sums_pin[:3], sums_o[:3]]
    small += [sums_co[:3], sums_ff, sums_out[:2]]
    extra = [small_out[:LC, 0], small_out[0:1, 128], (extent * FRAME).astype(jnp.float32)[None]]
    extra = jnp.pad(jnp.concatenate(extra), (0, HALF - LC - 2))[None]
    return (jnp.concatenate(small + [extra, w_in_grad, w_out_grad], axis=0), scale)


def adam_update(params, first_mom, second, gradient, decay_rate):
    first_new = adam_one * first_mom + (1.0 - adam_one) * gradient
    second_new = adam_two * second + (1.0 - adam_two) * gradient * gradient
    step_size = (
        first_new
        / (1.0 - adam_one**STEP)
        / (jnp.sqrt(second_new / (1.0 - adam_two**STEP)) + adam_eps)
    )
    return (params - learn_rate * (step_size + decay_rate * params), first_new, second_new)


def local(
    latents,
    target_noise,
    labels,
    timesteps,
    orient,
    extent,
    mat_params,
    mat_first,
    mat_second,
    mat_ema,
    vec_params,
    vec_first,
    vec_second,
    vec_ema,
):
    place = Place()
    length = mat_params.shape[0]
    rows = shard_rows(length * place.count, place.count)
    block = to_blocks(place, mat_params.astype(jnp.bfloat16), rows)
    table = lax.all_gather(block, ("dp", "rows"), axis=0, tiled=True)
    vec_len = vec_params.shape[0]
    vec_wide = -(-vec_len // 128) * 128
    padded = jnp.pad(vec_params, (0, vec_wide - vec_len)).reshape(-1, 128)
    vec_all = gather_small(place, padded).reshape(place.count, vec_wide)[:, :vec_len]
    vec_all = vec_all.reshape(-1).astype(jnp.bfloat16).astype(jnp.float32)
    vecs = unpack(vec_all, vec_layout())
    own = lambda values: pick(values, place.slot, 0)
    store = Store(place, rows)
    small, scale = train_step(
        place,
        store,
        table,
        vecs,
        latents,
        target_noise,
        own(labels),
        own(timesteps),
        own(orient),
        own(extent),
    )
    block_grad, square = scatter_sum(place, store.buffer, scale, rows)
    small = jnp.pad(small, ((0, -small.shape[0] % 8), (0, 0)))
    body = sum(record[1] for record in vec_layout()[:-1]) // WIDE
    lane = lax.broadcasted_iota(jnp.int32, small.shape, 1)
    line = lax.broadcasted_iota(jnp.int32, small.shape, 0)
    small = jnp.where((lane == SQUARE_AT) & (line == body), square, small)
    small = place.full(place.chip_sum(small))
    loss_sum, pixel_count = (small[body, LC], small[body, LC + 1])
    vec_flat = jnp.concatenate([small[:body].reshape(-1), small[body, :LC]])
    vec_flat = jnp.pad(vec_flat, (0, vec_len * place.count - vec_flat.shape[0]))
    shard_vec = lax.dynamic_slice(vec_flat, (vec_len * place.index,), (vec_len,))
    square = small[body, SQUARE_AT] + small[body, HALF + SQUARE_AT] + jnp.sum(vec_flat * vec_flat)
    shard_mat = from_blocks(place, block_grad, length)
    for i, name in enumerate(("w_in", "w_out")):
        values = small[body + 1 + 9 * LC * i : body + 1 + 9 * LC * (i + 1)]
        square = square + jnp.sum(values * values)
        owner, offset = divmod((store.places[name] - LEAD) * WIDE, length)
        old = lax.dynamic_slice(shard_mat, (offset,), (9 * LC * C,))
        new = jnp.where(place.index == owner, values.reshape(-1), old)
        shard_mat = lax.dynamic_update_slice(shard_mat, new, (offset,))
    inverse = 1.0 / pixel_count
    grad_norm = jnp.sqrt(square) * inverse
    factor = clip_norm / jnp.maximum(grad_norm, clip_norm) * inverse
    new_mat, mat_first_new, mat_second_new = adam_update(
        mat_params, mat_first, mat_second, shard_mat * factor, weight_decay
    )
    new_vec, vec_first_new, vec_second_new = adam_update(
        vec_params, vec_first, vec_second, shard_vec * factor, 0.0
    )
    ema_rate = min(ema_ceiling, (1.0 + STEP) / (10.0 + STEP))
    mat_ema_new = ema_rate * mat_ema + (1.0 - ema_rate) * new_mat
    vec_ema_new = ema_rate * vec_ema + (1.0 - ema_rate) * new_vec
    return (
        new_mat,
        mat_first_new,
        mat_second_new,
        mat_ema_new,
        new_vec,
        vec_first_new,
        vec_second_new,
        vec_ema_new,
        grad_norm,
        loss_sum,
        pixel_count,
    )


def solution(mesh):
    return jax.shard_map(
        local,
        mesh=mesh,
        in_specs=(
            P("dp", "rows", None, None),
            P("dp", "rows", None, None),
            P("dp"),
            P("dp"),
            P("dp"),
            P("dp"),
            P(("dp", "rows")),
            P(("dp", "rows")),
            P(("dp", "rows")),
            P(("dp", "rows")),
            P(("dp", "rows")),
            P(("dp", "rows")),
            P(("dp", "rows")),
            P(("dp", "rows")),
        ),
        out_specs=(
            P(("dp", "rows")),
            P(("dp", "rows")),
            P(("dp", "rows")),
            P(("dp", "rows")),
            P(("dp", "rows")),
            P(("dp", "rows")),
            P(("dp", "rows")),
            P(("dp", "rows")),
            P(),
            P(),
            P(),
        ),
        check_vma=False,
    )
```
